32 devices in a mesh: groups: 2 (over x), tile: 16 (over z, y, core).
Axes of the slice: x: 2, y: 2, z: 4, core: 2. Of those that a mesh axis runs over, the one named last changes fastest.
Arguments:
- grid_nodes: bfloat16 [8192, 512], P(('groups', 'tile')), parts along dimension 0, may hold values from -6 to 6
- mesh_nodes: bfloat16 [2048, 512], P(('groups', 'tile')), parts along dimension 0, may hold values from -6 to 6
- enc_edges: bfloat16 [12288, 512], P(('groups', 'tile')), parts along dimension 0, may hold values from -6 to 6
- dec_edges: bfloat16 [24576, 512], P(('groups', 'tile')), parts along dimension 0, may hold values from -6 to 6
- grid_cot: bfloat16 [8192, 512], P(('groups', 'tile')), parts along dimension 0, may hold values from -6 to 6
- mesh_cot: bfloat16 [2048, 512], P(('groups', 'tile')), parts along dimension 0, may hold values from -6 to 6
- enc_first: bfloat16 [1536, 512], replicated, may hold values from -0.15625 to 0.15625
- enc_second: bfloat16 [512, 512], replicated, may hold values from -0.25 to 0.25
- mesh_first: bfloat16 [1024, 512], replicated, may hold values from -0.1875 to 0.1875
- mesh_second: bfloat16 [512, 512], replicated, may hold values from -0.25 to 0.25
- dec_first: bfloat16 [1536, 512], replicated, may hold values from -0.15625 to 0.15625
- dec_second: bfloat16 [512, 512], replicated, may hold values from -0.25 to 0.25
- grid_first: bfloat16 [1024, 512], replicated, may hold values from -0.1875 to 0.1875
- grid_second: bfloat16 [512, 512], replicated, may hold values from -0.25 to 0.25
- send_index: int32 [288, 16], P(('groups', 'tile')), parts along dimension 0, may hold values from 0 to 255, as said below
- send_count: int32 [288], P(('groups', 'tile')), parts along dimension 0, may hold values from 4 to 16, as said below
- enc_grid: int32 [12288], P(('groups', 'tile')), parts along dimension 0, may hold values from 0 to 399, as said below
- enc_mesh: int32 [12288], P(('groups', 'tile')), parts along dimension 0, may hold values from 0 to 63
- dec_grid: int32 [24576], P(('groups', 'tile')), parts along dimension 0, may hold values from 0 to 399, as said below
- dec_mesh: int32 [24576], P(('groups', 'tile')), parts along dimension 0, may hold values from 0 to 63
Outputs:
- grid_out: bfloat16 [8192, 512], P(('groups', 'tile')), parts along dimension 0
- mesh_out: bfloat16 [2048, 512], P(('groups', 'tile')), parts along dimension 0
- grad_grid: float32 [8192, 512], P(('groups', 'tile')), parts along dimension 0
- grad_mesh: float32 [2048, 512], P(('groups', 'tile')), parts along dimension 0
The draws below stay inside these ranges and needn't reach their ends.
There are 2 independent parts, one for each index of `groups`. The reference program is written for one: setup_inputs(seed, part) draws one part's arguments, and reference() takes and returns one part's arrays. A program takes and returns all parts, laid end to end along the dimension named above; an argument that names none is the same for every part. Nothing has to cross between parts.
Inputs may be any that keep to these rules, and one draw needn't show every extreme that they name: `send_index`: row s * 9 + j holds distinct local grid rows of device s for its neighbour (s + o_j) mod 16; entries from send_count[s * 9 + j] on carry no row; no row of a device goes to two neighbours. `send_count`: rows from device s to its neighbour j; the count from (s + o_j) mod 16 back to s is the same, under entry (j + 4) mod 8 for j < 8 and under entry 8 for j = 8; in every draw one device receives 16 rows from each of its nine neighbours. `enc_grid`: a spot of the edge's device that is live; every live slot of a device is named by exactly one of its encoder edges. `dec_grid`: a spot of the edge's device that is live; every live slot of a device is named by exactly one of its decoder edges, and every grid node has exactly three decoder edges over all devices. `enc_mesh`: the encoder edge's mesh node among the 64 of the edge's device. `dec_mesh`: the decoder edge's mesh node among the 64 of the edge's device.
All inputs are finite; a program needn't handle non-finite values.
Results may differ from the reference program's by a relative error of at most 0.01.
Values may be sent and summed in bfloat16 or wider, within the bound.
No kernel may reach another device: no remote copies, remote signals or barrier semaphores. Data moves between devices by JAX's collectives and lax.ppermute only.
A program may use at most 128 MiB of HBM per device.

```python
import jax
import jax.numpy as jnp
from jax import lax

D = 512
GRID_DEV = 256
MESH_DEV = 64
CAP = 16
TW = 4
ENC_DEV = 384
DEC_DEV = 768
GRID = 4096
MESH = 1024
ENC = 6144
DEC = 12288
N_TILE = 16


def neighbour_offsets_drawn(peer_count):
    forward_half = [1, TW, TW + 1, TW - 1]
    return forward_half + [-offset for offset in forward_half] + [peer_count // 2]


def plan_tables(key):
    count_key = jax.random.fold_in(key, 17)
    forward_half = neighbour_offsets_drawn(N_TILE)[:4]
    half_count = N_TILE // 2
    base_counts = jax.random.randint(count_key, (N_TILE, 4), max(1, CAP // 4), CAP + 1)
    busiest = jax.random.randint(jax.random.fold_in(count_key, 1), (), 0, N_TILE)
    devices = jnp.arange(N_TILE)
    forced = jnp.stack([(devices == busiest) | (devices == (busiest - offset) % N_TILE) for offset in forward_half], axis=1)
    base_counts = jnp.where(forced, CAP, base_counts)
    backward_half = jnp.stack([jnp.roll(base_counts[:, column], offset) for column, offset in enumerate(forward_half)], axis=1)
    across_half = jax.random.randint(jax.random.fold_in(count_key, 2), (half_count,), max(1, CAP // 4), CAP + 1)
    across_half = jnp.where(jnp.arange(half_count) == busiest % half_count, CAP, across_half)
    across = jnp.concatenate([across_half, across_half])[:, None]
    counts = jnp.concatenate([base_counts, backward_half, across], axis=1).astype(jnp.int32)
    row_keys = jax.random.split(jax.random.fold_in(key, 23), N_TILE)
    orders = jax.vmap(lambda row_key: jax.random.permutation(row_key, GRID_DEV))(row_keys).astype(jnp.int32)
    return (counts, orders)


def received_live(counts):
    offsets = neighbour_offsets_drawn(N_TILE)
    incoming = jnp.stack([jnp.roll(counts[:, column], offset) for column, offset in enumerate(offsets)], axis=1)
    slot_iota = jnp.arange(CAP)[None, None, :]
    return (slot_iota < incoming[:, :, None]).reshape(N_TILE, 9 * CAP)


def permutations(key, length):
    row_keys = jax.random.split(key, N_TILE)
    return jax.vmap(lambda row_key: jax.random.permutation(row_key, length))(row_keys).astype(jnp.int32)


def compact_slots(slot_live):
    return jnp.argsort(1 - slot_live.astype(jnp.int32), axis=1, stable=True).astype(jnp.int32)


def draw_send_count(key, part):
    counts, orders = plan_tables(key)
    return counts.reshape(-1).astype(jnp.int32)


def draw_send_index(key, part):
    counts, orders = plan_tables(key)
    return orders[:, :9 * CAP].reshape(N_TILE * 9, CAP).astype(jnp.int32)


def draw_enc_grid(key, part):
    counts, orders = plan_tables(key)
    key = jax.random.fold_in(key, 5)
    slot_live = received_live(counts)
    received = jnp.sum(slot_live.astype(jnp.int32), axis=1)
    compact = compact_slots(slot_live)
    local_order = permutations(jax.random.fold_in(key, 1), GRID_DEV)
    edge_order = permutations(jax.random.fold_in(key, 2), ENC_DEV)
    edge_iota = jnp.broadcast_to(jnp.arange(ENC_DEV, dtype=jnp.int32)[None, :], (N_TILE, ENC_DEV))
    slot_pick = jnp.take_along_axis(compact, jnp.minimum(edge_iota, 9 * CAP - 1), axis=1) + GRID_DEV
    local_pick = jnp.take_along_axis(local_order, (edge_iota - received[:, None]) % GRID_DEV, axis=1)
    listed = jnp.where(edge_iota < received[:, None], slot_pick, local_pick)
    return jnp.take_along_axis(listed, edge_order, axis=1).reshape(-1).astype(jnp.int32)


def draw_dec_grid(key, part):
    counts, orders = plan_tables(key)
    key = jax.random.fold_in(key, 9)
    slot_live = received_live(counts)
    received = jnp.sum(slot_live.astype(jnp.int32), axis=1)
    compact = compact_slots(slot_live)
    send_slots = 9 * CAP
    send_live = jnp.arange(send_slots)[None, :] % CAP < jnp.repeat(counts, CAP, axis=1)
    device_rows = jnp.broadcast_to(jnp.arange(N_TILE)[:, None], (N_TILE, send_slots))
    sent = jnp.zeros((N_TILE, GRID_DEV), jnp.int32).at[device_rows, orders[:, :send_slots]].set(send_live.astype(jnp.int32))
    unsent_first = jnp.argsort(sent, axis=1, stable=True).astype(jnp.int32)
    pair_order = permutations(jax.random.fold_in(key, 1), GRID_DEV)
    edge_order = permutations(jax.random.fold_in(key, 2), DEC_DEV)
    edge_iota = jnp.broadcast_to(jnp.arange(DEC_DEV, dtype=jnp.int32)[None, :], (N_TILE, DEC_DEV))
    local_index = edge_iota - received[:, None]
    doubled = jnp.take_along_axis(pair_order, jnp.clip(local_index // 2, 0, GRID_DEV - 1), axis=1)
    single = jnp.take_along_axis(unsent_first, jnp.clip(local_index - 2 * GRID_DEV, 0, GRID_DEV - 1), axis=1)
    slot_pick = jnp.take_along_axis(compact, jnp.minimum(edge_iota, send_slots - 1), axis=1) + GRID_DEV
    listed = jnp.where(edge_iota < received[:, None], slot_pick, jnp.where(local_index < 2 * GRID_DEV, doubled, single))
    return jnp.take_along_axis(listed, edge_order, axis=1).reshape(-1).astype(jnp.int32)


def with_ends(drawn, stream_key, low, high):
    dims = drawn.shape
    place = [jax.random.randint(jax.random.fold_in(stream_key, axis), (), 0, dims[axis]) for axis in range(len(dims))]
    drawn = drawn.at[tuple(place)].set(low)
    longest = dims.index(max(dims))
    place[longest] = (place[longest] + 1) % dims[longest]
    return drawn.at[tuple(place)].set(high)


def level_of(key, dims, shards, least, high):
    level = 1.0
    for dim, shards_of in shards:
        heights = jax.random.uniform(jax.random.fold_in(jax.random.fold_in(key, 6), dim), (shards_of,), jnp.float32, least / len(shards), high / len(shards))
        level = level * jnp.repeat(jnp.exp(heights), dims[dim] // shards_of).reshape((-1,) + (1,) * (len(dims) - 1 - dim))
    return level


def centred(rng, extent, spread, limit, pieces=(), kind=jnp.bfloat16):
    values = spread * jax.random.normal(rng, extent, jnp.float32)
    if pieces:
        values = values * level_of(rng, extent, pieces, -0.22, 0.18)
    return jnp.clip(values, -limit, limit).astype(kind)


def setup_inputs(seed: int = 0, part: int = 0) -> dict:
    seeds = jax.random.split(jax.random.key(seed), 21)
    part_keys = jax.random.split(jax.random.fold_in(seeds[20], part), 21)
    return {
        "grid_nodes": centred(part_keys[0], (GRID, D), 1.0, 6.0, ((0, 16),)),
        "mesh_nodes": centred(part_keys[1], (MESH, D), 1.0, 6.0, ((0, 16),)),
        "enc_edges": centred(part_keys[2], (ENC, D), 1.0, 6.0, ((0, 16),)),
        "dec_edges": centred(part_keys[3], (DEC, D), 1.0, 6.0, ((0, 16),)),
        "grid_cot": centred(part_keys[4], (GRID, D), 1.0, 6.0, ((0, 16),)),
        "mesh_cot": centred(part_keys[5], (MESH, D), 1.0, 6.0, ((0, 16),)),
        "enc_first": centred(seeds[6], (3 * D, D), (3 * D) ** -0.5, 0.15625),
        "enc_second": centred(seeds[7], (D, D), D ** -0.5, 0.25),
        "mesh_first": centred(seeds[8], (2 * D, D), (2 * D) ** -0.5, 0.1875),
        "mesh_second": centred(seeds[9], (D, D), D ** -0.5, 0.25),
        "dec_first": centred(seeds[10], (3 * D, D), (3 * D) ** -0.5, 0.15625),
        "dec_second": centred(seeds[11], (D, D), D ** -0.5, 0.25),
        "grid_first": centred(seeds[12], (2 * D, D), (2 * D) ** -0.5, 0.1875),
        "grid_second": centred(seeds[13], (D, D), D ** -0.5, 0.25),
        "send_index": draw_send_index(jax.random.fold_in(jax.random.fold_in(seeds[20], part), 71), part),
        "send_count": draw_send_count(jax.random.fold_in(jax.random.fold_in(seeds[20], part), 71), part),
        "enc_grid": draw_enc_grid(jax.random.fold_in(jax.random.fold_in(seeds[20], part), 71), part),
        "enc_mesh": with_ends(jax.random.randint(part_keys[17], (ENC,), 0, MESH_DEV), jax.random.fold_in(part_keys[17], 1), 0, MESH_DEV - 1).astype(jnp.int32),
        "dec_grid": draw_dec_grid(jax.random.fold_in(jax.random.fold_in(seeds[20], part), 71), part),
        "dec_mesh": with_ends(jax.random.randint(part_keys[19], (DEC,), 0, MESH_DEV), jax.random.fold_in(part_keys[19], 1), 0, MESH_DEV - 1).astype(jnp.int32),
    }


def mixed_dot(left, right):
    return jnp.dot(left, right, preferred_element_type=jnp.float32)

def back_dot(left, right):
    return lax.dot_general(left, right, (((1,), (1,)), ((), ())), preferred_element_type=jnp.float32)

def exact_back(left, right):
    return lax.dot_general(left, right.astype(jnp.float32), (((1,), (1,)), ((), ())), precision=lax.Precision.HIGHEST, preferred_element_type=jnp.float32)

def normalize(values):
    centre = values - lax.optimization_barrier(jnp.mean(values, axis=-1, keepdims=True))
    scale_inv = lax.rsqrt(lax.optimization_barrier(jnp.mean(centre * centre, axis=-1, keepdims=True)) + 1e-05)
    return (centre * scale_inv, scale_inv)

def normalize_back(normed, scale_inv, upstream):
    return scale_inv * (upstream - lax.optimization_barrier(jnp.mean(upstream, axis=-1, keepdims=True)) - normed * lax.optimization_barrier(jnp.mean(upstream * normed, axis=-1, keepdims=True)))

def swish_slope(values):
    sigmoid = jax.nn.sigmoid(values)
    return sigmoid * (1.0 + values * (1.0 - sigmoid))

def neighbour_offsets(peer_count):
    forward_half = [1, TW, TW + 1, TW - 1]
    return forward_half + [-offset for offset in forward_half] + [peer_count // 2]

def node_forward(node_rows, incoming, first, second):
    features = node_rows.shape[1]
    pre_node = mixed_dot(node_rows, first[:features]) + mixed_dot(incoming, first[features:])
    act_node = jax.nn.silu(pre_node).astype(jnp.bfloat16)
    normed, scale_inv = normalize(mixed_dot(act_node, second))
    updated = (node_rows.astype(jnp.float32) + normed).astype(jnp.bfloat16)
    return (updated, (pre_node, normed, scale_inv))

def node_backward(stored, upstream, first, second):
    pre_node, normed, scale_inv = stored
    features = upstream.shape[1]
    grad_out = normalize_back(normed, scale_inv, upstream).astype(jnp.bfloat16)
    grad_pre = (back_dot(grad_out, second) * swish_slope(pre_node)).astype(jnp.bfloat16)
    return (upstream + back_dot(grad_pre, first[:features]), back_dot(grad_pre, first[features:]))

def edge_forward(spot_rows, mesh_proj, edge_rows, edge_weight, second, spot_ids, mesh_ids):
    pre_edge = spot_rows[spot_ids].astype(jnp.float32) + mesh_proj[mesh_ids] + mixed_dot(edge_rows, edge_weight)
    act_edge = jax.nn.silu(pre_edge).astype(jnp.bfloat16)
    normed, scale_inv = normalize(mixed_dot(act_edge, second))
    return (normed, (pre_edge, normed, scale_inv))

def edge_backward(stored, upstream, second):
    pre_edge, normed, scale_inv = stored
    grad_out = normalize_back(normed, scale_inv, upstream).astype(jnp.bfloat16)
    return back_dot(grad_out, second) * swish_slope(pre_edge)

def reference(grid_nodes, mesh_nodes, enc_edges, dec_edges, grid_cot, mesh_cot, enc_first, enc_second, mesh_first, mesh_second, dec_first, dec_second, grid_first, grid_second, send_index, send_count, enc_grid, enc_mesh, dec_grid, dec_mesh):
    features = D
    offsets = neighbour_offsets(N_TILE)
    link_count = len(offsets)
    slot_total = link_count * CAP
    spot_count = GRID_DEV + slot_total
    send_plan = send_index.reshape(N_TILE, link_count, CAP)
    counts = send_count.reshape(N_TILE, link_count)
    devices = jnp.arange(N_TILE, dtype=jnp.int32)
    senders = jnp.stack([(devices - offset) % N_TILE for offset in offsets], axis=1)
    link_ids = jnp.arange(link_count, dtype=jnp.int32)[None, :]
    blocks = send_plan[senders, link_ids]
    block_counts = counts[senders, link_ids]
    slot_rows = (senders[:, :, None] * GRID_DEV + blocks).reshape(N_TILE, slot_total)
    slot_live = (jnp.arange(CAP, dtype=jnp.int32)[None, None, :] < block_counts[:, :, None]).reshape(N_TILE, slot_total)
    own_rows = devices[:, None] * GRID_DEV + jnp.arange(GRID_DEV, dtype=jnp.int32)[None, :]
    position = jnp.concatenate([own_rows, slot_rows], axis=1)
    spot_live = jnp.concatenate([jnp.ones((N_TILE, GRID_DEV), dtype=bool), slot_live], axis=1)
    zero_row = jnp.zeros((), jnp.bfloat16)
    enc_proj = mixed_dot(grid_nodes, enc_first[:features]).astype(jnp.bfloat16)
    dec_proj = mixed_dot(grid_nodes, dec_first[:features]).astype(jnp.bfloat16)
    mesh_blocks = mesh_nodes.reshape(N_TILE, MESH_DEV, features)
    enc_blocks = enc_edges.reshape(N_TILE, ENC_DEV, features)
    dec_blocks = dec_edges.reshape(N_TILE, DEC_DEV, features)
    enc_spots = enc_grid.reshape(N_TILE, ENC_DEV)
    enc_nodes = enc_mesh.reshape(N_TILE, ENC_DEV)
    dec_spots = dec_grid.reshape(N_TILE, DEC_DEV)
    dec_nodes = dec_mesh.reshape(N_TILE, DEC_DEV)
    mesh_cots = mesh_cot.reshape(N_TILE, MESH_DEV, features)

    def forward_side(inputs):
        spot_ids, spot_flags, mesh_rows, enc_rows, dec_rows, enc_ids, enc_targets, dec_ids, dec_sources = inputs
        pe_rows = jnp.where(spot_flags[:, None], enc_proj[spot_ids], zero_row)
        pd_rows = jnp.where(spot_flags[:, None], dec_proj[spot_ids], zero_row)
        enc_msg, enc_stored = edge_forward(pe_rows, mixed_dot(mesh_rows, enc_first[features:2 * features]), enc_rows, enc_first[2 * features:], enc_second, enc_ids, enc_targets)
        mesh_agg = jax.ops.segment_sum(enc_msg, enc_targets, num_segments=MESH_DEV).astype(jnp.bfloat16)
        mesh_out, mesh_stored = node_forward(mesh_rows, mesh_agg, mesh_first, mesh_second)
        dec_msg, dec_stored = edge_forward(pd_rows, mixed_dot(mesh_out, dec_first[features:2 * features]), dec_rows, dec_first[2 * features:], dec_second, dec_ids, dec_sources)
        spot_msgs = jax.ops.segment_sum(dec_msg, dec_ids, num_segments=spot_count)
        return (mesh_out, spot_msgs, (enc_stored, mesh_stored, dec_stored))

    def forward_only(inputs):
        mesh_out, spot_msgs, unused = forward_side(inputs)
        return (mesh_out, spot_msgs[:GRID_DEV], spot_msgs[GRID_DEV:].astype(jnp.bfloat16))
    side_inputs = (position, spot_live, mesh_blocks, enc_blocks, dec_blocks, enc_spots, enc_nodes, dec_spots, dec_nodes)
    mesh_parts, local_msgs, slot_msgs = lax.map(forward_only, side_inputs)
    flat_slots = slot_rows.reshape(-1)
    live_flat = slot_live.reshape(-1, 1)
    grid_sum = local_msgs.reshape(-1, features) + jnp.zeros((N_TILE * GRID_DEV, features), jnp.float32).at[flat_slots].add(jnp.where(live_flat, slot_msgs.reshape(-1, features).astype(jnp.float32), 0.0))
    grid_out, grid_stored = node_forward(grid_nodes, grid_sum.astype(jnp.bfloat16), grid_first, grid_second)
    grid_grow, grid_gagg = node_backward(grid_stored, grid_cot.astype(jnp.float32), grid_first, grid_second)
    grad_proj = grid_gagg.astype(jnp.bfloat16)

    def backward_side(inputs):
        spot_ids, spot_flags = (inputs[0], inputs[1])
        enc_ids, enc_targets, dec_ids, dec_sources = (inputs[5], inputs[6], inputs[7], inputs[8])
        cot_rows = inputs[9]
        mesh_out, unused, stored_all = forward_side(inputs[:9])
        enc_stored, mesh_stored, dec_stored = stored_all
        grad_rows = jnp.where(spot_flags[:, None], grad_proj[spot_ids], zero_row)
        dec_gpre = edge_backward(dec_stored, grad_rows[dec_ids].astype(jnp.float32), dec_second)
        spot_gpd = jax.ops.segment_sum(dec_gpre, dec_ids, num_segments=spot_count)
        mesh_gin = cot_rows.astype(jnp.float32) + exact_back(jax.ops.segment_sum(dec_gpre, dec_sources, num_segments=MESH_DEV), dec_first[features:2 * features])
        mesh_grow, mesh_gagg = node_backward(mesh_stored, mesh_gin, mesh_first, mesh_second)
        enc_gpre = edge_backward(enc_stored, mesh_gagg[enc_targets], enc_second)
        spot_gpe = jax.ops.segment_sum(enc_gpre, enc_ids, num_segments=spot_count)
        grad_mesh = mesh_grow + exact_back(jax.ops.segment_sum(enc_gpre, enc_targets, num_segments=MESH_DEV), enc_first[features:2 * features])
        spot_grads = exact_back(spot_gpe, enc_first[:features]) + exact_back(spot_gpd, dec_first[:features])
        return (grad_mesh, spot_grads)
    grad_parts, spot_grads = lax.map(backward_side, side_inputs + (mesh_cots,))
    node_grads = spot_grads[:, :GRID_DEV].reshape(-1, features) + jnp.zeros((N_TILE * GRID_DEV, features), jnp.float32).at[flat_slots].add(jnp.where(live_flat, spot_grads[:, GRID_DEV:].reshape(-1, features), 0.0))
    grad_grid = grid_grow + node_grads
    return (grid_out, mesh_parts.reshape(-1, features), grad_grid, grad_parts.reshape(-1, features))
```

```python
import jax
import jax.numpy as jnp
from jax import lax
from jax.experimental import pallas as pl
from jax.experimental.pallas import tpu as pltpu
from jax.sharding import PartitionSpec as P

TW = 4
CHUNK = 32
F32 = jnp.float32
BF16 = jnp.bfloat16
VMEM_LIMIT = 30 * 1024 * 1024


def mm(left, right):
    return jnp.dot(left, right, preferred_element_type=F32)


def mm_t(left, right):
    return lax.dot_general(left, right, (((1,), (1,)), ((), ())), preferred_element_type=F32)


def sigmoid(values):
    return 0.5 * jnp.tanh(0.5 * values) + 0.5


def norm_rows(values):
    centre = values - jnp.mean(values, axis=-1, keepdims=True)
    scale_inv = lax.rsqrt(jnp.mean(centre * centre, axis=-1, keepdims=True) + 1e-05)
    return centre * scale_inv, scale_inv


def norm_back(normed, scale_inv, upstream):
    return scale_inv * (
        upstream
        - jnp.mean(upstream, axis=-1, keepdims=True)
        - normed * jnp.mean(upstream * normed, axis=-1, keepdims=True)
    )


def row_chunks(rows, size=CHUNK):
    return [slice(start, min(start + size, rows)) for start in range(0, rows, size)]


def activate(pre, act_ref, slope_ref):
    for rows in row_chunks(pre.shape[0]):
        part = pre[rows, :]
        gate = sigmoid(part)
        act = part * gate
        act_ref[rows, :] = act.astype(BF16)
        slope_ref[rows, :] = (gate + act * (1.0 - gate)).astype(BF16)


def norm_forward(raw, normed_ref, scale_ref):
    for rows in row_chunks(raw.shape[0]):
        normed, scale_inv = norm_rows(raw[rows, :])
        normed_ref[rows, :] = normed.astype(normed_ref.dtype)
        scale_ref[rows, :] = scale_inv


def norm_backward(normed_ref, scale_ref, upstream, out_ref):
    for rows in row_chunks(out_ref.shape[0]):
        out_ref[rows, :] = norm_back(
            normed_ref[rows, :].astype(F32), scale_ref[rows, :], upstream[rows, :].astype(F32)
        ).astype(BF16)


def times_slope(raw, slope_ref, out_ref):
    for rows in row_chunks(out_ref.shape[0]):
        out_ref[rows, :] = (raw[rows, :] * slope_ref[rows, :].astype(F32)).astype(BF16)


def stack(refs, columns):
    return jnp.concatenate([ref[:, columns] for ref in refs], axis=0)


def neighbour_offsets(peer_count):
    forward_half = [1, TW, TW + 1, TW - 1]
    return forward_half + [-offset for offset in forward_half] + [peer_count // 2]


def onehot_pair(spot_ref, mesh_ref, spots, by_edge_ref, by_spot_ref):
    edges, total = by_edge_ref.shape
    spot_row = spot_ref[...].astype(F32)
    mesh_row = mesh_ref[...].astype(F32) + float(spots)
    for rows in row_chunks(total, 64):
        ids = lax.broadcasted_iota(jnp.int32, (rows.stop - rows.start, edges), 0) + rows.start
        ids = ids.astype(F32)
        hit = (ids == spot_row) | (ids == mesh_row)
        by_spot_ref[rows, :] = jnp.where(hit, 1.0, 0.0).astype(BF16)
    for rows in row_chunks(edges, 128):
        spot_col = jnp.broadcast_to(spot_row[:, rows], (128, 128)).T
        mesh_col = jnp.broadcast_to(mesh_row[:, rows], (128, 128)).T
        for columns in row_chunks(total, 128):
            ids = lax.broadcasted_iota(jnp.int32, (128, 128), 1) + columns.start
            ids = ids.astype(F32)
            hit = (ids == spot_col) | (ids == mesh_col)
            by_edge_ref[rows, columns] = jnp.where(hit, 1.0, 0.0).astype(BF16)


class Fetched:
    def __init__(self, source, target, semaphore):
        self.copy = pltpu.make_async_copy(source, target, semaphore)
        self.target = target
        self.landed = False
        self.copy.start()

    def land(self):
        if not self.landed:
            self.copy.wait()
            self.landed = True

    def __getitem__(self, key):
        self.land()
        return self.target[key]


def call(body, name, inputs, outputs, scratch=(), flops=0):
    arrays, specs, moved, fetches = [], [], 0, []
    for place, entry in enumerate(inputs):
        if isinstance(entry, tuple):
            array, first, rows = entry
            specs.append(pl.BlockSpec(memory_space=pl.ANY))
            fetches.append((place, first, rows, (rows, array.shape[1]), array.dtype))
            moved += rows * array.shape[1] * array.dtype.itemsize
        else:
            array = entry
            smem = array.dtype == jnp.int32 and array.ndim == 1
            specs.append(pl.BlockSpec(memory_space=pltpu.SMEM if smem else pltpu.VMEM))
            moved += array.size * array.dtype.itemsize
        arrays.append(array)
    shapes = [jax.ShapeDtypeStruct(shape, dtype) for shape, dtype in outputs]
    for shape in shapes:
        moved += shape.size * shape.dtype.itemsize
    buffers = [pltpu.VMEM(shape, dtype) for _, _, _, shape, dtype in fetches]
    if fetches:
        buffers.append(pltpu.SemaphoreType.DMA((len(fetches),)))

    def kernel(*refs):
        refs = list(refs)
        if not fetches:
            body(*refs)
            return
        refs, targets, semaphores = (
            refs[: -len(buffers)],
            refs[-len(buffers) : -1],
            refs[-1],
        )
        waiting = []
        for slot, (place, first, rows, _, _) in enumerate(fetches):
            refs[place] = Fetched(
                refs[place].at[pl.ds(first, rows), :], targets[slot], semaphores.at[slot]
            )
            waiting.append(refs[place])
        body(*refs)
        for fetched in waiting:
            fetched.land()

    return pl.pallas_call(
        kernel,
        name=name,
        in_specs=specs,
        out_specs=[pl.BlockSpec(memory_space=pltpu.VMEM) for _ in shapes],
        out_shape=shapes,
        scratch_shapes=[pltpu.VMEM(shape, dtype) for shape, dtype in scratch] + buffers,
        compiler_params=pltpu.CompilerParams(vmem_limit_bytes=VMEM_LIMIT),
        cost_estimate=pl.CostEstimate(flops=flops, bytes_accessed=moved, transcendentals=0),
    )(*arrays)


def per_device(
    grid_nodes,
    mesh_nodes,
    enc_edges,
    dec_edges,
    grid_cot,
    mesh_cot,
    enc_first,
    enc_second,
    mesh_first,
    mesh_second,
    dec_first,
    dec_second,
    grid_first,
    grid_second,
    send_index,
    send_count,
    enc_grid,
    enc_mesh,
    dec_grid,
    dec_mesh,
):
    grid_count, feat = grid_nodes.shape
    mesh_count = mesh_nodes.shape[0]
    enc_count = enc_edges.shape[0]
    dec_count = dec_edges.shape[0]
    links, width = send_index.shape
    slots = links * width
    slots_pad = -(-slots // 128) * 128
    spots = grid_count + slots
    total = -(-(spots + mesh_count) // 128) * 128
    peer_count = lax.axis_size("tile")
    offsets = neighbour_offsets(peer_count)
    half = (links - 1) // 2
    reverse = [(j + half) % (links - 1) for j in range(links - 1)] + [links - 1]
    low, high = slice(0, feat), slice(feat, 2 * feat)
    mesh_rows = slice(spots, spots + mesh_count)

    def exchange(parts):
        return [
            lax.ppermute(part, "tile", [(s, (s + offset) % peer_count) for s in range(peer_count)])
            for part, offset in zip(parts, offsets)
        ]

    def pack(index_ref, count_ref, nodes_ref, cot_ref, select_ref, *out_refs):
        shape = (width, grid_count)
        eye = lax.broadcasted_iota(jnp.int32, (width, width), 0) == lax.broadcasted_iota(
            jnp.int32, (width, width), 1
        )
        lane = lax.broadcasted_iota(jnp.int32, shape, 1).astype(F32)
        place = lax.broadcasted_iota(jnp.int32, shape, 0)
        index = index_ref[...].astype(F32)
        picks = []
        for j in range(links):
            row = jnp.broadcast_to(index[j : j + 1, :], (width, width))
            column = jnp.sum(jnp.where(eye, row, 0.0), axis=1, keepdims=True)
            hit = (lane == column) & (place < count_ref[j])
            picks.append(jnp.where(hit, 1.0, 0.0).astype(BF16))
        select = jnp.concatenate(picks, axis=0)
        select_ref[:slots, :] = select
        select_ref[slots:, :] = jnp.zeros((slots_pad - slots, grid_count), BF16)
        sent_nodes = mm(select, nodes_ref[...]).astype(BF16)
        sent_cot = mm(select, cot_ref[...]).astype(BF16)
        for j, out_ref in enumerate(out_refs):
            rows = slice(j * width, (j + 1) * width)
            out_ref[:, low] = sent_nodes[rows, :]
            out_ref[:, high] = sent_cot[rows, :]

    select, *outgoing = call(
        pack,
        "pack_rows",
        [send_index, send_count, grid_nodes, grid_cot],
        [((slots_pad, grid_count), BF16)] + [((width, 2 * feat), BF16)] * links,
        flops=4 * slots * grid_count * feat,
    )
    arrived = exchange(outgoing)

    def local(
        select_ref,
        nodes_ref,
        mesh_ref,
        enc_edges_ref,
        dec_edges_ref,
        enc_wg_ref,
        enc_wm_ref,
        enc_we_ref,
        dec_wg_ref,
        dec_we_ref,
        mesh_wn_ref,
        enc_grid_ref,
        enc_mesh_ref,
        dec_grid_ref,
        dec_mesh_ref,
        select_t_ref,
        enc_part_ref,
        dec_part_ref,
        mesh_part_ref,
        enc_pick_ref,
        enc_pool_ref,
        dec_pick_ref,
        dec_pool_ref,
        table_ref,
    ):
        onehot_pair(enc_grid_ref, enc_mesh_ref, spots, enc_pick_ref, enc_pool_ref)
        onehot_pair(dec_grid_ref, dec_mesh_ref, spots, dec_pick_ref, dec_pool_ref)
        select_t_ref[...] = select_ref[...].astype(F32).T.astype(BF16)
        nodes = nodes_ref[...]
        mesh_part_ref[...] = mm(mesh_ref[...], mesh_wn_ref[...])
        table_ref[:grid_count, :] = mm(nodes, enc_wg_ref[...]).astype(BF16)
        table_ref[grid_count:, :] = jnp.zeros((total - grid_count, feat), BF16)
        table_ref[mesh_rows, :] = mm(mesh_ref[...], enc_wm_ref[...]).astype(BF16)
        enc_part_ref[...] = mm(enc_edges_ref[...], enc_we_ref[...])
        enc_part_ref[...] += mm(enc_pick_ref[...], table_ref[...])
        pd = mm(nodes, dec_wg_ref[...]).astype(BF16)
        dec_part_ref[...] = mm(dec_edges_ref[...], dec_we_ref[...])
        dec_part_ref[...] += mm(dec_pick_ref[:, :grid_count], pd)

    select_t, enc_part, dec_part, mesh_part, enc_pick, enc_pool, dec_pick, dec_pool = call(
        local,
        "local_products",
        [
            select,
            grid_nodes,
            mesh_nodes,
            enc_edges,
            dec_edges,
            (enc_first, 0, feat),
            (enc_first, feat, feat),
            (enc_first, 2 * feat, feat),
            (dec_first, 0, feat),
            (dec_first, 2 * feat, feat),
            (mesh_first, 0, feat),
            enc_grid.reshape(1, -1),
            enc_mesh.reshape(1, -1),
            dec_grid.reshape(1, -1),
            dec_mesh.reshape(1, -1),
        ],
        [
            ((grid_count, slots_pad), BF16),
            ((enc_count, feat), F32),
            ((dec_count, feat), F32),
            ((mesh_count, feat), F32),
            ((enc_count, total), BF16),
            ((total, enc_count), BF16),
            ((dec_count, total), BF16),
            ((total, dec_count), BF16),
        ],
        scratch=[((total, feat), BF16)],
        flops=2 * feat * (feat * (2 * grid_count + enc_count + dec_count) + total * dec_count),
    )

    def forward(*refs):
        arrived_refs, refs = refs[:links], refs[links:]
        (
            select_ref,
            enc_part_ref,
            dec_part_ref,
            mesh_part_ref,
            enc_pick_ref,
            enc_pool_ref,
            dec_pick_ref,
            dec_pool_ref,
            mesh_ref,
            enc_wg_ref,
            dec_wg_ref,
            enc_w2_ref,
            mesh_wa_ref,
            mesh_w2_ref,
            dec_wm_ref,
            dec_w2_ref,
        ) = refs[:16]
        refs = refs[16:]
        out_refs, refs = refs[:links], refs[links:]
        (
            mesh_out_ref,
            spot_ref,
            enc_normed_ref,
            enc_scale_ref,
            enc_slope_ref,
            dec_normed_ref,
            dec_scale_ref,
            dec_slope_ref,
            mesh_normed_ref,
            mesh_scale_ref,
            mesh_slope_ref,
            enc_act_ref,
            dec_act_ref,
            mesh_act_ref,
            table_ref,
        ) = refs
        rows = stack(arrived_refs, low)
        pe = mm(rows, enc_wg_ref[...]).astype(BF16)
        pre = enc_part_ref[...] + mm(enc_pick_ref[:, grid_count:spots], pe)
        activate(pre, enc_act_ref, enc_slope_ref)
        norm_forward(mm(enc_act_ref[...], enc_w2_ref[...]), enc_normed_ref, enc_scale_ref)
        agg = mm(enc_pool_ref[mesh_rows, :], enc_normed_ref[...]).astype(BF16)
        activate(mesh_part_ref[...] + mm(agg, mesh_wa_ref[...]), mesh_act_ref, mesh_slope_ref)
        norm_forward(mm(mesh_act_ref[...], mesh_w2_ref[...]), mesh_normed_ref, mesh_scale_ref)
        mesh_out = (mesh_ref[...].astype(F32) + mesh_normed_ref[...]).astype(BF16)
        mesh_out_ref[...] = mesh_out
        table_ref[:slots, :] = mm(rows, dec_wg_ref[...]).astype(BF16)
        table_ref[slots : slots + mesh_count, :] = mm(mesh_out, dec_wm_ref[...]).astype(BF16)
        table_ref[slots + mesh_count :, :] = jnp.zeros(
            (total - spots - mesh_count, feat), BF16
        )
        pre = dec_part_ref[...] + mm(dec_pick_ref[:, grid_count:], table_ref[...])
        activate(pre, dec_act_ref, dec_slope_ref)
        norm_forward(mm(dec_act_ref[...], dec_w2_ref[...]), dec_normed_ref, dec_scale_ref)
        spot_ref[...] = mm(dec_pool_ref[:spots, :], dec_normed_ref[...])
        shared = mm(select_ref[:slots, :], spot_ref[:grid_count, :].astype(BF16)).astype(BF16)
        for j, out_ref in enumerate(out_refs):
            start = grid_count + reverse[j] * width
            out_ref[:, low] = spot_ref[start : start + width, :].astype(BF16)
            out_ref[:, high] = shared[j * width : (j + 1) * width, :]

    edge_saved = [
        ((enc_count, feat), BF16),
        ((enc_count, 1), F32),
        ((enc_count, feat), BF16),
        ((dec_count, feat), BF16),
        ((dec_count, 1), F32),
        ((dec_count, feat), BF16),
        ((mesh_count, feat), F32),
        ((mesh_count, 1), F32),
        ((mesh_count, feat), BF16),
    ]
    results = call(
        forward,
        "edges_forward",
        [
            *arrived,
            select,
            enc_part,
            dec_part,
            mesh_part,
            enc_pick,
            enc_pool,
            dec_pick,
            dec_pool,
            mesh_nodes,
            (enc_first, 0, feat),
            (dec_first, 0, feat),
            (enc_second, 0, feat),
            (mesh_first, feat, feat),
            (mesh_second, 0, feat),
            (dec_first, feat, feat),
            (dec_second, 0, feat),
        ],
        [((width, 2 * feat), BF16)] * links
        + [((mesh_count, feat), BF16), ((spots, feat), F32)]
        + edge_saved,
        scratch=[
            ((enc_count, feat), BF16),
            ((dec_count, feat), BF16),
            ((mesh_count, feat), BF16),
            ((total - grid_count, feat), BF16),
        ],
        flops=2 * feat * feat * 2 * (enc_count + dec_count),
    )
    outgoing, results = results[:links], results[links:]
    mesh_out, spot_msg, *saved = results
    returned = exchange(outgoing)

    def node_part(*refs):
        arrived_refs, (nodes_ref, weight_ref, out_ref) = refs[:links], refs[links:]
        out_ref[:grid_count, :] = mm(nodes_ref[...], weight_ref[...])
        out_ref[grid_count:, :] = mm(stack(arrived_refs, low), weight_ref[...])

    (grid_part,) = call(
        node_part,
        "node_products",
        [*arrived, grid_nodes, (grid_first, 0, feat)],
        [((spots, feat), F32)],
        flops=2 * spots * feat * feat,
    )

    def backward(*refs):
        arrived_refs, returned_refs, refs = refs[:links], refs[links : 2 * links], refs[2 * links :]
        (
            spot_ref,
            grid_part_ref,
            select_t_ref,
            nodes_ref,
            cot_ref,
            mesh_cot_ref,
            enc_pick_ref,
            enc_pool_ref,
            dec_pick_ref,
            dec_pool_ref,
            grid_wa_ref,
            grid_w2_ref,
            dec_w2_ref,
            dec_wm_ref,
            mesh_wa_ref,
            mesh_w2_ref,
            enc_w2_ref,
            enc_wg_ref,
            dec_wg_ref,
            enc_normed_ref,
            enc_scale_ref,
            enc_slope_ref,
            dec_normed_ref,
            dec_scale_ref,
            dec_slope_ref,
            mesh_normed_ref,
            mesh_scale_ref,
            mesh_slope_ref,
        ) = refs[:28]
        refs = refs[28:]
        out_refs, refs = refs[:links], refs[links:]
        (
            grid_out_ref,
            grid_gpre_ref,
            gpe_ref,
            gpd_ref,
            mesh_gin_ref,
            mesh_gpre_ref,
            mesh_pool_ref,
            agg_ref,
            grid_act_ref,
            grid_slope_ref,
            grid_normed_ref,
            grid_scale_ref,
            grid_gout_ref,
            grid_gall_ref,
            spot_grad_ref,
            dec_gout_ref,
            mesh_gout_ref,
            enc_gout_ref,
        ) = refs
        back = [returned_refs[reverse[j]] for j in range(links)]
        agg_ref[:grid_count, :] = (
            spot_ref[:grid_count, :] + mm(select_t_ref[:, :slots], stack(back, low))
        ).astype(BF16)
        agg_ref[grid_count:, :] = (
            spot_ref[grid_count:, :] + stack(returned_refs, high).astype(F32)
        ).astype(BF16)
        activate(
            grid_part_ref[...] + mm(agg_ref[...], grid_wa_ref[...]), grid_act_ref, grid_slope_ref
        )
        norm_forward(mm(grid_act_ref[...], grid_w2_ref[...]), grid_normed_ref, grid_scale_ref)
        grid_out_ref[...] = (
            nodes_ref[...].astype(F32) + grid_normed_ref[:grid_count, :]
        ).astype(BF16)
        cot = jnp.concatenate([cot_ref[...], stack(arrived_refs, high)], axis=0)
        norm_backward(grid_normed_ref, grid_scale_ref, cot, grid_gout_ref)
        times_slope(mm_t(grid_gout_ref[...], grid_w2_ref[...]), grid_slope_ref, grid_gall_ref)
        grid_gpre_ref[...] = grid_gall_ref[:grid_count, :]
        spot_grad_ref[:spots, :] = mm_t(grid_gall_ref[...], grid_wa_ref[...]).astype(BF16)
        spot_grad_ref[spots:, :] = jnp.zeros((total - spots, feat), BF16)
        norm_backward(
            dec_normed_ref, dec_scale_ref, mm(dec_pick_ref[...], spot_grad_ref[...]), dec_gout_ref
        )
        times_slope(mm_t(dec_gout_ref[...], dec_w2_ref[...]), dec_slope_ref, dec_gout_ref)
        pooled = mm(dec_pool_ref[...], dec_gout_ref[...]).astype(BF16)
        gpd_ref[...] = pooled[:grid_count, :]
        slot_back = mm_t(pooled[grid_count:spots, :], dec_wg_ref[...])
        mesh_gin = mesh_cot_ref[...].astype(F32) + mm_t(pooled[mesh_rows, :], dec_wm_ref[...])
        mesh_gin_ref[...] = mesh_gin
        norm_backward(mesh_normed_ref, mesh_scale_ref, mesh_gin, mesh_gout_ref)
        times_slope(mm_t(mesh_gout_ref[...], mesh_w2_ref[...]), mesh_slope_ref, mesh_gpre_ref)
        gagg = mm_t(mesh_gpre_ref[...], mesh_wa_ref[...]).astype(BF16)
        norm_backward(
            enc_normed_ref, enc_scale_ref, mm(enc_pick_ref[:, mesh_rows], gagg), enc_gout_ref
        )
        times_slope(mm_t(enc_gout_ref[...], enc_w2_ref[...]), enc_slope_ref, enc_gout_ref)
        pooled = mm(enc_pool_ref[...], enc_gout_ref[...]).astype(BF16)
        gpe_ref[...] = pooled[:grid_count, :]
        mesh_pool_ref[...] = pooled[mesh_rows, :]
        slot_back = (slot_back + mm_t(pooled[grid_count:spots, :], enc_wg_ref[...])).astype(BF16)
        for j, out_ref in enumerate(out_refs):
            start = reverse[j] * width
            out_ref[...] = slot_back[start : start + width, :]

    results = call(
        backward,
        "edges_backward",
        [
            *arrived,
            *returned,
            spot_msg,
            grid_part,
            select_t,
            grid_nodes,
            grid_cot,
            mesh_cot,
            enc_pick,
            enc_pool,
            dec_pick,
            dec_pool,
            (grid_first, feat, feat),
            (grid_second, 0, feat),
            (dec_second, 0, feat),
            (dec_first, feat, feat),
            (mesh_first, feat, feat),
            (mesh_second, 0, feat),
            (enc_second, 0, feat),
            (enc_first, 0, feat),
            (dec_first, 0, feat),
            *saved,
        ],
        [((width, feat), BF16)] * links
        + [((grid_count, feat), BF16)] * 4
        + [((mesh_count, feat), F32), ((mesh_count, feat), BF16), ((mesh_count, feat), BF16)],
        scratch=[
            ((spots, feat), BF16),
            ((spots, feat), BF16),
            ((spots, feat), BF16),
            ((spots, feat), F32),
            ((spots, 1), F32),
            ((spots, feat), BF16),
            ((spots, feat), BF16),
            ((total, feat), BF16),
            ((dec_count, feat), BF16),
            ((mesh_count, feat), BF16),
            ((enc_count, feat), BF16),
        ],
        flops=2 * feat * feat * (4 * spots + 3 * dec_count + 2 * enc_count),
    )
    outgoing, results = results[:links], results[links:]
    grid_out, grid_gpre, gpe, gpd, mesh_gin, mesh_gpre, mesh_pool = results
    final = exchange(outgoing)

    def tail(
        cot_ref,
        grid_gpre_ref,
        gpe_ref,
        gpd_ref,
        mesh_gin_ref,
        mesh_gpre_ref,
        mesh_pool_ref,
        grid_wn_ref,
        enc_wg_ref,
        dec_wg_ref,
        mesh_wn_ref,
        enc_wm_ref,
        base_ref,
        grad_mesh_ref,
    ):
        base_ref[...] = (
            cot_ref[...].astype(F32)
            + mm_t(grid_gpre_ref[...], grid_wn_ref[...])
            + mm_t(gpe_ref[...], enc_wg_ref[...])
            + mm_t(gpd_ref[...], dec_wg_ref[...])
        )
        grad_mesh_ref[...] = (
            mesh_gin_ref[...]
            + mm_t(mesh_gpre_ref[...], mesh_wn_ref[...])
            + mm_t(mesh_pool_ref[...], enc_wm_ref[...])
        )

    base, grad_mesh = call(
        tail,
        "local_gradients",
        [
            grid_cot,
            grid_gpre,
            gpe,
            gpd,
            mesh_gin,
            mesh_gpre,
            mesh_pool,
            (grid_first, 0, feat),
            (enc_first, 0, feat),
            (dec_first, 0, feat),
            (mesh_first, 0, feat),
            (enc_first, feat, feat),
        ],
        [((grid_count, feat), F32), ((mesh_count, feat), F32)],
        flops=2 * feat * feat * 3 * grid_count,
    )

    def finish(*refs):
        back_refs, (base_ref, select_t_ref, out_ref) = refs[:links], refs[links:]
        back = [back_refs[reverse[j]] for j in range(links)]
        out_ref[...] = base_ref[...] + mm(
            select_t_ref[:, :slots], stack(back, slice(0, feat))
        )

    (grad_grid,) = call(
        finish,
        "add_returned",
        [*final, base, select_t],
        [((grid_count, feat), F32)],
        flops=2 * grid_count * slots * feat,
    )
    return (grid_out, mesh_out, grad_grid, grad_mesh)


def solution(mesh):
    rows = P(("groups", "tile"), None)
    flat = P(("groups", "tile"))
    in_specs = (rows,) * 6 + (P(),) * 8 + (rows,) + (flat,) * 5
    return jax.shard_map(
        per_device, mesh=mesh, in_specs=in_specs, out_specs=(rows,) * 4, check_vma=False
    )
```

```python
import jax
import jax.numpy as jnp
from jax import lax
from jax.experimental import pallas as pl
from jax.experimental.pallas import tpu as pltpu
from jax.sharding import PartitionSpec as P

TW = 4
CHUNK = 32
F32 = jnp.float32
BF16 = jnp.bfloat16
VMEM_LIMIT = 30 * 1024 * 1024


def mm(left, right):
    return jnp.dot(left, right, preferred_element_type=F32)


def mm_t(left, right):
    return lax.dot_general(left, right, (((1,), (1,)), ((), ())), preferred_element_type=F32)


def sigmoid(values):
    return 0.5 * jnp.tanh(0.5 * values) + 0.5


def norm_rows(values):
    centre = values - jnp.mean(values, axis=-1, keepdims=True)
    scale_inv = lax.rsqrt(jnp.mean(centre * centre, axis=-1, keepdims=True) + 1e-05)
    return centre * scale_inv, scale_inv


def norm_back(normed, scale_inv, upstream):
    return scale_inv * (
        upstream
        - jnp.mean(upstream, axis=-1, keepdims=True)
        - normed * jnp.mean(upstream * normed, axis=-1, keepdims=True)
    )


def row_chunks(rows, size=CHUNK):
    return [slice(start, min(start + size, rows)) for start in range(0, rows, size)]


def activate(pre, act_ref, slope_ref):
    for rows in row_chunks(pre.shape[0]):
        part = pre[rows, :]
        gate = sigmoid(part)
        act = part * gate
        act_ref[rows, :] = act.astype(BF16)
        slope_ref[rows, :] = (gate + act * (1.0 - gate)).astype(BF16)


def norm_forward(raw, normed_ref, scale_ref):
    for rows in row_chunks(raw.shape[0]):
        normed, scale_inv = norm_rows(raw[rows, :])
        normed_ref[rows, :] = normed.astype(normed_ref.dtype)
        scale_ref[rows, :] = scale_inv


def norm_backward(normed_ref, scale_ref, upstream, out_ref):
    for rows in row_chunks(out_ref.shape[0]):
        out_ref[rows, :] = norm_back(
            normed_ref[rows, :].astype(F32), scale_ref[rows, :], upstream[rows, :].astype(F32)
        ).astype(BF16)


def times_slope(raw, slope_ref, out_ref):
    for rows in row_chunks(out_ref.shape[0]):
        out_ref[rows, :] = (raw[rows, :] * slope_ref[rows, :].astype(F32)).astype(BF16)


def stack(refs, columns):
    return jnp.concatenate([ref[:, columns] for ref in refs], axis=0)


def neighbour_offsets(peer_count):
    forward_half = [1, TW, TW + 1, TW - 1]
    return forward_half + [-offset for offset in forward_half] + [peer_count // 2]


def onehot_pair(spot_ref, mesh_ref, spots, by_edge_ref, by_spot_ref):
    edges, total = by_edge_ref.shape
    spot_row = spot_ref[...].reshape(1, -1).astype(F32)
    mesh_row = mesh_ref[...].reshape(1, -1).astype(F32) + float(spots)
    for rows in row_chunks(total, 64):
        ids = lax.broadcasted_iota(jnp.int32, (rows.stop - rows.start, edges), 0) + rows.start
        ids = ids.astype(F32)
        hit = (ids == spot_row) | (ids == mesh_row)
        by_spot_ref[rows, :] = jnp.where(hit, 1.0, 0.0).astype(BF16)
    for rows in row_chunks(edges, 128):
        spot_col = jnp.broadcast_to(spot_row[:, rows], (128, 128)).T
        mesh_col = jnp.broadcast_to(mesh_row[:, rows], (128, 128)).T
        for columns in row_chunks(total, 128):
            ids = lax.broadcasted_iota(jnp.int32, (128, 128), 1) + columns.start
            ids = ids.astype(F32)
            hit = (ids == spot_col) | (ids == mesh_col)
            by_edge_ref[rows, columns] = jnp.where(hit, 1.0, 0.0).astype(BF16)


class Fetched:
    def __init__(self, source, target, semaphore):
        self.copy = pltpu.make_async_copy(source, target, semaphore)
        self.target = target
        self.landed = False
        self.copy.start()

    def land(self):
        if not self.landed:
            self.copy.wait()
            self.landed = True

    def __getitem__(self, key):
        self.land()
        return self.target[key]


def call(body, name, inputs, outputs, scratch=(), flops=0):
    arrays, specs, moved, fetches = [], [], 0, []
    for place, entry in enumerate(inputs):
        if isinstance(entry, tuple):
            array, first, rows = entry
            specs.append(pl.BlockSpec(memory_space=pltpu.HBM))
            shape = (rows,) + array.shape[1:]
            fetches.append((place, first, rows, shape, array.dtype))
            moved += rows * (array.size // array.shape[0]) * array.dtype.itemsize
        else:
            array = entry
            specs.append(pl.BlockSpec(memory_space=pltpu.VMEM))
            moved += array.size * array.dtype.itemsize
        arrays.append(array)
    shapes = [jax.ShapeDtypeStruct(shape, dtype) for shape, dtype in outputs]
    for shape in shapes:
        moved += shape.size * shape.dtype.itemsize
    buffers = [pltpu.VMEM(shape, dtype) for _, _, _, shape, dtype in fetches]
    if fetches:
        buffers.append(pltpu.SemaphoreType.DMA((len(fetches),)))

    def kernel(*refs):
        refs = list(refs)
        if not fetches:
            body(*refs)
            return
        refs, targets, semaphores = (
            refs[: -len(buffers)],
            refs[-len(buffers) : -1],
            refs[-1],
        )
        waiting = []
        for slot, (place, first, rows, shape, _) in enumerate(fetches):
            source = refs[place]
            if source.shape != shape:
                source = source.at[pl.ds(first, rows)]
            refs[place] = Fetched(source, targets[slot], semaphores.at[slot])
            waiting.append(refs[place])
        body(*refs)
        for fetched in waiting:
            fetched.land()

    return pl.pallas_call(
        kernel,
        name=name,
        in_specs=specs,
        out_specs=[pl.BlockSpec(memory_space=pltpu.VMEM) for _ in shapes],
        out_shape=shapes,
        scratch_shapes=[pltpu.VMEM(shape, dtype) for shape, dtype in scratch] + buffers,
        compiler_params=pltpu.CompilerParams(vmem_limit_bytes=VMEM_LIMIT),
        cost_estimate=pl.CostEstimate(flops=flops, bytes_accessed=moved, transcendentals=0),
    )(*arrays)


def per_device(
    grid_nodes,
    mesh_nodes,
    enc_edges,
    dec_edges,
    grid_cot,
    mesh_cot,
    enc_first,
    enc_second,
    mesh_first,
    mesh_second,
    dec_first,
    dec_second,
    grid_first,
    grid_second,
    send_index,
    send_count,
    enc_grid,
    enc_mesh,
    dec_grid,
    dec_mesh,
):
    grid_count, feat = grid_nodes.shape
    mesh_count = mesh_nodes.shape[0]
    enc_count = enc_edges.shape[0]
    dec_count = dec_edges.shape[0]
    links, width = send_index.shape
    slots = links * width
    slots_pad = -(-slots // 128) * 128
    spots = grid_count + slots
    total = -(-(spots + mesh_count) // 128) * 128
    peer_count = lax.axis_size("tile")
    offsets = neighbour_offsets(peer_count)
    half = (links - 1) // 2
    reverse = [(j + half) % (links - 1) for j in range(links - 1)] + [links - 1]
    low, high = slice(0, feat), slice(feat, 2 * feat)
    mesh_rows = slice(spots, spots + mesh_count)

    def exchange(parts):
        return [
            lax.ppermute(part, "tile", [(s, (s + offset) % peer_count) for s in range(peer_count)])
            for part, offset in zip(parts, offsets)
        ]

    def pack(index_ref, count_ref, nodes_ref, cot_ref, select_ref, *out_refs):
        def column(row):
            count = row.shape[1]
            eye = lax.broadcasted_iota(jnp.int32, (count, count), 0) == lax.broadcasted_iota(
                jnp.int32, (count, count), 1
            )
            return jnp.sum(
                jnp.where(eye, jnp.broadcast_to(row, (count, count)), 0.0), axis=1, keepdims=True
            )

        counts = column(count_ref[...].reshape(1, -1).astype(F32))
        place = lax.broadcasted_iota(jnp.int32, (links, width), 1).astype(F32)
        index = jnp.where(place < counts, index_ref[...].astype(F32), -1.0)
        lane = lax.broadcasted_iota(jnp.int32, (width, grid_count), 1).astype(F32)
        picks = [
            jnp.where(lane == column(index[j : j + 1, :]), 1.0, 0.0).astype(BF16)
            for j in range(links)
        ]
        select = jnp.concatenate(picks, axis=0)
        select_ref[:slots, :] = select
        select_ref[slots:, :] = jnp.zeros((slots_pad - slots, grid_count), BF16)
        sent_nodes = mm(select, nodes_ref[...]).astype(BF16)
        sent_cot = mm(select, cot_ref[...]).astype(BF16)
        for j, out_ref in enumerate(out_refs):
            rows = slice(j * width, (j + 1) * width)
            out_ref[:, low] = sent_nodes[rows, :]
            out_ref[:, high] = sent_cot[rows, :]

    select, *outgoing = call(
        pack,
        "pack_rows",
        [
            (send_index, 0, links),
            (send_count, 0, links),
            (grid_nodes, 0, grid_count),
            (grid_cot, 0, grid_count),
        ],
        [((slots_pad, grid_count), BF16)] + [((width, 2 * feat), BF16)] * links,
        flops=4 * slots * grid_count * feat,
    )
    arrived = exchange(outgoing)

    def local(
        select_ref,
        nodes_ref,
        mesh_ref,
        enc_edges_ref,
        dec_edges_ref,
        enc_wg_ref,
        enc_wm_ref,
        enc_we_ref,
        dec_wg_ref,
        dec_we_ref,
        mesh_wn_ref,
        enc_grid_ref,
        enc_mesh_ref,
        dec_grid_ref,
        dec_mesh_ref,
        select_t_ref,
        enc_part_ref,
        dec_part_ref,
        mesh_part_ref,
        enc_pick_ref,
        enc_pool_ref,
        dec_pick_ref,
        dec_pool_ref,
        table_ref,
    ):
        onehot_pair(enc_grid_ref, enc_mesh_ref, spots, enc_pick_ref, enc_pool_ref)
        onehot_pair(dec_grid_ref, dec_mesh_ref, spots, dec_pick_ref, dec_pool_ref)
        select_t_ref[...] = select_ref[...].astype(F32).T.astype(BF16)
        nodes = nodes_ref[...]
        mesh_part_ref[...] = mm(mesh_ref[...], mesh_wn_ref[...])
        table_ref[:grid_count, :] = mm(nodes, enc_wg_ref[...]).astype(BF16)
        table_ref[grid_count:, :] = jnp.zeros((total - grid_count, feat), BF16)
        table_ref[mesh_rows, :] = mm(mesh_ref[...], enc_wm_ref[...]).astype(BF16)
        enc_part_ref[...] = mm(enc_edges_ref[...], enc_we_ref[...])
        enc_part_ref[...] += mm(enc_pick_ref[...], table_ref[...])
        pd = mm(nodes, dec_wg_ref[...]).astype(BF16)
        dec_part_ref[...] = mm(dec_edges_ref[...], dec_we_ref[...])
        dec_part_ref[...] += mm(dec_pick_ref[:, :grid_count], pd)

    select_t, enc_part, dec_part, mesh_part, enc_pick, enc_pool, dec_pick, dec_pool = call(
        local,
        "local_products",
        [
            select,
            (grid_nodes, 0, grid_count),
            (mesh_nodes, 0, mesh_count),
            (enc_edges, 0, enc_count),
            (dec_edges, 0, dec_count),
            (enc_first, 0, feat),
            (enc_first, feat, feat),
            (enc_first, 2 * feat, feat),
            (dec_first, 0, feat),
            (dec_first, 2 * feat, feat),
            (mesh_first, 0, feat),
            (enc_grid, 0, enc_grid.shape[0]),
            (enc_mesh, 0, enc_mesh.shape[0]),
            (dec_grid, 0, dec_grid.shape[0]),
            (dec_mesh, 0, dec_mesh.shape[0]),
        ],
        [
            ((grid_count, slots_pad), BF16),
            ((enc_count, feat), F32),
            ((dec_count, feat), F32),
            ((mesh_count, feat), F32),
            ((enc_count, total), BF16),
            ((total, enc_count), BF16),
            ((dec_count, total), BF16),
            ((total, dec_count), BF16),
        ],
        scratch=[((total, feat), BF16)],
        flops=2 * feat * (feat * (2 * grid_count + enc_count + dec_count) + total * dec_count),
    )

    def forward(*refs):
        arrived_refs, refs = refs[:links], refs[links:]
        (
            select_ref,
            enc_part_ref,
            dec_part_ref,
            mesh_part_ref,
            enc_pick_ref,
            enc_pool_ref,
            dec_pick_ref,
            dec_pool_ref,
            mesh_ref,
            enc_wg_ref,
            dec_wg_ref,
            enc_w2_ref,
            mesh_wa_ref,
            mesh_w2_ref,
            dec_wm_ref,
            dec_w2_ref,
        ) = refs[:16]
        refs = refs[16:]
        out_refs, refs = refs[:links], refs[links:]
        (
            mesh_out_ref,
            spot_ref,
            enc_normed_ref,
            enc_scale_ref,
            enc_slope_ref,
            dec_normed_ref,
            dec_scale_ref,
            dec_slope_ref,
            mesh_normed_ref,
            mesh_scale_ref,
            mesh_slope_ref,
            enc_act_ref,
            dec_act_ref,
            mesh_act_ref,
            table_ref,
        ) = refs
        rows = stack(arrived_refs, low)
        pe = mm(rows, enc_wg_ref[low, :]).astype(BF16)
        pre = enc_part_ref[...] + mm(enc_pick_ref[:, grid_count:spots], pe)
        activate(pre, enc_act_ref, enc_slope_ref)
        norm_forward(mm(enc_act_ref[...], enc_w2_ref[...]), enc_normed_ref, enc_scale_ref)
        agg = mm(enc_pool_ref[mesh_rows, :], enc_normed_ref[...]).astype(BF16)
        activate(mesh_part_ref[...] + mm(agg, mesh_wa_ref[high, :]), mesh_act_ref, mesh_slope_ref)
        norm_forward(mm(mesh_act_ref[...], mesh_w2_ref[...]), mesh_normed_ref, mesh_scale_ref)
        mesh_out = (mesh_ref[...].astype(F32) + mesh_normed_ref[...]).astype(BF16)
        mesh_out_ref[...] = mesh_out
        table_ref[:slots, :] = mm(rows, dec_wg_ref[low, :]).astype(BF16)
        table_ref[slots : slots + mesh_count, :] = mm(mesh_out, dec_wm_ref[high, :]).astype(BF16)
        table_ref[slots + mesh_count :, :] = jnp.zeros(
            (total - spots - mesh_count, feat), BF16
        )
        pre = dec_part_ref[...] + mm(dec_pick_ref[:, grid_count:], table_ref[...])
        activate(pre, dec_act_ref, dec_slope_ref)
        norm_forward(mm(dec_act_ref[...], dec_w2_ref[...]), dec_normed_ref, dec_scale_ref)
        spot_ref[...] = mm(dec_pool_ref[:spots, :], dec_normed_ref[...])
        shared = mm(select_ref[:slots, :], spot_ref[:grid_count, :].astype(BF16)).astype(BF16)
        for j, out_ref in enumerate(out_refs):
            start = grid_count + reverse[j] * width
            out_ref[:, low] = spot_ref[start : start + width, :].astype(BF16)
            out_ref[:, high] = shared[j * width : (j + 1) * width, :]

    edge_saved = [
        ((enc_count, feat), BF16),
        ((enc_count, 1), F32),
        ((enc_count, feat), BF16),
        ((dec_count, feat), BF16),
        ((dec_count, 1), F32),
        ((dec_count, feat), BF16),
        ((mesh_count, feat), F32),
        ((mesh_count, 1), F32),
        ((mesh_count, feat), BF16),
    ]
    results = call(
        forward,
        "edges_forward",
        [
            *arrived,
            select,
            enc_part,
            dec_part,
            mesh_part,
            enc_pick,
            enc_pool,
            dec_pick,
            dec_pool,
            mesh_nodes,
            enc_first,
            dec_first,
            enc_second,
            mesh_first,
            mesh_second,
            dec_first,
            dec_second,
        ],
        [((width, 2 * feat), BF16)] * links
        + [((mesh_count, feat), BF16), ((spots, feat), F32)]
        + edge_saved,
        scratch=[
            ((enc_count, feat), BF16),
            ((dec_count, feat), BF16),
            ((mesh_count, feat), BF16),
            ((total - grid_count, feat), BF16),
        ],
        flops=2 * feat * feat * 2 * (enc_count + dec_count),
    )
    outgoing, results = results[:links], results[links:]
    mesh_out, spot_msg, *saved = results
    returned = exchange(outgoing)

    def node_part(*refs):
        arrived_refs, (nodes_ref, weight_ref, out_ref) = refs[:links], refs[links:]
        out_ref[:grid_count, :] = mm(nodes_ref[...], weight_ref[low, :])
        out_ref[grid_count:, :] = mm(stack(arrived_refs, low), weight_ref[low, :])

    (grid_part,) = call(
        node_part,
        "node_products",
        [*arrived, grid_nodes, grid_first],
        [((spots, feat), F32)],
        flops=2 * spots * feat * feat,
    )

    def backward(*refs):
        arrived_refs, returned_refs, refs = refs[:links], refs[links : 2 * links], refs[2 * links :]
        (
            spot_ref,
            grid_part_ref,
            select_t_ref,
            nodes_ref,
            cot_ref,
            mesh_cot_ref,
            enc_pick_ref,
            enc_pool_ref,
            dec_pick_ref,
            dec_pool_ref,
            grid_wa_ref,
            grid_w2_ref,
            dec_w2_ref,
            dec_wm_ref,
            mesh_wa_ref,
            mesh_w2_ref,
            enc_w2_ref,
            enc_wg_ref,
            dec_wg_ref,
            enc_normed_ref,
            enc_scale_ref,
            enc_slope_ref,
            dec_normed_ref,
            dec_scale_ref,
            dec_slope_ref,
            mesh_normed_ref,
            mesh_scale_ref,
            mesh_slope_ref,
        ) = refs[:28]
        refs = refs[28:]
        (
            slot_back_ref,
            grid_out_ref,
            grid_gpre_ref,
            gpe_ref,
            gpd_ref,
            mesh_gin_ref,
            mesh_gpre_ref,
            mesh_pool_ref,
            agg_ref,
            grid_act_ref,
            grid_slope_ref,
            grid_normed_ref,
            grid_scale_ref,
            grid_gout_ref,
            grid_gall_ref,
            spot_grad_ref,
            dec_gout_ref,
            mesh_gout_ref,
            enc_gout_ref,
        ) = refs
        back = [returned_refs[reverse[j]] for j in range(links)]
        agg_ref[:grid_count, :] = (
            spot_ref[:grid_count, :] + mm(select_t_ref[:, :slots], stack(back, low))
        ).astype(BF16)
        agg_ref[grid_count:, :] = (
            spot_ref[grid_count:, :] + stack(returned_refs, high).astype(F32)
        ).astype(BF16)
        activate(
            grid_part_ref[...] + mm(agg_ref[...], grid_wa_ref[high, :]), grid_act_ref, grid_slope_ref
        )
        norm_forward(mm(grid_act_ref[...], grid_w2_ref[...]), grid_normed_ref, grid_scale_ref)
        grid_out_ref[...] = (
            nodes_ref[...].astype(F32) + grid_normed_ref[:grid_count, :]
        ).astype(BF16)
        cot = jnp.concatenate([cot_ref[...], stack(arrived_refs, high)], axis=0)
        norm_backward(grid_normed_ref, grid_scale_ref, cot, grid_gout_ref)
        times_slope(mm_t(grid_gout_ref[...], grid_w2_ref[...]), grid_slope_ref, grid_gall_ref)
        grid_gpre_ref[...] = grid_gall_ref[:grid_count, :]
        spot_grad_ref[:spots, :] = mm_t(grid_gall_ref[...], grid_wa_ref[high, :]).astype(BF16)
        spot_grad_ref[spots:, :] = jnp.zeros((total - spots, feat), BF16)
        norm_backward(
            dec_normed_ref, dec_scale_ref, mm(dec_pick_ref[...], spot_grad_ref[...]), dec_gout_ref
        )
        times_slope(mm_t(dec_gout_ref[...], dec_w2_ref[...]), dec_slope_ref, dec_gout_ref)
        pooled = mm(dec_pool_ref[...], dec_gout_ref[...]).astype(BF16)
        gpd_ref[...] = pooled[:grid_count, :]
        slot_back = mm_t(pooled[grid_count:spots, :], dec_wg_ref[low, :])
        mesh_gin = mesh_cot_ref[...].astype(F32) + mm_t(pooled[mesh_rows, :], dec_wm_ref[high, :])
        mesh_gin_ref[...] = mesh_gin
        norm_backward(mesh_normed_ref, mesh_scale_ref, mesh_gin, mesh_gout_ref)
        times_slope(mm_t(mesh_gout_ref[...], mesh_w2_ref[...]), mesh_slope_ref, mesh_gpre_ref)
        gagg = mm_t(mesh_gpre_ref[...], mesh_wa_ref[high, :]).astype(BF16)
        norm_backward(
            enc_normed_ref, enc_scale_ref, mm(enc_pick_ref[:, mesh_rows], gagg), enc_gout_ref
        )
        times_slope(mm_t(enc_gout_ref[...], enc_w2_ref[...]), enc_slope_ref, enc_gout_ref)
        pooled = mm(enc_pool_ref[...], enc_gout_ref[...]).astype(BF16)
        gpe_ref[...] = pooled[:grid_count, :]
        mesh_pool_ref[...] = pooled[mesh_rows, :]
        slot_back = (slot_back + mm_t(pooled[grid_count:spots, :], enc_wg_ref[low, :])).astype(BF16)
        slot_back_ref[...] = slot_back

    results = call(
        backward,
        "edges_backward",
        [
            *arrived,
            *returned,
            spot_msg,
            grid_part,
            select_t,
            grid_nodes,
            grid_cot,
            mesh_cot,
            enc_pick,
            enc_pool,
            dec_pick,
            dec_pool,
            grid_first,
            grid_second,
            dec_second,
            dec_first,
            mesh_first,
            mesh_second,
            enc_second,
            enc_first,
            dec_first,
            *saved,
        ],
        [((slots, feat), BF16)]
        + [((grid_count, feat), BF16)] * 4
        + [((mesh_count, feat), F32), ((mesh_count, feat), BF16), ((mesh_count, feat), BF16)],
        scratch=[
            ((spots, feat), BF16),
            ((spots, feat), BF16),
            ((spots, feat), BF16),
            ((spots, feat), F32),
            ((spots, 1), F32),
            ((spots, feat), BF16),
            ((spots, feat), BF16),
            ((total, feat), BF16),
            ((dec_count, feat), BF16),
            ((mesh_count, feat), BF16),
            ((enc_count, feat), BF16),
        ],
        flops=2 * feat * feat * (4 * spots + 3 * dec_count + 2 * enc_count),
    )
    slot_back, grid_out, grid_gpre, gpe, gpd, mesh_gin, mesh_gpre, mesh_pool = results
    final = lax.all_gather(slot_back, "tile", axis=0, tiled=True)

    def tail(
        cot_ref,
        grid_gpre_ref,
        gpe_ref,
        gpd_ref,
        mesh_gin_ref,
        mesh_gpre_ref,
        mesh_pool_ref,
        grid_wn_ref,
        enc_wg_ref,
        dec_wg_ref,
        mesh_wn_ref,
        enc_wm_ref,
        base_ref,
        grad_mesh_ref,
    ):
        base_ref[...] = (
            cot_ref[...].astype(F32)
            + mm_t(grid_gpre_ref[...], grid_wn_ref[low, :])
            + mm_t(gpe_ref[...], enc_wg_ref[low, :])
            + mm_t(gpd_ref[...], dec_wg_ref[low, :])
        )
        grad_mesh_ref[...] = (
            mesh_gin_ref[...]
            + mm_t(mesh_gpre_ref[...], mesh_wn_ref[low, :])
            + mm_t(mesh_pool_ref[...], enc_wm_ref[high, :])
        )

    base, grad_mesh = call(
        tail,
        "local_gradients",
        [
            grid_cot,
            grid_gpre,
            gpe,
            gpd,
            mesh_gin,
            mesh_gpre,
            mesh_pool,
            grid_first,
            enc_first,
            dec_first,
            mesh_first,
            enc_first,
        ],
        [((grid_count, feat), F32), ((mesh_count, feat), F32)],
        flops=2 * feat * feat * 3 * grid_count,
    )

    def finish(all_ref, base_ref, select_t_ref, out_ref, back_ref, semaphores):
        own = lax.axis_index("tile")
        copies = []
        for j, offset in enumerate(offsets):
            holder = lax.rem(own + (offset + peer_count), peer_count)
            start = pl.multiple_of(holder * slots + j * width, width)
            rows = pl.ds(j * width, width)
            copies.append(
                pltpu.make_async_copy(
                    all_ref.at[pl.ds(start, width), :], back_ref.at[rows, :], semaphores.at[j]
                )
            )
            copies[-1].start()
        for copy in copies:
            copy.wait()
        out_ref[...] = base_ref[...] + mm(select_t_ref[:, :slots], back_ref[...])

    grad_grid = pl.pallas_call(
        finish,
        name="add_returned",
        in_specs=[
            pl.BlockSpec(memory_space=pl.ANY),
            pl.BlockSpec(memory_space=pltpu.VMEM),
            pl.BlockSpec(memory_space=pltpu.VMEM),
        ],
        out_specs=pl.BlockSpec(memory_space=pltpu.VMEM),
        out_shape=jax.ShapeDtypeStruct((grid_count, feat), F32),
        scratch_shapes=[pltpu.VMEM((slots, feat), BF16), pltpu.SemaphoreType.DMA((links,))],
        compiler_params=pltpu.CompilerParams(vmem_limit_bytes=VMEM_LIMIT),
    )(final, base, select_t)
    return (grid_out, mesh_out, grad_grid, grad_mesh)


def solution(mesh):
    rows = P(("groups", "tile"), None)
    flat = P(("groups", "tile"))
    in_specs = (rows,) * 6 + (P(),) * 8 + (rows,) + (flat,) * 5
    return jax.shard_map(
        per_device, mesh=mesh, in_specs=in_specs, out_specs=(rows,) * 4, check_vma=False
    )
```

```python
import jax
import jax.numpy as jnp
from jax import lax
from jax.experimental import pallas as pl
from jax.experimental.pallas import tpu as pltpu
from jax.sharding import PartitionSpec as P

TW = 4
CHUNK = 32
F32 = jnp.float32
BF16 = jnp.bfloat16
VMEM_LIMIT = 30 * 1024 * 1024


def mm(left, right):
    return jnp.dot(left, right, preferred_element_type=F32)


def mm_t(left, right):
    return lax.dot_general(left, right, (((1,), (1,)), ((), ())), preferred_element_type=F32)


def sigmoid(values):
    return 0.5 * jnp.tanh(0.5 * values) + 0.5


def norm_rows(values):
    centre = values - jnp.mean(values, axis=-1, keepdims=True)
    scale_inv = lax.rsqrt(jnp.mean(centre * centre, axis=-1, keepdims=True) + 1e-05)
    return centre * scale_inv, scale_inv


def norm_back(normed, scale_inv, upstream):
    return scale_inv * (
        upstream
        - jnp.mean(upstream, axis=-1, keepdims=True)
        - normed * jnp.mean(upstream * normed, axis=-1, keepdims=True)
    )


def row_chunks(rows, size=CHUNK):
    return [slice(start, min(start + size, rows)) for start in range(0, rows, size)]


def activate(pre, act_ref, slope_ref):
    for rows in row_chunks(pre.shape[0]):
        part = pre[rows, :]
        gate = sigmoid(part)
        act = part * gate
        act_ref[rows, :] = act.astype(BF16)
        slope_ref[rows, :] = (gate + act * (1.0 - gate)).astype(BF16)


def norm_forward(raw, normed_ref, scale_ref):
    for rows in row_chunks(raw.shape[0]):
        normed, scale_inv = norm_rows(raw[rows, :])
        normed_ref[rows, :] = normed.astype(normed_ref.dtype)
        scale_ref[rows, :] = scale_inv


def norm_backward(normed_ref, scale_ref, upstream, out_ref):
    for rows in row_chunks(out_ref.shape[0]):
        out_ref[rows, :] = norm_back(
            normed_ref[rows, :].astype(F32), scale_ref[rows, :], upstream[rows, :].astype(F32)
        ).astype(BF16)


def times_slope(raw, slope_ref, out_ref):
    for rows in row_chunks(out_ref.shape[0]):
        out_ref[rows, :] = (raw[rows, :] * slope_ref[rows, :].astype(F32)).astype(BF16)


def neighbour_offsets(peer_count):
    forward_half = [1, TW, TW + 1, TW - 1]
    return forward_half + [-offset for offset in forward_half] + [peer_count // 2]


def onehot_pair(spot_ref, mesh_ref, spots, by_edge_ref, by_spot_ref):
    edges, total = by_edge_ref.shape
    spot_row = spot_ref[...].reshape(1, -1).astype(F32)
    mesh_row = mesh_ref[...].reshape(1, -1).astype(F32) + float(spots)
    for rows in row_chunks(total, 64):
        ids = lax.broadcasted_iota(jnp.int32, (rows.stop - rows.start, edges), 0) + rows.start
        ids = ids.astype(F32)
        hit = (ids == spot_row) | (ids == mesh_row)
        by_spot_ref[rows, :] = jnp.where(hit, 1.0, 0.0).astype(BF16)
    for rows in row_chunks(edges, 128):
        spot_col = jnp.broadcast_to(spot_row[:, rows], (128, 128)).T
        mesh_col = jnp.broadcast_to(mesh_row[:, rows], (128, 128)).T
        for columns in row_chunks(total, 128):
            ids = lax.broadcasted_iota(jnp.int32, (128, 128), 1) + columns.start
            ids = ids.astype(F32)
            hit = (ids == spot_col) | (ids == mesh_col)
            by_edge_ref[rows, columns] = jnp.where(hit, 1.0, 0.0).astype(BF16)


class Fetched:
    def __init__(self, source, target, semaphore):
        self.copy = pltpu.make_async_copy(source, target, semaphore)
        self.target = target
        self.landed = False
        self.copy.start()

    def land(self):
        if not self.landed:
            self.copy.wait()
            self.landed = True

    def __getitem__(self, key):
        self.land()
        return self.target[key]


def call(body, name, inputs, outputs, scratch=(), flops=0):
    arrays, specs, moved, fetches = [], [], 0, []
    for place, entry in enumerate(inputs):
        if isinstance(entry, tuple):
            array, first, rows = entry
            array = pltpu.with_memory_space_constraint(array, pltpu.HBM)
            specs.append(pl.BlockSpec(memory_space=pltpu.HBM))
            shape = (rows,) + array.shape[1:]
            fetches.append((place, first, rows, shape, array.dtype))
            moved += rows * (array.size // array.shape[0]) * array.dtype.itemsize
        else:
            array = entry
            specs.append(pl.BlockSpec(memory_space=pltpu.VMEM))
            moved += array.size * array.dtype.itemsize
        arrays.append(array)
    shapes = [jax.ShapeDtypeStruct(shape, dtype) for shape, dtype in outputs]
    for shape in shapes:
        moved += shape.size * shape.dtype.itemsize
    buffers = [pltpu.VMEM(shape, dtype) for _, _, _, shape, dtype in fetches]
    if fetches:
        buffers.append(pltpu.SemaphoreType.DMA((len(fetches),)))

    def kernel(*refs):
        refs = list(refs)
        if not fetches:
            body(*refs)
            return
        refs, targets, semaphores = (
            refs[: -len(buffers)],
            refs[-len(buffers) : -1],
            refs[-1],
        )
        waiting = []
        for slot, (place, first, rows, shape, _) in enumerate(fetches):
            source = refs[place]
            if source.shape != shape:
                source = source.at[pl.ds(first, rows)]
            refs[place] = Fetched(source, targets[slot], semaphores.at[slot])
            waiting.append(refs[place])
        body(*refs)
        for fetched in waiting:
            fetched.land()

    return pl.pallas_call(
        kernel,
        name=name,
        in_specs=specs,
        out_specs=[pl.BlockSpec(memory_space=pltpu.VMEM) for _ in shapes],
        out_shape=shapes,
        scratch_shapes=[pltpu.VMEM(shape, dtype) for shape, dtype in scratch] + buffers,
        compiler_params=pltpu.CompilerParams(vmem_limit_bytes=VMEM_LIMIT),
        cost_estimate=pl.CostEstimate(flops=flops, bytes_accessed=moved, transcendentals=0),
    )(*arrays)


def per_device(
    grid_nodes,
    mesh_nodes,
    enc_edges,
    dec_edges,
    grid_cot,
    mesh_cot,
    enc_first,
    enc_second,
    mesh_first,
    mesh_second,
    dec_first,
    dec_second,
    grid_first,
    grid_second,
    send_index,
    send_count,
    enc_grid,
    enc_mesh,
    dec_grid,
    dec_mesh,
):
    grid_count, feat = grid_nodes.shape
    mesh_count = mesh_nodes.shape[0]
    enc_count = enc_edges.shape[0]
    dec_count = dec_edges.shape[0]
    links, width = send_index.shape
    slots = links * width
    slots_pad = -(-slots // 128) * 128
    spots = grid_count + slots
    total = -(-(spots + mesh_count) // 128) * 128
    peer_count = lax.axis_size("tile")
    offsets = neighbour_offsets(peer_count)
    half = (links - 1) // 2
    reverse = [(j + half) % (links - 1) for j in range(links - 1)] + [links - 1]
    low, high = slice(0, feat), slice(feat, 2 * feat)
    mesh_rows = slice(spots, spots + mesh_count)

    one, four, five, three = range(half)
    minus = [j + half for j in range(half)]
    across = links - 1
    peers = range(peer_count)

    def permute(part, even_step, odd_step):
        steps = (even_step, odd_step)
        return lax.ppermute(part, "tile", [(s, (s + steps[s % 2]) % peer_count) for s in peers])

    def exchange(parts):
        plus_two, minus_two, own_chip, plus_one, minus_one, three_off, opposite = parts
        plus_two = permute(plus_two, 4, 4)
        minus_two = permute(minus_two, -4, -4)
        own_chip = permute(own_chip, 1, -1)
        plus_one = permute(plus_one, 3, 1)
        minus_one = permute(minus_one, -1, -3)
        three_off = permute(three_off, -5, 5)
        opposite = permute(opposite, peer_count // 2, peer_count // 2)
        plus_passed = permute(plus_two, 1, -1)
        minus_passed = permute(minus_two, 1, -1)
        return [
            plus_two,
            minus_two,
            own_chip,
            plus_one,
            minus_one,
            three_off,
            opposite,
            plus_passed,
            minus_passed,
        ]

    def sent_shapes(columns):
        rows = (2, 2, 1, 1, 1, 1, 1)
        return [((count * width, columns), BF16) for count in rows]

    sent_count = len(sent_shapes(feat))

    def is_odd():
        return lax.rem(lax.axis_index("tile"), 2) == 1

    def send(refs, message, columns=slice(None)):
        odd = is_odd()

        def by_parity(even, odd_one):
            return jnp.where(odd, message(odd_one), message(even))

        plus_two, minus_two, own_chip, plus_one, minus_one, three_off, opposite = refs
        plus_two[:width, columns] = message(four)
        plus_two[width:, columns] = by_parity(five, three)
        minus_two[:width, columns] = message(minus[four])
        minus_two[width:, columns] = by_parity(minus[three], minus[five])
        own_chip[:, columns] = by_parity(one, minus[one])
        plus_one[:, columns] = by_parity(three, one)
        minus_one[:, columns] = by_parity(minus[one], minus[three])
        three_off[:, columns] = by_parity(minus[five], five)
        opposite[:, columns] = message(across)

    def receive(refs, columns=slice(None)):
        odd = is_odd()
        plus_two, minus_two, own_chip, plus_one, minus_one, three_off, opposite = refs[:7]
        plus_passed, minus_passed = refs[7:]
        first, second = slice(0, width), slice(width, 2 * width)
        own = own_chip[:, columns]
        near_plus, near_minus = plus_one[:, columns], minus_one[:, columns]
        far = three_off[:, columns]
        passed_plus, passed_minus = plus_passed[second, columns], minus_passed[second, columns]
        slot_rows = [None] * links
        slot_rows[one] = jnp.where(odd, own, near_plus)
        slot_rows[minus[one]] = jnp.where(odd, near_minus, own)
        slot_rows[three] = jnp.where(odd, near_plus, passed_plus)
        slot_rows[minus[three]] = jnp.where(odd, passed_minus, near_minus)
        slot_rows[five] = jnp.where(odd, passed_plus, far)
        slot_rows[minus[five]] = jnp.where(odd, far, passed_minus)
        slot_rows[four] = plus_two[first, columns]
        slot_rows[minus[four]] = minus_two[first, columns]
        slot_rows[across] = opposite[:, columns]
        return slot_rows

    def by_slot(refs, columns=slice(None)):
        return jnp.concatenate(receive(refs, columns), axis=0)

    def by_row(refs, columns=slice(None)):
        slot_rows = receive(refs, columns)
        return jnp.concatenate([slot_rows[reverse[j]] for j in range(links)], axis=0)

    def pack(index_ref, count_ref, nodes_ref, cot_ref, select_ref, *out_refs):
        def column(row):
            count = row.shape[1]
            eye = lax.broadcasted_iota(jnp.int32, (count, count), 0) == lax.broadcasted_iota(
                jnp.int32, (count, count), 1
            )
            return jnp.sum(
                jnp.where(eye, jnp.broadcast_to(row, (count, count)), 0.0), axis=1, keepdims=True
            )

        counts = column(count_ref[...].reshape(1, -1).astype(F32))
        place = lax.broadcasted_iota(jnp.int32, (links, width), 1).astype(F32)
        index = jnp.where(place < counts, index_ref[...].astype(F32), -1.0)
        lane = lax.broadcasted_iota(jnp.int32, (width, grid_count), 1).astype(F32)
        picks = [
            jnp.where(lane == column(index[j : j + 1, :]), 1.0, 0.0).astype(BF16)
            for j in range(links)
        ]
        select = jnp.concatenate(picks, axis=0)
        select_ref[:slots, :] = select
        select_ref[slots:, :] = jnp.zeros((slots_pad - slots, grid_count), BF16)
        sent_nodes = mm(select, nodes_ref[...]).astype(BF16)
        sent_cot = mm(select, cot_ref[...]).astype(BF16)
        send(out_refs, lambda j: sent_nodes[j * width : (j + 1) * width, :], low)
        send(out_refs, lambda j: sent_cot[j * width : (j + 1) * width, :], high)

    select, *outgoing = call(
        pack,
        "pack_rows",
        [
            (send_index, 0, links),
            (send_count, 0, links),
            (grid_nodes, 0, grid_count),
            (grid_cot, 0, grid_count),
        ],
        [((slots_pad, grid_count), BF16)] + sent_shapes(2 * feat),
        flops=4 * slots * grid_count * feat,
    )
    arrived = exchange(outgoing)

    def local(
        select_ref,
        nodes_ref,
        mesh_ref,
        enc_edges_ref,
        dec_edges_ref,
        enc_wg_ref,
        enc_wm_ref,
        enc_we_ref,
        dec_wg_ref,
        dec_we_ref,
        mesh_wn_ref,
        enc_grid_ref,
        enc_mesh_ref,
        dec_grid_ref,
        dec_mesh_ref,
        select_t_ref,
        enc_part_ref,
        dec_part_ref,
        mesh_part_ref,
        enc_pick_ref,
        enc_pool_ref,
        dec_pick_ref,
        dec_pool_ref,
        table_ref,
    ):
        onehot_pair(enc_grid_ref, enc_mesh_ref, spots, enc_pick_ref, enc_pool_ref)
        onehot_pair(dec_grid_ref, dec_mesh_ref, spots, dec_pick_ref, dec_pool_ref)
        select_t_ref[...] = select_ref[...].astype(F32).T.astype(BF16)
        nodes = nodes_ref[...]
        mesh_part_ref[...] = mm(mesh_ref[...], mesh_wn_ref[...])
        table_ref[:grid_count, :] = mm(nodes, enc_wg_ref[...]).astype(BF16)
        table_ref[grid_count:, :] = jnp.zeros((total - grid_count, feat), BF16)
        table_ref[mesh_rows, :] = mm(mesh_ref[...], enc_wm_ref[...]).astype(BF16)
        enc_part_ref[...] = mm(enc_edges_ref[...], enc_we_ref[...])
        enc_part_ref[...] += mm(enc_pick_ref[...], table_ref[...])
        pd = mm(nodes, dec_wg_ref[...]).astype(BF16)
        dec_part_ref[...] = mm(dec_edges_ref[...], dec_we_ref[...])
        dec_part_ref[...] += mm(dec_pick_ref[:, :grid_count], pd)

    select_t, enc_part, dec_part, mesh_part, enc_pick, enc_pool, dec_pick, dec_pool = call(
        local,
        "local_products",
        [
            select,
            (grid_nodes, 0, grid_count),
            (mesh_nodes, 0, mesh_count),
            (enc_edges, 0, enc_count),
            (dec_edges, 0, dec_count),
            (enc_first, 0, feat),
            (enc_first, feat, feat),
            (enc_first, 2 * feat, feat),
            (dec_first, 0, feat),
            (dec_first, 2 * feat, feat),
            (mesh_first, 0, feat),
            (enc_grid, 0, enc_grid.shape[0]),
            (enc_mesh, 0, enc_mesh.shape[0]),
            (dec_grid, 0, dec_grid.shape[0]),
            (dec_mesh, 0, dec_mesh.shape[0]),
        ],
        [
            ((grid_count, slots_pad), BF16),
            ((enc_count, feat), F32),
            ((dec_count, feat), F32),
            ((mesh_count, feat), F32),
            ((enc_count, total), BF16),
            ((total, enc_count), BF16),
            ((dec_count, total), BF16),
            ((total, dec_count), BF16),
        ],
        scratch=[((total, feat), BF16)],
        flops=2 * feat * (feat * (2 * grid_count + enc_count + dec_count) + total * dec_count),
    )

    def forward(*refs):
        arrived_refs, refs = refs[:links], refs[links:]
        (
            select_ref,
            enc_part_ref,
            dec_part_ref,
            mesh_part_ref,
            enc_pick_ref,
            enc_pool_ref,
            dec_pick_ref,
            dec_pool_ref,
            mesh_ref,
            enc_wg_ref,
            dec_wg_ref,
            enc_w2_ref,
            mesh_wa_ref,
            mesh_w2_ref,
            dec_wm_ref,
            dec_w2_ref,
        ) = refs[:16]
        refs = refs[16:]
        out_refs, refs = refs[:sent_count], refs[sent_count:]
        (
            mesh_out_ref,
            spot_ref,
            enc_normed_ref,
            enc_scale_ref,
            enc_slope_ref,
            dec_normed_ref,
            dec_scale_ref,
            dec_slope_ref,
            mesh_normed_ref,
            mesh_scale_ref,
            mesh_slope_ref,
            enc_act_ref,
            dec_act_ref,
            mesh_act_ref,
            table_ref,
        ) = refs
        rows = by_slot(arrived_refs, low)
        pe = mm(rows, enc_wg_ref[low, :]).astype(BF16)
        pre = enc_part_ref[...] + mm(enc_pick_ref[:, grid_count:spots], pe)
        activate(pre, enc_act_ref, enc_slope_ref)
        norm_forward(mm(enc_act_ref[...], enc_w2_ref[...]), enc_normed_ref, enc_scale_ref)
        agg = mm(enc_pool_ref[mesh_rows, :], enc_normed_ref[...]).astype(BF16)
        activate(mesh_part_ref[...] + mm(agg, mesh_wa_ref[high, :]), mesh_act_ref, mesh_slope_ref)
        norm_forward(mm(mesh_act_ref[...], mesh_w2_ref[...]), mesh_normed_ref, mesh_scale_ref)
        mesh_out = (mesh_ref[...].astype(F32) + mesh_normed_ref[...]).astype(BF16)
        mesh_out_ref[...] = mesh_out
        table_ref[:slots, :] = mm(rows, dec_wg_ref[low, :]).astype(BF16)
        table_ref[slots : slots + mesh_count, :] = mm(mesh_out, dec_wm_ref[high, :]).astype(BF16)
        table_ref[slots + mesh_count :, :] = jnp.zeros(
            (total - spots - mesh_count, feat), BF16
        )
        pre = dec_part_ref[...] + mm(dec_pick_ref[:, grid_count:], table_ref[...])
        activate(pre, dec_act_ref, dec_slope_ref)
        norm_forward(mm(dec_act_ref[...], dec_w2_ref[...]), dec_normed_ref, dec_scale_ref)
        spot_ref[...] = mm(dec_pool_ref[:spots, :], dec_normed_ref[...])
        shared = mm(select_ref[:slots, :], spot_ref[:grid_count, :].astype(BF16)).astype(BF16)
        slot_msg = spot_ref[grid_count:, :].astype(BF16)
        send(
            out_refs, lambda j: slot_msg[reverse[j] * width : (reverse[j] + 1) * width, :], low
        )
        send(out_refs, lambda j: shared[j * width : (j + 1) * width, :], high)

    edge_saved = [
        ((enc_count, feat), BF16),
        ((enc_count, 1), F32),
        ((enc_count, feat), BF16),
        ((dec_count, feat), BF16),
        ((dec_count, 1), F32),
        ((dec_count, feat), BF16),
        ((mesh_count, feat), F32),
        ((mesh_count, 1), F32),
        ((mesh_count, feat), BF16),
    ]
    results = call(
        forward,
        "edges_forward",
        [
            *arrived,
            select,
            enc_part,
            dec_part,
            mesh_part,
            enc_pick,
            enc_pool,
            dec_pick,
            dec_pool,
            mesh_nodes,
            enc_first,
            dec_first,
            enc_second,
            mesh_first,
            mesh_second,
            dec_first,
            dec_second,
        ],
        sent_shapes(2 * feat)
        + [((mesh_count, feat), BF16), ((spots, feat), F32)]
        + edge_saved,
        scratch=[
            ((enc_count, feat), BF16),
            ((dec_count, feat), BF16),
            ((mesh_count, feat), BF16),
            ((total - grid_count, feat), BF16),
        ],
        flops=2 * feat * feat * 2 * (enc_count + dec_count),
    )
    outgoing, results = results[:sent_count], results[sent_count:]
    mesh_out, spot_msg, *saved = results
    returned = exchange(outgoing)

    def node_part(*refs):
        arrived_refs, (nodes_ref, weight_ref, out_ref) = refs[:links], refs[links:]
        out_ref[:grid_count, :] = mm(nodes_ref[...], weight_ref[low, :])
        out_ref[grid_count:, :] = mm(by_slot(arrived_refs, low), weight_ref[low, :])

    (grid_part,) = call(
        node_part,
        "node_products",
        [*arrived, grid_nodes, grid_first],
        [((spots, feat), F32)],
        flops=2 * spots * feat * feat,
    )

    def backward(*refs):
        arrived_refs, returned_refs, refs = refs[:links], refs[links : 2 * links], refs[2 * links :]
        (
            spot_ref,
            grid_part_ref,
            select_t_ref,
            nodes_ref,
            cot_ref,
            mesh_cot_ref,
            enc_pick_ref,
            enc_pool_ref,
            dec_pick_ref,
            dec_pool_ref,
            grid_wa_ref,
            grid_w2_ref,
            dec_w2_ref,
            dec_wm_ref,
            mesh_wa_ref,
            mesh_w2_ref,
            enc_w2_ref,
            enc_wg_ref,
            dec_wg_ref,
            enc_normed_ref,
            enc_scale_ref,
            enc_slope_ref,
            dec_normed_ref,
            dec_scale_ref,
            dec_slope_ref,
            mesh_normed_ref,
            mesh_scale_ref,
            mesh_slope_ref,
        ) = refs[:28]
        refs = refs[28:]
        out_refs, refs = refs[:sent_count], refs[sent_count:]
        (
            grid_out_ref,
            grid_gpre_ref,
            gpe_ref,
            gpd_ref,
            mesh_gin_ref,
            mesh_gpre_ref,
            mesh_pool_ref,
            agg_ref,
            grid_act_ref,
            grid_slope_ref,
            grid_normed_ref,
            grid_scale_ref,
            grid_gout_ref,
            grid_gall_ref,
            spot_grad_ref,
            dec_gout_ref,
            mesh_gout_ref,
            enc_gout_ref,
        ) = refs
        agg_ref[:grid_count, :] = (
            spot_ref[:grid_count, :] + mm(select_t_ref[:, :slots], by_row(returned_refs, low))
        ).astype(BF16)
        agg_ref[grid_count:, :] = (
            spot_ref[grid_count:, :] + by_slot(returned_refs, high).astype(F32)
        ).astype(BF16)
        activate(
            grid_part_ref[...] + mm(agg_ref[...], grid_wa_ref[high, :]), grid_act_ref, grid_slope_ref
        )
        norm_forward(mm(grid_act_ref[...], grid_w2_ref[...]), grid_normed_ref, grid_scale_ref)
        grid_out_ref[...] = (
            nodes_ref[...].astype(F32) + grid_normed_ref[:grid_count, :]
        ).astype(BF16)
        cot = jnp.concatenate([cot_ref[...], by_slot(arrived_refs, high)], axis=0)
        norm_backward(grid_normed_ref, grid_scale_ref, cot, grid_gout_ref)
        times_slope(mm_t(grid_gout_ref[...], grid_w2_ref[...]), grid_slope_ref, grid_gall_ref)
        grid_gpre_ref[...] = grid_gall_ref[:grid_count, :]
        spot_grad_ref[:spots, :] = mm_t(grid_gall_ref[...], grid_wa_ref[high, :]).astype(BF16)
        spot_grad_ref[spots:, :] = jnp.zeros((total - spots, feat), BF16)
        norm_backward(
            dec_normed_ref, dec_scale_ref, mm(dec_pick_ref[...], spot_grad_ref[...]), dec_gout_ref
        )
        times_slope(mm_t(dec_gout_ref[...], dec_w2_ref[...]), dec_slope_ref, dec_gout_ref)
        pooled = mm(dec_pool_ref[...], dec_gout_ref[...]).astype(BF16)
        gpd_ref[...] = pooled[:grid_count, :]
        slot_back = mm_t(pooled[grid_count:spots, :], dec_wg_ref[low, :])
        mesh_gin = mesh_cot_ref[...].astype(F32) + mm_t(pooled[mesh_rows, :], dec_wm_ref[high, :])
        mesh_gin_ref[...] = mesh_gin
        norm_backward(mesh_normed_ref, mesh_scale_ref, mesh_gin, mesh_gout_ref)
        times_slope(mm_t(mesh_gout_ref[...], mesh_w2_ref[...]), mesh_slope_ref, mesh_gpre_ref)
        gagg = mm_t(mesh_gpre_ref[...], mesh_wa_ref[high, :]).astype(BF16)
        norm_backward(
            enc_normed_ref, enc_scale_ref, mm(enc_pick_ref[:, mesh_rows], gagg), enc_gout_ref
        )
        times_slope(mm_t(enc_gout_ref[...], enc_w2_ref[...]), enc_slope_ref, enc_gout_ref)
        pooled = mm(enc_pool_ref[...], enc_gout_ref[...]).astype(BF16)
        gpe_ref[...] = pooled[:grid_count, :]
        mesh_pool_ref[...] = pooled[mesh_rows, :]
        slot_back = (slot_back + mm_t(pooled[grid_count:spots, :], enc_wg_ref[low, :])).astype(BF16)
        send(out_refs, lambda j: slot_back[reverse[j] * width : (reverse[j] + 1) * width, :])

    results = call(
        backward,
        "edges_backward",
        [
            *arrived,
            *returned,
            spot_msg,
            grid_part,
            select_t,
            grid_nodes,
            grid_cot,
            mesh_cot,
            enc_pick,
            enc_pool,
            dec_pick,
            dec_pool,
            grid_first,
            grid_second,
            dec_second,
            dec_first,
            mesh_first,
            mesh_second,
            enc_second,
            enc_first,
            dec_first,
            *saved,
        ],
        sent_shapes(feat)
        + [((grid_count, feat), BF16)] * 4
        + [((mesh_count, feat), F32), ((mesh_count, feat), BF16), ((mesh_count, feat), BF16)],
        scratch=[
            ((spots, feat), BF16),
            ((spots, feat), BF16),
            ((spots, feat), BF16),
            ((spots, feat), F32),
            ((spots, 1), F32),
            ((spots, feat), BF16),
            ((spots, feat), BF16),
            ((total, feat), BF16),
            ((dec_count, feat), BF16),
            ((mesh_count, feat), BF16),
            ((enc_count, feat), BF16),
        ],
        flops=2 * feat * feat * (4 * spots + 3 * dec_count + 2 * enc_count),
    )
    outgoing, results = results[:sent_count], results[sent_count:]
    grid_out, grid_gpre, gpe, gpd, mesh_gin, mesh_gpre, mesh_pool = results
    final = exchange(outgoing)

    def tail(
        cot_ref,
        grid_gpre_ref,
        gpe_ref,
        gpd_ref,
        mesh_gin_ref,
        mesh_gpre_ref,
        mesh_pool_ref,
        grid_wn_ref,
        enc_wg_ref,
        dec_wg_ref,
        mesh_wn_ref,
        enc_wm_ref,
        base_ref,
        grad_mesh_ref,
    ):
        base_ref[...] = (
            cot_ref[...].astype(F32)
            + mm_t(grid_gpre_ref[...], grid_wn_ref[low, :])
            + mm_t(gpe_ref[...], enc_wg_ref[low, :])
            + mm_t(gpd_ref[...], dec_wg_ref[low, :])
        )
        grad_mesh_ref[...] = (
            mesh_gin_ref[...]
            + mm_t(mesh_gpre_ref[...], mesh_wn_ref[low, :])
            + mm_t(mesh_pool_ref[...], enc_wm_ref[high, :])
        )

    base, grad_mesh = call(
        tail,
        "local_gradients",
        [
            grid_cot,
            grid_gpre,
            gpe,
            gpd,
            mesh_gin,
            mesh_gpre,
            mesh_pool,
            grid_first,
            enc_first,
            dec_first,
            mesh_first,
            enc_first,
        ],
        [((grid_count, feat), F32), ((mesh_count, feat), F32)],
        flops=2 * feat * feat * 3 * grid_count,
    )

    def finish(*refs):
        back_refs, (base_ref, select_t_ref, out_ref) = refs[:links], refs[links:]
        out_ref[...] = base_ref[...] + mm(select_t_ref[:, :slots], by_row(back_refs))

    (grad_grid,) = call(
        finish,
        "add_returned",
        [*final, base, select_t],
        [((grid_count, feat), F32)],
        flops=2 * grid_count * slots * feat,
    )
    return (grid_out, mesh_out, grad_grid, grad_mesh)


def solution(mesh):
    rows = P(("groups", "tile"), None)
    flat = P(("groups", "tile"))
    in_specs = (rows,) * 6 + (P(),) * 8 + (rows,) + (flat,) * 5
    return jax.shard_map(
        per_device, mesh=mesh, in_specs=in_specs, out_specs=(rows,) * 4, check_vma=False
    )
```

```python
import jax
import jax.numpy as jnp
from jax import lax
from jax.experimental import pallas as pl
from jax.experimental.pallas import tpu as pltpu
from jax.sharding import PartitionSpec as P

TW = 4
CHUNK = 32
F32 = jnp.float32
BF16 = jnp.bfloat16
VMEM_LIMIT = 30 * 1024 * 1024


def mm(left, right):
    return jnp.dot(left, right, preferred_element_type=F32)


def mm_t(left, right):
    return lax.dot_general(left, right, (((1,), (1,)), ((), ())), preferred_element_type=F32)


def sigmoid(values):
    return 0.5 * jnp.tanh(0.5 * values) + 0.5


def norm_rows(values):
    centre = values - jnp.mean(values, axis=-1, keepdims=True)
    scale_inv = lax.rsqrt(jnp.mean(centre * centre, axis=-1, keepdims=True) + 1e-05)
    return centre * scale_inv, scale_inv


def norm_back(normed, scale_inv, upstream):
    return scale_inv * (
        upstream
        - jnp.mean(upstream, axis=-1, keepdims=True)
        - normed * jnp.mean(upstream * normed, axis=-1, keepdims=True)
    )


def row_chunks(rows, size=CHUNK):
    return [slice(start, min(start + size, rows)) for start in range(0, rows, size)]


def activate(pre, act_ref, slope_ref):
    for rows in row_chunks(pre.shape[0]):
        part = pre[rows, :]
        gate = sigmoid(part)
        act = part * gate
        act_ref[rows, :] = act.astype(BF16)
        slope_ref[rows, :] = (gate + act * (1.0 - gate)).astype(BF16)


def norm_forward(raw, normed_ref, scale_ref):
    for rows in row_chunks(raw.shape[0]):
        normed, scale_inv = norm_rows(raw[rows, :])
        normed_ref[rows, :] = normed.astype(normed_ref.dtype)
        scale_ref[rows, :] = scale_inv


def norm_backward(normed_ref, scale_ref, upstream, out_ref):
    for rows in row_chunks(out_ref.shape[0]):
        out_ref[rows, :] = norm_back(
            normed_ref[rows, :].astype(F32), scale_ref[rows, :], upstream[rows, :].astype(F32)
        ).astype(BF16)


def times_slope(raw, slope_ref, out_ref):
    for rows in row_chunks(out_ref.shape[0]):
        out_ref[rows, :] = (raw[rows, :] * slope_ref[rows, :].astype(F32)).astype(BF16)


def neighbour_offsets(peer_count):
    forward_half = [1, TW, TW + 1, TW - 1]
    return forward_half + [-offset for offset in forward_half] + [peer_count // 2]


def onehot_pair(spot_ref, mesh_ref, spots, by_edge_ref, by_spot_ref):
    edges, total = by_edge_ref.shape
    spot_row = spot_ref[...].reshape(1, -1).astype(F32)
    mesh_row = mesh_ref[...].reshape(1, -1).astype(F32) + float(spots)
    for rows in row_chunks(total, 64):
        ids = lax.broadcasted_iota(jnp.int32, (rows.stop - rows.start, edges), 0) + rows.start
        ids = ids.astype(F32)
        hit = (ids == spot_row) | (ids == mesh_row)
        by_spot_ref[rows, :] = jnp.where(hit, 1.0, 0.0).astype(BF16)
    for rows in row_chunks(edges, 128):
        spot_col = jnp.broadcast_to(spot_row[:, rows], (128, 128)).T
        mesh_col = jnp.broadcast_to(mesh_row[:, rows], (128, 128)).T
        for columns in row_chunks(total, 128):
            ids = lax.broadcasted_iota(jnp.int32, (128, 128), 1) + columns.start
            ids = ids.astype(F32)
            hit = (ids == spot_col) | (ids == mesh_col)
            by_edge_ref[rows, columns] = jnp.where(hit, 1.0, 0.0).astype(BF16)


class Fetched:
    def __init__(self, source, target, semaphore):
        self.copy = pltpu.make_async_copy(source, target, semaphore)
        self.target = target
        self.landed = False
        self.copy.start()

    def land(self):
        if not self.landed:
            self.copy.wait()
            self.landed = True

    def __getitem__(self, key):
        self.land()
        return self.target[key]


def call(body, name, inputs, outputs, scratch=(), flops=0):
    arrays, specs, moved, fetches = [], [], 0, []
    for place, entry in enumerate(inputs):
        if isinstance(entry, tuple):
            array, first, rows = entry
            array = pltpu.with_memory_space_constraint(array, pltpu.HBM)
            specs.append(pl.BlockSpec(memory_space=pltpu.HBM))
            shape = (rows,) + array.shape[1:]
            fetches.append((place, first, rows, shape, array.dtype))
            moved += rows * (array.size // array.shape[0]) * array.dtype.itemsize
        else:
            array = entry
            specs.append(pl.BlockSpec(memory_space=pltpu.VMEM))
            moved += array.size * array.dtype.itemsize
        arrays.append(array)
    shapes = [jax.ShapeDtypeStruct(shape, dtype) for shape, dtype in outputs]
    for shape in shapes:
        moved += shape.size * shape.dtype.itemsize
    buffers = [pltpu.VMEM(shape, dtype) for _, _, _, shape, dtype in fetches]
    if fetches:
        buffers.append(pltpu.SemaphoreType.DMA((len(fetches),)))

    def kernel(*refs):
        refs = list(refs)
        if not fetches:
            body(*refs)
            return
        refs, targets, semaphores = (
            refs[: -len(buffers)],
            refs[-len(buffers) : -1],
            refs[-1],
        )
        waiting = []
        for slot, (place, first, rows, shape, _) in enumerate(fetches):
            source = refs[place]
            if source.shape != shape:
                source = source.at[pl.ds(first, rows)]
            refs[place] = Fetched(source, targets[slot], semaphores.at[slot])
            waiting.append(refs[place])
        body(*refs)
        for fetched in waiting:
            fetched.land()

    return pl.pallas_call(
        kernel,
        name=name,
        in_specs=specs,
        out_specs=[pl.BlockSpec(memory_space=pltpu.VMEM) for _ in shapes],
        out_shape=shapes,
        scratch_shapes=[pltpu.VMEM(shape, dtype) for shape, dtype in scratch] + buffers,
        compiler_params=pltpu.CompilerParams(vmem_limit_bytes=VMEM_LIMIT),
        cost_estimate=pl.CostEstimate(flops=flops, bytes_accessed=moved, transcendentals=0),
    )(*arrays)


def per_device(
    grid_nodes,
    mesh_nodes,
    enc_edges,
    dec_edges,
    grid_cot,
    mesh_cot,
    enc_first,
    enc_second,
    mesh_first,
    mesh_second,
    dec_first,
    dec_second,
    grid_first,
    grid_second,
    send_index,
    send_count,
    enc_grid,
    enc_mesh,
    dec_grid,
    dec_mesh,
):
    grid_count, feat = grid_nodes.shape
    mesh_count = mesh_nodes.shape[0]
    enc_count = enc_edges.shape[0]
    dec_count = dec_edges.shape[0]
    links, width = send_index.shape
    slots = links * width
    slots_pad = -(-slots // 128) * 128
    spots = grid_count + slots
    total = -(-(spots + mesh_count) // 128) * 128
    peer_count = lax.axis_size("tile")
    offsets = neighbour_offsets(peer_count)
    half = (links - 1) // 2
    reverse = [(j + half) % (links - 1) for j in range(links - 1)] + [links - 1]
    low, high = slice(0, feat), slice(feat, 2 * feat)
    mesh_rows = slice(spots, spots + mesh_count)

    one, four, five, three = range(half)
    minus = [j + half for j in range(half)]
    across = links - 1
    peers = range(peer_count)

    def permute(part, even_step, odd_step):
        steps = (even_step, odd_step)
        return lax.ppermute(part, "tile", [(s, (s + steps[s % 2]) % peer_count) for s in peers])

    def lay_together(kept_ref, got_ref, next_ref, second_ref):
        next_ref[:width, :] = kept_ref[:width, :]
        next_ref[width:, :] = got_ref[width : 2 * width, :]
        second_ref[:width, :] = kept_ref[width : 2 * width, :]
        second_ref[width : 2 * width, :] = got_ref[3 * width :, :]
        second_ref[2 * width : 3 * width, :] = kept_ref[2 * width :, :]
        second_ref[3 * width :, :] = got_ref[2 * width : 3 * width, :]

    def exchange(parts):
        for_partner, three_off, opposite, kept = parts
        columns = kept.shape[1]
        got = permute(for_partner, 1, -1)
        opposite = permute(opposite, peer_count // 2, peer_count // 2)
        three_off = permute(three_off, -5, 5)
        next_chip, second_chip = call(
            lay_together,
            "lay_together",
            [kept, got],
            [((2 * width, columns), BF16), ((4 * width, columns), BF16)],
        )
        second_chip = permute(second_chip, -4, 4)
        next_chip = permute(next_chip, -2, 2)
        second_passed = permute(second_chip, 1, -1)
        next_passed = permute(next_chip, 1, -1)
        return [got, opposite, three_off, second_chip, next_chip, second_passed, next_passed]

    arrived_count = 7

    def sent_shapes(columns):
        return [((count * width, columns), BF16) for count in (4, 1, 1, 3)]

    sent_count = len(sent_shapes(feat))

    def is_odd():
        return lax.rem(lax.axis_index("tile"), 2) == 1

    def send(refs, message, columns=slice(None)):
        odd = is_odd()
        for_partner, three_off, opposite, kept = refs

        def block(place):
            return slice(place * width, (place + 1) * width)

        for place, step in enumerate((one, three, four, five)):
            ahead, behind = message(step), message(minus[step])
            for_partner[block(place), columns] = jnp.where(odd, behind, ahead)
            own = jnp.where(odd, ahead, behind)
            if step == five:
                three_off[:, columns] = own
            else:
                kept[block((one, four, three).index(step)), columns] = own
        opposite[:, columns] = message(across)

    def receive(refs, columns=slice(None)):
        odd = is_odd()
        got, opposite, three_off, second_chip, next_chip, second_passed, next_passed = refs

        def block(ref, place):
            return ref[place * width : (place + 1) * width, columns]

        pairs = {
            one: (block(got, 0), block(next_passed, 0)),
            three: (block(next_chip, 1), block(second_passed, 2)),
            four: (block(second_chip, 0), block(second_passed, 3)),
            five: (block(second_chip, 1), block(three_off, 0)),
        }
        slot_rows = [None] * links
        for step, (near, far) in pairs.items():
            slot_rows[step] = jnp.where(odd, near, far)
            slot_rows[minus[step]] = jnp.where(odd, far, near)
        slot_rows[across] = opposite[:, columns]
        return slot_rows

    def by_slot(refs, columns=slice(None)):
        return jnp.concatenate(receive(refs, columns), axis=0)

    def by_row(refs, columns=slice(None)):
        slot_rows = receive(refs, columns)
        return jnp.concatenate([slot_rows[reverse[j]] for j in range(links)], axis=0)

    def pack(index_ref, count_ref, nodes_ref, cot_ref, select_ref, *out_refs):
        def column(row):
            count = row.shape[1]
            eye = lax.broadcasted_iota(jnp.int32, (count, count), 0) == lax.broadcasted_iota(
                jnp.int32, (count, count), 1
            )
            return jnp.sum(
                jnp.where(eye, jnp.broadcast_to(row, (count, count)), 0.0), axis=1, keepdims=True
            )

        counts = column(count_ref[...].reshape(1, -1).astype(F32))
        place = lax.broadcasted_iota(jnp.int32, (links, width), 1).astype(F32)
        index = jnp.where(place < counts, index_ref[...].astype(F32), -1.0)
        lane = lax.broadcasted_iota(jnp.int32, (width, grid_count), 1).astype(F32)
        picks = [
            jnp.where(lane == column(index[j : j + 1, :]), 1.0, 0.0).astype(BF16)
            for j in range(links)
        ]
        select = jnp.concatenate(picks, axis=0)
        select_ref[:slots, :] = select
        select_ref[slots:, :] = jnp.zeros((slots_pad - slots, grid_count), BF16)
        sent_nodes = mm(select, nodes_ref[...]).astype(BF16)
        sent_cot = mm(select, cot_ref[...]).astype(BF16)
        send(out_refs, lambda j: sent_nodes[j * width : (j + 1) * width, :], low)
        send(out_refs, lambda j: sent_cot[j * width : (j + 1) * width, :], high)

    select, *outgoing = call(
        pack,
        "pack_rows",
        [
            (send_index, 0, links),
            (send_count, 0, links),
            (grid_nodes, 0, grid_count),
            (grid_cot, 0, grid_count),
        ],
        [((slots_pad, grid_count), BF16)] + sent_shapes(2 * feat),
        flops=4 * slots * grid_count * feat,
    )
    arrived = exchange(outgoing)

    def local(
        select_ref,
        nodes_ref,
        mesh_ref,
        enc_edges_ref,
        dec_edges_ref,
        enc_wg_ref,
        enc_wm_ref,
        enc_we_ref,
        dec_wg_ref,
        dec_we_ref,
        mesh_wn_ref,
        enc_grid_ref,
        enc_mesh_ref,
        dec_grid_ref,
        dec_mesh_ref,
        select_t_ref,
        enc_part_ref,
        dec_part_ref,
        mesh_part_ref,
        enc_pick_ref,
        enc_pool_ref,
        dec_pick_ref,
        dec_pool_ref,
        table_ref,
    ):
        onehot_pair(enc_grid_ref, enc_mesh_ref, spots, enc_pick_ref, enc_pool_ref)
        onehot_pair(dec_grid_ref, dec_mesh_ref, spots, dec_pick_ref, dec_pool_ref)
        select_t_ref[...] = select_ref[...].astype(F32).T.astype(BF16)
        nodes = nodes_ref[...]
        mesh_part_ref[...] = mm(mesh_ref[...], mesh_wn_ref[...])
        table_ref[:grid_count, :] = mm(nodes, enc_wg_ref[...]).astype(BF16)
        table_ref[grid_count:, :] = jnp.zeros((total - grid_count, feat), BF16)
        table_ref[mesh_rows, :] = mm(mesh_ref[...], enc_wm_ref[...]).astype(BF16)
        enc_part_ref[...] = mm(enc_edges_ref[...], enc_we_ref[...])
        enc_part_ref[...] += mm(enc_pick_ref[...], table_ref[...])
        pd = mm(nodes, dec_wg_ref[...]).astype(BF16)
        dec_part_ref[...] = mm(dec_edges_ref[...], dec_we_ref[...])
        dec_part_ref[...] += mm(dec_pick_ref[:, :grid_count], pd)

    select_t, enc_part, dec_part, mesh_part, enc_pick, enc_pool, dec_pick, dec_pool = call(
        local,
        "local_products",
        [
            select,
            (grid_nodes, 0, grid_count),
            (mesh_nodes, 0, mesh_count),
            (enc_edges, 0, enc_count),
            (dec_edges, 0, dec_count),
            (enc_first, 0, feat),
            (enc_first, feat, feat),
            (enc_first, 2 * feat, feat),
            (dec_first, 0, feat),
            (dec_first, 2 * feat, feat),
            (mesh_first, 0, feat),
            (enc_grid, 0, enc_grid.shape[0]),
            (enc_mesh, 0, enc_mesh.shape[0]),
            (dec_grid, 0, dec_grid.shape[0]),
            (dec_mesh, 0, dec_mesh.shape[0]),
        ],
        [
            ((grid_count, slots_pad), BF16),
            ((enc_count, feat), F32),
            ((dec_count, feat), F32),
            ((mesh_count, feat), F32),
            ((enc_count, total), BF16),
            ((total, enc_count), BF16),
            ((dec_count, total), BF16),
            ((total, dec_count), BF16),
        ],
        scratch=[((total, feat), BF16)],
        flops=2 * feat * (feat * (2 * grid_count + enc_count + dec_count) + total * dec_count),
    )

    def forward(*refs):
        arrived_refs, refs = refs[:arrived_count], refs[arrived_count:]
        (
            select_ref,
            enc_part_ref,
            dec_part_ref,
            mesh_part_ref,
            enc_pick_ref,
            enc_pool_ref,
            dec_pick_ref,
            dec_pool_ref,
            mesh_ref,
            enc_wg_ref,
            dec_wg_ref,
            enc_w2_ref,
            mesh_wa_ref,
            mesh_w2_ref,
            dec_wm_ref,
            dec_w2_ref,
        ) = refs[:16]
        refs = refs[16:]
        out_refs, refs = refs[:sent_count], refs[sent_count:]
        (
            mesh_out_ref,
            spot_ref,
            enc_normed_ref,
            enc_scale_ref,
            enc_slope_ref,
            dec_normed_ref,
            dec_scale_ref,
            dec_slope_ref,
            mesh_normed_ref,
            mesh_scale_ref,
            mesh_slope_ref,
            enc_act_ref,
            dec_act_ref,
            mesh_act_ref,
            table_ref,
        ) = refs
        rows = by_slot(arrived_refs, low)
        pe = mm(rows, enc_wg_ref[low, :]).astype(BF16)
        pre = enc_part_ref[...] + mm(enc_pick_ref[:, grid_count:spots], pe)
        activate(pre, enc_act_ref, enc_slope_ref)
        norm_forward(mm(enc_act_ref[...], enc_w2_ref[...]), enc_normed_ref, enc_scale_ref)
        agg = mm(enc_pool_ref[mesh_rows, :], enc_normed_ref[...]).astype(BF16)
        activate(mesh_part_ref[...] + mm(agg, mesh_wa_ref[high, :]), mesh_act_ref, mesh_slope_ref)
        norm_forward(mm(mesh_act_ref[...], mesh_w2_ref[...]), mesh_normed_ref, mesh_scale_ref)
        mesh_out = (mesh_ref[...].astype(F32) + mesh_normed_ref[...]).astype(BF16)
        mesh_out_ref[...] = mesh_out
        table_ref[:slots, :] = mm(rows, dec_wg_ref[low, :]).astype(BF16)
        table_ref[slots : slots + mesh_count, :] = mm(mesh_out, dec_wm_ref[high, :]).astype(BF16)
        table_ref[slots + mesh_count :, :] = jnp.zeros(
            (total - spots - mesh_count, feat), BF16
        )
        pre = dec_part_ref[...] + mm(dec_pick_ref[:, grid_count:], table_ref[...])
        activate(pre, dec_act_ref, dec_slope_ref)
        norm_forward(mm(dec_act_ref[...], dec_w2_ref[...]), dec_normed_ref, dec_scale_ref)
        spot_ref[...] = mm(dec_pool_ref[:spots, :], dec_normed_ref[...])
        shared = mm(select_ref[:slots, :], spot_ref[:grid_count, :].astype(BF16)).astype(BF16)
        slot_msg = spot_ref[grid_count:, :].astype(BF16)
        send(
            out_refs, lambda j: slot_msg[reverse[j] * width : (reverse[j] + 1) * width, :], low
        )
        send(out_refs, lambda j: shared[j * width : (j + 1) * width, :], high)

    edge_saved = [
        ((enc_count, feat), BF16),
        ((enc_count, 1), F32),
        ((enc_count, feat), BF16),
        ((dec_count, feat), BF16),
        ((dec_count, 1), F32),
        ((dec_count, feat), BF16),
        ((mesh_count, feat), F32),
        ((mesh_count, 1), F32),
        ((mesh_count, feat), BF16),
    ]
    results = call(
        forward,
        "edges_forward",
        [
            *arrived,
            select,
            enc_part,
            dec_part,
            mesh_part,
            enc_pick,
            enc_pool,
            dec_pick,
            dec_pool,
            mesh_nodes,
            enc_first,
            dec_first,
            enc_second,
            mesh_first,
            mesh_second,
            dec_first,
            dec_second,
        ],
        sent_shapes(2 * feat)
        + [((mesh_count, feat), BF16), ((spots, feat), F32)]
        + edge_saved,
        scratch=[
            ((enc_count, feat), BF16),
            ((dec_count, feat), BF16),
            ((mesh_count, feat), BF16),
            ((total - grid_count, feat), BF16),
        ],
        flops=2 * feat * feat * 2 * (enc_count + dec_count),
    )
    outgoing, results = results[:sent_count], results[sent_count:]
    mesh_out, spot_msg, *saved = results
    returned = exchange(outgoing)

    def node_part(*refs):
        arrived_refs = refs[:arrived_count]
        nodes_ref, weight_ref, out_ref = refs[arrived_count:]
        out_ref[:grid_count, :] = mm(nodes_ref[...], weight_ref[low, :])
        out_ref[grid_count:, :] = mm(by_slot(arrived_refs, low), weight_ref[low, :])

    (grid_part,) = call(
        node_part,
        "node_products",
        [*arrived, grid_nodes, grid_first],
        [((spots, feat), F32)],
        flops=2 * spots * feat * feat,
    )

    def backward(*refs):
        arrived_refs, refs = refs[:arrived_count], refs[arrived_count:]
        returned_refs, refs = refs[:arrived_count], refs[arrived_count:]
        (
            spot_ref,
            grid_part_ref,
            select_t_ref,
            nodes_ref,
            cot_ref,
            mesh_cot_ref,
            enc_pick_ref,
            enc_pool_ref,
            dec_pick_ref,
            dec_pool_ref,
            grid_wa_ref,
            grid_w2_ref,
            dec_w2_ref,
            dec_wm_ref,
            mesh_wa_ref,
            mesh_w2_ref,
            enc_w2_ref,
            enc_wg_ref,
            dec_wg_ref,
            enc_normed_ref,
            enc_scale_ref,
            enc_slope_ref,
            dec_normed_ref,
            dec_scale_ref,
            dec_slope_ref,
            mesh_normed_ref,
            mesh_scale_ref,
            mesh_slope_ref,
        ) = refs[:28]
        refs = refs[28:]
        out_refs, refs = refs[:sent_count], refs[sent_count:]
        (
            grid_out_ref,
            grid_gpre_ref,
            gpe_ref,
            gpd_ref,
            mesh_gin_ref,
            mesh_gpre_ref,
            mesh_pool_ref,
            agg_ref,
            grid_act_ref,
            grid_slope_ref,
            grid_normed_ref,
            grid_scale_ref,
            grid_gout_ref,
            grid_gall_ref,
            spot_grad_ref,
            dec_gout_ref,
            mesh_gout_ref,
            enc_gout_ref,
        ) = refs
        agg_ref[:grid_count, :] = (
            spot_ref[:grid_count, :] + mm(select_t_ref[:, :slots], by_row(returned_refs, low))
        ).astype(BF16)
        agg_ref[grid_count:, :] = (
            spot_ref[grid_count:, :] + by_slot(returned_refs, high).astype(F32)
        ).astype(BF16)
        activate(
            grid_part_ref[...] + mm(agg_ref[...], grid_wa_ref[high, :]), grid_act_ref, grid_slope_ref
        )
        norm_forward(mm(grid_act_ref[...], grid_w2_ref[...]), grid_normed_ref, grid_scale_ref)
        grid_out_ref[...] = (
            nodes_ref[...].astype(F32) + grid_normed_ref[:grid_count, :]
        ).astype(BF16)
        cot = jnp.concatenate([cot_ref[...], by_slot(arrived_refs, high)], axis=0)
        norm_backward(grid_normed_ref, grid_scale_ref, cot, grid_gout_ref)
        times_slope(mm_t(grid_gout_ref[...], grid_w2_ref[...]), grid_slope_ref, grid_gall_ref)
        grid_gpre_ref[...] = grid_gall_ref[:grid_count, :]
        spot_grad_ref[:spots, :] = mm_t(grid_gall_ref[...], grid_wa_ref[high, :]).astype(BF16)
        spot_grad_ref[spots:, :] = jnp.zeros((total - spots, feat), BF16)
        norm_backward(
            dec_normed_ref, dec_scale_ref, mm(dec_pick_ref[...], spot_grad_ref[...]), dec_gout_ref
        )
        times_slope(mm_t(dec_gout_ref[...], dec_w2_ref[...]), dec_slope_ref, dec_gout_ref)
        pooled = mm(dec_pool_ref[...], dec_gout_ref[...]).astype(BF16)
        gpd_ref[...] = pooled[:grid_count, :]
        slot_back = mm_t(pooled[grid_count:spots, :], dec_wg_ref[low, :])
        mesh_gin = mesh_cot_ref[...].astype(F32) + mm_t(pooled[mesh_rows, :], dec_wm_ref[high, :])
        mesh_gin_ref[...] = mesh_gin
        norm_backward(mesh_normed_ref, mesh_scale_ref, mesh_gin, mesh_gout_ref)
        times_slope(mm_t(mesh_gout_ref[...], mesh_w2_ref[...]), mesh_slope_ref, mesh_gpre_ref)
        gagg = mm_t(mesh_gpre_ref[...], mesh_wa_ref[high, :]).astype(BF16)
        norm_backward(
            enc_normed_ref, enc_scale_ref, mm(enc_pick_ref[:, mesh_rows], gagg), enc_gout_ref
        )
        times_slope(mm_t(enc_gout_ref[...], enc_w2_ref[...]), enc_slope_ref, enc_gout_ref)
        pooled = mm(enc_pool_ref[...], enc_gout_ref[...]).astype(BF16)
        gpe_ref[...] = pooled[:grid_count, :]
        mesh_pool_ref[...] = pooled[mesh_rows, :]
        slot_back = (slot_back + mm_t(pooled[grid_count:spots, :], enc_wg_ref[low, :])).astype(BF16)
        send(out_refs, lambda j: slot_back[reverse[j] * width : (reverse[j] + 1) * width, :])

    results = call(
        backward,
        "edges_backward",
        [
            *arrived,
            *returned,
            spot_msg,
            grid_part,
            select_t,
            grid_nodes,
            grid_cot,
            mesh_cot,
            enc_pick,
            enc_pool,
            dec_pick,
            dec_pool,
            grid_first,
            grid_second,
            dec_second,
            dec_first,
            mesh_first,
            mesh_second,
            enc_second,
            enc_first,
            dec_first,
            *saved,
        ],
        sent_shapes(feat)
        + [((grid_count, feat), BF16)] * 4
        + [((mesh_count, feat), F32), ((mesh_count, feat), BF16), ((mesh_count, feat), BF16)],
        scratch=[
            ((spots, feat), BF16),
            ((spots, feat), BF16),
            ((spots, feat), BF16),
            ((spots, feat), F32),
            ((spots, 1), F32),
            ((spots, feat), BF16),
            ((spots, feat), BF16),
            ((total, feat), BF16),
            ((dec_count, feat), BF16),
            ((mesh_count, feat), BF16),
            ((enc_count, feat), BF16),
        ],
        flops=2 * feat * feat * (4 * spots + 3 * dec_count + 2 * enc_count),
    )
    outgoing, results = results[:sent_count], results[sent_count:]
    grid_out, grid_gpre, gpe, gpd, mesh_gin, mesh_gpre, mesh_pool = results
    final = exchange(outgoing)

    def tail(
        cot_ref,
        grid_gpre_ref,
        gpe_ref,
        gpd_ref,
        mesh_gin_ref,
        mesh_gpre_ref,
        mesh_pool_ref,
        grid_wn_ref,
        enc_wg_ref,
        dec_wg_ref,
        mesh_wn_ref,
        enc_wm_ref,
        base_ref,
        grad_mesh_ref,
    ):
        base_ref[...] = (
            cot_ref[...].astype(F32)
            + mm_t(grid_gpre_ref[...], grid_wn_ref[low, :])
            + mm_t(gpe_ref[...], enc_wg_ref[low, :])
            + mm_t(gpd_ref[...], dec_wg_ref[low, :])
        )
        grad_mesh_ref[...] = (
            mesh_gin_ref[...]
            + mm_t(mesh_gpre_ref[...], mesh_wn_ref[low, :])
            + mm_t(mesh_pool_ref[...], enc_wm_ref[high, :])
        )

    base, grad_mesh = call(
        tail,
        "local_gradients",
        [
            grid_cot,
            grid_gpre,
            gpe,
            gpd,
            mesh_gin,
            mesh_gpre,
            mesh_pool,
            grid_first,
            enc_first,
            dec_first,
            mesh_first,
            enc_first,
        ],
        [((grid_count, feat), F32), ((mesh_count, feat), F32)],
        flops=2 * feat * feat * 3 * grid_count,
    )

    def finish(*refs):
        back_refs = refs[:arrived_count]
        base_ref, select_t_ref, out_ref = refs[arrived_count:]
        out_ref[...] = base_ref[...] + mm(select_t_ref[:, :slots], by_row(back_refs))

    (grad_grid,) = call(
        finish,
        "add_returned",
        [*final, base, select_t],
        [((grid_count, feat), F32)],
        flops=2 * grid_count * slots * feat,
    )
    return (grid_out, mesh_out, grad_grid, grad_mesh)


def solution(mesh):
    rows = P(("groups", "tile"), None)
    flat = P(("groups", "tile"))
    in_specs = (rows,) * 6 + (P(),) * 8 + (rows,) + (flat,) * 5
    return jax.shard_map(
        per_device, mesh=mesh, in_specs=in_specs, out_specs=(rows,) * 4, check_vma=False
    )
```

```python
import jax
import jax.numpy as jnp
from jax import lax
from jax.experimental import pallas as pl
from jax.experimental.pallas import tpu as pltpu
from jax.sharding import PartitionSpec as P

TW = 4
CHUNK = 32
F32 = jnp.float32
BF16 = jnp.bfloat16
VMEM_LIMIT = 30 * 1024 * 1024


def mm(left, right):
    return jnp.dot(left, right, preferred_element_type=F32)


def mm_t(left, right):
    return lax.dot_general(left, right, (((1,), (1,)), ((), ())), preferred_element_type=F32)


def sigmoid(values):
    return 0.5 * jnp.tanh(0.5 * values) + 0.5


def norm_rows(values):
    centre = values - jnp.mean(values, axis=-1, keepdims=True)
    scale_inv = lax.rsqrt(jnp.mean(centre * centre, axis=-1, keepdims=True) + 1e-05)
    return centre * scale_inv, scale_inv


def norm_back(normed, scale_inv, upstream):
    return scale_inv * (
        upstream
        - jnp.mean(upstream, axis=-1, keepdims=True)
        - normed * jnp.mean(upstream * normed, axis=-1, keepdims=True)
    )


def row_chunks(rows, size=CHUNK):
    return [slice(start, min(start + size, rows)) for start in range(0, rows, size)]


def activate(pre, act_ref, slope_ref):
    for rows in row_chunks(pre.shape[0]):
        part = pre[rows, :]
        gate = sigmoid(part)
        act = part * gate
        act_ref[rows, :] = act.astype(BF16)
        slope_ref[rows, :] = (gate + act * (1.0 - gate)).astype(BF16)


def norm_forward(raw, normed_ref, scale_ref):
    for rows in row_chunks(raw.shape[0]):
        normed, scale_inv = norm_rows(raw[rows, :])
        normed_ref[rows, :] = normed.astype(normed_ref.dtype)
        scale_ref[rows, :] = scale_inv


def norm_backward(normed_ref, scale_ref, upstream, out_ref):
    for rows in row_chunks(out_ref.shape[0]):
        out_ref[rows, :] = norm_back(
            normed_ref[rows, :].astype(F32), scale_ref[rows, :], upstream[rows, :].astype(F32)
        ).astype(BF16)


def times_slope(raw, slope_ref, out_ref):
    for rows in row_chunks(out_ref.shape[0]):
        out_ref[rows, :] = (raw[rows, :] * slope_ref[rows, :].astype(F32)).astype(BF16)


def neighbour_offsets(peer_count):
    forward_half = [1, TW, TW + 1, TW - 1]
    return forward_half + [-offset for offset in forward_half] + [peer_count // 2]


def onehot_pair(spot_ref, mesh_ref, spots, by_edge_ref, by_spot_ref):
    edges, total = by_edge_ref.shape
    spot_row = spot_ref[...].reshape(1, -1).astype(F32)
    mesh_row = mesh_ref[...].reshape(1, -1).astype(F32) + float(spots)
    for rows in row_chunks(total, 64):
        ids = lax.broadcasted_iota(jnp.int32, (rows.stop - rows.start, edges), 0) + rows.start
        ids = ids.astype(F32)
        hit = (ids == spot_row) | (ids == mesh_row)
        by_spot_ref[rows, :] = jnp.where(hit, 1.0, 0.0).astype(BF16)
    for rows in row_chunks(edges, 128):
        spot_col = jnp.broadcast_to(spot_row[:, rows], (128, 128)).T
        mesh_col = jnp.broadcast_to(mesh_row[:, rows], (128, 128)).T
        for columns in row_chunks(total, 128):
            ids = lax.broadcasted_iota(jnp.int32, (128, 128), 1) + columns.start
            ids = ids.astype(F32)
            hit = (ids == spot_col) | (ids == mesh_col)
            by_edge_ref[rows, columns] = jnp.where(hit, 1.0, 0.0).astype(BF16)


class Fetched:
    def __init__(self, source, target, semaphore):
        self.copy = pltpu.make_async_copy(source, target, semaphore)
        self.target = target
        self.landed = False
        self.copy.start()

    def land(self):
        if not self.landed:
            self.copy.wait()
            self.landed = True

    def __getitem__(self, key):
        self.land()
        return self.target[key]


def call(body, name, inputs, outputs, scratch=(), flops=0, loads=()):
    arrays, specs, moved, fetches = [], [], 0, []
    for place, entry in enumerate(inputs):
        if isinstance(entry, tuple):
            array, first, rows = entry
            array = pltpu.with_memory_space_constraint(array, pltpu.HBM)
            specs.append(pl.BlockSpec(memory_space=pltpu.HBM))
            shape = (rows,) + array.shape[1:]
            fetches.append((place, first, rows, shape, array.dtype))
            moved += rows * (array.size // array.shape[0]) * array.dtype.itemsize
        else:
            array = entry
            specs.append(pl.BlockSpec(memory_space=pltpu.VMEM))
            moved += array.size * array.dtype.itemsize
        arrays.append(array)
    for array in loads:
        arrays.append(pltpu.with_memory_space_constraint(array, pltpu.HBM))
        specs.append(pl.BlockSpec(memory_space=pltpu.HBM))
    shapes = [jax.ShapeDtypeStruct(shape, dtype) for shape, dtype in outputs]
    shapes += [jax.ShapeDtypeStruct(array.shape, array.dtype) for array in loads]
    for shape in shapes:
        moved += shape.size * shape.dtype.itemsize
    buffers = [pltpu.VMEM(shape, dtype) for _, _, _, shape, dtype in fetches]
    load_semaphores = [pltpu.SemaphoreType.DMA((len(loads),))] if loads else []
    if fetches:
        buffers.append(pltpu.SemaphoreType.DMA((len(fetches),)))

    def kernel(*refs):
        refs = list(refs)
        waiting = []
        targets, semaphores = [], None
        load_semaphore = refs.pop() if loads else None
        if fetches:
            refs, targets, semaphores = (
                refs[: -len(buffers)],
                refs[-len(buffers) : -1],
                refs[-1],
            )
        for slot, (place, first, rows, shape, _) in enumerate(fetches):
            source = refs[place]
            if source.shape != shape:
                source = source.at[pl.ds(first, rows)]
            refs[place] = Fetched(source, targets[slot], semaphores.at[slot])
            waiting.append(refs[place])
        first_load, last_out = len(inputs), len(arrays) + len(shapes)
        for slot in range(len(loads)):
            waiting.append(
                Fetched(
                    refs[first_load + slot],
                    refs[last_out - len(loads) + slot],
                    load_semaphore.at[slot],
                )
            )
        body(
            *refs[:first_load],
            *refs[len(arrays) : last_out - len(loads)],
            *refs[last_out:],
        )
        for fetched in waiting:
            fetched.land()

    return pl.pallas_call(
        kernel,
        name=name,
        in_specs=specs,
        out_specs=[pl.BlockSpec(memory_space=pltpu.VMEM) for _ in shapes],
        out_shape=shapes,
        scratch_shapes=[pltpu.VMEM(shape, dtype) for shape, dtype in scratch]
        + buffers
        + load_semaphores,
        compiler_params=pltpu.CompilerParams(vmem_limit_bytes=VMEM_LIMIT),
        cost_estimate=pl.CostEstimate(flops=flops, bytes_accessed=moved, transcendentals=0),
    )(*arrays)


def per_device(
    grid_nodes,
    mesh_nodes,
    enc_edges,
    dec_edges,
    grid_cot,
    mesh_cot,
    enc_first,
    enc_second,
    mesh_first,
    mesh_second,
    dec_first,
    dec_second,
    grid_first,
    grid_second,
    send_index,
    send_count,
    enc_grid,
    enc_mesh,
    dec_grid,
    dec_mesh,
):
    grid_count, feat = grid_nodes.shape
    mesh_count = mesh_nodes.shape[0]
    enc_count = enc_edges.shape[0]
    dec_count = dec_edges.shape[0]
    links, width = send_index.shape
    slots = links * width
    slots_pad = -(-slots // 128) * 128
    spots = grid_count + slots
    total = -(-(spots + mesh_count) // 128) * 128
    peer_count = lax.axis_size("tile")
    offsets = neighbour_offsets(peer_count)
    half = (links - 1) // 2
    reverse = [(j + half) % (links - 1) for j in range(links - 1)] + [links - 1]
    low, high = slice(0, feat), slice(feat, 2 * feat)
    mesh_rows = slice(spots, spots + mesh_count)

    one, four, five, three = range(half)
    minus = [j + half for j in range(half)]
    across = links - 1
    peers = range(peer_count)

    def permute(part, even_step, odd_step):
        steps = (even_step, odd_step)
        return lax.ppermute(part, "tile", [(s, (s + steps[s % 2]) % peer_count) for s in peers])

    def lay_together(kept_ref, got_ref, *rest):
        next_ref, second_ref = rest[-2:]
        next_ref[:width, :] = kept_ref[:width, :]
        next_ref[width:, :] = got_ref[width : 2 * width, :]
        second_ref[:width, :] = kept_ref[width : 2 * width, :]
        second_ref[width : 2 * width, :] = got_ref[3 * width :, :]
        second_ref[2 * width : 3 * width, :] = kept_ref[2 * width :, :]
        second_ref[3 * width :, :] = got_ref[2 * width : 3 * width, :]

    def exchange(parts, first_work=(), second_work=()):
        for_partner, three_off, opposite, kept = parts
        columns = kept.shape[1]
        got = permute(for_partner, 1, -1)
        opposite = permute(opposite, peer_count // 2, peer_count // 2)
        three_off = permute(three_off, -5, 5)
        next_chip, second_chip = call(
            lay_together,
            "lay_together",
            [kept, got, opposite, *first_work],
            [((2 * width, columns), BF16), ((4 * width, columns), BF16)],
        )
        second_chip = permute(second_chip, -4, 4)
        next_chip = permute(next_chip, -2, 2)
        if second_work:
            second_chip, next_chip, *second_work = lax.optimization_barrier(
                (second_chip, next_chip, *second_work)
            )
        else:
            second_chip, next_chip, three_off = lax.optimization_barrier(
                (second_chip, next_chip, three_off)
            )
        second_passed = permute(second_chip, 1, -1)
        next_passed = permute(next_chip, 1, -1)
        arrived = [got, opposite, three_off, second_chip, next_chip, second_passed, next_passed]
        return arrived, list(second_work)

    arrived_count = 7

    def sent_shapes(columns):
        return [((count * width, columns), BF16) for count in (4, 1, 1, 3)]

    sent_count = len(sent_shapes(feat))

    def is_odd():
        return lax.rem(lax.axis_index("tile"), 2) == 1

    def send(refs, message, columns=slice(None)):
        odd = is_odd()
        for_partner, three_off, opposite, kept = refs

        def block(place):
            return slice(place * width, (place + 1) * width)

        for place, step in enumerate((one, three, four, five)):
            ahead, behind = message(step), message(minus[step])
            for_partner[block(place), columns] = jnp.where(odd, behind, ahead)
            own = jnp.where(odd, ahead, behind)
            if step == five:
                three_off[:, columns] = own
            else:
                kept[block((one, four, three).index(step)), columns] = own
        opposite[:, columns] = message(across)

    def receive(refs, columns=slice(None)):
        odd = is_odd()
        got, opposite, three_off, second_chip, next_chip, second_passed, next_passed = refs

        def block(ref, place):
            return ref[place * width : (place + 1) * width, columns]

        pairs = {
            one: (block(got, 0), block(next_passed, 0)),
            three: (block(next_chip, 1), block(second_passed, 2)),
            four: (block(second_chip, 0), block(second_passed, 3)),
            five: (block(second_chip, 1), block(three_off, 0)),
        }
        slot_rows = [None] * links
        for step, (near, far) in pairs.items():
            slot_rows[step] = jnp.where(odd, near, far)
            slot_rows[minus[step]] = jnp.where(odd, far, near)
        slot_rows[across] = opposite[:, columns]
        return slot_rows

    def by_slot(refs, columns=slice(None)):
        return jnp.concatenate(receive(refs, columns), axis=0)

    def by_row(refs, columns=slice(None)):
        slot_rows = receive(refs, columns)
        return jnp.concatenate([slot_rows[reverse[j]] for j in range(links)], axis=0)

    def pack(index_ref, count_ref, nodes_ref, cot_ref, select_ref, *out_refs):
        def column(row):
            count = row.shape[1]
            eye = lax.broadcasted_iota(jnp.int32, (count, count), 0) == lax.broadcasted_iota(
                jnp.int32, (count, count), 1
            )
            return jnp.sum(
                jnp.where(eye, jnp.broadcast_to(row, (count, count)), 0.0), axis=1, keepdims=True
            )

        counts = column(count_ref[...].reshape(1, -1).astype(F32))
        place = lax.broadcasted_iota(jnp.int32, (links, width), 1).astype(F32)
        index = jnp.where(place < counts, index_ref[...].astype(F32), -1.0)
        lane = lax.broadcasted_iota(jnp.int32, (width, grid_count), 1).astype(F32)
        picks = [
            jnp.where(lane == column(index[j : j + 1, :]), 1.0, 0.0).astype(BF16)
            for j in range(links)
        ]
        select = jnp.concatenate(picks, axis=0)
        select_ref[:slots, :] = select
        select_ref[slots:, :] = jnp.zeros((slots_pad - slots, grid_count), BF16)
        sent_nodes = mm(select, nodes_ref[...]).astype(BF16)
        sent_cot = mm(select, cot_ref[...]).astype(BF16)
        send(out_refs, lambda j: sent_nodes[j * width : (j + 1) * width, :], low)
        send(out_refs, lambda j: sent_cot[j * width : (j + 1) * width, :], high)

    select, *outgoing = call(
        pack,
        "pack_rows",
        [
            (send_index, 0, links),
            (send_count, 0, links),
            (grid_nodes, 0, grid_count),
            (grid_cot, 0, grid_count),
        ],
        [((slots_pad, grid_count), BF16)] + sent_shapes(2 * feat),
        flops=4 * slots * grid_count * feat,
    )
    def tables(
        select_ref,
        enc_grid_ref,
        enc_mesh_ref,
        dec_grid_ref,
        dec_mesh_ref,
        select_t_ref,
        enc_pick_ref,
        enc_pool_ref,
        dec_pick_ref,
        dec_pool_ref,
    ):
        select_t_ref[...] = select_ref[...].astype(F32).T.astype(BF16)
        onehot_pair(enc_grid_ref, enc_mesh_ref, spots, enc_pick_ref, enc_pool_ref)
        onehot_pair(dec_grid_ref, dec_mesh_ref, spots, dec_pick_ref, dec_pool_ref)

    (
        select_t,
        enc_pick,
        enc_pool,
        dec_pick,
        dec_pool,
        enc_first,
        enc_edges,
        mesh_first,
        grid_rows,
        mesh_nodes,
        dec_first,
        dec_edges,
    ) = call(
        tables,
        "index_tables",
        [
            select,
            (enc_grid, 0, enc_count),
            (enc_mesh, 0, enc_count),
            (dec_grid, 0, dec_count),
            (dec_mesh, 0, dec_count),
        ],
        [
            ((grid_count, slots_pad), BF16),
            ((enc_count, total), BF16),
            ((total, enc_count), BF16),
            ((dec_count, total), BF16),
            ((total, dec_count), BF16),
        ],
        loads=[
            enc_first,
            enc_edges,
            mesh_first,
            grid_nodes,
            mesh_nodes,
            dec_first,
            dec_edges,
        ],
    )

    def enc_local(
        nodes_ref,
        mesh_ref,
        enc_edges_ref,
        enc_first_ref,
        mesh_first_ref,
        enc_pick_ref,
        enc_part_ref,
        mesh_part_ref,
        table_ref,
    ):
        table_ref[:grid_count, :] = mm(nodes_ref[...], enc_first_ref[low, :]).astype(BF16)
        table_ref[grid_count:, :] = jnp.zeros((total - grid_count, feat), BF16)
        table_ref[mesh_rows, :] = mm(mesh_ref[...], enc_first_ref[high, :]).astype(BF16)
        enc_part_ref[...] = mm(enc_edges_ref[...], enc_first_ref[2 * feat :, :])
        enc_part_ref[...] += mm(enc_pick_ref[...], table_ref[...])
        mesh_part_ref[...] = mm(mesh_ref[...], mesh_first_ref[low, :])

    enc_part, mesh_part = call(
        enc_local,
        "enc_local_products",
        [grid_rows, mesh_nodes, enc_edges, enc_first, mesh_first, enc_pick],
        [((enc_count, feat), F32), ((mesh_count, feat), F32)],
        scratch=[((total, feat), BF16)],
        flops=2 * feat * feat * (grid_count + 2 * enc_count),
    )

    def dec_local(nodes_ref, dec_edges_ref, dec_first_ref, dec_pick_ref, dec_part_ref):
        pd = mm(nodes_ref[...], dec_first_ref[low, :]).astype(BF16)
        dec_part_ref[...] = mm(dec_edges_ref[...], dec_first_ref[2 * feat :, :])
        dec_part_ref[...] += mm(dec_pick_ref[:, :grid_count], pd)

    (dec_part,) = call(
        dec_local,
        "dec_local_products",
        [grid_rows, dec_edges, dec_first, dec_pick],
        [((dec_count, feat), F32)],
        flops=2 * feat * feat * (grid_count + 2 * dec_count),
    )
    arrived, (enc_part, mesh_part) = exchange(outgoing, [select_t], [enc_part, mesh_part])

    def forward(*refs):
        arrived_refs, refs = refs[:arrived_count], refs[arrived_count:]
        (
            select_ref,
            enc_part_ref,
            dec_part_ref,
            mesh_part_ref,
            enc_pick_ref,
            enc_pool_ref,
            dec_pick_ref,
            dec_pool_ref,
            mesh_ref,
            enc_wg_ref,
            dec_wg_ref,
            enc_w2_ref,
            mesh_wa_ref,
            mesh_w2_ref,
            dec_wm_ref,
            dec_w2_ref,
        ) = refs[:16]
        refs = refs[16:]
        out_refs, refs = refs[:sent_count], refs[sent_count:]
        (
            mesh_out_ref,
            spot_ref,
            enc_normed_ref,
            enc_scale_ref,
            enc_slope_ref,
            dec_normed_ref,
            dec_scale_ref,
            dec_slope_ref,
            mesh_normed_ref,
            mesh_scale_ref,
            mesh_slope_ref,
            enc_act_ref,
            dec_act_ref,
            mesh_act_ref,
            table_ref,
        ) = refs
        rows = by_slot(arrived_refs, low)
        pe = mm(rows, enc_wg_ref[low, :]).astype(BF16)
        pre = enc_part_ref[...] + mm(enc_pick_ref[:, grid_count:spots], pe)
        activate(pre, enc_act_ref, enc_slope_ref)
        norm_forward(mm(enc_act_ref[...], enc_w2_ref[...]), enc_normed_ref, enc_scale_ref)
        agg = mm(enc_pool_ref[mesh_rows, :], enc_normed_ref[...]).astype(BF16)
        activate(mesh_part_ref[...] + mm(agg, mesh_wa_ref[high, :]), mesh_act_ref, mesh_slope_ref)
        norm_forward(mm(mesh_act_ref[...], mesh_w2_ref[...]), mesh_normed_ref, mesh_scale_ref)
        mesh_out = (mesh_ref[...].astype(F32) + mesh_normed_ref[...]).astype(BF16)
        mesh_out_ref[...] = mesh_out
        table_ref[:slots, :] = mm(rows, dec_wg_ref[low, :]).astype(BF16)
        table_ref[slots : slots + mesh_count, :] = mm(mesh_out, dec_wm_ref[high, :]).astype(BF16)
        table_ref[slots + mesh_count :, :] = jnp.zeros(
            (total - spots - mesh_count, feat), BF16
        )
        pre = dec_part_ref[...] + mm(dec_pick_ref[:, grid_count:], table_ref[...])
        activate(pre, dec_act_ref, dec_slope_ref)
        norm_forward(mm(dec_act_ref[...], dec_w2_ref[...]), dec_normed_ref, dec_scale_ref)
        spot_ref[...] = mm(dec_pool_ref[:spots, :], dec_normed_ref[...])
        shared = mm(select_ref[:slots, :], spot_ref[:grid_count, :].astype(BF16)).astype(BF16)
        slot_msg = spot_ref[grid_count:, :].astype(BF16)
        send(
            out_refs, lambda j: slot_msg[reverse[j] * width : (reverse[j] + 1) * width, :], low
        )
        send(out_refs, lambda j: shared[j * width : (j + 1) * width, :], high)

    edge_saved = [
        ((enc_count, feat), BF16),
        ((enc_count, 1), F32),
        ((enc_count, feat), BF16),
        ((dec_count, feat), BF16),
        ((dec_count, 1), F32),
        ((dec_count, feat), BF16),
        ((mesh_count, feat), F32),
        ((mesh_count, 1), F32),
        ((mesh_count, feat), BF16),
    ]
    results = call(
        forward,
        "edges_forward",
        [
            *arrived,
            select,
            enc_part,
            dec_part,
            mesh_part,
            enc_pick,
            enc_pool,
            dec_pick,
            dec_pool,
            mesh_nodes,
            enc_first,
            dec_first,
            enc_second,
            mesh_first,
            mesh_second,
            dec_first,
            dec_second,
        ],
        sent_shapes(2 * feat)
        + [((mesh_count, feat), BF16), ((spots, feat), F32)]
        + edge_saved,
        scratch=[
            ((enc_count, feat), BF16),
            ((dec_count, feat), BF16),
            ((mesh_count, feat), BF16),
            ((total - grid_count, feat), BF16),
        ],
        flops=2 * feat * feat * 2 * (enc_count + dec_count),
    )
    outgoing, results = results[:sent_count], results[sent_count:]
    mesh_out, spot_msg, *saved = results
    returned, _ = exchange(outgoing)

    def node_part(*refs):
        arrived_refs = refs[:arrived_count]
        nodes_ref, weight_ref, out_ref = refs[arrived_count:]
        out_ref[:grid_count, :] = mm(nodes_ref[...], weight_ref[low, :])
        out_ref[grid_count:, :] = mm(by_slot(arrived_refs, low), weight_ref[low, :])

    (grid_part,) = call(
        node_part,
        "node_products",
        [*arrived, grid_rows, grid_first],
        [((spots, feat), F32)],
        flops=2 * spots * feat * feat,
    )

    def backward(*refs):
        arrived_refs, refs = refs[:arrived_count], refs[arrived_count:]
        returned_refs, refs = refs[:arrived_count], refs[arrived_count:]
        (
            spot_ref,
            grid_part_ref,
            select_t_ref,
            nodes_ref,
            cot_ref,
            mesh_cot_ref,
            enc_pick_ref,
            enc_pool_ref,
            dec_pick_ref,
            dec_pool_ref,
            grid_wa_ref,
            grid_w2_ref,
            dec_w2_ref,
            dec_wm_ref,
            mesh_wa_ref,
            mesh_w2_ref,
            enc_w2_ref,
            enc_wg_ref,
            dec_wg_ref,
            enc_normed_ref,
            enc_scale_ref,
            enc_slope_ref,
            dec_normed_ref,
            dec_scale_ref,
            dec_slope_ref,
            mesh_normed_ref,
            mesh_scale_ref,
            mesh_slope_ref,
        ) = refs[:28]
        refs = refs[28:]
        out_refs, refs = refs[:sent_count], refs[sent_count:]
        (
            grid_out_ref,
            grid_gpre_ref,
            gpe_ref,
            gpd_ref,
            mesh_gin_ref,
            mesh_gpre_ref,
            mesh_pool_ref,
            agg_ref,
            grid_act_ref,
            grid_slope_ref,
            grid_normed_ref,
            grid_scale_ref,
            grid_gout_ref,
            grid_gall_ref,
            spot_grad_ref,
            dec_gout_ref,
            mesh_gout_ref,
            enc_gout_ref,
        ) = refs
        agg_ref[:grid_count, :] = (
            spot_ref[:grid_count, :] + mm(select_t_ref[:, :slots], by_row(returned_refs, low))
        ).astype(BF16)
        agg_ref[grid_count:, :] = (
            spot_ref[grid_count:, :] + by_slot(returned_refs, high).astype(F32)
        ).astype(BF16)
        activate(
            grid_part_ref[...] + mm(agg_ref[...], grid_wa_ref[high, :]), grid_act_ref, grid_slope_ref
        )
        norm_forward(mm(grid_act_ref[...], grid_w2_ref[...]), grid_normed_ref, grid_scale_ref)
        grid_out_ref[...] = (
            nodes_ref[...].astype(F32) + grid_normed_ref[:grid_count, :]
        ).astype(BF16)
        cot = jnp.concatenate([cot_ref[...], by_slot(arrived_refs, high)], axis=0)
        norm_backward(grid_normed_ref, grid_scale_ref, cot, grid_gout_ref)
        times_slope(mm_t(grid_gout_ref[...], grid_w2_ref[...]), grid_slope_ref, grid_gall_ref)
        grid_gpre_ref[...] = grid_gall_ref[:grid_count, :]
        spot_grad_ref[:spots, :] = mm_t(grid_gall_ref[...], grid_wa_ref[high, :]).astype(BF16)
        spot_grad_ref[spots:, :] = jnp.zeros((total - spots, feat), BF16)
        norm_backward(
            dec_normed_ref, dec_scale_ref, mm(dec_pick_ref[...], spot_grad_ref[...]), dec_gout_ref
        )
        times_slope(mm_t(dec_gout_ref[...], dec_w2_ref[...]), dec_slope_ref, dec_gout_ref)
        pooled = mm(dec_pool_ref[...], dec_gout_ref[...]).astype(BF16)
        gpd_ref[...] = pooled[:grid_count, :]
        slot_back = mm_t(pooled[grid_count:spots, :], dec_wg_ref[low, :])
        mesh_gin = mesh_cot_ref[...].astype(F32) + mm_t(pooled[mesh_rows, :], dec_wm_ref[high, :])
        mesh_gin_ref[...] = mesh_gin
        norm_backward(mesh_normed_ref, mesh_scale_ref, mesh_gin, mesh_gout_ref)
        times_slope(mm_t(mesh_gout_ref[...], mesh_w2_ref[...]), mesh_slope_ref, mesh_gpre_ref)
        gagg = mm_t(mesh_gpre_ref[...], mesh_wa_ref[high, :]).astype(BF16)
        norm_backward(
            enc_normed_ref, enc_scale_ref, mm(enc_pick_ref[:, mesh_rows], gagg), enc_gout_ref
        )
        times_slope(mm_t(enc_gout_ref[...], enc_w2_ref[...]), enc_slope_ref, enc_gout_ref)
        pooled = mm(enc_pool_ref[...], enc_gout_ref[...]).astype(BF16)
        gpe_ref[...] = pooled[:grid_count, :]
        mesh_pool_ref[...] = pooled[mesh_rows, :]
        slot_back = (slot_back + mm_t(pooled[grid_count:spots, :], enc_wg_ref[low, :])).astype(BF16)
        send(out_refs, lambda j: slot_back[reverse[j] * width : (reverse[j] + 1) * width, :])

    results = call(
        backward,
        "edges_backward",
        [
            *arrived,
            *returned,
            spot_msg,
            grid_part,
            select_t,
            grid_rows,
            grid_cot,
            mesh_cot,
            enc_pick,
            enc_pool,
            dec_pick,
            dec_pool,
            grid_first,
            grid_second,
            dec_second,
            dec_first,
            mesh_first,
            mesh_second,
            enc_second,
            enc_first,
            dec_first,
            *saved,
        ],
        sent_shapes(feat)
        + [((grid_count, feat), BF16)] * 4
        + [((mesh_count, feat), F32), ((mesh_count, feat), BF16), ((mesh_count, feat), BF16)],
        scratch=[
            ((spots, feat), BF16),
            ((spots, feat), BF16),
            ((spots, feat), BF16),
            ((spots, feat), F32),
            ((spots, 1), F32),
            ((spots, feat), BF16),
            ((spots, feat), BF16),
            ((total, feat), BF16),
            ((dec_count, feat), BF16),
            ((mesh_count, feat), BF16),
            ((enc_count, feat), BF16),
        ],
        flops=2 * feat * feat * (4 * spots + 3 * dec_count + 2 * enc_count),
    )
    outgoing, results = results[:sent_count], results[sent_count:]
    grid_out, grid_gpre, gpe, gpd, mesh_gin, mesh_gpre, mesh_pool = results
    final, _ = exchange(outgoing)

    def tail(
        cot_ref,
        grid_gpre_ref,
        gpe_ref,
        gpd_ref,
        mesh_gin_ref,
        mesh_gpre_ref,
        mesh_pool_ref,
        grid_wn_ref,
        enc_wg_ref,
        dec_wg_ref,
        mesh_wn_ref,
        enc_wm_ref,
        base_ref,
        grad_mesh_ref,
    ):
        base_ref[...] = (
            cot_ref[...].astype(F32)
            + mm_t(grid_gpre_ref[...], grid_wn_ref[low, :])
            + mm_t(gpe_ref[...], enc_wg_ref[low, :])
            + mm_t(gpd_ref[...], dec_wg_ref[low, :])
        )
        grad_mesh_ref[...] = (
            mesh_gin_ref[...]
            + mm_t(mesh_gpre_ref[...], mesh_wn_ref[low, :])
            + mm_t(mesh_pool_ref[...], enc_wm_ref[high, :])
        )

    base, grad_mesh = call(
        tail,
        "local_gradients",
        [
            grid_cot,
            grid_gpre,
            gpe,
            gpd,
            mesh_gin,
            mesh_gpre,
            mesh_pool,
            grid_first,
            enc_first,
            dec_first,
            mesh_first,
            enc_first,
        ],
        [((grid_count, feat), F32), ((mesh_count, feat), F32)],
        flops=2 * feat * feat * 3 * grid_count,
    )

    def finish(*refs):
        back_refs = refs[:arrived_count]
        base_ref, select_t_ref, out_ref = refs[arrived_count:]
        out_ref[...] = base_ref[...] + mm(select_t_ref[:, :slots], by_row(back_refs))

    (grad_grid,) = call(
        finish,
        "add_returned",
        [*final, base, select_t],
        [((grid_count, feat), F32)],
        flops=2 * grid_count * slots * feat,
    )
    return (grid_out, mesh_out, grad_grid, grad_mesh)


def solution(mesh):
    rows = P(("groups", "tile"), None)
    flat = P(("groups", "tile"))
    in_specs = (rows,) * 6 + (P(),) * 8 + (rows,) + (flat,) * 5
    return jax.shard_map(
        per_device, mesh=mesh, in_specs=in_specs, out_specs=(rows,) * 4, check_vma=False
    )
```

```python
import jax
import jax.numpy as jnp
from jax import lax
from jax.experimental import pallas as pl
from jax.experimental.pallas import tpu as pltpu
from jax.sharding import PartitionSpec as P

TW = 4
CHUNK = 32
F32 = jnp.float32
BF16 = jnp.bfloat16
VMEM_LIMIT = 30 * 1024 * 1024


def mm(left, right):
    return jnp.dot(left, right, preferred_element_type=F32)


def mm_t(left, right):
    return lax.dot_general(left, right, (((1,), (1,)), ((), ())), preferred_element_type=F32)


def sigmoid(values):
    return 0.5 * jnp.tanh(0.5 * values) + 0.5


def norm_rows(values):
    centre = values - jnp.mean(values, axis=-1, keepdims=True)
    scale_inv = lax.rsqrt(jnp.mean(centre * centre, axis=-1, keepdims=True) + 1e-05)
    return centre * scale_inv, scale_inv


def norm_back(normed, scale_inv, upstream):
    return scale_inv * (
        upstream
        - jnp.mean(upstream, axis=-1, keepdims=True)
        - normed * jnp.mean(upstream * normed, axis=-1, keepdims=True)
    )


def row_chunks(rows, size=CHUNK):
    return [slice(start, min(start + size, rows)) for start in range(0, rows, size)]


def activate(pre, act_ref, slope_ref):
    for rows in row_chunks(pre.shape[0]):
        part = pre[rows, :]
        gate = sigmoid(part)
        act = part * gate
        act_ref[rows, :] = act.astype(BF16)
        slope_ref[rows, :] = (gate + act * (1.0 - gate)).astype(BF16)


def norm_forward(raw, normed_ref, scale_ref):
    for rows in row_chunks(raw.shape[0]):
        normed, scale_inv = norm_rows(raw[rows, :])
        normed_ref[rows, :] = normed.astype(normed_ref.dtype)
        scale_ref[rows, :] = scale_inv


def norm_backward(normed_ref, scale_ref, upstream, out_ref):
    for rows in row_chunks(out_ref.shape[0]):
        out_ref[rows, :] = norm_back(
            normed_ref[rows, :].astype(F32), scale_ref[rows, :], upstream[rows, :].astype(F32)
        ).astype(BF16)


def times_slope(raw, slope_ref, out_ref):
    for rows in row_chunks(out_ref.shape[0]):
        out_ref[rows, :] = (raw[rows, :] * slope_ref[rows, :].astype(F32)).astype(BF16)


def neighbour_offsets(peer_count):
    forward_half = [1, TW, TW + 1, TW - 1]
    return forward_half + [-offset for offset in forward_half] + [peer_count // 2]


def onehot_pair(spot_ref, mesh_ref, spots, mesh_count, by_edge_ref, by_spot_ref):
    edges, total = by_edge_ref.shape
    spot_row = spot_ref[...].reshape(1, -1).astype(F32)
    mesh_row = mesh_ref[...].reshape(1, -1).astype(F32) + float(spots)

    def ids(shape, axis, start):
        return (lax.broadcasted_iota(jnp.int32, shape, axis) + start).astype(F32)

    def ones(hit):
        return jnp.where(hit, 1.0, 0.0).astype(BF16)

    for row, first, count in ((spot_row, 0, spots), (mesh_row, spots, mesh_count)):
        for rows in row_chunks(count, 80):
            rows = slice(rows.start + first, rows.stop + first)
            shape = (rows.stop - rows.start, edges)
            by_spot_ref[rows, :] = ones(ids(shape, 0, rows.start) == row)
    by_spot_ref[spots + mesh_count :, :] = jnp.zeros((total - spots - mesh_count, edges), BF16)
    for rows in row_chunks(edges, 128):
        spot_col = jnp.broadcast_to(spot_row[:, rows], (128, 128)).T
        mesh_col = jnp.broadcast_to(mesh_row[:, rows], (128, 128)).T
        for columns in row_chunks(total, 128):
            lane = ids((128, 128), 1, columns.start)
            hit = None
            if columns.start < spots:
                hit = lane == spot_col
            if columns.stop > spots:
                mesh_hit = lane == mesh_col
                hit = mesh_hit if hit is None else hit | mesh_hit
            by_edge_ref[rows, columns] = ones(hit)


class Fetched:
    def __init__(self, source, target, semaphore):
        self.copy = pltpu.make_async_copy(source, target, semaphore)
        self.target = target
        self.landed = False
        self.copy.start()

    def land(self):
        if not self.landed:
            self.copy.wait()
            self.landed = True

    def __getitem__(self, key):
        self.land()
        return self.target[key]


def call(body, name, inputs, outputs, scratch=(), flops=0):
    arrays, specs, moved, fetches = [], [], 0, []
    for place, entry in enumerate(inputs):
        if isinstance(entry, tuple):
            array, first, rows = entry
            array = pltpu.with_memory_space_constraint(array, pltpu.HBM)
            specs.append(pl.BlockSpec(memory_space=pltpu.HBM))
            shape = (rows,) + array.shape[1:]
            fetches.append((place, first, rows, shape, array.dtype))
            moved += rows * (array.size // array.shape[0]) * array.dtype.itemsize
        else:
            array = entry
            specs.append(pl.BlockSpec(memory_space=pltpu.VMEM))
            moved += array.size * array.dtype.itemsize
        arrays.append(array)
    shapes = [jax.ShapeDtypeStruct(shape, dtype) for shape, dtype in outputs]
    for shape in shapes:
        moved += shape.size * shape.dtype.itemsize
    buffers = [pltpu.VMEM(shape, dtype) for _, _, _, shape, dtype in fetches]
    if fetches:
        buffers.append(pltpu.SemaphoreType.DMA((len(fetches),)))

    def kernel(*refs):
        refs = list(refs)
        waiting = []
        if fetches:
            targets, semaphores = refs[-len(buffers) : -1], refs[-1]
            refs = refs[: -len(buffers)]
        for slot, (place, first, rows, shape, _) in enumerate(fetches):
            source = refs[place]
            if source.shape != shape:
                source = source.at[pl.ds(first, rows)]
            refs[place] = Fetched(source, targets[slot], semaphores.at[slot])
            waiting.append(refs[place])
        body(*refs)
        for fetched in waiting:
            fetched.land()

    return pl.pallas_call(
        kernel,
        name=name,
        in_specs=specs,
        out_specs=[pl.BlockSpec(memory_space=pltpu.VMEM) for _ in shapes],
        out_shape=shapes,
        scratch_shapes=[pltpu.VMEM(shape, dtype) for shape, dtype in scratch]
        + buffers,
        compiler_params=pltpu.CompilerParams(vmem_limit_bytes=VMEM_LIMIT),
        cost_estimate=pl.CostEstimate(flops=flops, bytes_accessed=moved, transcendentals=0),
    )(*arrays)


def per_device(
    grid_nodes,
    mesh_nodes,
    enc_edges,
    dec_edges,
    grid_cot,
    mesh_cot,
    enc_first,
    enc_second,
    mesh_first,
    mesh_second,
    dec_first,
    dec_second,
    grid_first,
    grid_second,
    send_index,
    send_count,
    enc_grid,
    enc_mesh,
    dec_grid,
    dec_mesh,
):
    grid_count, feat = grid_nodes.shape
    mesh_count = mesh_nodes.shape[0]
    enc_count = enc_edges.shape[0]
    dec_count = dec_edges.shape[0]
    links, width = send_index.shape
    slots = links * width
    slots_pad = -(-slots // 128) * 128
    spots = grid_count + slots
    total = -(-(spots + mesh_count) // 128) * 128
    peer_count = lax.axis_size("tile")
    offsets = neighbour_offsets(peer_count)
    half = (links - 1) // 2
    reverse = [(j + half) % (links - 1) for j in range(links - 1)] + [links - 1]
    low, high = slice(0, feat), slice(feat, 2 * feat)
    mesh_rows = slice(spots, spots + mesh_count)

    one, four, five, three = range(half)
    minus = [j + half for j in range(half)]
    across = links - 1
    peers = range(peer_count)

    def permute(part, even_step, odd_step):
        steps = (even_step, odd_step)
        return lax.ppermute(part, "tile", [(s, (s + steps[s % 2]) % peer_count) for s in peers])

    def exchange(parts):
        plus_two, minus_two, own_chip, plus_one, minus_one, three_off, opposite = parts
        plus_two = permute(plus_two, 4, 4)
        plus_one = permute(plus_one, 3, 1)
        minus_two = permute(minus_two, -4, -4)
        minus_one = permute(minus_one, -1, -3)
        three_off = permute(three_off, -5, 5)
        opposite = permute(opposite, peer_count // 2, peer_count // 2)
        plus_two, own_chip = lax.optimization_barrier((plus_two, own_chip))
        plus_passed = permute(plus_two, 1, -1)
        minus_passed = permute(minus_two, 1, -1)
        own_chip = permute(own_chip, 1, -1)
        return [
            plus_two,
            minus_two,
            own_chip,
            plus_one,
            minus_one,
            three_off,
            opposite,
            plus_passed,
            minus_passed,
        ]

    arrived_count = 9

    def sent_shapes(columns):
        rows = (2, 2, 1, 1, 1, 1, 1)
        return [((count * width, columns), BF16) for count in rows]

    sent_count = len(sent_shapes(feat))

    def is_odd():
        return lax.rem(lax.axis_index("tile"), 2) == 1

    def send(refs, message, columns=slice(None)):
        odd = is_odd()

        def by_parity(even, odd_one):
            return jnp.where(odd, message(odd_one), message(even))

        plus_two, minus_two, own_chip, plus_one, minus_one, three_off, opposite = refs
        plus_two[:width, columns] = message(four)
        plus_two[width:, columns] = by_parity(five, three)
        minus_two[:width, columns] = message(minus[four])
        minus_two[width:, columns] = by_parity(minus[three], minus[five])
        own_chip[:, columns] = by_parity(one, minus[one])
        plus_one[:, columns] = by_parity(three, one)
        minus_one[:, columns] = by_parity(minus[one], minus[three])
        three_off[:, columns] = by_parity(minus[five], five)
        opposite[:, columns] = message(across)

    def receive(refs, columns=slice(None)):
        odd = is_odd()
        plus_two, minus_two, own_chip, plus_one, minus_one, three_off, opposite = refs[:7]
        plus_passed, minus_passed = refs[7:]
        first, second = slice(0, width), slice(width, 2 * width)
        own = own_chip[:, columns]
        near_plus, near_minus = plus_one[:, columns], minus_one[:, columns]
        far = three_off[:, columns]
        passed_plus, passed_minus = plus_passed[second, columns], minus_passed[second, columns]
        slot_rows = [None] * links
        slot_rows[one] = jnp.where(odd, own, near_plus)
        slot_rows[minus[one]] = jnp.where(odd, near_minus, own)
        slot_rows[three] = jnp.where(odd, near_plus, passed_plus)
        slot_rows[minus[three]] = jnp.where(odd, passed_minus, near_minus)
        slot_rows[five] = jnp.where(odd, passed_plus, far)
        slot_rows[minus[five]] = jnp.where(odd, far, passed_minus)
        slot_rows[four] = plus_two[first, columns]
        slot_rows[minus[four]] = minus_two[first, columns]
        slot_rows[across] = opposite[:, columns]
        return slot_rows

    def by_slot(refs, columns=slice(None)):
        return jnp.concatenate(receive(refs, columns), axis=0)

    def by_row(refs, columns=slice(None)):
        slot_rows = receive(refs, columns)
        return jnp.concatenate([slot_rows[reverse[j]] for j in range(links)], axis=0)

    def pack(index_ref, count_ref, nodes_ref, cot_ref, select_ref, *out_refs):
        def column(row):
            count = row.shape[1]
            eye = lax.broadcasted_iota(jnp.int32, (count, count), 0) == lax.broadcasted_iota(
                jnp.int32, (count, count), 1
            )
            return jnp.sum(
                jnp.where(eye, jnp.broadcast_to(row, (count, count)), 0.0), axis=1, keepdims=True
            )

        counts = column(count_ref[...].reshape(1, -1).astype(F32))
        place = lax.broadcasted_iota(jnp.int32, (links, width), 1).astype(F32)
        index = jnp.where(place < counts, index_ref[...].astype(F32), -1.0)
        lane = lax.broadcasted_iota(jnp.int32, (width, grid_count), 1).astype(F32)
        picks = [
            jnp.where(lane == column(index[j : j + 1, :]), 1.0, 0.0).astype(BF16)
            for j in range(links)
        ]
        select = jnp.concatenate(picks, axis=0)
        select_ref[:slots, :] = select
        select_ref[slots:, :] = jnp.zeros((slots_pad - slots, grid_count), BF16)
        sent_nodes = mm(select, nodes_ref[...]).astype(BF16)
        sent_cot = mm(select, cot_ref[...]).astype(BF16)
        send(out_refs, lambda j: sent_nodes[j * width : (j + 1) * width, :], low)
        send(out_refs, lambda j: sent_cot[j * width : (j + 1) * width, :], high)

    select, *outgoing = call(
        pack,
        "pack_rows",
        [
            (send_index, 0, links),
            (send_count, 0, links),
            (grid_nodes, 0, grid_count),
            (grid_cot, 0, grid_count),
        ],
        [((slots_pad, grid_count), BF16)] + sent_shapes(2 * feat),
        flops=4 * slots * grid_count * feat,
    )
    arrived = exchange(outgoing)

    def local(
        select_ref,
        nodes_ref,
        mesh_ref,
        enc_edges_ref,
        dec_edges_ref,
        enc_wg_ref,
        enc_wm_ref,
        enc_we_ref,
        dec_wg_ref,
        dec_we_ref,
        mesh_wn_ref,
        enc_grid_ref,
        enc_mesh_ref,
        dec_grid_ref,
        dec_mesh_ref,
        select_t_ref,
        enc_part_ref,
        dec_part_ref,
        mesh_part_ref,
        enc_pick_ref,
        enc_pool_ref,
        dec_pick_ref,
        dec_pool_ref,
        table_ref,
    ):
        onehot_pair(enc_grid_ref, enc_mesh_ref, spots, mesh_count, enc_pick_ref, enc_pool_ref)
        onehot_pair(dec_grid_ref, dec_mesh_ref, spots, mesh_count, dec_pick_ref, dec_pool_ref)
        select_t_ref[...] = select_ref[...].astype(F32).T.astype(BF16)
        nodes = nodes_ref[...]
        mesh_part_ref[...] = mm(mesh_ref[...], mesh_wn_ref[...])
        table_ref[:grid_count, :] = mm(nodes, enc_wg_ref[...]).astype(BF16)
        table_ref[grid_count:, :] = jnp.zeros((total - grid_count, feat), BF16)
        table_ref[mesh_rows, :] = mm(mesh_ref[...], enc_wm_ref[...]).astype(BF16)
        enc_part_ref[...] = mm(enc_edges_ref[...], enc_we_ref[...])
        enc_part_ref[...] += mm(enc_pick_ref[...], table_ref[...])
        pd = mm(nodes, dec_wg_ref[...]).astype(BF16)
        dec_part_ref[...] = mm(dec_edges_ref[...], dec_we_ref[...])
        dec_part_ref[...] += mm(dec_pick_ref[:, :grid_count], pd)

    select_t, enc_part, dec_part, mesh_part, enc_pick, enc_pool, dec_pick, dec_pool = call(
        local,
        "local_products",
        [
            select,
            (grid_nodes, 0, grid_count),
            (mesh_nodes, 0, mesh_count),
            (enc_edges, 0, enc_count),
            (dec_edges, 0, dec_count),
            (enc_first, 0, feat),
            (enc_first, feat, feat),
            (enc_first, 2 * feat, feat),
            (dec_first, 0, feat),
            (dec_first, 2 * feat, feat),
            (mesh_first, 0, feat),
            (enc_grid, 0, enc_grid.shape[0]),
            (enc_mesh, 0, enc_mesh.shape[0]),
            (dec_grid, 0, dec_grid.shape[0]),
            (dec_mesh, 0, dec_mesh.shape[0]),
        ],
        [
            ((grid_count, slots_pad), BF16),
            ((enc_count, feat), F32),
            ((dec_count, feat), F32),
            ((mesh_count, feat), F32),
            ((enc_count, total), BF16),
            ((total, enc_count), BF16),
            ((dec_count, total), BF16),
            ((total, dec_count), BF16),
        ],
        scratch=[((total, feat), BF16)],
        flops=2 * feat * (feat * (2 * grid_count + enc_count + dec_count) + total * dec_count),
    )

    def forward(*refs):
        arrived_refs, refs = refs[:arrived_count], refs[arrived_count:]
        (
            select_ref,
            enc_part_ref,
            dec_part_ref,
            mesh_part_ref,
            enc_pick_ref,
            enc_pool_ref,
            dec_pick_ref,
            dec_pool_ref,
            mesh_ref,
            enc_wg_ref,
            dec_wg_ref,
            enc_w2_ref,
            mesh_wa_ref,
            mesh_w2_ref,
            dec_wm_ref,
            dec_w2_ref,
        ) = refs[:16]
        refs = refs[16:]
        out_refs, refs = refs[:sent_count], refs[sent_count:]
        (
            mesh_out_ref,
            spot_ref,
            enc_normed_ref,
            enc_scale_ref,
            enc_slope_ref,
            dec_normed_ref,
            dec_scale_ref,
            dec_slope_ref,
            mesh_normed_ref,
            mesh_scale_ref,
            mesh_slope_ref,
            enc_act_ref,
            dec_act_ref,
            mesh_act_ref,
            table_ref,
        ) = refs
        rows = by_slot(arrived_refs, low)
        pe = mm(rows, enc_wg_ref[low, :]).astype(BF16)
        pre = enc_part_ref[...] + mm(enc_pick_ref[:, grid_count:spots], pe)
        activate(pre, enc_act_ref, enc_slope_ref)
        norm_forward(mm(enc_act_ref[...], enc_w2_ref[...]), enc_normed_ref, enc_scale_ref)
        agg = mm(enc_pool_ref[mesh_rows, :], enc_normed_ref[...]).astype(BF16)
        activate(mesh_part_ref[...] + mm(agg, mesh_wa_ref[high, :]), mesh_act_ref, mesh_slope_ref)
        norm_forward(mm(mesh_act_ref[...], mesh_w2_ref[...]), mesh_normed_ref, mesh_scale_ref)
        mesh_out = (mesh_ref[...].astype(F32) + mesh_normed_ref[...]).astype(BF16)
        mesh_out_ref[...] = mesh_out
        table_ref[:slots, :] = mm(rows, dec_wg_ref[low, :]).astype(BF16)
        table_ref[slots : slots + mesh_count, :] = mm(mesh_out, dec_wm_ref[high, :]).astype(BF16)
        table_ref[slots + mesh_count :, :] = jnp.zeros(
            (total - spots - mesh_count, feat), BF16
        )
        pre = dec_part_ref[...] + mm(dec_pick_ref[:, grid_count:], table_ref[...])
        activate(pre, dec_act_ref, dec_slope_ref)
        norm_forward(mm(dec_act_ref[...], dec_w2_ref[...]), dec_normed_ref, dec_scale_ref)
        spot_ref[...] = mm(dec_pool_ref[:spots, :], dec_normed_ref[...])
        shared = mm(select_ref[:slots, :], spot_ref[:grid_count, :].astype(BF16)).astype(BF16)
        slot_msg = spot_ref[grid_count:, :].astype(BF16)
        send(
            out_refs, lambda j: slot_msg[reverse[j] * width : (reverse[j] + 1) * width, :], low
        )
        send(out_refs, lambda j: shared[j * width : (j + 1) * width, :], high)

    edge_saved = [
        ((enc_count, feat), BF16),
        ((enc_count, 1), F32),
        ((enc_count, feat), BF16),
        ((dec_count, feat), BF16),
        ((dec_count, 1), F32),
        ((dec_count, feat), BF16),
        ((mesh_count, feat), F32),
        ((mesh_count, 1), F32),
        ((mesh_count, feat), BF16),
    ]
    results = call(
        forward,
        "edges_forward",
        [
            *arrived,
            select,
            enc_part,
            dec_part,
            mesh_part,
            enc_pick,
            enc_pool,
            dec_pick,
            dec_pool,
            mesh_nodes,
            enc_first,
            dec_first,
            enc_second,
            mesh_first,
            mesh_second,
            dec_first,
            dec_second,
        ],
        sent_shapes(2 * feat)
        + [((mesh_count, feat), BF16), ((spots, feat), F32)]
        + edge_saved,
        scratch=[
            ((enc_count, feat), BF16),
            ((dec_count, feat), BF16),
            ((mesh_count, feat), BF16),
            ((total - grid_count, feat), BF16),
        ],
        flops=2 * feat * feat * 2 * (enc_count + dec_count),
    )
    outgoing, results = results[:sent_count], results[sent_count:]
    mesh_out, spot_msg, *saved = results
    returned = exchange(outgoing)

    def node_part(*refs):
        arrived_refs = refs[:arrived_count]
        nodes_ref, weight_ref, out_ref = refs[arrived_count:]
        out_ref[:grid_count, :] = mm(nodes_ref[...], weight_ref[low, :])
        out_ref[grid_count:, :] = mm(by_slot(arrived_refs, low), weight_ref[low, :])

    (grid_part,) = call(
        node_part,
        "node_products",
        [*arrived, grid_nodes, grid_first],
        [((spots, feat), F32)],
        flops=16 * spots * feat * feat,
    )

    def backward(*refs):
        arrived_refs, refs = refs[:arrived_count], refs[arrived_count:]
        returned_refs, refs = refs[:arrived_count], refs[arrived_count:]
        (
            spot_ref,
            grid_part_ref,
            select_t_ref,
            nodes_ref,
            cot_ref,
            mesh_cot_ref,
            enc_pick_ref,
            enc_pool_ref,
            dec_pick_ref,
            dec_pool_ref,
            grid_wa_ref,
            grid_w2_ref,
            dec_w2_ref,
            dec_wm_ref,
            mesh_wa_ref,
            mesh_w2_ref,
            enc_w2_ref,
            enc_wg_ref,
            dec_wg_ref,
            enc_normed_ref,
            enc_scale_ref,
            enc_slope_ref,
            dec_normed_ref,
            dec_scale_ref,
            dec_slope_ref,
            mesh_normed_ref,
            mesh_scale_ref,
            mesh_slope_ref,
        ) = refs[:28]
        refs = refs[28:]
        out_refs, refs = refs[:sent_count], refs[sent_count:]
        (
            grid_out_ref,
            grid_gpre_ref,
            gpe_ref,
            gpd_ref,
            mesh_gin_ref,
            mesh_gpre_ref,
            mesh_pool_ref,
            agg_ref,
            grid_act_ref,
            grid_slope_ref,
            grid_normed_ref,
            grid_scale_ref,
            grid_gout_ref,
            grid_gall_ref,
            spot_grad_ref,
            dec_gout_ref,
            mesh_gout_ref,
            enc_gout_ref,
        ) = refs
        agg_ref[:grid_count, :] = (
            spot_ref[:grid_count, :] + mm(select_t_ref[:, :slots], by_row(returned_refs, low))
        ).astype(BF16)
        agg_ref[grid_count:, :] = (
            spot_ref[grid_count:, :] + by_slot(returned_refs, high).astype(F32)
        ).astype(BF16)
        activate(
            grid_part_ref[...] + mm(agg_ref[...], grid_wa_ref[high, :]), grid_act_ref, grid_slope_ref
        )
        norm_forward(mm(grid_act_ref[...], grid_w2_ref[...]), grid_normed_ref, grid_scale_ref)
        grid_out_ref[...] = (
            nodes_ref[...].astype(F32) + grid_normed_ref[:grid_count, :]
        ).astype(BF16)
        cot = jnp.concatenate([cot_ref[...], by_slot(arrived_refs, high)], axis=0)
        norm_backward(grid_normed_ref, grid_scale_ref, cot, grid_gout_ref)
        times_slope(mm_t(grid_gout_ref[...], grid_w2_ref[...]), grid_slope_ref, grid_gall_ref)
        grid_gpre_ref[...] = grid_gall_ref[:grid_count, :]
        spot_grad_ref[:spots, :] = mm_t(grid_gall_ref[...], grid_wa_ref[high, :]).astype(BF16)
        spot_grad_ref[spots:, :] = jnp.zeros((total - spots, feat), BF16)
        norm_backward(
            dec_normed_ref, dec_scale_ref, mm(dec_pick_ref[...], spot_grad_ref[...]), dec_gout_ref
        )
        times_slope(mm_t(dec_gout_ref[...], dec_w2_ref[...]), dec_slope_ref, dec_gout_ref)
        pooled = mm(dec_pool_ref[...], dec_gout_ref[...]).astype(BF16)
        gpd_ref[...] = pooled[:grid_count, :]
        slot_back = mm_t(pooled[grid_count:spots, :], dec_wg_ref[low, :])
        mesh_gin = mesh_cot_ref[...].astype(F32) + mm_t(pooled[mesh_rows, :], dec_wm_ref[high, :])
        mesh_gin_ref[...] = mesh_gin
        norm_backward(mesh_normed_ref, mesh_scale_ref, mesh_gin, mesh_gout_ref)
        times_slope(mm_t(mesh_gout_ref[...], mesh_w2_ref[...]), mesh_slope_ref, mesh_gpre_ref)
        gagg = mm_t(mesh_gpre_ref[...], mesh_wa_ref[high, :]).astype(BF16)
        norm_backward(
            enc_normed_ref, enc_scale_ref, mm(enc_pick_ref[:, mesh_rows], gagg), enc_gout_ref
        )
        times_slope(mm_t(enc_gout_ref[...], enc_w2_ref[...]), enc_slope_ref, enc_gout_ref)
        pooled = mm(enc_pool_ref[...], enc_gout_ref[...]).astype(BF16)
        gpe_ref[...] = pooled[:grid_count, :]
        mesh_pool_ref[...] = pooled[mesh_rows, :]
        slot_back = (slot_back + mm_t(pooled[grid_count:spots, :], enc_wg_ref[low, :])).astype(BF16)
        send(out_refs, lambda j: slot_back[reverse[j] * width : (reverse[j] + 1) * width, :])

    results = call(
        backward,
        "edges_backward",
        [
            *arrived,
            *returned,
            spot_msg,
            grid_part,
            select_t,
            grid_nodes,
            grid_cot,
            mesh_cot,
            enc_pick,
            enc_pool,
            dec_pick,
            dec_pool,
            grid_first,
            grid_second,
            dec_second,
            dec_first,
            mesh_first,
            mesh_second,
            enc_second,
            enc_first,
            dec_first,
            *saved,
        ],
        sent_shapes(feat)
        + [((grid_count, feat), BF16)] * 4
        + [((mesh_count, feat), F32), ((mesh_count, feat), BF16), ((mesh_count, feat), BF16)],
        scratch=[
            ((spots, feat), BF16),
            ((spots, feat), BF16),
            ((spots, feat), BF16),
            ((spots, feat), F32),
            ((spots, 1), F32),
            ((spots, feat), BF16),
            ((spots, feat), BF16),
            ((total, feat), BF16),
            ((dec_count, feat), BF16),
            ((mesh_count, feat), BF16),
            ((enc_count, feat), BF16),
        ],
        flops=2 * feat * feat * (4 * spots + 3 * dec_count + 2 * enc_count),
    )
    outgoing, results = results[:sent_count], results[sent_count:]
    grid_out, grid_gpre, gpe, gpd, mesh_gin, mesh_gpre, mesh_pool = results
    final = exchange(outgoing)

    def tail(
        cot_ref,
        grid_gpre_ref,
        gpe_ref,
        gpd_ref,
        mesh_gin_ref,
        mesh_gpre_ref,
        mesh_pool_ref,
        grid_wn_ref,
        enc_wg_ref,
        dec_wg_ref,
        mesh_wn_ref,
        enc_wm_ref,
        base_ref,
        grad_mesh_ref,
    ):
        base_ref[...] = (
            cot_ref[...].astype(F32)
            + mm_t(grid_gpre_ref[...], grid_wn_ref[low, :])
            + mm_t(gpe_ref[...], enc_wg_ref[low, :])
            + mm_t(gpd_ref[...], dec_wg_ref[low, :])
        )
        grad_mesh_ref[...] = (
            mesh_gin_ref[...]
            + mm_t(mesh_gpre_ref[...], mesh_wn_ref[low, :])
            + mm_t(mesh_pool_ref[...], enc_wm_ref[high, :])
        )

    base, grad_mesh = call(
        tail,
        "local_gradients",
        [
            grid_cot,
            grid_gpre,
            gpe,
            gpd,
            mesh_gin,
            mesh_gpre,
            mesh_pool,
            grid_first,
            enc_first,
            dec_first,
            mesh_first,
            enc_first,
        ],
        [((grid_count, feat), F32), ((mesh_count, feat), F32)],
        flops=2 * feat * feat * 3 * grid_count,
    )

    def finish(*refs):
        back_refs = refs[:arrived_count]
        base_ref, select_t_ref, out_ref = refs[arrived_count:]
        out_ref[...] = base_ref[...] + mm(select_t_ref[:, :slots], by_row(back_refs))

    (grad_grid,) = call(
        finish,
        "add_returned",
        [*final, base, select_t],
        [((grid_count, feat), F32)],
        flops=2 * grid_count * slots * feat,
    )
    return (grid_out, mesh_out, grad_grid, grad_mesh)


def solution(mesh):
    rows = P(("groups", "tile"), None)
    flat = P(("groups", "tile"))
    in_specs = (rows,) * 6 + (P(),) * 8 + (rows,) + (flat,) * 5
    return jax.shard_map(
        per_device, mesh=mesh, in_specs=in_specs, out_specs=(rows,) * 4, check_vma=False
    )
```

```python
import jax
import jax.numpy as jnp
from jax import lax
from jax.experimental import pallas as pl
from jax.experimental.pallas import tpu as pltpu
from jax.sharding import PartitionSpec as P

TW = 4
CHUNK = 32
F32 = jnp.float32
BF16 = jnp.bfloat16
VMEM_LIMIT = 30 * 1024 * 1024


def mm(left, right):
    return jnp.dot(left, right, preferred_element_type=F32)


def mm_t(left, right):
    return lax.dot_general(left, right, (((1,), (1,)), ((), ())), preferred_element_type=F32)


def sigmoid(values):
    return 0.5 * jnp.tanh(0.5 * values) + 0.5


def norm_rows(values):
    centre = values - jnp.mean(values, axis=-1, keepdims=True)
    scale_inv = lax.rsqrt(jnp.mean(centre * centre, axis=-1, keepdims=True) + 1e-05)
    return centre * scale_inv, scale_inv


def norm_back(normed, scale_inv, upstream):
    return scale_inv * (
        upstream
        - jnp.mean(upstream, axis=-1, keepdims=True)
        - normed * jnp.mean(upstream * normed, axis=-1, keepdims=True)
    )


def row_chunks(rows, size=CHUNK):
    return [slice(start, min(start + size, rows)) for start in range(0, rows, size)]


def row_blocks(rows, parts):
    size = -(-rows // (16 * parts)) * 16
    return row_chunks(rows, size)


def inner_chunks(block):
    return [
        (slice(part.start, part.stop), slice(block.start + part.start, block.start + part.stop))
        for part in row_chunks(block.stop - block.start)
    ]


def activate(pre, act_ref, slope_ref, block):
    for inner, rows in inner_chunks(block):
        part = pre[inner, :]
        gate = sigmoid(part)
        act = part * gate
        act_ref[rows, :] = act.astype(BF16)
        slope_ref[rows, :] = (gate + act * (1.0 - gate)).astype(BF16)


def norm_forward(raw, normed_ref, scale_ref, block):
    for inner, rows in inner_chunks(block):
        normed, scale_inv = norm_rows(raw[inner, :])
        normed_ref[rows, :] = normed.astype(normed_ref.dtype)
        scale_ref[rows, :] = scale_inv


def norm_backward(normed_ref, scale_ref, upstream, out_ref, block):
    for inner, rows in inner_chunks(block):
        out_ref[rows, :] = norm_back(
            normed_ref[rows, :].astype(F32), scale_ref[rows, :], upstream[inner, :].astype(F32)
        ).astype(BF16)


def times_slope(raw, slope_ref, out_ref, block):
    for inner, rows in inner_chunks(block):
        out_ref[rows, :] = (raw[inner, :] * slope_ref[rows, :].astype(F32)).astype(BF16)


def neighbour_offsets(peer_count):
    forward_half = [1, TW, TW + 1, TW - 1]
    return forward_half + [-offset for offset in forward_half] + [peer_count // 2]


def onehot_pair(spot_ref, mesh_ref, spots, mesh_count, by_edge_ref, by_spot_ref):
    edges, total = by_edge_ref.shape
    spot_row = spot_ref[...].reshape(1, -1)
    mesh_row = mesh_ref[...].reshape(1, -1) + spots

    def ones(hit):
        return jnp.where(hit, 1.0, 0.0).astype(BF16)

    for row, first, count in ((spot_row, 0, spots), (mesh_row, spots, mesh_count)):
        for rows in row_chunks(count, 16):
            ids = lax.broadcasted_iota(jnp.int32, (16, edges), 0)
            rows = slice(rows.start + first, rows.stop + first)
            by_spot_ref[rows, :] = ones(ids == row - rows.start)
    by_spot_ref[spots + mesh_count :, :] = jnp.zeros((total - spots - mesh_count, edges), BF16)
    lane = lax.broadcasted_iota(jnp.int32, (1, 128), 1)
    for rows in row_chunks(edges, 128):
        spot_col = jnp.broadcast_to(spot_row[:, rows], (128, 128)).T
        mesh_col = jnp.broadcast_to(mesh_row[:, rows], (128, 128)).T
        for columns in row_chunks(total, 128):
            hit = None
            if columns.start < spots:
                hit = lane + columns.start == spot_col
            if columns.stop > spots:
                mesh_hit = lane + columns.start == mesh_col
                hit = mesh_hit if hit is None else hit | mesh_hit
            by_edge_ref[rows, columns] = ones(hit)


class Fetched:
    def __init__(self, source, target, semaphore):
        self.copy = pltpu.make_async_copy(source, target, semaphore)
        self.target = target
        self.landed = False
        self.copy.start()

    def land(self):
        if not self.landed:
            self.copy.wait()
            self.landed = True

    def __getitem__(self, key):
        self.land()
        return self.target[key]


def call(body, name, inputs, outputs, scratch=(), flops=0):
    arrays, specs, moved, fetches = [], [], 0, []
    for place, entry in enumerate(inputs):
        if isinstance(entry, tuple):
            array, first, rows = entry
            array = pltpu.with_memory_space_constraint(array, pltpu.HBM)
            specs.append(pl.BlockSpec(memory_space=pltpu.HBM))
            shape = (rows,) + array.shape[1:]
            fetches.append((place, first, rows, shape, array.dtype))
            moved += rows * (array.size // array.shape[0]) * array.dtype.itemsize
        else:
            array = entry
            specs.append(pl.BlockSpec(memory_space=pltpu.VMEM))
            moved += array.size * array.dtype.itemsize
        arrays.append(array)
    shapes = [jax.ShapeDtypeStruct(shape, dtype) for shape, dtype in outputs]
    for shape in shapes:
        moved += shape.size * shape.dtype.itemsize
    buffers = [pltpu.VMEM(shape, dtype) for _, _, _, shape, dtype in fetches]
    if fetches:
        buffers.append(pltpu.SemaphoreType.DMA((len(fetches),)))

    def kernel(*refs):
        refs = list(refs)
        waiting = []
        if fetches:
            targets, semaphores = refs[-len(buffers) : -1], refs[-1]
            refs = refs[: -len(buffers)]
        for slot, (place, first, rows, shape, _) in enumerate(fetches):
            source = refs[place]
            if source.shape != shape:
                source = source.at[pl.ds(first, rows)]
            refs[place] = Fetched(source, targets[slot], semaphores.at[slot])
            waiting.append(refs[place])
        body(*refs)
        for fetched in waiting:
            fetched.land()

    return pl.pallas_call(
        kernel,
        name=name,
        in_specs=specs,
        out_specs=[pl.BlockSpec(memory_space=pltpu.VMEM) for _ in shapes],
        out_shape=shapes,
        scratch_shapes=[pltpu.VMEM(shape, dtype) for shape, dtype in scratch]
        + buffers,
        compiler_params=pltpu.CompilerParams(vmem_limit_bytes=VMEM_LIMIT),
        cost_estimate=pl.CostEstimate(flops=flops, bytes_accessed=moved, transcendentals=0),
    )(*arrays)


def per_device(
    grid_nodes,
    mesh_nodes,
    enc_edges,
    dec_edges,
    grid_cot,
    mesh_cot,
    enc_first,
    enc_second,
    mesh_first,
    mesh_second,
    dec_first,
    dec_second,
    grid_first,
    grid_second,
    send_index,
    send_count,
    enc_grid,
    enc_mesh,
    dec_grid,
    dec_mesh,
):
    grid_count, feat = grid_nodes.shape
    mesh_count = mesh_nodes.shape[0]
    enc_count = enc_edges.shape[0]
    dec_count = dec_edges.shape[0]
    links, width = send_index.shape
    slots = links * width
    slots_pad = -(-slots // 128) * 128
    spots = grid_count + slots
    total = -(-(spots + mesh_count) // 128) * 128
    peer_count = lax.axis_size("tile")
    offsets = neighbour_offsets(peer_count)
    half = (links - 1) // 2
    reverse = [(j + half) % (links - 1) for j in range(links - 1)] + [links - 1]
    low, high = slice(0, feat), slice(feat, 2 * feat)
    mesh_rows = slice(spots, spots + mesh_count)

    one, four, five, three = range(half)
    minus = [j + half for j in range(half)]
    across = links - 1
    peers = range(peer_count)

    def permute(part, steps, odd_row_steps=None):
        rows = (steps, odd_row_steps or steps)
        pairs = [(s, (s + rows[s // TW % 2][s % 2]) % peer_count) for s in peers]
        return lax.ppermute(part, "tile", pairs)

    def exchange(parts):
        late_pair, early_pair, behind_one, ahead_three, five_off, opposite, own_chip = parts
        late_pair = permute(late_pair, (-4, -4), (4, 4))
        early_pair = permute(early_pair, (4, 4), (-4, -4))
        behind_one = permute(behind_one, (-1, 1))
        ahead_three = permute(ahead_three, (3, -3))
        five_off = permute(five_off, (-5, 5))
        opposite = permute(opposite, (peer_count // 2, peer_count // 2))
        late_pair, own_chip = lax.optimization_barrier((late_pair, own_chip))
        late_passed = permute(late_pair, (1, -1))
        own_chip = permute(own_chip, (1, -1))
        early_passed = permute(early_pair, (1, -1))
        return [
            late_pair,
            early_pair,
            behind_one,
            ahead_three,
            five_off,
            opposite,
            own_chip,
            late_passed,
            early_passed,
        ]

    arrived_count = 9

    def sent_shapes(columns):
        rows = (2, 2, 1, 1, 1, 1, 1)
        return [((count * width, columns), BF16) for count in rows]

    sent_count = len(sent_shapes(feat))

    def place_bits():
        own = lax.axis_index("tile")
        return lax.rem(own, 2) == 1, lax.rem(lax.div(own, TW), 2) == 1

    def send(refs, message, columns=slice(None)):
        odd, odd_row = place_bits()

        def by_parity(even, odd_one):
            return jnp.where(odd, message(odd_one), message(even))

        late_pair, early_pair, behind_one, ahead_three, five_off, opposite, own_chip = refs
        first, second = slice(0, width), slice(width, 2 * width)
        ahead = message(four), by_parity(five, three)
        behind = message(minus[four]), by_parity(minus[three], minus[five])
        for rows, go_ahead, go_behind in zip((first, second), ahead, behind):
            late_pair[rows, columns] = jnp.where(odd_row, go_ahead, go_behind)
            early_pair[rows, columns] = jnp.where(odd_row, go_behind, go_ahead)
        behind_one[:, columns] = by_parity(minus[one], one)
        ahead_three[:, columns] = by_parity(three, minus[three])
        five_off[:, columns] = by_parity(minus[five], five)
        opposite[:, columns] = message(across)
        own_chip[:, columns] = by_parity(one, minus[one])

    def receive(refs, columns=slice(None)):
        odd, odd_row = place_bits()
        late_pair, early_pair, behind_one, ahead_three, five_off, opposite, own_chip = refs[:7]
        late_passed, early_passed = refs[7:]
        first, second = slice(0, width), slice(width, 2 * width)
        near, near_three = behind_one[:, columns], ahead_three[:, columns]
        far, own = five_off[:, columns], own_chip[:, columns]
        late_rows, early_rows = late_passed[second, columns], early_passed[second, columns]
        from_behind = jnp.where(odd_row, early_rows, late_rows)
        from_ahead = jnp.where(odd_row, late_rows, early_rows)
        late_rows, early_rows = late_pair[first, columns], early_pair[first, columns]
        slot_rows = [None] * links
        slot_rows[one] = jnp.where(odd, own, near)
        slot_rows[minus[one]] = jnp.where(odd, near, own)
        slot_rows[three] = jnp.where(odd, near_three, from_behind)
        slot_rows[minus[three]] = jnp.where(odd, from_ahead, near_three)
        slot_rows[five] = jnp.where(odd, from_behind, far)
        slot_rows[minus[five]] = jnp.where(odd, far, from_ahead)
        slot_rows[four] = jnp.where(odd_row, early_rows, late_rows)
        slot_rows[minus[four]] = jnp.where(odd_row, late_rows, early_rows)
        slot_rows[across] = opposite[:, columns]
        return slot_rows

    def by_slot(refs, columns=slice(None)):
        return jnp.concatenate(receive(refs, columns), axis=0)

    def by_row(refs, columns=slice(None)):
        slot_rows = receive(refs, columns)
        return jnp.concatenate([slot_rows[reverse[j]] for j in range(links)], axis=0)

    def pack(index_ref, count_ref, nodes_ref, cot_ref, select_ref, *out_refs):
        def column(row):
            count = row.shape[1]
            eye = lax.broadcasted_iota(jnp.int32, (count, count), 0) == lax.broadcasted_iota(
                jnp.int32, (count, count), 1
            )
            return jnp.sum(
                jnp.where(eye, jnp.broadcast_to(row, (count, count)), 0.0), axis=1, keepdims=True
            )

        counts = column(count_ref[...].reshape(1, -1).astype(F32))
        place = lax.broadcasted_iota(jnp.int32, (links, width), 1).astype(F32)
        index = jnp.where(place < counts, index_ref[...].astype(F32), -1.0)
        lane = lax.broadcasted_iota(jnp.int32, (width, grid_count), 1).astype(F32)
        picks = [
            jnp.where(lane == column(index[j : j + 1, :]), 1.0, 0.0).astype(BF16)
            for j in range(links)
        ]
        select = jnp.concatenate(picks, axis=0)
        select_ref[:slots, :] = select
        select_ref[slots:, :] = jnp.zeros((slots_pad - slots, grid_count), BF16)
        sent_nodes = mm(select, nodes_ref[...]).astype(BF16)
        sent_cot = mm(select, cot_ref[...]).astype(BF16)
        send(out_refs, lambda j: sent_nodes[j * width : (j + 1) * width, :], low)
        send(out_refs, lambda j: sent_cot[j * width : (j + 1) * width, :], high)

    select, *outgoing = call(
        pack,
        "pack_rows",
        [
            (send_index, 0, links),
            (send_count, 0, links),
            (grid_nodes, 0, grid_count),
            (grid_cot, 0, grid_count),
        ],
        [((slots_pad, grid_count), BF16)] + sent_shapes(2 * feat),
        flops=4 * slots * grid_count * feat,
    )
    arrived = exchange(outgoing)

    def local(
        select_ref,
        nodes_ref,
        mesh_ref,
        enc_edges_ref,
        dec_edges_ref,
        enc_wg_ref,
        enc_wm_ref,
        enc_we_ref,
        dec_wg_ref,
        dec_we_ref,
        mesh_wn_ref,
        enc_grid_ref,
        enc_mesh_ref,
        dec_grid_ref,
        dec_mesh_ref,
        select_t_ref,
        enc_part_ref,
        dec_part_ref,
        mesh_part_ref,
        enc_pick_ref,
        enc_pool_ref,
        dec_pick_ref,
        dec_pool_ref,
        table_ref,
    ):
        onehot_pair(enc_grid_ref, enc_mesh_ref, spots, mesh_count, enc_pick_ref, enc_pool_ref)
        onehot_pair(dec_grid_ref, dec_mesh_ref, spots, mesh_count, dec_pick_ref, dec_pool_ref)
        select_t_ref[...] = select_ref[...].astype(F32).T.astype(BF16)
        nodes = nodes_ref[...]
        mesh_part_ref[...] = mm(mesh_ref[...], mesh_wn_ref[...])
        table_ref[:grid_count, :] = mm(nodes, enc_wg_ref[...]).astype(BF16)
        table_ref[grid_count:, :] = jnp.zeros((total - grid_count, feat), BF16)
        table_ref[mesh_rows, :] = mm(mesh_ref[...], enc_wm_ref[...]).astype(BF16)
        enc_part_ref[...] = mm(enc_edges_ref[...], enc_we_ref[...])
        enc_part_ref[...] += mm(enc_pick_ref[...], table_ref[...])
        pd = mm(nodes, dec_wg_ref[...]).astype(BF16)
        dec_part_ref[...] = mm(dec_edges_ref[...], dec_we_ref[...])
        dec_part_ref[...] += mm(dec_pick_ref[:, :grid_count], pd)

    select_t, enc_part, dec_part, mesh_part, enc_pick, enc_pool, dec_pick, dec_pool = call(
        local,
        "local_products",
        [
            select,
            (grid_nodes, 0, grid_count),
            (mesh_nodes, 0, mesh_count),
            (enc_edges, 0, enc_count),
            (dec_edges, 0, dec_count),
            (enc_first, 0, feat),
            (enc_first, feat, feat),
            (enc_first, 2 * feat, feat),
            (dec_first, 0, feat),
            (dec_first, 2 * feat, feat),
            (mesh_first, 0, feat),
            (enc_grid, 0, enc_grid.shape[0]),
            (enc_mesh, 0, enc_mesh.shape[0]),
            (dec_grid, 0, dec_grid.shape[0]),
            (dec_mesh, 0, dec_mesh.shape[0]),
        ],
        [
            ((grid_count, slots_pad), BF16),
            ((enc_count, feat), F32),
            ((dec_count, feat), F32),
            ((mesh_count, feat), F32),
            ((enc_count, total), BF16),
            ((total, enc_count), BF16),
            ((dec_count, total), BF16),
            ((total, dec_count), BF16),
        ],
        scratch=[((total, feat), BF16)],
        flops=2 * feat * (feat * (2 * grid_count + enc_count + dec_count) + total * dec_count),
    )

    def forward(*refs):
        arrived_refs, refs = refs[:arrived_count], refs[arrived_count:]
        (
            select_ref,
            enc_part_ref,
            dec_part_ref,
            mesh_part_ref,
            enc_pick_ref,
            enc_pool_ref,
            dec_pick_ref,
            dec_pool_ref,
            mesh_ref,
            enc_wg_ref,
            dec_wg_ref,
            enc_w2_ref,
            mesh_wa_ref,
            mesh_w2_ref,
            dec_wm_ref,
            dec_w2_ref,
        ) = refs[:16]
        refs = refs[16:]
        out_refs, refs = refs[:sent_count], refs[sent_count:]
        (
            mesh_out_ref,
            spot_ref,
            enc_normed_ref,
            enc_scale_ref,
            enc_slope_ref,
            dec_normed_ref,
            dec_scale_ref,
            dec_slope_ref,
            mesh_normed_ref,
            mesh_scale_ref,
            mesh_slope_ref,
            enc_act_ref,
            dec_act_ref,
            mesh_act_ref,
            table_ref,
        ) = refs
        rows = by_slot(arrived_refs, low)
        pe = mm(rows, enc_wg_ref[low, :]).astype(BF16)
        for block in row_blocks(enc_count, 3):
            pre = enc_part_ref[block, :] + mm(enc_pick_ref[block, grid_count:spots], pe)
            activate(pre, enc_act_ref, enc_slope_ref, block)
            raw = mm(enc_act_ref[block, :], enc_w2_ref[...])
            norm_forward(raw, enc_normed_ref, enc_scale_ref, block)
        agg = mm(enc_pool_ref[mesh_rows, :], enc_normed_ref[...]).astype(BF16)
        whole = slice(0, mesh_count)
        pre = mesh_part_ref[...] + mm(agg, mesh_wa_ref[high, :])
        activate(pre, mesh_act_ref, mesh_slope_ref, whole)
        raw = mm(mesh_act_ref[...], mesh_w2_ref[...])
        norm_forward(raw, mesh_normed_ref, mesh_scale_ref, whole)
        mesh_out = (mesh_ref[...].astype(F32) + mesh_normed_ref[...]).astype(BF16)
        mesh_out_ref[...] = mesh_out
        table_ref[:slots, :] = mm(rows, dec_wg_ref[low, :]).astype(BF16)
        table_ref[slots : slots + mesh_count, :] = mm(mesh_out, dec_wm_ref[high, :]).astype(BF16)
        table_ref[slots + mesh_count :, :] = jnp.zeros(
            (total - spots - mesh_count, feat), BF16
        )
        for block in row_blocks(dec_count, 3):
            pre = dec_part_ref[block, :] + mm(dec_pick_ref[block, grid_count:], table_ref[...])
            activate(pre, dec_act_ref, dec_slope_ref, block)
            raw = mm(dec_act_ref[block, :], dec_w2_ref[...])
            norm_forward(raw, dec_normed_ref, dec_scale_ref, block)
        spot_ref[...] = mm(dec_pool_ref[:spots, :], dec_normed_ref[...])
        shared = mm(select_ref[:slots, :], spot_ref[:grid_count, :].astype(BF16)).astype(BF16)
        slot_msg = spot_ref[grid_count:, :].astype(BF16)
        send(
            out_refs, lambda j: slot_msg[reverse[j] * width : (reverse[j] + 1) * width, :], low
        )
        send(out_refs, lambda j: shared[j * width : (j + 1) * width, :], high)

    edge_saved = [
        ((enc_count, feat), BF16),
        ((enc_count, 1), F32),
        ((enc_count, feat), BF16),
        ((dec_count, feat), BF16),
        ((dec_count, 1), F32),
        ((dec_count, feat), BF16),
        ((mesh_count, feat), F32),
        ((mesh_count, 1), F32),
        ((mesh_count, feat), BF16),
    ]
    results = call(
        forward,
        "edges_forward",
        [
            *arrived,
            select,
            enc_part,
            dec_part,
            mesh_part,
            enc_pick,
            enc_pool,
            dec_pick,
            dec_pool,
            mesh_nodes,
            enc_first,
            dec_first,
            enc_second,
            mesh_first,
            mesh_second,
            dec_first,
            dec_second,
        ],
        sent_shapes(2 * feat)
        + [((mesh_count, feat), BF16), ((spots, feat), F32)]
        + edge_saved,
        scratch=[
            ((enc_count, feat), BF16),
            ((dec_count, feat), BF16),
            ((mesh_count, feat), BF16),
            ((total - grid_count, feat), BF16),
        ],
        flops=2 * feat * feat * 2 * (enc_count + dec_count),
    )
    outgoing, results = results[:sent_count], results[sent_count:]
    mesh_out, spot_msg, *saved = results
    returned = exchange(outgoing)

    def node_part(*refs):
        arrived_refs = refs[:arrived_count]
        nodes_ref, weight_ref, out_ref = refs[arrived_count:]
        out_ref[:grid_count, :] = mm(nodes_ref[...], weight_ref[low, :])
        out_ref[grid_count:, :] = mm(by_slot(arrived_refs, low), weight_ref[low, :])

    (grid_part,) = call(
        node_part,
        "node_products",
        [*arrived, grid_nodes, grid_first],
        [((spots, feat), F32)],
        flops=16 * spots * feat * feat,
    )

    def backward(*refs):
        arrived_refs, refs = refs[:arrived_count], refs[arrived_count:]
        returned_refs, refs = refs[:arrived_count], refs[arrived_count:]
        (
            spot_ref,
            grid_part_ref,
            select_t_ref,
            nodes_ref,
            cot_ref,
            mesh_cot_ref,
            enc_pick_ref,
            enc_pool_ref,
            dec_pick_ref,
            dec_pool_ref,
            grid_wa_ref,
            grid_w2_ref,
            dec_w2_ref,
            dec_wm_ref,
            mesh_wa_ref,
            mesh_w2_ref,
            enc_w2_ref,
            enc_wg_ref,
            dec_wg_ref,
            enc_normed_ref,
            enc_scale_ref,
            enc_slope_ref,
            dec_normed_ref,
            dec_scale_ref,
            dec_slope_ref,
            mesh_normed_ref,
            mesh_scale_ref,
            mesh_slope_ref,
        ) = refs[:28]
        refs = refs[28:]
        out_refs, refs = refs[:sent_count], refs[sent_count:]
        (
            grid_out_ref,
            grid_gpre_ref,
            gpe_ref,
            gpd_ref,
            mesh_gin_ref,
            mesh_gpre_ref,
            mesh_pool_ref,
            agg_ref,
            cot_rows_ref,
            grid_act_ref,
            grid_slope_ref,
            grid_normed_ref,
            grid_scale_ref,
            grid_gout_ref,
            grid_gall_ref,
            spot_grad_ref,
            dec_gout_ref,
            mesh_gout_ref,
            enc_gout_ref,
        ) = refs
        agg_ref[:grid_count, :] = (
            spot_ref[:grid_count, :] + mm(select_t_ref[:, :slots], by_row(returned_refs, low))
        ).astype(BF16)
        agg_ref[grid_count:, :] = (
            spot_ref[grid_count:, :] + by_slot(returned_refs, high).astype(F32)
        ).astype(BF16)
        cot_rows_ref[:grid_count, :] = cot_ref[...]
        cot_rows_ref[grid_count:, :] = by_slot(arrived_refs, high)
        spot_grad_ref[spots:, :] = jnp.zeros((total - spots, feat), BF16)
        for block in row_blocks(spots, 2):
            pre = grid_part_ref[block, :] + mm(agg_ref[block, :], grid_wa_ref[high, :])
            activate(pre, grid_act_ref, grid_slope_ref, block)
            raw = mm(grid_act_ref[block, :], grid_w2_ref[...])
            norm_forward(raw, grid_normed_ref, grid_scale_ref, block)
            norm_backward(
                grid_normed_ref, grid_scale_ref, cot_rows_ref[block, :], grid_gout_ref, block
            )
            raw = mm_t(grid_gout_ref[block, :], grid_w2_ref[...])
            times_slope(raw, grid_slope_ref, grid_gall_ref, block)
            spot_grad_ref[block, :] = mm_t(
                grid_gall_ref[block, :], grid_wa_ref[high, :]
            ).astype(BF16)
        grid_out_ref[...] = (
            nodes_ref[...].astype(F32) + grid_normed_ref[:grid_count, :]
        ).astype(BF16)
        grid_gpre_ref[...] = grid_gall_ref[:grid_count, :]
        for block in row_blocks(dec_count, 3):
            upstream = mm(dec_pick_ref[block, :], spot_grad_ref[...])
            norm_backward(dec_normed_ref, dec_scale_ref, upstream, dec_gout_ref, block)
            raw = mm_t(dec_gout_ref[block, :], dec_w2_ref[...])
            times_slope(raw, dec_slope_ref, dec_gout_ref, block)
        pooled = mm(dec_pool_ref[...], dec_gout_ref[...]).astype(BF16)
        gpd_ref[...] = pooled[:grid_count, :]
        slot_back = mm_t(pooled[grid_count:spots, :], dec_wg_ref[low, :])
        mesh_gin = mesh_cot_ref[...].astype(F32) + mm_t(
            pooled[mesh_rows, :], dec_wm_ref[high, :]
        )
        mesh_gin_ref[...] = mesh_gin
        whole = slice(0, mesh_count)
        norm_backward(mesh_normed_ref, mesh_scale_ref, mesh_gin, mesh_gout_ref, whole)
        raw = mm_t(mesh_gout_ref[...], mesh_w2_ref[...])
        times_slope(raw, mesh_slope_ref, mesh_gpre_ref, whole)
        gagg = mm_t(mesh_gpre_ref[...], mesh_wa_ref[high, :]).astype(BF16)
        for block in row_blocks(enc_count, 3):
            upstream = mm(enc_pick_ref[block, mesh_rows], gagg)
            norm_backward(enc_normed_ref, enc_scale_ref, upstream, enc_gout_ref, block)
            raw = mm_t(enc_gout_ref[block, :], enc_w2_ref[...])
            times_slope(raw, enc_slope_ref, enc_gout_ref, block)
        pooled = mm(enc_pool_ref[...], enc_gout_ref[...]).astype(BF16)
        gpe_ref[...] = pooled[:grid_count, :]
        mesh_pool_ref[...] = pooled[mesh_rows, :]
        slot_back = (slot_back + mm_t(pooled[grid_count:spots, :], enc_wg_ref[low, :])).astype(BF16)
        send(out_refs, lambda j: slot_back[reverse[j] * width : (reverse[j] + 1) * width, :])

    results = call(
        backward,
        "edges_backward",
        [
            *arrived,
            *returned,
            spot_msg,
            grid_part,
            select_t,
            grid_nodes,
            grid_cot,
            mesh_cot,
            enc_pick,
            enc_pool,
            dec_pick,
            dec_pool,
            grid_first,
            grid_second,
            dec_second,
            dec_first,
            mesh_first,
            mesh_second,
            enc_second,
            enc_first,
            dec_first,
            *saved,
        ],
        sent_shapes(feat)
        + [((grid_count, feat), BF16)] * 4
        + [((mesh_count, feat), F32), ((mesh_count, feat), BF16), ((mesh_count, feat), BF16)],
        scratch=[
            ((spots, feat), BF16),
            ((spots, feat), BF16),
            ((spots, feat), BF16),
            ((spots, feat), BF16),
            ((spots, feat), F32),
            ((spots, 1), F32),
            ((spots, feat), BF16),
            ((spots, feat), BF16),
            ((total, feat), BF16),
            ((dec_count, feat), BF16),
            ((mesh_count, feat), BF16),
            ((enc_count, feat), BF16),
        ],
        flops=2 * feat * feat * (4 * spots + 3 * dec_count + 2 * enc_count),
    )
    outgoing, results = results[:sent_count], results[sent_count:]
    grid_out, grid_gpre, gpe, gpd, mesh_gin, mesh_gpre, mesh_pool = results
    final = exchange(outgoing)

    def tail(
        cot_ref,
        grid_gpre_ref,
        gpe_ref,
        gpd_ref,
        mesh_gin_ref,
        mesh_gpre_ref,
        mesh_pool_ref,
        grid_wn_ref,
        enc_wg_ref,
        dec_wg_ref,
        mesh_wn_ref,
        enc_wm_ref,
        base_ref,
        grad_mesh_ref,
    ):
        base_ref[...] = (
            cot_ref[...].astype(F32)
            + mm_t(grid_gpre_ref[...], grid_wn_ref[low, :])
            + mm_t(gpe_ref[...], enc_wg_ref[low, :])
            + mm_t(gpd_ref[...], dec_wg_ref[low, :])
        )
        grad_mesh_ref[...] = (
            mesh_gin_ref[...]
            + mm_t(mesh_gpre_ref[...], mesh_wn_ref[low, :])
            + mm_t(mesh_pool_ref[...], enc_wm_ref[high, :])
        )

    base, grad_mesh = call(
        tail,
        "local_gradients",
        [
            grid_cot,
            grid_gpre,
            gpe,
            gpd,
            mesh_gin,
            mesh_gpre,
            mesh_pool,
            grid_first,
            enc_first,
            dec_first,
            mesh_first,
            enc_first,
        ],
        [((grid_count, feat), F32), ((mesh_count, feat), F32)],
        flops=2 * feat * feat * 3 * grid_count,
    )

    def finish(*refs):
        back_refs = refs[:arrived_count]
        base_ref, select_t_ref, out_ref = refs[arrived_count:]
        out_ref[...] = base_ref[...] + mm(select_t_ref[:, :slots], by_row(back_refs))

    (grad_grid,) = call(
        finish,
        "add_returned",
        [*final, base, select_t],
        [((grid_count, feat), F32)],
        flops=2 * grid_count * slots * feat,
    )
    return (grid_out, mesh_out, grad_grid, grad_mesh)


def solution(mesh):
    rows = P(("groups", "tile"), None)
    flat = P(("groups", "tile"))
    in_specs = (rows,) * 6 + (P(),) * 8 + (rows,) + (flat,) * 5
    return jax.shard_map(
        per_device, mesh=mesh, in_specs=in_specs, out_specs=(rows,) * 4, check_vma=False
    )
```

```python
import jax
import jax.numpy as jnp
from jax import lax
from jax.experimental import pallas as pl
from jax.experimental.pallas import tpu as pltpu
from jax.sharding import PartitionSpec as P

TW = 4
CHUNK = 32
F32 = jnp.float32
BF16 = jnp.bfloat16
VMEM_LIMIT = 30 * 1024 * 1024


def mm(left, right):
    return jnp.dot(left, right, preferred_element_type=F32)


def mm_t(left, right):
    return lax.dot_general(left, right, (((1,), (1,)), ((), ())), preferred_element_type=F32)


def sigmoid(values):
    return 0.5 * jnp.tanh(0.5 * values) + 0.5


def norm_rows(values):
    centre = values - jnp.mean(values, axis=-1, keepdims=True)
    scale_inv = lax.rsqrt(jnp.mean(centre * centre, axis=-1, keepdims=True) + 1e-05)
    return centre * scale_inv, scale_inv


def norm_back(normed, scale_inv, upstream):
    return scale_inv * (
        upstream
        - jnp.mean(upstream, axis=-1, keepdims=True)
        - normed * jnp.mean(upstream * normed, axis=-1, keepdims=True)
    )


def row_chunks(rows, size=CHUNK):
    return [slice(start, min(start + size, rows)) for start in range(0, rows, size)]


def row_blocks(rows, parts):
    size = -(-rows // (16 * parts)) * 16
    return row_chunks(rows, size)


def inner_chunks(block):
    return [
        (slice(part.start, part.stop), slice(block.start + part.start, block.start + part.stop))
        for part in row_chunks(block.stop - block.start)
    ]


def activate(pre, act_ref, slope_ref, block):
    for inner, rows in inner_chunks(block):
        part = pre[inner, :]
        gate = sigmoid(part)
        act = part * gate
        act_ref[rows, :] = act.astype(BF16)
        slope_ref[rows, :] = (gate + act * (1.0 - gate)).astype(BF16)


def norm_forward(raw, normed_ref, scale_ref, block):
    for inner, rows in inner_chunks(block):
        normed, scale_inv = norm_rows(raw[inner, :])
        normed_ref[rows, :] = normed.astype(normed_ref.dtype)
        scale_ref[rows, :] = scale_inv


def norm_backward(normed_ref, scale_ref, upstream, out_ref, block):
    for inner, rows in inner_chunks(block):
        out_ref[rows, :] = norm_back(
            normed_ref[rows, :].astype(F32), scale_ref[rows, :], upstream[inner, :].astype(F32)
        ).astype(BF16)


def times_slope(raw, slope_ref, out_ref, block):
    for inner, rows in inner_chunks(block):
        out_ref[rows, :] = (raw[inner, :] * slope_ref[rows, :].astype(F32)).astype(BF16)


def neighbour_offsets(peer_count):
    forward_half = [1, TW, TW + 1, TW - 1]
    return forward_half + [-offset for offset in forward_half] + [peer_count // 2]


def onehot_pair(spot_ref, mesh_ref, spots, mesh_count, by_edge_ref, by_spot_ref):
    edges, total = by_edge_ref.shape
    spot_row = spot_ref[...].reshape(1, -1)
    mesh_row = mesh_ref[...].reshape(1, -1) + spots
    one, zero = jnp.ones((), BF16), jnp.zeros((), BF16)

    def ones(ids, index):
        shape = jnp.broadcast_shapes(ids.shape, index.shape)
        hit = jnp.broadcast_to(ids, shape) == jnp.broadcast_to(index, shape)
        return jnp.where(hit, jnp.broadcast_to(one, shape), jnp.broadcast_to(zero, shape))

    for row, first, count in ((spot_row, 0, spots), (mesh_row, spots, mesh_count)):
        ids = lax.broadcasted_iota(jnp.int32, (16, edges), 0).astype(jnp.int16)
        wide = jnp.broadcast_to(row, (16, edges)).astype(jnp.int16)
        for rows in row_chunks(count, 16):
            rows = slice(rows.start + first, rows.stop + first)
            by_spot_ref[rows, :] = ones(ids, wide - jnp.int16(rows.start))
    by_spot_ref[spots + mesh_count :, :] = jnp.zeros((total - spots - mesh_count, edges), BF16)
    lane = lax.broadcasted_iota(jnp.int32, (16, 128), 1).astype(jnp.int16)
    for rows in row_chunks(edges, 128):
        spot_col = jnp.broadcast_to(spot_row[:, rows], (128, 128)).T.astype(jnp.int16)
        mesh_col = jnp.broadcast_to(mesh_row[:, rows], (128, 128)).T.astype(jnp.int16)
        for columns in row_chunks(total, 128):
            for part in row_chunks(128, 16):
                place = slice(rows.start + part.start, rows.start + part.stop)
                ids = lane + jnp.int16(columns.start)
                hits = []
                if columns.start < spots:
                    hits.append(ones(ids, spot_col[part, :]))
                if columns.stop > spots:
                    hits.append(ones(ids, mesh_col[part, :]))
                by_edge_ref[place, columns] = sum(hits[1:], hits[0])


class Fetched:
    def __init__(self, source, target, semaphore):
        self.copy = pltpu.make_async_copy(source, target, semaphore)
        self.target = target
        self.landed = False
        self.copy.start()

    def land(self):
        if not self.landed:
            self.copy.wait()
            self.landed = True

    def __getitem__(self, key):
        self.land()
        return self.target[key]


def call(body, name, inputs, outputs, scratch=(), flops=0):
    arrays, specs, moved, fetches = [], [], 0, []
    for place, entry in enumerate(inputs):
        if isinstance(entry, tuple):
            array, first, rows = entry
            array = pltpu.with_memory_space_constraint(array, pltpu.HBM)
            specs.append(pl.BlockSpec(memory_space=pltpu.HBM))
            shape = (rows,) + array.shape[1:]
            fetches.append((place, first, rows, shape, array.dtype))
            moved += rows * (array.size // array.shape[0]) * array.dtype.itemsize
        else:
            array = entry
            specs.append(pl.BlockSpec(memory_space=pltpu.VMEM))
            moved += array.size * array.dtype.itemsize
        arrays.append(array)
    shapes = [jax.ShapeDtypeStruct(shape, dtype) for shape, dtype in outputs]
    for shape in shapes:
        moved += shape.size * shape.dtype.itemsize
    buffers = [pltpu.VMEM(shape, dtype) for _, _, _, shape, dtype in fetches]
    if fetches:
        buffers.append(pltpu.SemaphoreType.DMA((len(fetches),)))

    def kernel(*refs):
        refs = list(refs)
        waiting = []
        if fetches:
            targets, semaphores = refs[-len(buffers) : -1], refs[-1]
            refs = refs[: -len(buffers)]
        for slot, (place, first, rows, shape, _) in enumerate(fetches):
            source = refs[place]
            if source.shape != shape:
                source = source.at[pl.ds(first, rows)]
            refs[place] = Fetched(source, targets[slot], semaphores.at[slot])
            waiting.append(refs[place])
        body(*refs)
        for fetched in waiting:
            fetched.land()

    return pl.pallas_call(
        kernel,
        name=name,
        in_specs=specs,
        out_specs=[pl.BlockSpec(memory_space=pltpu.VMEM) for _ in shapes],
        out_shape=shapes,
        scratch_shapes=[pltpu.VMEM(shape, dtype) for shape, dtype in scratch]
        + buffers,
        compiler_params=pltpu.CompilerParams(vmem_limit_bytes=VMEM_LIMIT),
        cost_estimate=pl.CostEstimate(flops=flops, bytes_accessed=moved, transcendentals=0),
    )(*arrays)


def per_device(
    grid_nodes,
    mesh_nodes,
    enc_edges,
    dec_edges,
    grid_cot,
    mesh_cot,
    enc_first,
    enc_second,
    mesh_first,
    mesh_second,
    dec_first,
    dec_second,
    grid_first,
    grid_second,
    send_index,
    send_count,
    enc_grid,
    enc_mesh,
    dec_grid,
    dec_mesh,
):
    grid_count, feat = grid_nodes.shape
    mesh_count = mesh_nodes.shape[0]
    enc_count = enc_edges.shape[0]
    dec_count = dec_edges.shape[0]
    links, width = send_index.shape
    slots = links * width
    slots_pad = -(-slots // 128) * 128
    spots = grid_count + slots
    total = -(-(spots + mesh_count) // 128) * 128
    peer_count = lax.axis_size("tile")
    offsets = neighbour_offsets(peer_count)
    half = (links - 1) // 2
    reverse = [(j + half) % (links - 1) for j in range(links - 1)] + [links - 1]
    low, high = slice(0, feat), slice(feat, 2 * feat)
    mesh_rows = slice(spots, spots + mesh_count)

    one, four, five, three = range(half)
    minus = [j + half for j in range(half)]
    across = links - 1
    peers = range(peer_count)

    def permute(part, steps, odd_row_steps=None):
        rows = (steps, odd_row_steps or steps)
        pairs = [(s, (s + rows[s // TW % 2][s % 2]) % peer_count) for s in peers]
        return lax.ppermute(part, "tile", pairs)

    def exchange(parts):
        late_pair, early_pair, behind_one, ahead_three, five_off, opposite, own_chip = parts
        late_pair = permute(late_pair, (-4, -4), (4, 4))
        early_pair = permute(early_pair, (4, 4), (-4, -4))
        behind_one = permute(behind_one, (-1, 1))
        ahead_three = permute(ahead_three, (3, -3))
        five_off = permute(five_off, (-5, 5))
        opposite = permute(opposite, (peer_count // 2, peer_count // 2))
        late_pair, own_chip = lax.optimization_barrier((late_pair, own_chip))
        late_passed = permute(late_pair, (1, -1))
        own_chip = permute(own_chip, (1, -1))
        early_passed = permute(early_pair, (1, -1))
        return [
            late_pair,
            early_pair,
            behind_one,
            ahead_three,
            five_off,
            opposite,
            own_chip,
            late_passed,
            early_passed,
        ]

    arrived_count = 9

    def sent_shapes(columns):
        rows = (2, 2, 1, 1, 1, 1, 1)
        return [((count * width, columns), BF16) for count in rows]

    sent_count = len(sent_shapes(feat))

    def place_bits():
        own = lax.axis_index("tile")
        return lax.rem(own, 2) == 1, lax.rem(lax.div(own, TW), 2) == 1

    def send(refs, message, columns=slice(None)):
        odd, odd_row = place_bits()

        def by_parity(even, odd_one):
            return jnp.where(odd, message(odd_one), message(even))

        late_pair, early_pair, behind_one, ahead_three, five_off, opposite, own_chip = refs
        first, second = slice(0, width), slice(width, 2 * width)
        ahead = message(four), by_parity(five, three)
        behind = message(minus[four]), by_parity(minus[three], minus[five])
        for rows, go_ahead, go_behind in zip((first, second), ahead, behind):
            late_pair[rows, columns] = jnp.where(odd_row, go_ahead, go_behind)
            early_pair[rows, columns] = jnp.where(odd_row, go_behind, go_ahead)
        behind_one[:, columns] = by_parity(minus[one], one)
        ahead_three[:, columns] = by_parity(three, minus[three])
        five_off[:, columns] = by_parity(minus[five], five)
        opposite[:, columns] = message(across)
        own_chip[:, columns] = by_parity(one, minus[one])

    def receive(refs, columns=slice(None)):
        odd, odd_row = place_bits()
        late_pair, early_pair, behind_one, ahead_three, five_off, opposite, own_chip = refs[:7]
        late_passed, early_passed = refs[7:]
        first, second = slice(0, width), slice(width, 2 * width)
        near, near_three = behind_one[:, columns], ahead_three[:, columns]
        far, own = five_off[:, columns], own_chip[:, columns]
        late_rows, early_rows = late_passed[second, columns], early_passed[second, columns]
        from_behind = jnp.where(odd_row, early_rows, late_rows)
        from_ahead = jnp.where(odd_row, late_rows, early_rows)
        late_rows, early_rows = late_pair[first, columns], early_pair[first, columns]
        slot_rows = [None] * links
        slot_rows[one] = jnp.where(odd, own, near)
        slot_rows[minus[one]] = jnp.where(odd, near, own)
        slot_rows[three] = jnp.where(odd, near_three, from_behind)
        slot_rows[minus[three]] = jnp.where(odd, from_ahead, near_three)
        slot_rows[five] = jnp.where(odd, from_behind, far)
        slot_rows[minus[five]] = jnp.where(odd, far, from_ahead)
        slot_rows[four] = jnp.where(odd_row, early_rows, late_rows)
        slot_rows[minus[four]] = jnp.where(odd_row, late_rows, early_rows)
        slot_rows[across] = opposite[:, columns]
        return slot_rows

    def by_slot(refs, columns=slice(None)):
        return jnp.concatenate(receive(refs, columns), axis=0)

    def by_row(refs, columns=slice(None)):
        slot_rows = receive(refs, columns)
        return jnp.concatenate([slot_rows[reverse[j]] for j in range(links)], axis=0)

    def pack(index_ref, count_ref, nodes_ref, cot_ref, select_ref, *out_refs):
        def column(row):
            count = row.shape[1]
            eye = lax.broadcasted_iota(jnp.int32, (count, count), 0) == lax.broadcasted_iota(
                jnp.int32, (count, count), 1
            )
            return jnp.sum(
                jnp.where(eye, jnp.broadcast_to(row, (count, count)), 0.0), axis=1, keepdims=True
            )

        counts = column(count_ref[...].reshape(1, -1).astype(F32))
        place = lax.broadcasted_iota(jnp.int32, (links, width), 1).astype(F32)
        index = jnp.where(place < counts, index_ref[...].astype(F32), -1.0)
        lane = lax.broadcasted_iota(jnp.int32, (width, grid_count), 1).astype(F32)
        picks = [
            jnp.where(lane == column(index[j : j + 1, :]), 1.0, 0.0).astype(BF16)
            for j in range(links)
        ]
        select = jnp.concatenate(picks, axis=0)
        select_ref[:slots, :] = select
        select_ref[slots:, :] = jnp.zeros((slots_pad - slots, grid_count), BF16)
        sent_nodes = mm(select, nodes_ref[...]).astype(BF16)
        sent_cot = mm(select, cot_ref[...]).astype(BF16)
        send(out_refs, lambda j: sent_nodes[j * width : (j + 1) * width, :], low)
        send(out_refs, lambda j: sent_cot[j * width : (j + 1) * width, :], high)

    select, *outgoing = call(
        pack,
        "pack_rows",
        [
            (send_index, 0, links),
            (send_count, 0, links),
            (grid_nodes, 0, grid_count),
            (grid_cot, 0, grid_count),
        ],
        [((slots_pad, grid_count), BF16)] + sent_shapes(2 * feat),
        flops=4 * slots * grid_count * feat,
    )
    arrived = exchange(outgoing)

    def local(
        select_ref,
        nodes_ref,
        mesh_ref,
        enc_edges_ref,
        dec_edges_ref,
        enc_wg_ref,
        enc_wm_ref,
        enc_we_ref,
        dec_wg_ref,
        dec_we_ref,
        mesh_wn_ref,
        enc_grid_ref,
        enc_mesh_ref,
        dec_grid_ref,
        dec_mesh_ref,
        select_t_ref,
        enc_part_ref,
        dec_part_ref,
        mesh_part_ref,
        enc_pick_ref,
        enc_pool_ref,
        dec_pick_ref,
        dec_pool_ref,
        table_ref,
    ):
        onehot_pair(enc_grid_ref, enc_mesh_ref, spots, mesh_count, enc_pick_ref, enc_pool_ref)
        onehot_pair(dec_grid_ref, dec_mesh_ref, spots, mesh_count, dec_pick_ref, dec_pool_ref)
        select_t_ref[...] = select_ref[...].astype(F32).T.astype(BF16)
        nodes = nodes_ref[...]
        mesh_part_ref[...] = mm(mesh_ref[...], mesh_wn_ref[...])
        table_ref[:grid_count, :] = mm(nodes, enc_wg_ref[...]).astype(BF16)
        table_ref[grid_count:, :] = jnp.zeros((total - grid_count, feat), BF16)
        table_ref[mesh_rows, :] = mm(mesh_ref[...], enc_wm_ref[...]).astype(BF16)
        enc_part_ref[...] = mm(enc_edges_ref[...], enc_we_ref[...])
        enc_part_ref[...] += mm(enc_pick_ref[...], table_ref[...])
        pd = mm(nodes, dec_wg_ref[...]).astype(BF16)
        dec_part_ref[...] = mm(dec_edges_ref[...], dec_we_ref[...])
        dec_part_ref[...] += mm(dec_pick_ref[:, :grid_count], pd)

    select_t, enc_part, dec_part, mesh_part, enc_pick, enc_pool, dec_pick, dec_pool = call(
        local,
        "local_products",
        [
            select,
            (grid_nodes, 0, grid_count),
            (mesh_nodes, 0, mesh_count),
            (enc_edges, 0, enc_count),
            (dec_edges, 0, dec_count),
            (enc_first, 0, feat),
            (enc_first, feat, feat),
            (enc_first, 2 * feat, feat),
            (dec_first, 0, feat),
            (dec_first, 2 * feat, feat),
            (mesh_first, 0, feat),
            (enc_grid, 0, enc_grid.shape[0]),
            (enc_mesh, 0, enc_mesh.shape[0]),
            (dec_grid, 0, dec_grid.shape[0]),
            (dec_mesh, 0, dec_mesh.shape[0]),
        ],
        [
            ((grid_count, slots_pad), BF16),
            ((enc_count, feat), F32),
            ((dec_count, feat), F32),
            ((mesh_count, feat), F32),
            ((enc_count, total), BF16),
            ((total, enc_count), BF16),
            ((dec_count, total), BF16),
            ((total, dec_count), BF16),
        ],
        scratch=[((total, feat), BF16)],
        flops=2 * feat * (feat * (2 * grid_count + enc_count + dec_count) + total * dec_count),
    )

    def forward(*refs):
        arrived_refs, refs = refs[:arrived_count], refs[arrived_count:]
        (
            select_ref,
            enc_part_ref,
            dec_part_ref,
            mesh_part_ref,
            enc_pick_ref,
            enc_pool_ref,
            dec_pick_ref,
            dec_pool_ref,
            mesh_ref,
            enc_wg_ref,
            dec_wg_ref,
            enc_w2_ref,
            mesh_wa_ref,
            mesh_w2_ref,
            dec_wm_ref,
            dec_w2_ref,
        ) = refs[:16]
        refs = refs[16:]
        out_refs, refs = refs[:sent_count], refs[sent_count:]
        (
            mesh_out_ref,
            spot_ref,
            enc_normed_ref,
            enc_scale_ref,
            enc_slope_ref,
            dec_normed_ref,
            dec_scale_ref,
            dec_slope_ref,
            mesh_normed_ref,
            mesh_scale_ref,
            mesh_slope_ref,
            enc_act_ref,
            dec_act_ref,
            mesh_act_ref,
            table_ref,
        ) = refs
        rows = by_slot(arrived_refs, low)
        pe = mm(rows, enc_wg_ref[low, :]).astype(BF16)
        for block in row_blocks(enc_count, 1):
            pre = enc_part_ref[block, :] + mm(enc_pick_ref[block, grid_count:spots], pe)
            activate(pre, enc_act_ref, enc_slope_ref, block)
            raw = mm(enc_act_ref[block, :], enc_w2_ref[...])
            norm_forward(raw, enc_normed_ref, enc_scale_ref, block)
        agg = mm(enc_pool_ref[mesh_rows, :], enc_normed_ref[...]).astype(BF16)
        whole = slice(0, mesh_count)
        pre = mesh_part_ref[...] + mm(agg, mesh_wa_ref[high, :])
        activate(pre, mesh_act_ref, mesh_slope_ref, whole)
        raw = mm(mesh_act_ref[...], mesh_w2_ref[...])
        norm_forward(raw, mesh_normed_ref, mesh_scale_ref, whole)
        mesh_out = (mesh_ref[...].astype(F32) + mesh_normed_ref[...]).astype(BF16)
        mesh_out_ref[...] = mesh_out
        table_ref[:slots, :] = mm(rows, dec_wg_ref[low, :]).astype(BF16)
        table_ref[slots : slots + mesh_count, :] = mm(mesh_out, dec_wm_ref[high, :]).astype(BF16)
        table_ref[slots + mesh_count :, :] = jnp.zeros(
            (total - spots - mesh_count, feat), BF16
        )
        for block in row_blocks(dec_count, 1):
            pre = dec_part_ref[block, :] + mm(dec_pick_ref[block, grid_count:], table_ref[...])
            activate(pre, dec_act_ref, dec_slope_ref, block)
            raw = mm(dec_act_ref[block, :], dec_w2_ref[...])
            norm_forward(raw, dec_normed_ref, dec_scale_ref, block)
        spot_ref[...] = mm(dec_pool_ref[:spots, :], dec_normed_ref[...])
        shared = mm(select_ref[:slots, :], spot_ref[:grid_count, :].astype(BF16)).astype(BF16)
        slot_msg = spot_ref[grid_count:, :].astype(BF16)
        send(
            out_refs, lambda j: slot_msg[reverse[j] * width : (reverse[j] + 1) * width, :], low
        )
        send(out_refs, lambda j: shared[j * width : (j + 1) * width, :], high)

    edge_saved = [
        ((enc_count, feat), BF16),
        ((enc_count, 1), F32),
        ((enc_count, feat), BF16),
        ((dec_count, feat), BF16),
        ((dec_count, 1), F32),
        ((dec_count, feat), BF16),
        ((mesh_count, feat), F32),
        ((mesh_count, 1), F32),
        ((mesh_count, feat), BF16),
    ]
    results = call(
        forward,
        "edges_forward",
        [
            *arrived,
            select,
            enc_part,
            dec_part,
            mesh_part,
            enc_pick,
            enc_pool,
            dec_pick,
            dec_pool,
            mesh_nodes,
            enc_first,
            dec_first,
            enc_second,
            mesh_first,
            mesh_second,
            dec_first,
            dec_second,
        ],
        sent_shapes(2 * feat)
        + [((mesh_count, feat), BF16), ((spots, feat), F32)]
        + edge_saved,
        scratch=[
            ((enc_count, feat), BF16),
            ((dec_count, feat), BF16),
            ((mesh_count, feat), BF16),
            ((total - grid_count, feat), BF16),
        ],
        flops=2 * feat * feat * 2 * (enc_count + dec_count),
    )
    outgoing, results = results[:sent_count], results[sent_count:]
    mesh_out, spot_msg, *saved = results
    returned = exchange(outgoing)

    turned = [
        (grid_first, feat),
        (grid_second, 0),
        (dec_second, 0),
        (dec_first, feat),
        (mesh_first, feat),
        (mesh_second, 0),
        (enc_second, 0),
        (enc_first, 0),
        (dec_first, 0),
    ]

    def node_part(*refs):
        arrived_refs, refs = refs[:arrived_count], refs[arrived_count:]
        (nodes_ref, weight_ref, _), refs = refs[:3], refs[3:]
        weight_refs, (out_ref, *turned_refs) = refs[: len(turned)], refs[len(turned) :]
        out_ref[:grid_count, :] = mm(nodes_ref[...], weight_ref[low, :])
        out_ref[grid_count:, :] = mm(by_slot(arrived_refs, low), weight_ref[low, :])
        for ref, (_, first), turned_ref in zip(weight_refs, turned, turned_refs):
            turned_ref[...] = ref[first : first + feat, :].T

    grid_part, *turned_weights = call(
        node_part,
        "node_products",
        [*arrived, grid_nodes, grid_first, mesh_out, *[weight for weight, _ in turned]],
        [((spots, feat), F32)] + [((feat, feat), BF16)] * len(turned),
        flops=16 * spots * feat * feat,
    )

    def backward(*refs):
        arrived_refs, refs = refs[:arrived_count], refs[arrived_count:]
        returned_refs, refs = refs[:arrived_count], refs[arrived_count:]
        (
            spot_ref,
            grid_part_ref,
            select_t_ref,
            nodes_ref,
            cot_ref,
            mesh_cot_ref,
            enc_pick_ref,
            enc_pool_ref,
            dec_pick_ref,
            dec_pool_ref,
            grid_wa_ref,
            grid_w2_ref,
            grid_wat_ref,
            grid_w2t_ref,
            dec_w2t_ref,
            dec_wmt_ref,
            mesh_wat_ref,
            mesh_w2t_ref,
            enc_w2t_ref,
            enc_wgt_ref,
            dec_wgt_ref,
            enc_normed_ref,
            enc_scale_ref,
            enc_slope_ref,
            dec_normed_ref,
            dec_scale_ref,
            dec_slope_ref,
            mesh_normed_ref,
            mesh_scale_ref,
            mesh_slope_ref,
        ) = refs[:30]
        refs = refs[30:]
        out_refs, refs = refs[:sent_count], refs[sent_count:]
        (
            grid_out_ref,
            grid_gpre_ref,
            gpe_ref,
            gpd_ref,
            mesh_gin_ref,
            mesh_gpre_ref,
            mesh_pool_ref,
            agg_ref,
            cot_rows_ref,
            grid_act_ref,
            grid_slope_ref,
            grid_normed_ref,
            grid_scale_ref,
            grid_gout_ref,
            grid_gall_ref,
            spot_grad_ref,
            dec_gout_ref,
            mesh_gout_ref,
            enc_gout_ref,
        ) = refs
        agg_ref[:grid_count, :] = (
            spot_ref[:grid_count, :] + mm(select_t_ref[:, :slots], by_row(returned_refs, low))
        ).astype(BF16)
        agg_ref[grid_count:, :] = (
            spot_ref[grid_count:, :] + by_slot(returned_refs, high).astype(F32)
        ).astype(BF16)
        cot_rows_ref[:grid_count, :] = cot_ref[...]
        cot_rows_ref[grid_count:, :] = by_slot(arrived_refs, high)
        spot_grad_ref[spots:, :] = jnp.zeros((total - spots, feat), BF16)
        for block in row_blocks(spots, 1):
            pre = grid_part_ref[block, :] + mm(agg_ref[block, :], grid_wa_ref[high, :])
            activate(pre, grid_act_ref, grid_slope_ref, block)
            raw = mm(grid_act_ref[block, :], grid_w2_ref[...])
            norm_forward(raw, grid_normed_ref, grid_scale_ref, block)
            norm_backward(
                grid_normed_ref, grid_scale_ref, cot_rows_ref[block, :], grid_gout_ref, block
            )
            raw = mm(grid_gout_ref[block, :], grid_w2t_ref[...])
            times_slope(raw, grid_slope_ref, grid_gall_ref, block)
            spot_grad_ref[block, :] = mm(grid_gall_ref[block, :], grid_wat_ref[...]).astype(BF16)
        grid_out_ref[...] = (
            nodes_ref[...].astype(F32) + grid_normed_ref[:grid_count, :]
        ).astype(BF16)
        grid_gpre_ref[...] = grid_gall_ref[:grid_count, :]
        for block in row_blocks(dec_count, 1):
            upstream = mm(dec_pick_ref[block, :], spot_grad_ref[...])
            norm_backward(dec_normed_ref, dec_scale_ref, upstream, dec_gout_ref, block)
            raw = mm(dec_gout_ref[block, :], dec_w2t_ref[...])
            times_slope(raw, dec_slope_ref, dec_gout_ref, block)
        pooled = mm(dec_pool_ref[...], dec_gout_ref[...]).astype(BF16)
        gpd_ref[...] = pooled[:grid_count, :]
        slot_back = mm(pooled[grid_count:spots, :], dec_wgt_ref[...])
        mesh_gin = mesh_cot_ref[...].astype(F32) + mm(pooled[mesh_rows, :], dec_wmt_ref[...])
        mesh_gin_ref[...] = mesh_gin
        whole = slice(0, mesh_count)
        norm_backward(mesh_normed_ref, mesh_scale_ref, mesh_gin, mesh_gout_ref, whole)
        raw = mm(mesh_gout_ref[...], mesh_w2t_ref[...])
        times_slope(raw, mesh_slope_ref, mesh_gpre_ref, whole)
        gagg = mm(mesh_gpre_ref[...], mesh_wat_ref[...]).astype(BF16)
        for block in row_blocks(enc_count, 1):
            upstream = mm(enc_pick_ref[block, mesh_rows], gagg)
            norm_backward(enc_normed_ref, enc_scale_ref, upstream, enc_gout_ref, block)
            raw = mm(enc_gout_ref[block, :], enc_w2t_ref[...])
            times_slope(raw, enc_slope_ref, enc_gout_ref, block)
        pooled = mm(enc_pool_ref[...], enc_gout_ref[...]).astype(BF16)
        gpe_ref[...] = pooled[:grid_count, :]
        mesh_pool_ref[...] = pooled[mesh_rows, :]
        slot_back = (slot_back + mm(pooled[grid_count:spots, :], enc_wgt_ref[...])).astype(BF16)
        send(out_refs, lambda j: slot_back[reverse[j] * width : (reverse[j] + 1) * width, :])

    results = call(
        backward,
        "edges_backward",
        [
            *arrived,
            *returned,
            spot_msg,
            grid_part,
            select_t,
            grid_nodes,
            grid_cot,
            mesh_cot,
            enc_pick,
            enc_pool,
            dec_pick,
            dec_pool,
            grid_first,
            grid_second,
            *turned_weights,
            *saved,
        ],
        sent_shapes(feat)
        + [((grid_count, feat), BF16)] * 4
        + [((mesh_count, feat), F32), ((mesh_count, feat), BF16), ((mesh_count, feat), BF16)],
        scratch=[
            ((spots, feat), BF16),
            ((spots, feat), BF16),
            ((spots, feat), BF16),
            ((spots, feat), BF16),
            ((spots, feat), F32),
            ((spots, 1), F32),
            ((spots, feat), BF16),
            ((spots, feat), BF16),
            ((total, feat), BF16),
            ((dec_count, feat), BF16),
            ((mesh_count, feat), BF16),
            ((enc_count, feat), BF16),
        ],
        flops=2 * feat * feat * (4 * spots + 3 * dec_count + 2 * enc_count),
    )
    outgoing, results = results[:sent_count], results[sent_count:]
    grid_out, grid_gpre, gpe, gpd, mesh_gin, mesh_gpre, mesh_pool = results
    final = exchange(outgoing)

    def tail(
        cot_ref,
        grid_gpre_ref,
        gpe_ref,
        gpd_ref,
        mesh_gin_ref,
        mesh_gpre_ref,
        mesh_pool_ref,
        grid_wn_ref,
        enc_wg_ref,
        dec_wg_ref,
        mesh_wn_ref,
        enc_wm_ref,
        base_ref,
        grad_mesh_ref,
    ):
        base_ref[...] = (
            cot_ref[...].astype(F32)
            + mm_t(grid_gpre_ref[...], grid_wn_ref[low, :])
            + mm_t(gpe_ref[...], enc_wg_ref[low, :])
            + mm_t(gpd_ref[...], dec_wg_ref[low, :])
        )
        grad_mesh_ref[...] = (
            mesh_gin_ref[...]
            + mm_t(mesh_gpre_ref[...], mesh_wn_ref[low, :])
            + mm_t(mesh_pool_ref[...], enc_wm_ref[high, :])
        )

    base, grad_mesh = call(
        tail,
        "local_gradients",
        [
            grid_cot,
            grid_gpre,
            gpe,
            gpd,
            mesh_gin,
            mesh_gpre,
            mesh_pool,
            grid_first,
            enc_first,
            dec_first,
            mesh_first,
            enc_first,
        ],
        [((grid_count, feat), F32), ((mesh_count, feat), F32)],
        flops=2 * feat * feat * 3 * grid_count,
    )

    def finish(*refs):
        back_refs = refs[:arrived_count]
        base_ref, select_t_ref, out_ref = refs[arrived_count:]
        out_ref[...] = base_ref[...] + mm(select_t_ref[:, :slots], by_row(back_refs))

    (grad_grid,) = call(
        finish,
        "add_returned",
        [*final, base, select_t],
        [((grid_count, feat), F32)],
        flops=2 * grid_count * slots * feat,
    )
    return (grid_out, mesh_out, grad_grid, grad_mesh)


def solution(mesh):
    rows = P(("groups", "tile"), None)
    flat = P(("groups", "tile"))
    in_specs = (rows,) * 6 + (P(),) * 8 + (rows,) + (flat,) * 5
    return jax.shard_map(
        per_device, mesh=mesh, in_specs=in_specs, out_specs=(rows,) * 4, check_vma=False
    )
```

```python
import jax
import jax.numpy as jnp
from jax import lax
from jax.experimental import pallas as pl
from jax.experimental.pallas import tpu as pltpu
from jax.sharding import PartitionSpec as P

TW = 4
CHUNK = 32
ROUND_FLOPS = 2 * 10**10
F32 = jnp.float32
BF16 = jnp.bfloat16
VMEM_LIMIT = 30 * 1024 * 1024


def mm(left, right):
    return jnp.dot(left, right, preferred_element_type=F32)


def mm_t(left, right):
    return lax.dot_general(left, right, (((1,), (1,)), ((), ())), preferred_element_type=F32)


def sigmoid(values):
    return 0.5 * jnp.tanh(0.5 * values) + 0.5


def norm_rows(values):
    centre = values - jnp.mean(values, axis=-1, keepdims=True)
    scale_inv = lax.rsqrt(jnp.mean(centre * centre, axis=-1, keepdims=True) + 1e-05)
    return centre * scale_inv, scale_inv


def norm_back(normed, scale_inv, upstream):
    return scale_inv * (
        upstream
        - jnp.mean(upstream, axis=-1, keepdims=True)
        - normed * jnp.mean(upstream * normed, axis=-1, keepdims=True)
    )


def row_chunks(rows, size=CHUNK):
    return [slice(start, min(start + size, rows)) for start in range(0, rows, size)]


def row_blocks(rows, parts):
    size = -(-rows // (16 * parts)) * 16
    return row_chunks(rows, size)


def inner_chunks(block):
    return [
        (slice(part.start, part.stop), slice(block.start + part.start, block.start + part.stop))
        for part in row_chunks(block.stop - block.start)
    ]


def activate(pre, act_ref, slope_ref, block):
    for inner, rows in inner_chunks(block):
        part = pre[inner, :]
        gate = sigmoid(part)
        act = part * gate
        act_ref[rows, :] = act.astype(BF16)
        slope_ref[rows, :] = (gate + act * (1.0 - gate)).astype(BF16)


def norm_forward(raw, normed_ref, scale_ref, block):
    for inner, rows in inner_chunks(block):
        normed, scale_inv = norm_rows(raw[inner, :])
        normed_ref[rows, :] = normed.astype(normed_ref.dtype)
        scale_ref[rows, :] = scale_inv


def norm_backward(normed_ref, scale_ref, upstream, out_ref, block):
    for inner, rows in inner_chunks(block):
        out_ref[rows, :] = norm_back(
            normed_ref[rows, :].astype(F32), scale_ref[rows, :], upstream[inner, :].astype(F32)
        ).astype(BF16)


def times_slope(raw, slope_ref, out_ref, block):
    for inner, rows in inner_chunks(block):
        out_ref[rows, :] = (raw[inner, :] * slope_ref[rows, :].astype(F32)).astype(BF16)


def neighbour_offsets(peer_count):
    forward_half = [1, TW, TW + 1, TW - 1]
    return forward_half + [-offset for offset in forward_half] + [peer_count // 2]


def onehot_pair(spot_ref, mesh_ref, spots, mesh_count, by_edge_ref, by_spot_ref):
    edges, total = by_edge_ref.shape
    spot_row = spot_ref[...].reshape(1, -1)
    mesh_row = mesh_ref[...].reshape(1, -1) + spots
    one, zero = jnp.ones((), BF16), jnp.zeros((), BF16)

    def ones(ids, index):
        shape = jnp.broadcast_shapes(ids.shape, index.shape)
        hit = jnp.broadcast_to(ids, shape) == jnp.broadcast_to(index, shape)
        return jnp.where(hit, jnp.broadcast_to(one, shape), jnp.broadcast_to(zero, shape))

    for row, first, count in ((spot_row, 0, spots), (mesh_row, spots, mesh_count)):
        ids = lax.broadcasted_iota(jnp.int32, (16, edges), 0).astype(jnp.int16)
        wide = jnp.broadcast_to(row, (16, edges)).astype(jnp.int16)
        for rows in row_chunks(count, 16):
            rows = slice(rows.start + first, rows.stop + first)
            by_spot_ref[rows, :] = ones(ids, wide - jnp.int16(rows.start))
    by_spot_ref[spots + mesh_count :, :] = jnp.zeros((total - spots - mesh_count, edges), BF16)
    lane = lax.broadcasted_iota(jnp.int32, (16, 128), 1).astype(jnp.int16)
    for rows in row_chunks(edges, 128):
        spot_col = jnp.broadcast_to(spot_row[:, rows], (128, 128)).T.astype(jnp.int16)
        mesh_col = jnp.broadcast_to(mesh_row[:, rows], (128, 128)).T.astype(jnp.int16)
        for columns in row_chunks(total, 128):
            for part in row_chunks(128, 16):
                place = slice(rows.start + part.start, rows.start + part.stop)
                ids = lane + jnp.int16(columns.start)
                hits = []
                if columns.start < spots:
                    hits.append(ones(ids, spot_col[part, :]))
                if columns.stop > spots:
                    hits.append(ones(ids, mesh_col[part, :]))
                by_edge_ref[place, columns] = sum(hits[1:], hits[0])


class Fetched:
    def __init__(self, source, target, semaphore):
        self.copy = pltpu.make_async_copy(source, target, semaphore)
        self.target = target
        self.landed = False
        self.copy.start()

    def land(self):
        if not self.landed:
            self.copy.wait()
            self.landed = True

    def __getitem__(self, key):
        self.land()
        return self.target[key]


def call(body, name, inputs, outputs, scratch=(), flops=0):
    arrays, specs, moved, fetches = [], [], 0, []
    for place, entry in enumerate(inputs):
        if isinstance(entry, tuple):
            array, first, rows = entry
            array = pltpu.with_memory_space_constraint(array, pltpu.HBM)
            specs.append(pl.BlockSpec(memory_space=pltpu.HBM))
            shape = (rows,) + array.shape[1:]
            fetches.append((place, first, rows, shape, array.dtype))
            moved += rows * (array.size // array.shape[0]) * array.dtype.itemsize
        else:
            array = entry
            specs.append(pl.BlockSpec(memory_space=pltpu.VMEM))
            moved += array.size * array.dtype.itemsize
        arrays.append(array)
    shapes = [jax.ShapeDtypeStruct(shape, dtype) for shape, dtype in outputs]
    for shape in shapes:
        moved += shape.size * shape.dtype.itemsize
    buffers = [pltpu.VMEM(shape, dtype) for _, _, _, shape, dtype in fetches]
    if fetches:
        buffers.append(pltpu.SemaphoreType.DMA((len(fetches),)))

    def kernel(*refs):
        refs = list(refs)
        waiting = []
        if fetches:
            targets, semaphores = refs[-len(buffers) : -1], refs[-1]
            refs = refs[: -len(buffers)]
        for slot, (place, first, rows, shape, _) in enumerate(fetches):
            source = refs[place]
            if source.shape != shape:
                source = source.at[pl.ds(first, rows)]
            refs[place] = Fetched(source, targets[slot], semaphores.at[slot])
            waiting.append(refs[place])
        body(*refs)
        for fetched in waiting:
            fetched.land()

    return pl.pallas_call(
        kernel,
        name=name,
        in_specs=specs,
        out_specs=[pl.BlockSpec(memory_space=pltpu.VMEM) for _ in shapes],
        out_shape=shapes,
        scratch_shapes=[pltpu.VMEM(shape, dtype) for shape, dtype in scratch]
        + buffers,
        compiler_params=pltpu.CompilerParams(vmem_limit_bytes=VMEM_LIMIT),
        cost_estimate=pl.CostEstimate(flops=flops, bytes_accessed=moved, transcendentals=0),
    )(*arrays)


def per_device(
    grid_nodes,
    mesh_nodes,
    enc_edges,
    dec_edges,
    grid_cot,
    mesh_cot,
    enc_first,
    enc_second,
    mesh_first,
    mesh_second,
    dec_first,
    dec_second,
    grid_first,
    grid_second,
    send_index,
    send_count,
    enc_grid,
    enc_mesh,
    dec_grid,
    dec_mesh,
):
    grid_count, feat = grid_nodes.shape
    mesh_count = mesh_nodes.shape[0]
    enc_count = enc_edges.shape[0]
    dec_count = dec_edges.shape[0]
    links, width = send_index.shape
    slots = links * width
    slots_pad = -(-slots // 128) * 128
    spots = grid_count + slots
    total = -(-(spots + mesh_count) // 128) * 128
    peer_count = lax.axis_size("tile")
    offsets = neighbour_offsets(peer_count)
    half = (links - 1) // 2
    reverse = [(j + half) % (links - 1) for j in range(links - 1)] + [links - 1]
    low, high = slice(0, feat), slice(feat, 2 * feat)
    mesh_rows = slice(spots, spots + mesh_count)

    one, four, five, three = range(half)
    minus = [j + half for j in range(half)]
    across = links - 1
    peers = range(peer_count)

    def permute(part, steps, odd_row_steps=None):
        rows = (steps, odd_row_steps or steps)
        pairs = [(s, (s + rows[s // TW % 2][s % 2]) % peer_count) for s in peers]
        return lax.ppermute(part, "tile", pairs)

    def exchange(parts):
        late_pair, early_pair, behind_one, ahead_three, five_off, opposite, own_chip = parts
        late_pair = permute(late_pair, (-4, -4), (4, 4))
        early_pair = permute(early_pair, (4, 4), (-4, -4))
        behind_one = permute(behind_one, (-1, 1))
        ahead_three = permute(ahead_three, (3, -3))
        five_off = permute(five_off, (-5, 5))
        opposite = permute(opposite, (peer_count // 2, peer_count // 2))
        late_pair, own_chip = lax.optimization_barrier((late_pair, own_chip))
        late_passed = permute(late_pair, (1, -1))
        own_chip = permute(own_chip, (1, -1))
        early_passed = permute(early_pair, (1, -1))
        return [
            late_pair,
            early_pair,
            behind_one,
            ahead_three,
            five_off,
            opposite,
            own_chip,
            late_passed,
            early_passed,
        ]

    arrived_count = 9

    def sent_shapes(columns):
        rows = (2, 2, 1, 1, 1, 1, 1)
        return [((count * width, columns), BF16) for count in rows]

    sent_count = len(sent_shapes(feat))

    def place_bits():
        own = lax.axis_index("tile")
        return lax.rem(own, 2) == 1, lax.rem(lax.div(own, TW), 2) == 1

    def send(refs, message, columns=slice(None)):
        odd, odd_row = place_bits()

        def by_parity(even, odd_one):
            return jnp.where(odd, message(odd_one), message(even))

        late_pair, early_pair, behind_one, ahead_three, five_off, opposite, own_chip = refs
        first, second = slice(0, width), slice(width, 2 * width)
        ahead = message(four), by_parity(five, three)
        behind = message(minus[four]), by_parity(minus[three], minus[five])
        for rows, go_ahead, go_behind in zip((first, second), ahead, behind):
            late_pair[rows, columns] = jnp.where(odd_row, go_ahead, go_behind)
            early_pair[rows, columns] = jnp.where(odd_row, go_behind, go_ahead)
        behind_one[:, columns] = by_parity(minus[one], one)
        ahead_three[:, columns] = by_parity(three, minus[three])
        five_off[:, columns] = by_parity(minus[five], five)
        opposite[:, columns] = message(across)
        own_chip[:, columns] = by_parity(one, minus[one])

    def receive(refs, columns=slice(None)):
        odd, odd_row = place_bits()
        late_pair, early_pair, behind_one, ahead_three, five_off, opposite, own_chip = refs[:7]
        late_passed, early_passed = refs[7:]
        first, second = slice(0, width), slice(width, 2 * width)
        near, near_three = behind_one[:, columns], ahead_three[:, columns]
        far, own = five_off[:, columns], own_chip[:, columns]
        late_rows, early_rows = late_passed[second, columns], early_passed[second, columns]
        from_behind = jnp.where(odd_row, early_rows, late_rows)
        from_ahead = jnp.where(odd_row, late_rows, early_rows)
        late_rows, early_rows = late_pair[first, columns], early_pair[first, columns]
        slot_rows = [None] * links
        slot_rows[one] = jnp.where(odd, own, near)
        slot_rows[minus[one]] = jnp.where(odd, near, own)
        slot_rows[three] = jnp.where(odd, near_three, from_behind)
        slot_rows[minus[three]] = jnp.where(odd, from_ahead, near_three)
        slot_rows[five] = jnp.where(odd, from_behind, far)
        slot_rows[minus[five]] = jnp.where(odd, far, from_ahead)
        slot_rows[four] = jnp.where(odd_row, early_rows, late_rows)
        slot_rows[minus[four]] = jnp.where(odd_row, late_rows, early_rows)
        slot_rows[across] = opposite[:, columns]
        return slot_rows

    def by_slot(refs, columns=slice(None)):
        return jnp.concatenate(receive(refs, columns), axis=0)

    def by_row(refs, columns=slice(None)):
        slot_rows = receive(refs, columns)
        return jnp.concatenate([slot_rows[reverse[j]] for j in range(links)], axis=0)

    def pack(index_ref, count_ref, nodes_ref, cot_ref, select_ref, *out_refs):
        def column(row):
            count = row.shape[1]
            eye = lax.broadcasted_iota(jnp.int32, (count, count), 0) == lax.broadcasted_iota(
                jnp.int32, (count, count), 1
            )
            return jnp.sum(
                jnp.where(eye, jnp.broadcast_to(row, (count, count)), 0.0), axis=1, keepdims=True
            )

        counts = column(count_ref[...].reshape(1, -1).astype(F32))
        place = lax.broadcasted_iota(jnp.int32, (links, width), 1).astype(F32)
        index = jnp.where(place < counts, index_ref[...].astype(F32), -1.0)
        lane = lax.broadcasted_iota(jnp.int32, (width, grid_count), 1).astype(F32)
        picks = [
            jnp.where(lane == column(index[j : j + 1, :]), 1.0, 0.0).astype(BF16)
            for j in range(links)
        ]
        select = jnp.concatenate(picks, axis=0)
        select_ref[:slots, :] = select
        select_ref[slots:, :] = jnp.zeros((slots_pad - slots, grid_count), BF16)
        sent_nodes = mm(select, nodes_ref[...]).astype(BF16)
        sent_cot = mm(select, cot_ref[...]).astype(BF16)
        send(out_refs, lambda j: sent_nodes[j * width : (j + 1) * width, :], low)
        send(out_refs, lambda j: sent_cot[j * width : (j + 1) * width, :], high)

    select, *outgoing = call(
        pack,
        "pack_rows",
        [
            (send_index, 0, links),
            (send_count, 0, links),
            (grid_nodes, 0, grid_count),
            (grid_cot, 0, grid_count),
        ],
        [((slots_pad, grid_count), BF16)] + sent_shapes(2 * feat),
        flops=4 * slots * grid_count * feat,
    )
    def turn(select_ref, select_t_ref):
        select_t_ref[...] = select_ref[...].astype(F32).T.astype(BF16)

    (select_t,) = call(
        turn, "turn_select", [select], [((grid_count, slots_pad), BF16)], flops=ROUND_FLOPS
    )
    *outgoing, select_t = lax.optimization_barrier((*outgoing, select_t))
    arrived = exchange(outgoing)

    def local(
        nodes_ref,
        mesh_ref,
        enc_edges_ref,
        dec_edges_ref,
        enc_first_ref,
        dec_first_ref,
        mesh_first_ref,
        enc_grid_ref,
        enc_mesh_ref,
        dec_grid_ref,
        dec_mesh_ref,
        enc_part_ref,
        dec_part_ref,
        mesh_part_ref,
        enc_pick_ref,
        enc_pool_ref,
        dec_pick_ref,
        dec_pool_ref,
        table_ref,
    ):
        onehot_pair(enc_grid_ref, enc_mesh_ref, spots, mesh_count, enc_pick_ref, enc_pool_ref)
        onehot_pair(dec_grid_ref, dec_mesh_ref, spots, mesh_count, dec_pick_ref, dec_pool_ref)
        nodes = nodes_ref[...]
        mesh_part_ref[...] = mm(mesh_ref[...], mesh_first_ref[low, :])
        table_ref[:grid_count, :] = mm(nodes, enc_first_ref[low, :]).astype(BF16)
        table_ref[grid_count:, :] = jnp.zeros((total - grid_count, feat), BF16)
        table_ref[mesh_rows, :] = mm(mesh_ref[...], enc_first_ref[high, :]).astype(BF16)
        enc_part_ref[...] = mm(enc_edges_ref[...], enc_first_ref[2 * feat :, :])
        enc_part_ref[...] += mm(enc_pick_ref[...], table_ref[...])
        pd = mm(nodes, dec_first_ref[low, :]).astype(BF16)
        dec_part_ref[...] = mm(dec_edges_ref[...], dec_first_ref[2 * feat :, :])
        dec_part_ref[...] += mm(dec_pick_ref[:, :grid_count], pd)

    enc_part, dec_part, mesh_part, enc_pick, enc_pool, dec_pick, dec_pool = call(
        local,
        "local_products",
        [
            grid_nodes,
            mesh_nodes,
            enc_edges,
            dec_edges,
            enc_first,
            dec_first,
            mesh_first,
            enc_grid,
            enc_mesh,
            dec_grid,
            dec_mesh,
        ],
        [
            ((enc_count, feat), F32),
            ((dec_count, feat), F32),
            ((mesh_count, feat), F32),
            ((enc_count, total), BF16),
            ((total, enc_count), BF16),
            ((dec_count, total), BF16),
            ((total, dec_count), BF16),
        ],
        scratch=[((total, feat), BF16)],
        flops=2 * feat * (feat * (2 * grid_count + enc_count + dec_count) + total * dec_count),
    )

    def forward(*refs):
        arrived_refs, refs = refs[:arrived_count], refs[arrived_count:]
        (
            select_ref,
            enc_part_ref,
            dec_part_ref,
            mesh_part_ref,
            enc_pick_ref,
            enc_pool_ref,
            dec_pick_ref,
            dec_pool_ref,
            mesh_ref,
            enc_wg_ref,
            dec_wg_ref,
            enc_w2_ref,
            mesh_wa_ref,
            mesh_w2_ref,
            dec_wm_ref,
            dec_w2_ref,
        ) = refs[:16]
        refs = refs[16:]
        out_refs, refs = refs[:sent_count], refs[sent_count:]
        (
            mesh_out_ref,
            spot_ref,
            enc_normed_ref,
            enc_scale_ref,
            enc_slope_ref,
            dec_normed_ref,
            dec_scale_ref,
            dec_slope_ref,
            mesh_normed_ref,
            mesh_scale_ref,
            mesh_slope_ref,
            enc_act_ref,
            dec_act_ref,
            mesh_act_ref,
            table_ref,
        ) = refs
        rows = by_slot(arrived_refs, low)
        pe = mm(rows, enc_wg_ref[low, :]).astype(BF16)
        for block in row_blocks(enc_count, 1):
            pre = enc_part_ref[block, :] + mm(enc_pick_ref[block, grid_count:spots], pe)
            activate(pre, enc_act_ref, enc_slope_ref, block)
            raw = mm(enc_act_ref[block, :], enc_w2_ref[...])
            norm_forward(raw, enc_normed_ref, enc_scale_ref, block)
        agg = mm(enc_pool_ref[mesh_rows, :], enc_normed_ref[...]).astype(BF16)
        whole = slice(0, mesh_count)
        pre = mesh_part_ref[...] + mm(agg, mesh_wa_ref[high, :])
        activate(pre, mesh_act_ref, mesh_slope_ref, whole)
        raw = mm(mesh_act_ref[...], mesh_w2_ref[...])
        norm_forward(raw, mesh_normed_ref, mesh_scale_ref, whole)
        mesh_out = (mesh_ref[...].astype(F32) + mesh_normed_ref[...]).astype(BF16)
        mesh_out_ref[...] = mesh_out
        table_ref[:slots, :] = mm(rows, dec_wg_ref[low, :]).astype(BF16)
        table_ref[slots : slots + mesh_count, :] = mm(mesh_out, dec_wm_ref[high, :]).astype(BF16)
        table_ref[slots + mesh_count :, :] = jnp.zeros(
            (total - spots - mesh_count, feat), BF16
        )
        for block in row_blocks(dec_count, 1):
            pre = dec_part_ref[block, :] + mm(dec_pick_ref[block, grid_count:], table_ref[...])
            activate(pre, dec_act_ref, dec_slope_ref, block)
            raw = mm(dec_act_ref[block, :], dec_w2_ref[...])
            norm_forward(raw, dec_normed_ref, dec_scale_ref, block)
        spot_ref[...] = mm(dec_pool_ref[:spots, :], dec_normed_ref[...])
        shared = mm(select_ref[:slots, :], spot_ref[:grid_count, :].astype(BF16)).astype(BF16)
        slot_msg = spot_ref[grid_count:, :].astype(BF16)
        send(
            out_refs, lambda j: slot_msg[reverse[j] * width : (reverse[j] + 1) * width, :], low
        )
        send(out_refs, lambda j: shared[j * width : (j + 1) * width, :], high)

    edge_saved = [
        ((enc_count, feat), BF16),
        ((enc_count, 1), F32),
        ((enc_count, feat), BF16),
        ((dec_count, feat), BF16),
        ((dec_count, 1), F32),
        ((dec_count, feat), BF16),
        ((mesh_count, feat), F32),
        ((mesh_count, 1), F32),
        ((mesh_count, feat), BF16),
    ]
    results = call(
        forward,
        "edges_forward",
        [
            *arrived,
            select,
            enc_part,
            dec_part,
            mesh_part,
            enc_pick,
            enc_pool,
            dec_pick,
            dec_pool,
            mesh_nodes,
            enc_first,
            dec_first,
            enc_second,
            mesh_first,
            mesh_second,
            dec_first,
            dec_second,
        ],
        sent_shapes(2 * feat)
        + [((mesh_count, feat), BF16), ((spots, feat), F32)]
        + edge_saved,
        scratch=[
            ((enc_count, feat), BF16),
            ((dec_count, feat), BF16),
            ((mesh_count, feat), BF16),
            ((total - grid_count, feat), BF16),
        ],
        flops=2 * feat * feat * 2 * (enc_count + dec_count),
    )
    outgoing, results = results[:sent_count], results[sent_count:]
    mesh_out, spot_msg, *saved = results
    returned = exchange(outgoing)

    def node_part(*refs):
        arrived_refs = refs[:arrived_count]
        nodes_ref, weight_ref, out_ref = refs[arrived_count:]
        out_ref[:grid_count, :] = mm(nodes_ref[...], weight_ref[low, :])
        out_ref[grid_count:, :] = mm(by_slot(arrived_refs, low), weight_ref[low, :])

    (grid_part,) = call(
        node_part,
        "node_products",
        [*arrived, grid_nodes, grid_first],
        [((spots, feat), F32)],
        flops=16 * spots * feat * feat,
    )

    def backward(*refs):
        arrived_refs, refs = refs[:arrived_count], refs[arrived_count:]
        returned_refs, refs = refs[:arrived_count], refs[arrived_count:]
        (
            spot_ref,
            grid_part_ref,
            select_t_ref,
            nodes_ref,
            cot_ref,
            mesh_cot_ref,
            enc_pick_ref,
            enc_pool_ref,
            dec_pick_ref,
            dec_pool_ref,
            grid_wa_ref,
            grid_w2_ref,
            dec_w2_ref,
            dec_wm_ref,
            mesh_wa_ref,
            mesh_w2_ref,
            enc_w2_ref,
            enc_wg_ref,
            dec_wg_ref,
            enc_normed_ref,
            enc_scale_ref,
            enc_slope_ref,
            dec_normed_ref,
            dec_scale_ref,
            dec_slope_ref,
            mesh_normed_ref,
            mesh_scale_ref,
            mesh_slope_ref,
        ) = refs[:28]
        refs = refs[28:]
        out_refs, refs = refs[:sent_count], refs[sent_count:]
        (
            grid_out_ref,
            grid_gpre_ref,
            gpe_ref,
            gpd_ref,
            mesh_gin_ref,
            mesh_gpre_ref,
            mesh_pool_ref,
            agg_ref,
            cot_rows_ref,
            grid_act_ref,
            grid_slope_ref,
            grid_normed_ref,
            grid_scale_ref,
            grid_gout_ref,
            grid_gall_ref,
            spot_grad_ref,
            dec_gout_ref,
            mesh_gout_ref,
            enc_gout_ref,
        ) = refs
        agg_ref[:grid_count, :] = (
            spot_ref[:grid_count, :] + mm(select_t_ref[:, :slots], by_row(returned_refs, low))
        ).astype(BF16)
        agg_ref[grid_count:, :] = (
            spot_ref[grid_count:, :] + by_slot(returned_refs, high).astype(F32)
        ).astype(BF16)
        cot_rows_ref[:grid_count, :] = cot_ref[...]
        cot_rows_ref[grid_count:, :] = by_slot(arrived_refs, high)
        spot_grad_ref[spots:, :] = jnp.zeros((total - spots, feat), BF16)
        for block in row_blocks(spots, 1):
            pre = grid_part_ref[block, :] + mm(agg_ref[block, :], grid_wa_ref[high, :])
            activate(pre, grid_act_ref, grid_slope_ref, block)
            raw = mm(grid_act_ref[block, :], grid_w2_ref[...])
            norm_forward(raw, grid_normed_ref, grid_scale_ref, block)
            norm_backward(
                grid_normed_ref, grid_scale_ref, cot_rows_ref[block, :], grid_gout_ref, block
            )
            raw = mm_t(grid_gout_ref[block, :], grid_w2_ref[...])
            times_slope(raw, grid_slope_ref, grid_gall_ref, block)
            spot_grad_ref[block, :] = mm_t(
                grid_gall_ref[block, :], grid_wa_ref[high, :]
            ).astype(BF16)
        grid_out_ref[...] = (
            nodes_ref[...].astype(F32) + grid_normed_ref[:grid_count, :]
        ).astype(BF16)
        grid_gpre_ref[...] = grid_gall_ref[:grid_count, :]
        for block in row_blocks(dec_count, 1):
            upstream = mm(dec_pick_ref[block, :], spot_grad_ref[...])
            norm_backward(dec_normed_ref, dec_scale_ref, upstream, dec_gout_ref, block)
            raw = mm_t(dec_gout_ref[block, :], dec_w2_ref[...])
            times_slope(raw, dec_slope_ref, dec_gout_ref, block)
        pooled = mm(dec_pool_ref[...], dec_gout_ref[...]).astype(BF16)
        gpd_ref[...] = pooled[:grid_count, :]
        slot_back = mm_t(pooled[grid_count:spots, :], dec_wg_ref[low, :])
        mesh_gin = mesh_cot_ref[...].astype(F32) + mm_t(pooled[mesh_rows, :], dec_wm_ref[high, :])
        mesh_gin_ref[...] = mesh_gin
        whole = slice(0, mesh_count)
        norm_backward(mesh_normed_ref, mesh_scale_ref, mesh_gin, mesh_gout_ref, whole)
        raw = mm_t(mesh_gout_ref[...], mesh_w2_ref[...])
        times_slope(raw, mesh_slope_ref, mesh_gpre_ref, whole)
        gagg = mm_t(mesh_gpre_ref[...], mesh_wa_ref[high, :]).astype(BF16)
        for block in row_blocks(enc_count, 1):
            upstream = mm(enc_pick_ref[block, mesh_rows], gagg)
            norm_backward(enc_normed_ref, enc_scale_ref, upstream, enc_gout_ref, block)
            raw = mm_t(enc_gout_ref[block, :], enc_w2_ref[...])
            times_slope(raw, enc_slope_ref, enc_gout_ref, block)
        pooled = mm(enc_pool_ref[...], enc_gout_ref[...]).astype(BF16)
        gpe_ref[...] = pooled[:grid_count, :]
        mesh_pool_ref[...] = pooled[mesh_rows, :]
        slot_back = (slot_back + mm_t(pooled[grid_count:spots, :], enc_wg_ref[low, :])).astype(BF16)
        send(out_refs, lambda j: slot_back[reverse[j] * width : (reverse[j] + 1) * width, :])

    results = call(
        backward,
        "edges_backward",
        [
            *arrived,
            *returned,
            spot_msg,
            grid_part,
            select_t,
            grid_nodes,
            grid_cot,
            mesh_cot,
            enc_pick,
            enc_pool,
            dec_pick,
            dec_pool,
            grid_first,
            grid_second,
            dec_second,
            dec_first,
            mesh_first,
            mesh_second,
            enc_second,
            enc_first,
            dec_first,
            *saved,
        ],
        sent_shapes(feat)
        + [((grid_count, feat), BF16)] * 4
        + [((mesh_count, feat), F32), ((mesh_count, feat), BF16), ((mesh_count, feat), BF16)],
        scratch=[
            ((spots, feat), BF16),
            ((spots, feat), BF16),
            ((spots, feat), BF16),
            ((spots, feat), BF16),
            ((spots, feat), F32),
            ((spots, 1), F32),
            ((spots, feat), BF16),
            ((spots, feat), BF16),
            ((total, feat), BF16),
            ((dec_count, feat), BF16),
            ((mesh_count, feat), BF16),
            ((enc_count, feat), BF16),
        ],
        flops=2 * feat * feat * (4 * spots + 3 * dec_count + 2 * enc_count),
    )
    outgoing, results = results[:sent_count], results[sent_count:]
    grid_out, grid_gpre, gpe, gpd, mesh_gin, mesh_gpre, mesh_pool = results
    final = exchange(outgoing)

    def tail(
        cot_ref,
        grid_gpre_ref,
        gpe_ref,
        gpd_ref,
        mesh_gin_ref,
        mesh_gpre_ref,
        mesh_pool_ref,
        grid_wn_ref,
        enc_wg_ref,
        dec_wg_ref,
        mesh_wn_ref,
        enc_wm_ref,
        base_ref,
        grad_mesh_ref,
    ):
        base_ref[...] = (
            cot_ref[...].astype(F32)
            + mm_t(grid_gpre_ref[...], grid_wn_ref[low, :])
            + mm_t(gpe_ref[...], enc_wg_ref[low, :])
            + mm_t(gpd_ref[...], dec_wg_ref[low, :])
        )
        grad_mesh_ref[...] = (
            mesh_gin_ref[...]
            + mm_t(mesh_gpre_ref[...], mesh_wn_ref[low, :])
            + mm_t(mesh_pool_ref[...], enc_wm_ref[high, :])
        )

    base, grad_mesh = call(
        tail,
        "local_gradients",
        [
            grid_cot,
            grid_gpre,
            gpe,
            gpd,
            mesh_gin,
            mesh_gpre,
            mesh_pool,
            grid_first,
            enc_first,
            dec_first,
            mesh_first,
            enc_first,
        ],
        [((grid_count, feat), F32), ((mesh_count, feat), F32)],
        flops=2 * feat * feat * 3 * grid_count,
    )

    def finish(*refs):
        back_refs = refs[:arrived_count]
        base_ref, select_t_ref, out_ref = refs[arrived_count:]
        out_ref[...] = base_ref[...] + mm(select_t_ref[:, :slots], by_row(back_refs))

    (grad_grid,) = call(
        finish,
        "add_returned",
        [*final, base, select_t],
        [((grid_count, feat), F32)],
        flops=2 * grid_count * slots * feat,
    )
    return (grid_out, mesh_out, grad_grid, grad_mesh)


def solution(mesh):
    rows = P(("groups", "tile"), None)
    flat = P(("groups", "tile"))
    in_specs = (rows,) * 6 + (P(),) * 8 + (rows,) + (flat,) * 5
    return jax.shard_map(
        per_device, mesh=mesh, in_specs=in_specs, out_specs=(rows,) * 4, check_vma=False
    )
```

```python
import jax
import jax.numpy as jnp
from jax import lax
from jax.experimental import pallas as pl
from jax.experimental.pallas import tpu as pltpu
from jax.sharding import PartitionSpec as P

TW = 4
CHUNK = 32
ROUND_FLOPS = 2 * 10**10
F32 = jnp.float32
BF16 = jnp.bfloat16
VMEM_LIMIT = 30 * 1024 * 1024


def mm(left, right):
    return jnp.dot(left, right, preferred_element_type=F32)


def mm_t(left, right):
    return lax.dot_general(left, right, (((1,), (1,)), ((), ())), preferred_element_type=F32)


def centred(values, axis):
    values = values.astype(F32)
    return values - jnp.mean(values, axis=axis, keepdims=True)


def silu_and_slope(pre):
    half = 0.5 * pre
    lifted = 1.0 + jnp.tanh(half)
    return half * lifted, lifted * (0.5 + 0.5 * half * (2.0 - lifted))


def silu(pre):
    half = 0.5 * pre
    return half * (1.0 + jnp.tanh(half))


def scale_rows(raw):
    return lax.rsqrt(jnp.mean(raw * raw, axis=-1, keepdims=True) + 1e-05)


def norm_back(normed, scale_inv, upstream):
    return scale_inv * (upstream - normed * jnp.mean(upstream * normed, axis=-1, keepdims=True))


def row_chunks(rows, size=CHUNK):
    return [slice(start, min(start + size, rows)) for start in range(0, rows, size)]


def write_silu(pre, act_ref):
    for rows in row_chunks(pre.shape[0]):
        act_ref[rows, :] = silu(pre[rows, :]).astype(BF16)


def write_norm(raw, normed_ref, scale_ref):
    for rows in row_chunks(raw.shape[0]):
        part = raw[rows, :]
        scale_inv = scale_rows(part)
        normed_ref[rows, :] = (part * scale_inv).astype(normed_ref.dtype)
        scale_ref[rows, :] = jnp.broadcast_to(
            scale_inv, (part.shape[0], scale_ref.shape[1])
        ).astype(scale_ref.dtype)


def write_slope(pre_ref, slope_ref):
    for rows in row_chunks(pre_ref.shape[0]):
        slope_ref[rows, :] = silu_and_slope(pre_ref[rows, :])[1].astype(BF16)


def edge_back(upstream, normed_ref, scale_ref, upstream_ref, product_ref, out_ref):
    edges, features = normed_ref.shape
    lanes = scale_ref.shape[1]
    for rows in row_chunks(edges):
        part = upstream[rows, :].astype(BF16)
        upstream_ref[rows, :] = part
        product_ref[rows, :] = part * normed_ref[rows, :]
    ones = jnp.full((features, lanes), 1.0 / features, BF16)
    means = mm(product_ref[...], ones).astype(BF16)
    for rows in row_chunks(edges):
        mean, scale_inv = means[rows, :], scale_ref[rows, :]
        for columns in row_chunks(features, lanes):
            out_ref[rows, columns] = scale_inv * (
                upstream_ref[rows, columns] - normed_ref[rows, columns] * mean
            )


def times_slope(raw, slope_ref, out_ref):
    for rows in row_chunks(out_ref.shape[0]):
        out_ref[rows, :] = raw[rows, :].astype(BF16) * slope_ref[rows, :]


def neighbour_offsets(peer_count):
    forward_half = [1, TW, TW + 1, TW - 1]
    return forward_half + [-offset for offset in forward_half] + [peer_count // 2]


def onehot_pair(spot_ref, mesh_ref, spots, mesh_count, by_edge_ref, by_spot_ref):
    edges, total = by_edge_ref.shape
    spot_row = spot_ref[...].reshape(1, -1)
    mesh_row = mesh_ref[...].reshape(1, -1) + spots
    one, zero = jnp.ones((), BF16), jnp.zeros((), BF16)

    def ones(ids, index):
        shape = jnp.broadcast_shapes(ids.shape, index.shape)
        hit = jnp.broadcast_to(ids, shape) == jnp.broadcast_to(index, shape)
        return jnp.where(hit, jnp.broadcast_to(one, shape), jnp.broadcast_to(zero, shape))

    for row, first, count in ((spot_row, 0, spots), (mesh_row, spots, mesh_count)):
        ids = lax.broadcasted_iota(jnp.int32, (16, edges), 0).astype(jnp.int16)
        wide = jnp.broadcast_to(row, (16, edges)).astype(jnp.int16)
        for rows in row_chunks(count, 16):
            rows = slice(rows.start + first, rows.stop + first)
            by_spot_ref[rows, :] = ones(ids, wide - jnp.int16(rows.start))
    by_spot_ref[spots + mesh_count :, :] = jnp.zeros((total - spots - mesh_count, edges), BF16)
    lane = lax.broadcasted_iota(jnp.int32, (16, 128), 1).astype(jnp.int16)
    for rows in row_chunks(edges, 128):
        spot_col = jnp.broadcast_to(spot_row[:, rows], (128, 128)).T.astype(jnp.int16)
        mesh_col = jnp.broadcast_to(mesh_row[:, rows], (128, 128)).T.astype(jnp.int16)
        for columns in row_chunks(total, 128):
            for part in row_chunks(128, 16):
                place = slice(rows.start + part.start, rows.start + part.stop)
                ids = lane + jnp.int16(columns.start)
                hits = []
                if columns.start < spots:
                    hits.append(ones(ids, spot_col[part, :]))
                if columns.stop > spots:
                    hits.append(ones(ids, mesh_col[part, :]))
                by_edge_ref[place, columns] = sum(hits[1:], hits[0])


class Fetched:
    def __init__(self, source, target, semaphore):
        self.copy = pltpu.make_async_copy(source, target, semaphore)
        self.target = target
        self.landed = False
        self.copy.start()

    def land(self):
        if not self.landed:
            self.copy.wait()
            self.landed = True

    def __getitem__(self, key):
        self.land()
        return self.target[key]


def call(body, name, inputs, outputs, scratch=(), flops=0):
    arrays, specs, moved, fetches = [], [], 0, []
    for place, entry in enumerate(inputs):
        if isinstance(entry, tuple):
            array, first, rows = entry
            array = pltpu.with_memory_space_constraint(array, pltpu.HBM)
            specs.append(pl.BlockSpec(memory_space=pltpu.HBM))
            shape = (rows,) + array.shape[1:]
            fetches.append((place, first, rows, shape, array.dtype))
            moved += rows * (array.size // array.shape[0]) * array.dtype.itemsize
        else:
            array = entry
            specs.append(pl.BlockSpec(memory_space=pltpu.VMEM))
            moved += array.size * array.dtype.itemsize
        arrays.append(array)
    shapes = [jax.ShapeDtypeStruct(shape, dtype) for shape, dtype in outputs]
    for shape in shapes:
        moved += shape.size * shape.dtype.itemsize
    buffers = [pltpu.VMEM(shape, dtype) for _, _, _, shape, dtype in fetches]
    if fetches:
        buffers.append(pltpu.SemaphoreType.DMA((len(fetches),)))

    def kernel(*refs):
        refs = list(refs)
        waiting = []
        if fetches:
            targets, semaphores = refs[-len(buffers) : -1], refs[-1]
            refs = refs[: -len(buffers)]
        for slot, (place, first, rows, shape, _) in enumerate(fetches):
            source = refs[place]
            if source.shape != shape:
                source = source.at[pl.ds(first, rows)]
            refs[place] = Fetched(source, targets[slot], semaphores.at[slot])
            waiting.append(refs[place])
        body(*refs)
        for fetched in waiting:
            fetched.land()

    return pl.pallas_call(
        kernel,
        name=name,
        in_specs=specs,
        out_specs=[pl.BlockSpec(memory_space=pltpu.VMEM) for _ in shapes],
        out_shape=shapes,
        scratch_shapes=[pltpu.VMEM(shape, dtype) for shape, dtype in scratch]
        + buffers,
        compiler_params=pltpu.CompilerParams(vmem_limit_bytes=VMEM_LIMIT),
        cost_estimate=pl.CostEstimate(flops=flops, bytes_accessed=moved, transcendentals=0),
    )(*arrays)


def per_device(
    grid_nodes,
    mesh_nodes,
    enc_edges,
    dec_edges,
    grid_cot,
    mesh_cot,
    enc_first,
    enc_second,
    mesh_first,
    mesh_second,
    dec_first,
    dec_second,
    grid_first,
    grid_second,
    send_index,
    send_count,
    enc_grid,
    enc_mesh,
    dec_grid,
    dec_mesh,
):
    grid_count, feat = grid_nodes.shape
    mesh_count = mesh_nodes.shape[0]
    enc_count = enc_edges.shape[0]
    dec_count = dec_edges.shape[0]
    links, width = send_index.shape
    slots = links * width
    slots_pad = -(-slots // 128) * 128
    spots = grid_count + slots
    total = -(-(spots + mesh_count) // 128) * 128
    peer_count = lax.axis_size("tile")
    offsets = neighbour_offsets(peer_count)
    half = (links - 1) // 2
    reverse = [(j + half) % (links - 1) for j in range(links - 1)] + [links - 1]
    low, high = slice(0, feat), slice(feat, 2 * feat)
    mesh_rows = slice(spots, spots + mesh_count)

    one, four, five, three = range(half)
    minus = [j + half for j in range(half)]
    across = links - 1
    peers = range(peer_count)

    def permute(part, steps, odd_row_steps=None):
        rows = (steps, odd_row_steps or steps)
        pairs = [(s, (s + rows[s // TW % 2][s % 2]) % peer_count) for s in peers]
        return lax.ppermute(part, "tile", pairs)

    def exchange(parts):
        late_pair, early_pair, behind_one, ahead_three, five_off, opposite, own_chip = parts
        late_pair = permute(late_pair, (-4, -4), (4, 4))
        early_pair = permute(early_pair, (4, 4), (-4, -4))
        behind_one = permute(behind_one, (-1, 1))
        ahead_three = permute(ahead_three, (3, -3))
        five_off = permute(five_off, (-5, 5))
        opposite = permute(opposite, (peer_count // 2, peer_count // 2))
        late_pair, own_chip = lax.optimization_barrier((late_pair, own_chip))
        late_passed = permute(late_pair, (1, -1))
        own_chip = permute(own_chip, (1, -1))
        early_passed = permute(early_pair, (1, -1))
        return [
            late_pair,
            early_pair,
            behind_one,
            ahead_three,
            five_off,
            opposite,
            own_chip,
            late_passed,
            early_passed,
        ]

    arrived_count = 9

    def sent_shapes(columns):
        rows = (2, 2, 1, 1, 1, 1, 1)
        return [((count * width, columns), BF16) for count in rows]

    sent_count = len(sent_shapes(feat))

    def place_bits():
        own = lax.axis_index("tile")
        return lax.rem(own, 2) == 1, lax.rem(lax.div(own, TW), 2) == 1

    def send(refs, message, columns=slice(None)):
        odd, odd_row = place_bits()

        def by_parity(even, odd_one):
            return jnp.where(odd, message(odd_one), message(even))

        late_pair, early_pair, behind_one, ahead_three, five_off, opposite, own_chip = refs
        first, second = slice(0, width), slice(width, 2 * width)
        ahead = message(four), by_parity(five, three)
        behind = message(minus[four]), by_parity(minus[three], minus[five])
        for rows, go_ahead, go_behind in zip((first, second), ahead, behind):
            late_pair[rows, columns] = jnp.where(odd_row, go_ahead, go_behind)
            early_pair[rows, columns] = jnp.where(odd_row, go_behind, go_ahead)
        behind_one[:, columns] = by_parity(minus[one], one)
        ahead_three[:, columns] = by_parity(three, minus[three])
        five_off[:, columns] = by_parity(minus[five], five)
        opposite[:, columns] = message(across)
        own_chip[:, columns] = by_parity(one, minus[one])

    def receive(refs, columns=slice(None)):
        odd, odd_row = place_bits()
        late_pair, early_pair, behind_one, ahead_three, five_off, opposite, own_chip = refs[:7]
        late_passed, early_passed = refs[7:]
        first, second = slice(0, width), slice(width, 2 * width)
        near, near_three = behind_one[:, columns], ahead_three[:, columns]
        far, own = five_off[:, columns], own_chip[:, columns]
        late_rows, early_rows = late_passed[second, columns], early_passed[second, columns]
        from_behind = jnp.where(odd_row, early_rows, late_rows)
        from_ahead = jnp.where(odd_row, late_rows, early_rows)
        late_rows, early_rows = late_pair[first, columns], early_pair[first, columns]
        slot_rows = [None] * links
        slot_rows[one] = jnp.where(odd, own, near)
        slot_rows[minus[one]] = jnp.where(odd, near, own)
        slot_rows[three] = jnp.where(odd, near_three, from_behind)
        slot_rows[minus[three]] = jnp.where(odd, from_ahead, near_three)
        slot_rows[five] = jnp.where(odd, from_behind, far)
        slot_rows[minus[five]] = jnp.where(odd, far, from_ahead)
        slot_rows[four] = jnp.where(odd_row, early_rows, late_rows)
        slot_rows[minus[four]] = jnp.where(odd_row, late_rows, early_rows)
        slot_rows[across] = opposite[:, columns]
        return slot_rows

    def by_slot(refs, columns=slice(None)):
        return jnp.concatenate(receive(refs, columns), axis=0)

    def by_row(refs, columns=slice(None)):
        slot_rows = receive(refs, columns)
        return jnp.concatenate([slot_rows[reverse[j]] for j in range(links)], axis=0)

    def pack(index_ref, count_ref, nodes_ref, cot_ref, select_ref, *out_refs):
        def column(row):
            count = row.shape[1]
            eye = lax.broadcasted_iota(jnp.int32, (count, count), 0) == lax.broadcasted_iota(
                jnp.int32, (count, count), 1
            )
            return jnp.sum(
                jnp.where(eye, jnp.broadcast_to(row, (count, count)), 0.0), axis=1, keepdims=True
            )

        counts = column(count_ref[...].reshape(1, -1).astype(F32))
        place = lax.broadcasted_iota(jnp.int32, (links, width), 1).astype(F32)
        index = jnp.where(place < counts, index_ref[...].astype(F32), -1.0)
        lane = lax.broadcasted_iota(jnp.int32, (width, grid_count), 1).astype(F32)
        picks = [
            jnp.where(lane == column(index[j : j + 1, :]), 1.0, 0.0).astype(BF16)
            for j in range(links)
        ]
        select = jnp.concatenate(picks, axis=0)
        select_ref[:slots, :] = select
        select_ref[slots:, :] = jnp.zeros((slots_pad - slots, grid_count), BF16)
        sent_nodes = mm(select, nodes_ref[...]).astype(BF16)
        sent_cot = mm(select, cot_ref[...]).astype(BF16)
        send(out_refs, lambda j: sent_nodes[j * width : (j + 1) * width, :], low)
        send(out_refs, lambda j: sent_cot[j * width : (j + 1) * width, :], high)

    select, *outgoing = call(
        pack,
        "pack_rows",
        [
            (send_index, 0, links),
            (send_count, 0, links),
            (grid_nodes, 0, grid_count),
            (grid_cot, 0, grid_count),
        ],
        [((slots_pad, grid_count), BF16)] + sent_shapes(2 * feat),
        flops=4 * slots * grid_count * feat,
    )
    def turn(select_ref, select_t_ref):
        select_t_ref[...] = select_ref[...].astype(F32).T.astype(BF16)

    (select_t,) = call(
        turn, "turn_select", [select], [((grid_count, slots_pad), BF16)], flops=ROUND_FLOPS
    )
    *outgoing, select_t = lax.optimization_barrier((*outgoing, select_t))
    arrived = exchange(outgoing)

    def local(
        nodes_ref,
        mesh_ref,
        enc_edges_ref,
        dec_edges_ref,
        enc_first_ref,
        dec_first_ref,
        mesh_first_ref,
        enc_grid_ref,
        enc_mesh_ref,
        dec_grid_ref,
        dec_mesh_ref,
        enc_second_ref,
        mesh_second_ref,
        dec_second_ref,
        enc_part_ref,
        dec_part_ref,
        mesh_part_ref,
        enc_pick_ref,
        enc_pool_ref,
        dec_pick_ref,
        dec_pool_ref,
        enc_centred_ref,
        mesh_centred_ref,
        dec_centred_ref,
        table_ref,
    ):
        onehot_pair(enc_grid_ref, enc_mesh_ref, spots, mesh_count, enc_pick_ref, enc_pool_ref)
        onehot_pair(dec_grid_ref, dec_mesh_ref, spots, mesh_count, dec_pick_ref, dec_pool_ref)
        enc_centred_ref[...] = centred(enc_second_ref[...], 1).astype(BF16)
        mesh_centred_ref[...] = centred(mesh_second_ref[...], 1).astype(BF16)
        dec_centred_ref[...] = centred(dec_second_ref[...], 1).astype(BF16)
        nodes = nodes_ref[...]
        mesh_part_ref[...] = mm(mesh_ref[...], mesh_first_ref[low, :])
        table_ref[:grid_count, :] = mm(nodes, enc_first_ref[low, :]).astype(BF16)
        table_ref[grid_count:, :] = jnp.zeros((total - grid_count, feat), BF16)
        table_ref[mesh_rows, :] = mm(mesh_ref[...], enc_first_ref[high, :]).astype(BF16)
        enc_part_ref[...] = mm(enc_edges_ref[...], enc_first_ref[2 * feat :, :])
        enc_part_ref[...] += mm(enc_pick_ref[...], table_ref[...])
        pd = mm(nodes, dec_first_ref[low, :]).astype(BF16)
        dec_part_ref[...] = mm(dec_edges_ref[...], dec_first_ref[2 * feat :, :])
        dec_part_ref[...] += mm(dec_pick_ref[:, :grid_count], pd)

    (
        enc_part,
        dec_part,
        mesh_part,
        enc_pick,
        enc_pool,
        dec_pick,
        dec_pool,
        enc_centred,
        mesh_centred,
        dec_centred,
    ) = call(
        local,
        "local_products",
        [
            grid_nodes,
            mesh_nodes,
            enc_edges,
            dec_edges,
            enc_first,
            dec_first,
            mesh_first,
            enc_grid,
            enc_mesh,
            dec_grid,
            dec_mesh,
            enc_second,
            mesh_second,
            dec_second,
        ],
        [
            ((enc_count, feat), F32),
            ((dec_count, feat), F32),
            ((mesh_count, feat), F32),
            ((enc_count, total), BF16),
            ((total, enc_count), BF16),
            ((dec_count, total), BF16),
            ((total, dec_count), BF16),
        ]
        + [((feat, feat), BF16)] * 3,
        scratch=[((total, feat), BF16)],
        flops=2 * feat * (feat * (2 * grid_count + enc_count + dec_count) + total * dec_count),
    )

    def forward(*refs):
        arrived_refs, refs = refs[:arrived_count], refs[arrived_count:]
        (
            select_ref,
            enc_part_ref,
            dec_part_ref,
            mesh_part_ref,
            enc_pick_ref,
            enc_pool_ref,
            dec_pick_ref,
            dec_pool_ref,
            mesh_ref,
            enc_wg_ref,
            dec_wg_ref,
            enc_w2_ref,
            mesh_wa_ref,
            mesh_w2_ref,
            dec_wm_ref,
            dec_w2_ref,
        ) = refs[:16]
        refs = refs[16:]
        out_refs, refs = refs[:sent_count], refs[sent_count:]
        (
            spot_ref,
            enc_normed_ref,
            enc_scale_ref,
            enc_pre_ref,
            dec_normed_ref,
            dec_scale_ref,
            dec_pre_ref,
            mesh_normed_ref,
            mesh_scale_ref,
            mesh_pre_ref,
            enc_act_ref,
            dec_act_ref,
            mesh_act_ref,
            table_ref,
        ) = refs
        rows = by_slot(arrived_refs, low)
        pe = mm(rows, enc_wg_ref[low, :]).astype(BF16)
        enc_pre_ref[...] = enc_part_ref[...] + mm(enc_pick_ref[:, grid_count:spots], pe)
        write_silu(enc_pre_ref, enc_act_ref)
        write_norm(mm(enc_act_ref[...], enc_w2_ref[...]), enc_normed_ref, enc_scale_ref)
        agg = mm(enc_pool_ref[mesh_rows, :], enc_normed_ref[...]).astype(BF16)
        mesh_pre_ref[...] = mesh_part_ref[...] + mm(agg, mesh_wa_ref[high, :])
        write_silu(mesh_pre_ref, mesh_act_ref)
        write_norm(mm(mesh_act_ref[...], mesh_w2_ref[...]), mesh_normed_ref, mesh_scale_ref)
        mesh_out = (mesh_ref[...].astype(F32) + mesh_normed_ref[...]).astype(BF16)
        table_ref[:slots, :] = mm(rows, dec_wg_ref[low, :]).astype(BF16)
        table_ref[slots : slots + mesh_count, :] = mm(mesh_out, dec_wm_ref[high, :]).astype(BF16)
        table_ref[slots + mesh_count :, :] = jnp.zeros(
            (total - spots - mesh_count, feat), BF16
        )
        dec_pre_ref[...] = dec_part_ref[...] + mm(dec_pick_ref[:, grid_count:], table_ref[...])
        write_silu(dec_pre_ref, dec_act_ref)
        write_norm(mm(dec_act_ref[...], dec_w2_ref[...]), dec_normed_ref, dec_scale_ref)
        spot_ref[...] = mm(dec_pool_ref[:spots, :], dec_normed_ref[...])
        shared = mm(select_ref[:slots, :], spot_ref[:grid_count, :].astype(BF16)).astype(BF16)
        slot_msg = spot_ref[grid_count:, :].astype(BF16)
        send(
            out_refs, lambda j: slot_msg[reverse[j] * width : (reverse[j] + 1) * width, :], low
        )
        send(out_refs, lambda j: shared[j * width : (j + 1) * width, :], high)

    lanes = 128
    saved_shapes = [
        ((enc_count, feat), BF16),
        ((enc_count, lanes), BF16),
        ((enc_count, feat), F32),
        ((dec_count, feat), BF16),
        ((dec_count, lanes), BF16),
        ((dec_count, feat), F32),
        ((mesh_count, feat), F32),
        ((mesh_count, 1), F32),
        ((mesh_count, feat), F32),
    ]
    results = call(
        forward,
        "edges_forward",
        [
            *arrived,
            select,
            enc_part,
            dec_part,
            mesh_part,
            enc_pick,
            enc_pool,
            dec_pick,
            dec_pool,
            mesh_nodes,
            enc_first,
            dec_first,
            enc_centred,
            mesh_first,
            mesh_centred,
            dec_first,
            dec_centred,
        ],
        sent_shapes(2 * feat)
        + [((spots, feat), F32)]
        + saved_shapes,
        scratch=[
            ((enc_count, feat), BF16),
            ((dec_count, feat), BF16),
            ((mesh_count, feat), BF16),
            ((total - grid_count, feat), BF16),
        ],
        flops=2 * feat * feat * 2 * (enc_count + dec_count),
    )
    outgoing, results = results[:sent_count], results[sent_count:]
    spot_msg, *saved = results
    enc_normed, enc_scale, enc_pre, dec_normed, dec_scale, dec_pre = saved[:6]
    mesh_normed, mesh_scale, mesh_pre = saved[6:]
    returned = exchange(outgoing)

    def between(*refs):
        arrived_refs, refs = refs[:arrived_count], refs[arrived_count:]
        (
            nodes_ref,
            grid_first_ref,
            grid_second_ref,
            cot_ref,
            mesh_first_ref,
            mesh_ref,
            mesh_normed_ref,
            enc_pre_ref,
            dec_pre_ref,
            mesh_pre_ref,
            part_ref,
            cot_rows_ref,
            grid_w2_ref,
            grid_wa_ref,
            mesh_wa_ref,
            mesh_out_ref,
            enc_slope_ref,
            dec_slope_ref,
            mesh_slope_ref,
        ) = refs
        part_ref[:grid_count, :] = mm(nodes_ref[...], grid_first_ref[low, :])
        part_ref[grid_count:, :] = mm(by_slot(arrived_refs, low), grid_first_ref[low, :])
        mesh_out_ref[...] = (mesh_ref[...].astype(F32) + mesh_normed_ref[...]).astype(BF16)
        cot_rows_ref[:grid_count, :] = centred(cot_ref[...], 1)
        cot_rows_ref[grid_count:, :] = centred(by_slot(arrived_refs, high), 1)
        grid_w2_ref[...] = centred(grid_second_ref[...], 1).astype(BF16)
        grid_wa_ref[...] = centred(grid_first_ref[high, :], 0).astype(BF16)
        mesh_wa_ref[...] = centred(mesh_first_ref[high, :], 0).astype(BF16)
        write_slope(enc_pre_ref, enc_slope_ref)
        write_slope(dec_pre_ref, dec_slope_ref)
        write_slope(mesh_pre_ref, mesh_slope_ref)

    (
        grid_part,
        cot_rows,
        grid_w2_centred,
        grid_wa_centred,
        mesh_wa_centred,
        mesh_out,
        enc_slope,
        dec_slope,
        mesh_slope,
    ) = call(
        between,
        "slopes_and_nodes",
        [
            *arrived,
            grid_nodes,
            grid_first,
            grid_second,
            grid_cot,
            mesh_first,
            mesh_nodes,
            mesh_normed,
            enc_pre,
            dec_pre,
            mesh_pre,
        ],
        [((spots, feat), F32)] * 2
        + [((feat, feat), BF16)] * 3
        + [
            ((mesh_count, feat), BF16),
            ((enc_count, feat), BF16),
            ((dec_count, feat), BF16),
            ((mesh_count, feat), BF16),
        ],
        flops=16 * spots * feat * feat,
    )

    def backward(*refs):
        returned_refs, refs = refs[:arrived_count], refs[arrived_count:]
        (
            spot_ref,
            grid_part_ref,
            select_t_ref,
            cot_rows_ref,
            mesh_cot_ref,
            enc_pick_ref,
            enc_pool_ref,
            dec_pick_ref,
            dec_pool_ref,
            grid_wa_ref,
            grid_wac_ref,
            grid_w2_ref,
            grid_w2c_ref,
            dec_w2_ref,
            dec_wm_ref,
            mesh_wac_ref,
            mesh_w2_ref,
            enc_w2_ref,
            enc_wg_ref,
            dec_wg_ref,
            enc_normed_ref,
            enc_scale_ref,
            enc_slope_ref,
            dec_normed_ref,
            dec_scale_ref,
            dec_slope_ref,
            mesh_normed_ref,
            mesh_scale_ref,
            mesh_slope_ref,
        ) = refs[:29]
        refs = refs[29:]
        out_refs, refs = refs[:sent_count], refs[sent_count:]
        (
            grid_normed_ref,
            grid_gpre_ref,
            gpe_ref,
            gpd_ref,
            mesh_gin_ref,
            mesh_gpre_ref,
            mesh_pool_ref,
            agg_ref,
            grid_act_ref,
            grid_slope_ref,
            grid_gout_ref,
            spot_grad_ref,
            dec_up_ref,
            dec_product_ref,
            dec_gout_ref,
            mesh_gout_ref,
            enc_up_ref,
            enc_product_ref,
            enc_gout_ref,
        ) = refs
        agg_ref[:grid_count, :] = (
            spot_ref[:grid_count, :] + mm(select_t_ref[:, :slots], by_row(returned_refs, low))
        ).astype(BF16)
        agg_ref[grid_count:, :] = (
            spot_ref[grid_count:, :] + by_slot(returned_refs, high).astype(F32)
        ).astype(BF16)
        pre = grid_part_ref[...] + mm(agg_ref[...], grid_wa_ref[high, :])
        for rows in row_chunks(spots):
            act, slope = silu_and_slope(pre[rows, :])
            grid_act_ref[rows, :] = act.astype(BF16)
            grid_slope_ref[rows, :] = slope.astype(BF16)
        raw = mm(grid_act_ref[...], grid_w2c_ref[...])
        for rows in row_chunks(spots):
            part = raw[rows, :]
            scale_inv = scale_rows(part)
            normed = part * scale_inv
            grid_normed_ref[rows, :] = normed
            grid_gout_ref[rows, :] = norm_back(normed, scale_inv, cot_rows_ref[rows, :]).astype(
                BF16
            )
        times_slope(mm_t(grid_gout_ref[...], grid_w2_ref[...]), grid_slope_ref, grid_gpre_ref)
        spot_grad_ref[:spots, :] = mm_t(grid_gpre_ref[...], grid_wac_ref[...]).astype(BF16)
        spot_grad_ref[spots:, :] = jnp.zeros((total - spots, feat), BF16)
        edge_back(
            mm(dec_pick_ref[...], spot_grad_ref[...]),
            dec_normed_ref,
            dec_scale_ref,
            dec_up_ref,
            dec_product_ref,
            dec_gout_ref,
        )
        times_slope(mm_t(dec_gout_ref[...], dec_w2_ref[...]), dec_slope_ref, dec_gout_ref)
        pooled = mm(dec_pool_ref[...], dec_gout_ref[...]).astype(BF16)
        gpd_ref[...] = pooled[:grid_count, :]
        slot_back = mm_t(pooled[grid_count:spots, :], dec_wg_ref[low, :])
        mesh_gin = mesh_cot_ref[...].astype(F32) + mm_t(pooled[mesh_rows, :], dec_wm_ref[high, :])
        mesh_gin_ref[...] = mesh_gin
        mesh_gout_ref[...] = norm_back(
            mesh_normed_ref[...], mesh_scale_ref[...], centred(mesh_gin, 1)
        ).astype(BF16)
        times_slope(mm_t(mesh_gout_ref[...], mesh_w2_ref[...]), mesh_slope_ref, mesh_gpre_ref)
        gagg = mm_t(mesh_gpre_ref[...], mesh_wac_ref[...]).astype(BF16)
        edge_back(
            mm(enc_pick_ref[:, mesh_rows], gagg),
            enc_normed_ref,
            enc_scale_ref,
            enc_up_ref,
            enc_product_ref,
            enc_gout_ref,
        )
        times_slope(mm_t(enc_gout_ref[...], enc_w2_ref[...]), enc_slope_ref, enc_gout_ref)
        pooled = mm(enc_pool_ref[...], enc_gout_ref[...]).astype(BF16)
        gpe_ref[...] = pooled[:grid_count, :]
        mesh_pool_ref[...] = pooled[mesh_rows, :]
        slot_back = (
            slot_back + mm_t(pooled[grid_count:spots, :], enc_wg_ref[low, :])
        ).astype(BF16)
        send(out_refs, lambda j: slot_back[reverse[j] * width : (reverse[j] + 1) * width, :])

    results = call(
        backward,
        "edges_backward",
        [
            *returned,
            spot_msg,
            grid_part,
            select_t,
            cot_rows,
            mesh_cot,
            enc_pick,
            enc_pool,
            dec_pick,
            dec_pool,
            grid_first,
            grid_wa_centred,
            grid_second,
            grid_w2_centred,
            dec_second,
            dec_first,
            mesh_wa_centred,
            mesh_second,
            enc_second,
            enc_first,
            dec_first,
            enc_normed,
            enc_scale,
            enc_slope,
            dec_normed,
            dec_scale,
            dec_slope,
            mesh_normed,
            mesh_scale,
            mesh_slope,
        ],
        sent_shapes(feat)
        + [
            ((spots, feat), F32),
            ((spots, feat), BF16),
            ((grid_count, feat), BF16),
            ((grid_count, feat), BF16),
            ((mesh_count, feat), F32),
            ((mesh_count, feat), BF16),
            ((mesh_count, feat), BF16),
        ],
        scratch=[((spots, feat), BF16)] * 4
        + [((total, feat), BF16)]
        + [((dec_count, feat), BF16)] * 3
        + [((mesh_count, feat), BF16)]
        + [((enc_count, feat), BF16)] * 3,
        flops=2 * feat * feat * (4 * spots + 3 * dec_count + 2 * enc_count),
    )
    outgoing, results = results[:sent_count], results[sent_count:]
    grid_normed, grid_gpre, gpe, gpd, mesh_gin, mesh_gpre, mesh_pool = results
    final = exchange(outgoing)

    def tail(
        nodes_ref,
        grid_normed_ref,
        cot_ref,
        grid_gpre_ref,
        gpe_ref,
        gpd_ref,
        mesh_gin_ref,
        mesh_gpre_ref,
        mesh_pool_ref,
        grid_wn_ref,
        enc_wg_ref,
        dec_wg_ref,
        mesh_wn_ref,
        enc_wm_ref,
        base_ref,
        grad_mesh_ref,
        grid_out_ref,
    ):
        grid_out_ref[...] = (
            nodes_ref[...].astype(F32) + grid_normed_ref[:grid_count, :]
        ).astype(BF16)
        base_ref[...] = (
            cot_ref[...].astype(F32)
            + mm_t(grid_gpre_ref[:grid_count, :], grid_wn_ref[low, :])
            + mm_t(gpe_ref[...], enc_wg_ref[low, :])
            + mm_t(gpd_ref[...], dec_wg_ref[low, :])
        )
        grad_mesh_ref[...] = (
            mesh_gin_ref[...]
            + mm_t(mesh_gpre_ref[...], mesh_wn_ref[low, :])
            + mm_t(mesh_pool_ref[...], enc_wm_ref[high, :])
        )

    base, grad_mesh, grid_out = call(
        tail,
        "local_gradients",
        [
            grid_nodes,
            grid_normed,
            grid_cot,
            grid_gpre,
            gpe,
            gpd,
            mesh_gin,
            mesh_gpre,
            mesh_pool,
            grid_first,
            enc_first,
            dec_first,
            mesh_first,
            enc_first,
        ],
        [((grid_count, feat), F32), ((mesh_count, feat), F32), ((grid_count, feat), BF16)],
        flops=2 * feat * feat * 3 * grid_count,
    )

    def finish(*refs):
        back_refs = refs[:arrived_count]
        base_ref, select_t_ref, out_ref = refs[arrived_count:]
        out_ref[...] = base_ref[...] + mm(select_t_ref[:, :slots], by_row(back_refs))

    (grad_grid,) = call(
        finish,
        "add_returned",
        [*final, base, select_t],
        [((grid_count, feat), F32)],
        flops=2 * grid_count * slots * feat,
    )
    return (grid_out, mesh_out, grad_grid, grad_mesh)


def solution(mesh):
    rows = P(("groups", "tile"), None)
    flat = P(("groups", "tile"))
    in_specs = (rows,) * 6 + (P(),) * 8 + (rows,) + (flat,) * 5
    return jax.shard_map(
        per_device, mesh=mesh, in_specs=in_specs, out_specs=(rows,) * 4, check_vma=False
    )
```

```python
import jax
import jax.numpy as jnp
from jax import lax
from jax.experimental import pallas as pl
from jax.experimental.pallas import tpu as pltpu
from jax.sharding import PartitionSpec as P

TW = 4
CHUNK = 32
ROUND_FLOPS = 2 * 10**10
F32 = jnp.float32
BF16 = jnp.bfloat16
VMEM_LIMIT = 30 * 1024 * 1024


def mm(left, right):
    return jnp.dot(left, right, preferred_element_type=F32)


def mm_t(left, right):
    return lax.dot_general(left, right, (((1,), (1,)), ((), ())), preferred_element_type=F32)


def centred(values, axis):
    values = values.astype(F32)
    return values - jnp.mean(values, axis=axis, keepdims=True)


def silu_and_slope(pre):
    half = 0.5 * pre
    lifted = 1.0 + jnp.tanh(half)
    return half * lifted, lifted * (0.5 + 0.5 * half * (2.0 - lifted))


def silu(pre):
    half = 0.5 * pre
    return half * (1.0 + jnp.tanh(half))


def scale_rows(raw):
    return lax.rsqrt(jnp.mean(raw * raw, axis=-1, keepdims=True) + 1e-05)


def row_chunks(rows, size=CHUNK):
    return [slice(start, min(start + size, rows)) for start in range(0, rows, size)]


def write_silu(pre, act_ref):
    for rows in row_chunks(pre.shape[0]):
        act_ref[rows, :] = silu(pre[rows, :]).astype(BF16)


def write_norm(raw, normed_ref, scale_ref):
    for rows in row_chunks(raw.shape[0]):
        part = raw[rows, :]
        scale_inv = scale_rows(part)
        normed_ref[rows, :] = (part * scale_inv).astype(normed_ref.dtype)
        scale_ref[rows, :] = scale_inv


def write_slopes(pre_ref, normed_ref, scale_ref, second_ref, gain_ref, turned_ref):
    raw = mm_t(normed_ref[...], second_ref[...])
    for rows in row_chunks(pre_ref.shape[0]):
        gain = silu_and_slope(pre_ref[rows, :])[1] * scale_ref[rows, :]
        gain_ref[rows, :] = gain.astype(BF16)
        turned_ref[rows, :] = (gain * raw[rows, :]).astype(BF16)


def edge_back(both, normed_ref, gain_ref, turned_ref, out_ref):
    edges, features = normed_ref.shape
    for rows in row_chunks(edges):
        mean = jnp.mean(
            both[rows, :features] * normed_ref[rows, :].astype(F32), axis=-1, keepdims=True
        )
        out_ref[rows, :] = (
            gain_ref[rows, :] * both[rows, features:].astype(BF16)
            - turned_ref[rows, :] * mean.astype(BF16)
        )


def neighbour_offsets(peer_count):
    forward_half = [1, TW, TW + 1, TW - 1]
    return forward_half + [-offset for offset in forward_half] + [peer_count // 2]


def onehot_pair(spot_ref, mesh_ref, spots, mesh_count, by_edge_ref, by_spot_ref):
    edges, total = by_edge_ref.shape
    spot_row = spot_ref[...].reshape(1, -1)
    mesh_row = mesh_ref[...].reshape(1, -1) + spots
    one, zero = jnp.ones((), BF16), jnp.zeros((), BF16)

    def ones(ids, index):
        shape = jnp.broadcast_shapes(ids.shape, index.shape)
        hit = jnp.broadcast_to(ids, shape) == jnp.broadcast_to(index, shape)
        return jnp.where(hit, jnp.broadcast_to(one, shape), jnp.broadcast_to(zero, shape))

    for row, first, count in ((spot_row, 0, spots), (mesh_row, spots, mesh_count)):
        ids = lax.broadcasted_iota(jnp.int32, (16, edges), 0).astype(jnp.int16)
        wide = jnp.broadcast_to(row, (16, edges)).astype(jnp.int16)
        for rows in row_chunks(count, 16):
            rows = slice(rows.start + first, rows.stop + first)
            by_spot_ref[rows, :] = ones(ids, wide - jnp.int16(rows.start))
    by_spot_ref[spots + mesh_count :, :] = jnp.zeros((total - spots - mesh_count, edges), BF16)
    lane = lax.broadcasted_iota(jnp.int32, (16, 128), 1).astype(jnp.int16)
    for rows in row_chunks(edges, 128):
        spot_col = jnp.broadcast_to(spot_row[:, rows], (128, 128)).T.astype(jnp.int16)
        mesh_col = jnp.broadcast_to(mesh_row[:, rows], (128, 128)).T.astype(jnp.int16)
        for columns in row_chunks(total, 128):
            for part in row_chunks(128, 16):
                place = slice(rows.start + part.start, rows.start + part.stop)
                ids = lane + jnp.int16(columns.start)
                hits = []
                if columns.start < spots:
                    hits.append(ones(ids, spot_col[part, :]))
                if columns.stop > spots:
                    hits.append(ones(ids, mesh_col[part, :]))
                by_edge_ref[place, columns] = sum(hits[1:], hits[0])


class Fetched:
    def __init__(self, source, target, semaphore):
        self.copy = pltpu.make_async_copy(source, target, semaphore)
        self.target = target
        self.landed = False
        self.copy.start()

    def land(self):
        if not self.landed:
            self.copy.wait()
            self.landed = True

    def __getitem__(self, key):
        self.land()
        return self.target[key]


def call(body, name, inputs, outputs, scratch=(), flops=0):
    arrays, specs, moved, fetches = [], [], 0, []
    for place, entry in enumerate(inputs):
        if isinstance(entry, tuple):
            array, first, rows = entry
            array = pltpu.with_memory_space_constraint(array, pltpu.HBM)
            specs.append(pl.BlockSpec(memory_space=pltpu.HBM))
            shape = (rows,) + array.shape[1:]
            fetches.append((place, first, rows, shape, array.dtype))
            moved += rows * (array.size // array.shape[0]) * array.dtype.itemsize
        else:
            array = entry
            specs.append(pl.BlockSpec(memory_space=pltpu.VMEM))
            moved += array.size * array.dtype.itemsize
        arrays.append(array)
    shapes = [jax.ShapeDtypeStruct(shape, dtype) for shape, dtype in outputs]
    for shape in shapes:
        moved += shape.size * shape.dtype.itemsize
    buffers = [pltpu.VMEM(shape, dtype) for _, _, _, shape, dtype in fetches]
    if fetches:
        buffers.append(pltpu.SemaphoreType.DMA((len(fetches),)))

    def kernel(*refs):
        refs = list(refs)
        waiting = []
        if fetches:
            targets, semaphores = refs[-len(buffers) : -1], refs[-1]
            refs = refs[: -len(buffers)]
        for slot, (place, first, rows, shape, _) in enumerate(fetches):
            source = refs[place]
            if source.shape != shape:
                source = source.at[pl.ds(first, rows)]
            refs[place] = Fetched(source, targets[slot], semaphores.at[slot])
            waiting.append(refs[place])
        body(*refs)
        for fetched in waiting:
            fetched.land()

    return pl.pallas_call(
        kernel,
        name=name,
        in_specs=specs,
        out_specs=[pl.BlockSpec(memory_space=pltpu.VMEM) for _ in shapes],
        out_shape=shapes,
        scratch_shapes=[pltpu.VMEM(shape, dtype) for shape, dtype in scratch]
        + buffers,
        compiler_params=pltpu.CompilerParams(vmem_limit_bytes=VMEM_LIMIT),
        cost_estimate=pl.CostEstimate(flops=flops, bytes_accessed=moved, transcendentals=0),
    )(*arrays)


def per_device(
    grid_nodes,
    mesh_nodes,
    enc_edges,
    dec_edges,
    grid_cot,
    mesh_cot,
    enc_first,
    enc_second,
    mesh_first,
    mesh_second,
    dec_first,
    dec_second,
    grid_first,
    grid_second,
    send_index,
    send_count,
    enc_grid,
    enc_mesh,
    dec_grid,
    dec_mesh,
):
    grid_count, feat = grid_nodes.shape
    mesh_count = mesh_nodes.shape[0]
    enc_count = enc_edges.shape[0]
    dec_count = dec_edges.shape[0]
    links, width = send_index.shape
    slots = links * width
    slots_pad = -(-slots // 128) * 128
    spots = grid_count + slots
    total = -(-(spots + mesh_count) // 128) * 128
    peer_count = lax.axis_size("tile")
    offsets = neighbour_offsets(peer_count)
    half = (links - 1) // 2
    reverse = [(j + half) % (links - 1) for j in range(links - 1)] + [links - 1]
    low, high = slice(0, feat), slice(feat, 2 * feat)
    mesh_rows = slice(spots, spots + mesh_count)

    one, four, five, three = range(half)
    minus = [j + half for j in range(half)]
    across = links - 1
    peers = range(peer_count)

    def permute(part, steps, odd_row_steps=None):
        rows = (steps, odd_row_steps or steps)
        pairs = [(s, (s + rows[s // TW % 2][s % 2]) % peer_count) for s in peers]
        return lax.ppermute(part, "tile", pairs)

    def exchange(parts):
        late_pair, early_pair, behind_one, ahead_three, five_off, opposite, own_chip = parts
        late_pair = permute(late_pair, (-4, -4), (4, 4))
        early_pair = permute(early_pair, (4, 4), (-4, -4))
        behind_one = permute(behind_one, (-1, 1))
        ahead_three = permute(ahead_three, (3, -3))
        five_off = permute(five_off, (-5, 5))
        opposite = permute(opposite, (peer_count // 2, peer_count // 2))
        late_pair, own_chip = lax.optimization_barrier((late_pair, own_chip))
        late_passed = permute(late_pair, (1, -1))
        own_chip = permute(own_chip, (1, -1))
        early_passed = permute(early_pair, (1, -1))
        return [
            late_pair,
            early_pair,
            behind_one,
            ahead_three,
            five_off,
            opposite,
            own_chip,
            late_passed,
            early_passed,
        ]

    arrived_count = 9

    def sent_shapes(columns):
        rows = (2, 2, 1, 1, 1, 1, 1)
        return [((count * width, columns), BF16) for count in rows]

    sent_count = len(sent_shapes(feat))

    def place_bits():
        own = lax.axis_index("tile")
        return lax.rem(own, 2) == 1, lax.rem(lax.div(own, TW), 2) == 1

    def send(refs, message, columns=slice(None)):
        odd, odd_row = place_bits()

        def by_parity(even, odd_one):
            return jnp.where(odd, message(odd_one), message(even))

        late_pair, early_pair, behind_one, ahead_three, five_off, opposite, own_chip = refs
        first, second = slice(0, width), slice(width, 2 * width)
        ahead = message(four), by_parity(five, three)
        behind = message(minus[four]), by_parity(minus[three], minus[five])
        for rows, go_ahead, go_behind in zip((first, second), ahead, behind):
            late_pair[rows, columns] = jnp.where(odd_row, go_ahead, go_behind)
            early_pair[rows, columns] = jnp.where(odd_row, go_behind, go_ahead)
        behind_one[:, columns] = by_parity(minus[one], one)
        ahead_three[:, columns] = by_parity(three, minus[three])
        five_off[:, columns] = by_parity(minus[five], five)
        opposite[:, columns] = message(across)
        own_chip[:, columns] = by_parity(one, minus[one])

    def receive(refs, columns=slice(None)):
        odd, odd_row = place_bits()
        late_pair, early_pair, behind_one, ahead_three, five_off, opposite, own_chip = refs[:7]
        late_passed, early_passed = refs[7:]
        first, second = slice(0, width), slice(width, 2 * width)
        near, near_three = behind_one[:, columns], ahead_three[:, columns]
        far, own = five_off[:, columns], own_chip[:, columns]
        late_rows, early_rows = late_passed[second, columns], early_passed[second, columns]
        from_behind = jnp.where(odd_row, early_rows, late_rows)
        from_ahead = jnp.where(odd_row, late_rows, early_rows)
        late_rows, early_rows = late_pair[first, columns], early_pair[first, columns]
        slot_rows = [None] * links
        slot_rows[one] = jnp.where(odd, own, near)
        slot_rows[minus[one]] = jnp.where(odd, near, own)
        slot_rows[three] = jnp.where(odd, near_three, from_behind)
        slot_rows[minus[three]] = jnp.where(odd, from_ahead, near_three)
        slot_rows[five] = jnp.where(odd, from_behind, far)
        slot_rows[minus[five]] = jnp.where(odd, far, from_ahead)
        slot_rows[four] = jnp.where(odd_row, early_rows, late_rows)
        slot_rows[minus[four]] = jnp.where(odd_row, late_rows, early_rows)
        slot_rows[across] = opposite[:, columns]
        return slot_rows

    def by_slot(refs, columns=slice(None)):
        return jnp.concatenate(receive(refs, columns), axis=0)

    def by_row(refs, columns=slice(None)):
        slot_rows = receive(refs, columns)
        return jnp.concatenate([slot_rows[reverse[j]] for j in range(links)], axis=0)

    def pack(index_ref, count_ref, nodes_ref, cot_ref, select_ref, *out_refs):
        def column(row):
            count = row.shape[1]
            eye = lax.broadcasted_iota(jnp.int32, (count, count), 0) == lax.broadcasted_iota(
                jnp.int32, (count, count), 1
            )
            return jnp.sum(
                jnp.where(eye, jnp.broadcast_to(row, (count, count)), 0.0), axis=1, keepdims=True
            )

        counts = column(count_ref[...].reshape(1, -1).astype(F32))
        place = lax.broadcasted_iota(jnp.int32, (links, width), 1).astype(F32)
        index = jnp.where(place < counts, index_ref[...].astype(F32), -1.0)
        lane = lax.broadcasted_iota(jnp.int32, (width, grid_count), 1).astype(F32)
        picks = [
            jnp.where(lane == column(index[j : j + 1, :]), 1.0, 0.0).astype(BF16)
            for j in range(links)
        ]
        select = jnp.concatenate(picks, axis=0)
        select_ref[:slots, :] = select
        select_ref[slots:, :] = jnp.zeros((slots_pad - slots, grid_count), BF16)
        sent_nodes = mm(select, nodes_ref[...]).astype(BF16)
        sent_cot = mm(select, cot_ref[...]).astype(BF16)
        send(out_refs, lambda j: sent_nodes[j * width : (j + 1) * width, :], low)
        send(out_refs, lambda j: sent_cot[j * width : (j + 1) * width, :], high)

    select, *outgoing = call(
        pack,
        "pack_rows",
        [
            (send_index, 0, links),
            (send_count, 0, links),
            (grid_nodes, 0, grid_count),
            (grid_cot, 0, grid_count),
        ],
        [((slots_pad, grid_count), BF16)] + sent_shapes(2 * feat),
        flops=4 * slots * grid_count * feat,
    )
    def turn(select_ref, select_t_ref):
        select_t_ref[...] = select_ref[...].astype(F32).T.astype(BF16)

    (select_t,) = call(
        turn, "turn_select", [select], [((grid_count, slots_pad), BF16)], flops=ROUND_FLOPS
    )
    *outgoing, select_t = lax.optimization_barrier((*outgoing, select_t))
    arrived = exchange(outgoing)

    def local(
        select_ref,
        nodes_ref,
        mesh_ref,
        enc_edges_ref,
        dec_edges_ref,
        enc_first_ref,
        dec_first_ref,
        mesh_first_ref,
        enc_grid_ref,
        enc_mesh_ref,
        dec_grid_ref,
        dec_mesh_ref,
        enc_second_ref,
        mesh_second_ref,
        dec_second_ref,
        enc_part_ref,
        dec_part_ref,
        mesh_part_ref,
        enc_pick_ref,
        enc_pool_ref,
        dec_pick_ref,
        dec_pool_ref,
        enc_centred_ref,
        dec_centred_ref,
        mesh_wide_ref,
        mesh_base_ref,
        shared_pool_ref,
        table_ref,
    ):
        onehot_pair(enc_grid_ref, enc_mesh_ref, spots, mesh_count, enc_pick_ref, enc_pool_ref)
        onehot_pair(dec_grid_ref, dec_mesh_ref, spots, mesh_count, dec_pick_ref, dec_pool_ref)
        enc_centred_ref[...] = centred(enc_second_ref[...], 1).astype(BF16)
        mesh_centred = centred(mesh_second_ref[...], 1).astype(BF16)
        mesh_wide_ref[:, low] = mesh_centred
        mesh_wide_ref[:, high] = mm(mesh_centred, dec_first_ref[high, :]).astype(BF16)
        mesh_base_ref[...] = mm(mesh_ref[...], dec_first_ref[high, :])
        shared_pool_ref[...] = mm(
            select_ref[:slots, :], dec_pool_ref[:grid_count, :]
        ).astype(BF16)
        dec_centred_ref[...] = centred(dec_second_ref[...], 1).astype(BF16)
        nodes = nodes_ref[...]
        mesh_part_ref[...] = mm(mesh_ref[...], mesh_first_ref[low, :])
        table_ref[:grid_count, :] = mm(nodes, enc_first_ref[low, :]).astype(BF16)
        table_ref[grid_count:, :] = jnp.zeros((total - grid_count, feat), BF16)
        table_ref[mesh_rows, :] = mm(mesh_ref[...], enc_first_ref[high, :]).astype(BF16)
        enc_part_ref[...] = mm(enc_edges_ref[...], enc_first_ref[2 * feat :, :])
        enc_part_ref[...] += mm(enc_pick_ref[...], table_ref[...])
        pd = mm(nodes, dec_first_ref[low, :]).astype(BF16)
        dec_part_ref[...] = mm(dec_edges_ref[...], dec_first_ref[2 * feat :, :])
        dec_part_ref[...] += mm(dec_pick_ref[:, :grid_count], pd)

    (
        enc_part,
        dec_part,
        mesh_part,
        enc_pick,
        enc_pool,
        dec_pick,
        dec_pool,
        enc_centred,
        dec_centred,
        mesh_wide,
        mesh_base,
        shared_pool,
    ) = call(
        local,
        "local_products",
        [
            select,
            grid_nodes,
            mesh_nodes,
            enc_edges,
            dec_edges,
            enc_first,
            dec_first,
            mesh_first,
            enc_grid,
            enc_mesh,
            dec_grid,
            dec_mesh,
            enc_second,
            mesh_second,
            dec_second,
        ],
        [
            ((enc_count, feat), F32),
            ((dec_count, feat), F32),
            ((mesh_count, feat), F32),
            ((enc_count, total), BF16),
            ((total, enc_count), BF16),
            ((dec_count, total), BF16),
            ((total, dec_count), BF16),
        ]
        + [
            ((feat, feat), BF16),
            ((feat, feat), BF16),
            ((feat, 2 * feat), BF16),
            ((mesh_count, feat), F32),
            ((slots, dec_count), BF16),
        ],
        scratch=[((total, feat), BF16)],
        flops=2 * feat * (feat * (2 * grid_count + enc_count + dec_count) + total * dec_count),
    )

    def forward(*refs):
        arrived_refs, refs = refs[:arrived_count], refs[arrived_count:]
        (
            shared_pool_ref,
            enc_part_ref,
            dec_part_ref,
            mesh_part_ref,
            enc_pick_ref,
            enc_pool_ref,
            dec_pick_ref,
            dec_pool_ref,
            enc_wg_ref,
            dec_wg_ref,
            enc_w2_ref,
            mesh_wa_ref,
            mesh_w2_ref,
            mesh_base_ref,
            dec_w2_ref,
        ) = refs[:15]
        refs = refs[15:]
        out_refs, refs = refs[:sent_count], refs[sent_count:]
        (
            spot_ref,
            enc_normed_ref,
            enc_scale_ref,
            enc_pre_ref,
            dec_normed_ref,
            dec_scale_ref,
            dec_pre_ref,
            mesh_normed_ref,
            mesh_scale_ref,
            mesh_pre_ref,
            enc_act_ref,
            dec_act_ref,
            mesh_act_ref,
            table_ref,
        ) = refs
        rows = by_slot(arrived_refs, low)
        pe = mm(rows, enc_wg_ref[low, :]).astype(BF16)
        enc_pre_ref[...] = enc_part_ref[...] + mm(enc_pick_ref[:, grid_count:spots], pe)
        write_silu(enc_pre_ref, enc_act_ref)
        write_norm(mm(enc_act_ref[...], enc_w2_ref[...]), enc_normed_ref, enc_scale_ref)
        agg = mm(enc_pool_ref[mesh_rows, :], enc_normed_ref[...]).astype(BF16)
        mesh_pre_ref[...] = mesh_part_ref[...] + mm(agg, mesh_wa_ref[high, :])
        write_silu(mesh_pre_ref, mesh_act_ref)
        both = mm(mesh_act_ref[...], mesh_w2_ref[...])
        write_norm(both[:, low], mesh_normed_ref, mesh_scale_ref)
        mesh_sent = mesh_base_ref[...] + mesh_scale_ref[...] * both[:, high]
        table_ref[:slots, :] = mm(rows, dec_wg_ref[low, :]).astype(BF16)
        table_ref[slots : slots + mesh_count, :] = mesh_sent.astype(BF16)
        table_ref[slots + mesh_count :, :] = jnp.zeros(
            (total - spots - mesh_count, feat), BF16
        )
        dec_pre_ref[...] = dec_part_ref[...] + mm(dec_pick_ref[:, grid_count:], table_ref[...])
        write_silu(dec_pre_ref, dec_act_ref)
        write_norm(mm(dec_act_ref[...], dec_w2_ref[...]), dec_normed_ref, dec_scale_ref)
        spot_ref[...] = mm(dec_pool_ref[:spots, :], dec_normed_ref[...])
        shared = mm(shared_pool_ref[...], dec_normed_ref[...]).astype(BF16)
        slot_msg = spot_ref[grid_count:, :].astype(BF16)
        send(
            out_refs, lambda j: slot_msg[reverse[j] * width : (reverse[j] + 1) * width, :], low
        )
        send(out_refs, lambda j: shared[j * width : (j + 1) * width, :], high)

    saved_shapes = [
        ((enc_count, feat), BF16),
        ((enc_count, 1), F32),
        ((enc_count, feat), F32),
        ((dec_count, feat), BF16),
        ((dec_count, 1), F32),
        ((dec_count, feat), F32),
        ((mesh_count, feat), F32),
        ((mesh_count, 1), F32),
        ((mesh_count, feat), F32),
    ]
    results = call(
        forward,
        "edges_forward",
        [
            *arrived,
            shared_pool,
            enc_part,
            dec_part,
            mesh_part,
            enc_pick,
            enc_pool,
            dec_pick,
            dec_pool,
            enc_first,
            dec_first,
            enc_centred,
            mesh_first,
            mesh_wide,
            mesh_base,
            dec_centred,
        ],
        sent_shapes(2 * feat)
        + [((spots, feat), F32)]
        + saved_shapes,
        scratch=[
            ((enc_count, feat), BF16),
            ((dec_count, feat), BF16),
            ((mesh_count, feat), BF16),
            ((total - grid_count, feat), BF16),
        ],
        flops=2 * feat * feat * 2 * (enc_count + dec_count),
    )
    outgoing, results = results[:sent_count], results[sent_count:]
    spot_msg, *saved = results
    enc_normed, enc_scale, enc_pre, dec_normed, dec_scale, dec_pre = saved[:6]
    mesh_normed, mesh_scale, mesh_pre = saved[6:]
    returned = exchange(outgoing)

    def between(*refs):
        arrived_refs, refs = refs[:arrived_count], refs[arrived_count:]
        (
            nodes_ref,
            grid_first_ref,
            grid_second_ref,
            cot_ref,
            mesh_first_ref,
            mesh_second_ref,
            dec_first_ref,
            dec_second_ref,
            enc_second_ref,
            mesh_ref,
            mesh_cot_ref,
            enc_normed_ref,
            enc_scale_ref,
            enc_pre_ref,
            dec_normed_ref,
            dec_scale_ref,
            dec_pre_ref,
            mesh_normed_ref,
            mesh_pre_ref,
            mesh_wide_ref,
            part_ref,
            cot_rows_ref,
            cot_turned_ref,
            grid_wide_ref,
            grid_back_ref,
            mesh_in_ref,
            mesh_back_ref,
            mesh_out_ref,
            mesh_cot_turned_ref,
            mesh_slope_ref,
            mesh_turned_ref,
            enc_gain_ref,
            enc_turned_ref,
            dec_gain_ref,
            dec_turned_ref,
        ) = refs
        part_ref[:grid_count, :] = mm(nodes_ref[...], grid_first_ref[low, :])
        part_ref[grid_count:, :] = mm(by_slot(arrived_refs, low), grid_first_ref[low, :])
        mesh_out_ref[...] = (mesh_ref[...].astype(F32) + mesh_normed_ref[...]).astype(BF16)
        cot_rows_ref[:grid_count, :] = cot_ref[...]
        cot_rows_ref[grid_count:, :] = by_slot(arrived_refs, high)
        second = centred(grid_second_ref[...], 1).astype(BF16)
        grid_wide_ref[:, low] = second
        grid_wide_ref[:, high] = mm_t(second, grid_second_ref[...]).astype(BF16)
        cot_turned_ref[...] = mm_t(cot_rows_ref[...], second)
        grid_back_ref[low, :] = centred(grid_first_ref[high, :], 0).astype(BF16)
        grid_back_ref[high, :] = mm(dec_second_ref[...], grid_back_ref[low, :]).astype(BF16)
        mesh_back_ref[low, :] = centred(mesh_first_ref[high, :], 0).astype(BF16)
        mesh_back_ref[high, :] = mm(enc_second_ref[...], mesh_back_ref[low, :]).astype(BF16)
        mesh_in_ref[low, :] = dec_first_ref[high, :]
        mesh_in_ref[high, :] = mm(mesh_wide_ref[:, low], dec_first_ref[high, :]).astype(BF16)
        mesh_cot_turned_ref[...] = mm_t(mesh_cot_ref[...], mesh_wide_ref[:, low])
        mesh_turned_ref[...] = mm_t(mesh_normed_ref[...].astype(BF16), mesh_second_ref[...])
        mesh_slope_ref[...] = silu_and_slope(mesh_pre_ref[...])[1]
        write_slopes(
            enc_pre_ref,
            enc_normed_ref,
            enc_scale_ref,
            enc_second_ref,
            enc_gain_ref,
            enc_turned_ref,
        )
        write_slopes(
            dec_pre_ref,
            dec_normed_ref,
            dec_scale_ref,
            dec_second_ref,
            dec_gain_ref,
            dec_turned_ref,
        )

    (
        grid_part,
        cot_rows,
        cot_turned,
        grid_wide,
        grid_back,
        mesh_in,
        mesh_back,
        mesh_out,
        mesh_cot_turned,
        mesh_slope,
        mesh_turned,
        enc_gain,
        enc_turned,
        dec_gain,
        dec_turned,
    ) = call(
        between,
        "slopes_and_nodes",
        [
            *arrived,
            grid_nodes,
            grid_first,
            grid_second,
            grid_cot,
            mesh_first,
            mesh_second,
            dec_first,
            dec_second,
            enc_second,
            mesh_nodes,
            mesh_cot,
            enc_normed,
            enc_scale,
            enc_pre,
            dec_normed,
            dec_scale,
            dec_pre,
            mesh_normed,
            mesh_pre,
            mesh_wide,
        ],
        [
            ((spots, feat), F32),
            ((spots, feat), BF16),
            ((spots, feat), F32),
            ((feat, 2 * feat), BF16),
            ((2 * feat, feat), BF16),
            ((2 * feat, feat), BF16),
            ((2 * feat, feat), BF16),
            ((mesh_count, feat), BF16),
            ((mesh_count, feat), F32),
            ((mesh_count, feat), F32),
            ((mesh_count, feat), F32),
            ((enc_count, feat), BF16),
            ((enc_count, feat), BF16),
            ((dec_count, feat), BF16),
            ((dec_count, feat), BF16),
        ],
        flops=16 * spots * feat * feat,
    )

    def backward(*refs):
        returned_refs, refs = refs[:arrived_count], refs[arrived_count:]
        (
            spot_ref,
            grid_part_ref,
            select_t_ref,
            cot_rows_ref,
            cot_turned_ref,
            mesh_cot_ref,
            mesh_cot_turned_ref,
            enc_pick_ref,
            enc_pool_ref,
            dec_pick_ref,
            dec_pool_ref,
            grid_first_ref,
            grid_wide_ref,
            grid_back_ref,
            mesh_in_ref,
            mesh_back_ref,
            enc_first_ref,
            dec_first_ref,
            enc_normed_ref,
            enc_gain_ref,
            enc_turned_ref,
            dec_normed_ref,
            dec_gain_ref,
            dec_turned_ref,
            mesh_normed_ref,
            mesh_scale_ref,
            mesh_slope_ref,
            mesh_turned_ref,
        ) = refs[:28]
        refs = refs[28:]
        out_refs, refs = refs[:sent_count], refs[sent_count:]
        (
            grid_normed_ref,
            grid_gpre_ref,
            gpe_ref,
            gpd_ref,
            mesh_gin_ref,
            mesh_gpre_ref,
            mesh_pool_ref,
            agg_ref,
            grid_act_ref,
            grid_slope_ref,
            spot_grad_ref,
            dec_gpre_ref,
            enc_gpre_ref,
        ) = refs
        agg_ref[:grid_count, :] = (
            spot_ref[:grid_count, :] + mm(select_t_ref[:, :slots], by_row(returned_refs, low))
        ).astype(BF16)
        agg_ref[grid_count:, :] = (
            spot_ref[grid_count:, :] + by_slot(returned_refs, high).astype(F32)
        ).astype(BF16)
        pre = grid_part_ref[...] + mm(agg_ref[...], grid_first_ref[high, :])
        for rows in row_chunks(spots):
            act, slope = silu_and_slope(pre[rows, :])
            grid_act_ref[rows, :] = act.astype(BF16)
            grid_slope_ref[rows, :] = slope
        both = mm(grid_act_ref[...], grid_wide_ref[...])
        for rows in row_chunks(spots):
            part = both[rows, low]
            scale_inv = scale_rows(part)
            normed = part * scale_inv
            grid_normed_ref[rows, :] = normed
            mean = jnp.mean(cot_rows_ref[rows, :].astype(F32) * normed, axis=-1, keepdims=True)
            raw = scale_inv * (cot_turned_ref[rows, :] - (mean * scale_inv) * both[rows, high])
            grid_gpre_ref[rows, :] = (raw * grid_slope_ref[rows, :]).astype(BF16)
        spot_grad_ref[:spots, :] = mm_t(grid_gpre_ref[...], grid_back_ref[...]).astype(BF16)
        spot_grad_ref[spots:, :] = jnp.zeros((total - spots, 2 * feat), BF16)
        edge_back(
            mm(dec_pick_ref[...], spot_grad_ref[...]),
            dec_normed_ref,
            dec_gain_ref,
            dec_turned_ref,
            dec_gpre_ref,
        )
        mesh_sum = mm(dec_pool_ref[mesh_rows, :], dec_gpre_ref[...]).astype(BF16)
        both = mm_t(mesh_sum, mesh_in_ref[...])
        mesh_gin = mesh_cot_ref[...].astype(F32) + both[:, low]
        mesh_gin_ref[...] = mesh_gin
        mean = jnp.mean(mesh_gin * mesh_normed_ref[...], axis=-1, keepdims=True)
        raw = mesh_cot_turned_ref[...] + both[:, high] - mean * mesh_turned_ref[...]
        mesh_gpre_ref[...] = (mesh_scale_ref[...] * raw * mesh_slope_ref[...]).astype(BF16)
        mesh_gagg = mm_t(mesh_gpre_ref[...], mesh_back_ref[...]).astype(BF16)
        pooled = mm(dec_pool_ref[:spots, :], dec_gpre_ref[...]).astype(BF16)
        gpd_ref[...] = pooled[:grid_count, :]
        slot_back = mm_t(pooled[grid_count:, :], dec_first_ref[low, :])
        edge_back(
            mm(enc_pick_ref[:, mesh_rows], mesh_gagg),
            enc_normed_ref,
            enc_gain_ref,
            enc_turned_ref,
            enc_gpre_ref,
        )
        pooled = mm(enc_pool_ref[...], enc_gpre_ref[...]).astype(BF16)
        gpe_ref[...] = pooled[:grid_count, :]
        mesh_pool_ref[...] = pooled[mesh_rows, :]
        slot_back = (
            slot_back + mm_t(pooled[grid_count:spots, :], enc_first_ref[low, :])
        ).astype(BF16)
        send(out_refs, lambda j: slot_back[reverse[j] * width : (reverse[j] + 1) * width, :])

    results = call(
        backward,
        "edges_backward",
        [
            *returned,
            spot_msg,
            grid_part,
            select_t,
            cot_rows,
            cot_turned,
            mesh_cot,
            mesh_cot_turned,
            enc_pick,
            enc_pool,
            dec_pick,
            dec_pool,
            grid_first,
            grid_wide,
            grid_back,
            mesh_in,
            mesh_back,
            enc_first,
            dec_first,
            enc_normed,
            enc_gain,
            enc_turned,
            dec_normed,
            dec_gain,
            dec_turned,
            mesh_normed,
            mesh_scale,
            mesh_slope,
            mesh_turned,
        ],
        sent_shapes(feat)
        + [
            ((spots, feat), F32),
            ((spots, feat), BF16),
            ((grid_count, feat), BF16),
            ((grid_count, feat), BF16),
            ((mesh_count, feat), F32),
            ((mesh_count, feat), BF16),
            ((mesh_count, feat), BF16),
        ],
        scratch=[
            ((spots, feat), BF16),
            ((spots, feat), BF16),
            ((spots, feat), F32),
            ((total, 2 * feat), BF16),
            ((dec_count, feat), BF16),
            ((enc_count, feat), BF16),
        ],
        flops=2 * feat * feat * (4 * spots + 3 * dec_count + 2 * enc_count),
    )
    outgoing, results = results[:sent_count], results[sent_count:]
    grid_normed, grid_gpre, gpe, gpd, mesh_gin, mesh_gpre, mesh_pool = results
    final = exchange(outgoing)

    def tail(
        nodes_ref,
        grid_normed_ref,
        cot_ref,
        grid_gpre_ref,
        gpe_ref,
        gpd_ref,
        mesh_gin_ref,
        mesh_gpre_ref,
        mesh_pool_ref,
        grid_wn_ref,
        enc_wg_ref,
        dec_wg_ref,
        mesh_wn_ref,
        enc_wm_ref,
        base_ref,
        grad_mesh_ref,
        grid_out_ref,
    ):
        grid_out_ref[...] = (
            nodes_ref[...].astype(F32) + grid_normed_ref[:grid_count, :]
        ).astype(BF16)
        base_ref[...] = (
            cot_ref[...].astype(F32)
            + mm_t(grid_gpre_ref[:grid_count, :], grid_wn_ref[low, :])
            + mm_t(gpe_ref[...], enc_wg_ref[low, :])
            + mm_t(gpd_ref[...], dec_wg_ref[low, :])
        )
        grad_mesh_ref[...] = (
            mesh_gin_ref[...]
            + mm_t(mesh_gpre_ref[...], mesh_wn_ref[low, :])
            + mm_t(mesh_pool_ref[...], enc_wm_ref[high, :])
        )

    base, grad_mesh, grid_out = call(
        tail,
        "local_gradients",
        [
            grid_nodes,
            grid_normed,
            grid_cot,
            grid_gpre,
            gpe,
            gpd,
            mesh_gin,
            mesh_gpre,
            mesh_pool,
            grid_first,
            enc_first,
            dec_first,
            mesh_first,
            enc_first,
        ],
        [((grid_count, feat), F32), ((mesh_count, feat), F32), ((grid_count, feat), BF16)],
        flops=2 * feat * feat * 3 * grid_count,
    )

    def finish(*refs):
        back_refs = refs[:arrived_count]
        base_ref, select_t_ref, out_ref = refs[arrived_count:]
        out_ref[...] = base_ref[...] + mm(select_t_ref[:, :slots], by_row(back_refs))

    (grad_grid,) = call(
        finish,
        "add_returned",
        [*final, base, select_t],
        [((grid_count, feat), F32)],
        flops=2 * grid_count * slots * feat,
    )
    return (grid_out, mesh_out, grad_grid, grad_mesh)


def solution(mesh):
    rows = P(("groups", "tile"), None)
    flat = P(("groups", "tile"))
    in_specs = (rows,) * 6 + (P(),) * 8 + (rows,) + (flat,) * 5
    return jax.shard_map(
        per_device, mesh=mesh, in_specs=in_specs, out_specs=(rows,) * 4, check_vma=False
    )
```

```python
import jax
import jax.numpy as jnp
from jax import lax
from jax.experimental import pallas as pl
from jax.experimental.pallas import tpu as pltpu
from jax.sharding import PartitionSpec as P

TW = 4
CHUNK = 32
ROUND_FLOPS = 2 * 10**10
F32 = jnp.float32
BF16 = jnp.bfloat16
VMEM_LIMIT = 30 * 1024 * 1024


def mm(left, right):
    return jnp.dot(left, right, preferred_element_type=F32)


def mm_t(left, right):
    return lax.dot_general(left, right, (((1,), (1,)), ((), ())), preferred_element_type=F32)


def centred(values, axis):
    values = values.astype(F32)
    return values - jnp.mean(values, axis=axis, keepdims=True)


def silu_and_slope(pre):
    half = 0.5 * pre
    lifted = 1.0 + jnp.tanh(half)
    return half * lifted, lifted * (0.5 + 0.5 * half * (2.0 - lifted))


def silu(pre):
    half = 0.5 * pre
    return half * (1.0 + jnp.tanh(half))


def scale_rows(raw):
    return lax.rsqrt(jnp.mean(raw * raw, axis=-1, keepdims=True) + 1e-05)


def row_chunks(rows, size=CHUNK):
    return [slice(start, min(start + size, rows)) for start in range(0, rows, size)]


def write_silu(pre, act_ref):
    for rows in row_chunks(pre.shape[0]):
        act_ref[rows, :] = silu(pre[rows, :]).astype(BF16)


def write_norm(raw, normed_ref, scale_ref):
    for rows in row_chunks(raw.shape[0]):
        part = raw[rows, :]
        scale_inv = scale_rows(part)
        normed_ref[rows, :] = (part * scale_inv).astype(normed_ref.dtype)
        scale_ref[rows, :] = scale_inv


def write_slopes(pre_ref, normed_ref, scale_ref, second_ref, gain_ref, turned_ref):
    raw = mm_t(normed_ref[...], second_ref[...])
    for rows in row_chunks(pre_ref.shape[0]):
        gain = silu_and_slope(pre_ref[rows, :])[1] * scale_ref[rows, :]
        gain_ref[rows, :] = gain.astype(BF16)
        turned_ref[rows, :] = (gain * raw[rows, :]).astype(BF16)


def edge_back(both, normed_ref, gain_ref, turned_ref, out_ref):
    edges, features = normed_ref.shape
    for rows in row_chunks(edges):
        mean = jnp.mean(
            both[rows, :features] * normed_ref[rows, :].astype(F32), axis=-1, keepdims=True
        )
        out_ref[rows, :] = (
            gain_ref[rows, :] * both[rows, features:].astype(BF16)
            - turned_ref[rows, :] * mean.astype(BF16)
        )


def neighbour_offsets(peer_count):
    forward_half = [1, TW, TW + 1, TW - 1]
    return forward_half + [-offset for offset in forward_half] + [peer_count // 2]


def onehot_pair(spot_ref, mesh_ref, spots, mesh_count, by_edge_ref, by_spot_ref):
    edges, total = by_edge_ref.shape
    spot_row = spot_ref[...].reshape(1, -1)
    mesh_row = mesh_ref[...].reshape(1, -1) + spots
    one, zero = jnp.ones((), BF16), jnp.zeros((), BF16)

    def ones(ids, index):
        shape = jnp.broadcast_shapes(ids.shape, index.shape)
        hit = jnp.broadcast_to(ids, shape) == jnp.broadcast_to(index, shape)
        return jnp.where(hit, jnp.broadcast_to(one, shape), jnp.broadcast_to(zero, shape))

    for row, first, count in ((spot_row, 0, spots), (mesh_row, spots, mesh_count)):
        ids = lax.broadcasted_iota(jnp.int32, (16, edges), 0).astype(jnp.int16)
        wide = jnp.broadcast_to(row, (16, edges)).astype(jnp.int16)
        for rows in row_chunks(count, 16):
            rows = slice(rows.start + first, rows.stop + first)
            by_spot_ref[rows, :] = ones(ids, wide - jnp.int16(rows.start))
    by_spot_ref[spots + mesh_count :, :] = jnp.zeros((total - spots - mesh_count, edges), BF16)
    lane = lax.broadcasted_iota(jnp.int32, (16, 128), 1).astype(jnp.int16)
    for rows in row_chunks(edges, 128):
        spot_col = jnp.broadcast_to(spot_row[:, rows], (128, 128)).T.astype(jnp.int16)
        mesh_col = jnp.broadcast_to(mesh_row[:, rows], (128, 128)).T.astype(jnp.int16)
        for columns in row_chunks(total, 128):
            for part in row_chunks(128, 16):
                place = slice(rows.start + part.start, rows.start + part.stop)
                ids = lane + jnp.int16(columns.start)
                hits = []
                if columns.start < spots:
                    hits.append(ones(ids, spot_col[part, :]))
                if columns.stop > spots:
                    hits.append(ones(ids, mesh_col[part, :]))
                by_edge_ref[place, columns] = sum(hits[1:], hits[0])


class Fetched:
    def __init__(self, source, target, semaphore):
        self.copy = pltpu.make_async_copy(source, target, semaphore)
        self.target = target
        self.landed = False
        self.copy.start()

    def land(self):
        if not self.landed:
            self.copy.wait()
            self.landed = True

    def __getitem__(self, key):
        self.land()
        return self.target[key]


def call(body, name, inputs, outputs, scratch=(), flops=0):
    arrays, specs, moved, fetches = [], [], 0, []
    for place, entry in enumerate(inputs):
        if isinstance(entry, tuple):
            array, first, rows = entry
            array = pltpu.with_memory_space_constraint(array, pltpu.HBM)
            specs.append(pl.BlockSpec(memory_space=pltpu.HBM))
            shape = (rows,) + array.shape[1:]
            fetches.append((place, first, rows, shape, array.dtype))
            moved += rows * (array.size // array.shape[0]) * array.dtype.itemsize
        else:
            array = entry
            specs.append(pl.BlockSpec(memory_space=pltpu.VMEM))
            moved += array.size * array.dtype.itemsize
        arrays.append(array)
    shapes = [jax.ShapeDtypeStruct(shape, dtype) for shape, dtype in outputs]
    for shape in shapes:
        moved += shape.size * shape.dtype.itemsize
    buffers = [pltpu.VMEM(shape, dtype) for _, _, _, shape, dtype in fetches]
    if fetches:
        buffers.append(pltpu.SemaphoreType.DMA((len(fetches),)))

    def kernel(*refs):
        refs = list(refs)
        waiting = []
        if fetches:
            targets, semaphores = refs[-len(buffers) : -1], refs[-1]
            refs = refs[: -len(buffers)]
        for slot, (place, first, rows, shape, _) in enumerate(fetches):
            source = refs[place]
            if source.shape != shape:
                source = source.at[pl.ds(first, rows)]
            refs[place] = Fetched(source, targets[slot], semaphores.at[slot])
            waiting.append(refs[place])
        body(*refs)
        for fetched in waiting:
            fetched.land()

    return pl.pallas_call(
        kernel,
        name=name,
        in_specs=specs,
        out_specs=[pl.BlockSpec(memory_space=pltpu.VMEM) for _ in shapes],
        out_shape=shapes,
        scratch_shapes=[pltpu.VMEM(shape, dtype) for shape, dtype in scratch]
        + buffers,
        compiler_params=pltpu.CompilerParams(vmem_limit_bytes=VMEM_LIMIT),
        cost_estimate=pl.CostEstimate(flops=flops, bytes_accessed=moved, transcendentals=0),
    )(*arrays)


def per_device(
    grid_nodes,
    mesh_nodes,
    enc_edges,
    dec_edges,
    grid_cot,
    mesh_cot,
    enc_first,
    enc_second,
    mesh_first,
    mesh_second,
    dec_first,
    dec_second,
    grid_first,
    grid_second,
    send_index,
    send_count,
    enc_grid,
    enc_mesh,
    dec_grid,
    dec_mesh,
):
    grid_count, feat = grid_nodes.shape
    mesh_count = mesh_nodes.shape[0]
    enc_count = enc_edges.shape[0]
    dec_count = dec_edges.shape[0]
    links, width = send_index.shape
    slots = links * width
    slots_pad = -(-slots // 128) * 128
    spots = grid_count + slots
    total = -(-(spots + mesh_count) // 128) * 128
    peer_count = lax.axis_size("tile")
    offsets = neighbour_offsets(peer_count)
    half = (links - 1) // 2
    reverse = [(j + half) % (links - 1) for j in range(links - 1)] + [links - 1]
    low, high = slice(0, feat), slice(feat, 2 * feat)
    mesh_rows = slice(spots, spots + mesh_count)

    one, four, five, three = range(half)
    minus = [j + half for j in range(half)]
    across = links - 1
    peers = range(peer_count)

    def permute(part, steps, odd_row_steps=None):
        rows = (steps, odd_row_steps or steps)
        pairs = [(s, (s + rows[s // TW % 2][s % 2]) % peer_count) for s in peers]
        return lax.ppermute(part, "tile", pairs)

    def exchange(parts):
        late_pair, early_pair, behind_one, ahead_three, five_off, opposite, own_chip = parts
        late_pair = permute(late_pair, (-4, -4), (4, 4))
        early_pair = permute(early_pair, (4, 4), (-4, -4))
        behind_one = permute(behind_one, (-1, 1))
        ahead_three = permute(ahead_three, (3, -3))
        five_off = permute(five_off, (-5, 5))
        opposite = permute(opposite, (peer_count // 2, peer_count // 2))
        late_pair, own_chip = lax.optimization_barrier((late_pair, own_chip))
        late_passed = permute(late_pair, (1, -1))
        own_chip = permute(own_chip, (1, -1))
        early_passed = permute(early_pair, (1, -1))
        return [
            late_pair,
            early_pair,
            behind_one,
            ahead_three,
            five_off,
            opposite,
            own_chip,
            late_passed,
            early_passed,
        ]

    arrived_count = 9

    def sent_shapes(columns):
        rows = (2, 2, 1, 1, 1, 1, 1)
        return [((count * width, columns), BF16) for count in rows]

    sent_count = len(sent_shapes(feat))

    def place_bits():
        own = lax.axis_index("tile")
        return lax.rem(own, 2) == 1, lax.rem(lax.div(own, TW), 2) == 1

    def send(refs, message, columns=slice(None)):
        odd, odd_row = place_bits()

        def by_parity(even, odd_one):
            return jnp.where(odd, message(odd_one), message(even))

        late_pair, early_pair, behind_one, ahead_three, five_off, opposite, own_chip = refs
        first, second = slice(0, width), slice(width, 2 * width)
        ahead = message(four), by_parity(five, three)
        behind = message(minus[four]), by_parity(minus[three], minus[five])
        for rows, go_ahead, go_behind in zip((first, second), ahead, behind):
            late_pair[rows, columns] = jnp.where(odd_row, go_ahead, go_behind)
            early_pair[rows, columns] = jnp.where(odd_row, go_behind, go_ahead)
        behind_one[:, columns] = by_parity(minus[one], one)
        ahead_three[:, columns] = by_parity(three, minus[three])
        five_off[:, columns] = by_parity(minus[five], five)
        opposite[:, columns] = message(across)
        own_chip[:, columns] = by_parity(one, minus[one])

    def receive(refs, columns=slice(None)):
        odd, odd_row = place_bits()
        late_pair, early_pair, behind_one, ahead_three, five_off, opposite, own_chip = refs[:7]
        late_passed, early_passed = refs[7:]
        first, second = slice(0, width), slice(width, 2 * width)
        near, near_three = behind_one[:, columns], ahead_three[:, columns]
        far, own = five_off[:, columns], own_chip[:, columns]
        late_rows, early_rows = late_passed[second, columns], early_passed[second, columns]
        from_behind = jnp.where(odd_row, early_rows, late_rows)
        from_ahead = jnp.where(odd_row, late_rows, early_rows)
        late_rows, early_rows = late_pair[first, columns], early_pair[first, columns]
        slot_rows = [None] * links
        slot_rows[one] = jnp.where(odd, own, near)
        slot_rows[minus[one]] = jnp.where(odd, near, own)
        slot_rows[three] = jnp.where(odd, near_three, from_behind)
        slot_rows[minus[three]] = jnp.where(odd, from_ahead, near_three)
        slot_rows[five] = jnp.where(odd, from_behind, far)
        slot_rows[minus[five]] = jnp.where(odd, far, from_ahead)
        slot_rows[four] = jnp.where(odd_row, early_rows, late_rows)
        slot_rows[minus[four]] = jnp.where(odd_row, late_rows, early_rows)
        slot_rows[across] = opposite[:, columns]
        return slot_rows

    def by_slot(refs, columns=slice(None)):
        return jnp.concatenate(receive(refs, columns), axis=0)

    def by_row(refs, columns=slice(None)):
        slot_rows = receive(refs, columns)
        return jnp.concatenate([slot_rows[reverse[j]] for j in range(links)], axis=0)

    def pack(index_ref, count_ref, nodes_ref, cot_ref, select_ref, *out_refs):
        def column(row):
            count = row.shape[1]
            eye = lax.broadcasted_iota(jnp.int32, (count, count), 0) == lax.broadcasted_iota(
                jnp.int32, (count, count), 1
            )
            return jnp.sum(
                jnp.where(eye, jnp.broadcast_to(row, (count, count)), 0.0), axis=1, keepdims=True
            )

        counts = column(count_ref[...].reshape(1, -1).astype(F32))
        place = lax.broadcasted_iota(jnp.int32, (links, width), 1).astype(F32)
        index = jnp.where(place < counts, index_ref[...].astype(F32), -1.0)
        lane = lax.broadcasted_iota(jnp.int32, (width, grid_count), 1).astype(F32)
        picks = [
            jnp.where(lane == column(index[j : j + 1, :]), 1.0, 0.0).astype(BF16)
            for j in range(links)
        ]
        select = jnp.concatenate(picks, axis=0)
        select_ref[:slots, :] = select
        select_ref[slots:, :] = jnp.zeros((slots_pad - slots, grid_count), BF16)
        sent_nodes = mm(select, nodes_ref[...]).astype(BF16)
        sent_cot = mm(select, cot_ref[...]).astype(BF16)
        send(out_refs, lambda j: sent_nodes[j * width : (j + 1) * width, :], low)
        send(out_refs, lambda j: sent_cot[j * width : (j + 1) * width, :], high)

    select, *outgoing = call(
        pack,
        "pack_rows",
        [
            (send_index, 0, links),
            (send_count, 0, links),
            (grid_nodes, 0, grid_count),
            (grid_cot, 0, grid_count),
        ],
        [((slots_pad, grid_count), BF16)] + sent_shapes(2 * feat),
        flops=4 * slots * grid_count * feat,
    )
    def turn(select_ref, select_t_ref):
        select_t_ref[...] = select_ref[...].astype(F32).T.astype(BF16)

    (select_t,) = call(
        turn, "turn_select", [select], [((grid_count, slots_pad), BF16)], flops=ROUND_FLOPS
    )
    *outgoing, select_t = lax.optimization_barrier((*outgoing, select_t))
    arrived = exchange(outgoing)

    def local(
        select_ref,
        nodes_ref,
        mesh_ref,
        enc_edges_ref,
        dec_edges_ref,
        enc_first_ref,
        dec_first_ref,
        mesh_first_ref,
        enc_grid_ref,
        enc_mesh_ref,
        dec_grid_ref,
        dec_mesh_ref,
        enc_second_ref,
        mesh_second_ref,
        dec_second_ref,
        enc_part_ref,
        dec_part_ref,
        mesh_part_ref,
        enc_pick_ref,
        enc_pool_ref,
        dec_pick_ref,
        dec_pool_ref,
        enc_centred_ref,
        dec_centred_ref,
        mesh_wide_ref,
        mesh_base_ref,
        shared_pool_ref,
        table_ref,
    ):
        onehot_pair(enc_grid_ref, enc_mesh_ref, spots, mesh_count, enc_pick_ref, enc_pool_ref)
        onehot_pair(dec_grid_ref, dec_mesh_ref, spots, mesh_count, dec_pick_ref, dec_pool_ref)
        enc_centred_ref[...] = centred(enc_second_ref[...], 1).astype(BF16)
        mesh_centred = centred(mesh_second_ref[...], 1).astype(BF16)
        mesh_wide_ref[:, low] = mesh_centred
        mesh_wide_ref[:, high] = mm(mesh_centred, dec_first_ref[high, :]).astype(BF16)
        mesh_base_ref[...] = mm(mesh_ref[...], dec_first_ref[high, :])
        shared_pool_ref[...] = mm(
            select_ref[:slots, :], dec_pool_ref[:grid_count, :]
        ).astype(BF16)
        dec_centred_ref[...] = centred(dec_second_ref[...], 1).astype(BF16)
        nodes = nodes_ref[...]
        mesh_part_ref[...] = mm(mesh_ref[...], mesh_first_ref[low, :])
        table_ref[:grid_count, :] = mm(nodes, enc_first_ref[low, :]).astype(BF16)
        table_ref[grid_count:, :] = jnp.zeros((total - grid_count, feat), BF16)
        table_ref[mesh_rows, :] = mm(mesh_ref[...], enc_first_ref[high, :]).astype(BF16)
        enc_part_ref[...] = mm(enc_edges_ref[...], enc_first_ref[2 * feat :, :])
        enc_part_ref[...] += mm(enc_pick_ref[...], table_ref[...])
        pd = mm(nodes, dec_first_ref[low, :]).astype(BF16)
        dec_part_ref[...] = mm(dec_edges_ref[...], dec_first_ref[2 * feat :, :])
        dec_part_ref[...] += mm(dec_pick_ref[:, :grid_count], pd)

    (
        enc_part,
        dec_part,
        mesh_part,
        enc_pick,
        enc_pool,
        dec_pick,
        dec_pool,
        enc_centred,
        dec_centred,
        mesh_wide,
        mesh_base,
        shared_pool,
    ) = call(
        local,
        "local_products",
        [
            select,
            grid_nodes,
            mesh_nodes,
            enc_edges,
            dec_edges,
            enc_first,
            dec_first,
            mesh_first,
            enc_grid,
            enc_mesh,
            dec_grid,
            dec_mesh,
            enc_second,
            mesh_second,
            dec_second,
        ],
        [
            ((enc_count, feat), F32),
            ((dec_count, feat), F32),
            ((mesh_count, feat), F32),
            ((enc_count, total), BF16),
            ((total, enc_count), BF16),
            ((dec_count, total), BF16),
            ((total, dec_count), BF16),
        ]
        + [
            ((feat, feat), BF16),
            ((feat, feat), BF16),
            ((feat, 2 * feat), BF16),
            ((mesh_count, feat), F32),
            ((slots, dec_count), BF16),
        ],
        scratch=[((total, feat), BF16)],
        flops=2 * feat * (feat * (2 * grid_count + enc_count + dec_count) + total * dec_count),
    )

    def forward(*refs):
        arrived_refs, refs = refs[:arrived_count], refs[arrived_count:]
        (
            shared_pool_ref,
            enc_part_ref,
            dec_part_ref,
            mesh_part_ref,
            enc_pick_ref,
            enc_pool_ref,
            dec_pick_ref,
            dec_pool_ref,
            enc_wg_ref,
            dec_wg_ref,
            enc_w2_ref,
            mesh_wa_ref,
            mesh_w2_ref,
            mesh_base_ref,
            dec_w2_ref,
        ) = refs[:15]
        refs = refs[15:]
        out_refs, refs = refs[:sent_count], refs[sent_count:]
        (
            spot_ref,
            enc_normed_ref,
            enc_scale_ref,
            enc_pre_ref,
            dec_normed_ref,
            dec_scale_ref,
            dec_pre_ref,
            mesh_normed_ref,
            mesh_scale_ref,
            mesh_pre_ref,
            enc_act_ref,
            dec_act_ref,
            mesh_act_ref,
            table_ref,
        ) = refs
        rows = by_slot(arrived_refs, low)
        pe = mm(rows, enc_wg_ref[low, :]).astype(BF16)
        enc_pre_ref[...] = enc_part_ref[...] + mm(enc_pick_ref[:, grid_count:spots], pe)
        write_silu(enc_pre_ref, enc_act_ref)
        write_norm(mm(enc_act_ref[...], enc_w2_ref[...]), enc_normed_ref, enc_scale_ref)
        agg = mm(enc_pool_ref[mesh_rows, :], enc_normed_ref[...]).astype(BF16)
        mesh_pre_ref[...] = mesh_part_ref[...] + mm(agg, mesh_wa_ref[high, :])
        write_silu(mesh_pre_ref, mesh_act_ref)
        both = mm(mesh_act_ref[...], mesh_w2_ref[...])
        write_norm(both[:, low], mesh_normed_ref, mesh_scale_ref)
        mesh_sent = mesh_base_ref[...] + mesh_scale_ref[...] * both[:, high]
        table_ref[:slots, :] = mm(rows, dec_wg_ref[low, :]).astype(BF16)
        table_ref[slots : slots + mesh_count, :] = mesh_sent.astype(BF16)
        table_ref[slots + mesh_count :, :] = jnp.zeros(
            (total - spots - mesh_count, feat), BF16
        )
        dec_pre_ref[...] = dec_part_ref[...] + mm(dec_pick_ref[:, grid_count:], table_ref[...])
        write_silu(dec_pre_ref, dec_act_ref)
        write_norm(mm(dec_act_ref[...], dec_w2_ref[...]), dec_normed_ref, dec_scale_ref)
        spot_ref[...] = mm(dec_pool_ref[:spots, :], dec_normed_ref[...])
        shared = mm(shared_pool_ref[...], dec_normed_ref[...]).astype(BF16)
        slot_msg = spot_ref[grid_count:, :].astype(BF16)
        send(
            out_refs, lambda j: slot_msg[reverse[j] * width : (reverse[j] + 1) * width, :], low
        )
        send(out_refs, lambda j: shared[j * width : (j + 1) * width, :], high)

    saved_shapes = [
        ((enc_count, feat), BF16),
        ((enc_count, 1), F32),
        ((enc_count, feat), F32),
        ((dec_count, feat), BF16),
        ((dec_count, 1), F32),
        ((dec_count, feat), F32),
        ((mesh_count, feat), F32),
        ((mesh_count, 1), F32),
        ((mesh_count, feat), F32),
    ]
    results = call(
        forward,
        "edges_forward",
        [
            *arrived,
            shared_pool,
            enc_part,
            dec_part,
            mesh_part,
            enc_pick,
            enc_pool,
            dec_pick,
            dec_pool,
            enc_first,
            dec_first,
            enc_centred,
            mesh_first,
            mesh_wide,
            mesh_base,
            dec_centred,
        ],
        sent_shapes(2 * feat)
        + [((spots, feat), F32)]
        + saved_shapes,
        scratch=[
            ((enc_count, feat), BF16),
            ((dec_count, feat), BF16),
            ((mesh_count, feat), BF16),
            ((total - grid_count, feat), BF16),
        ],
        flops=2 * feat * feat * 2 * (enc_count + dec_count),
    )
    outgoing, results = results[:sent_count], results[sent_count:]
    spot_msg, *saved = results
    enc_normed, enc_scale, enc_pre, dec_normed, dec_scale, dec_pre = saved[:6]
    mesh_normed, mesh_scale, mesh_pre = saved[6:]
    returned = exchange(outgoing)

    def between(*refs):
        arrived_refs, refs = refs[:arrived_count], refs[arrived_count:]
        (
            nodes_ref,
            grid_first_ref,
            grid_second_ref,
            cot_ref,
            mesh_second_ref,
            dec_second_ref,
            mesh_ref,
            mesh_cot_ref,
            dec_normed_ref,
            dec_scale_ref,
            dec_pre_ref,
            mesh_normed_ref,
            mesh_pre_ref,
            mesh_wide_ref,
            part_ref,
            cot_rows_ref,
            cot_turned_ref,
            grid_wide_ref,
            grid_back_ref,
            mesh_out_ref,
            mesh_cot_turned_ref,
            mesh_slope_ref,
            mesh_turned_ref,
            dec_gain_ref,
            dec_turned_ref,
        ) = refs
        part_ref[:grid_count, :] = mm(nodes_ref[...], grid_first_ref[low, :])
        part_ref[grid_count:, :] = mm(by_slot(arrived_refs, low), grid_first_ref[low, :])
        mesh_out_ref[...] = (mesh_ref[...].astype(F32) + mesh_normed_ref[...]).astype(BF16)
        cot_rows_ref[:grid_count, :] = cot_ref[...]
        cot_rows_ref[grid_count:, :] = by_slot(arrived_refs, high)
        second = centred(grid_second_ref[...], 1).astype(BF16)
        grid_wide_ref[:, low] = second
        grid_wide_ref[:, high] = mm_t(second, grid_second_ref[...]).astype(BF16)
        cot_turned_ref[...] = mm_t(cot_rows_ref[...], second)
        grid_back_ref[low, :] = centred(grid_first_ref[high, :], 0).astype(BF16)
        grid_back_ref[high, :] = mm(dec_second_ref[...], grid_back_ref[low, :]).astype(BF16)
        mesh_cot_turned_ref[...] = mm_t(mesh_cot_ref[...], mesh_wide_ref[:, low])
        mesh_turned_ref[...] = mm_t(mesh_normed_ref[...].astype(BF16), mesh_second_ref[...])
        mesh_slope_ref[...] = silu_and_slope(mesh_pre_ref[...])[1]
        write_slopes(
            dec_pre_ref,
            dec_normed_ref,
            dec_scale_ref,
            dec_second_ref,
            dec_gain_ref,
            dec_turned_ref,
        )

    (
        grid_part,
        cot_rows,
        cot_turned,
        grid_wide,
        grid_back,
        mesh_out,
        mesh_cot_turned,
        mesh_slope,
        mesh_turned,
        dec_gain,
        dec_turned,
    ) = call(
        between,
        "slopes_and_nodes",
        [
            *arrived,
            grid_nodes,
            grid_first,
            grid_second,
            grid_cot,
            mesh_second,
            dec_second,
            mesh_nodes,
            mesh_cot,
            dec_normed,
            dec_scale,
            dec_pre,
            mesh_normed,
            mesh_pre,
            mesh_wide,
        ],
        [
            ((spots, feat), F32),
            ((spots, feat), BF16),
            ((spots, feat), F32),
            ((feat, 2 * feat), BF16),
            ((2 * feat, feat), BF16),
            ((mesh_count, feat), BF16),
            ((mesh_count, feat), F32),
            ((mesh_count, feat), F32),
            ((mesh_count, feat), F32),
            ((dec_count, feat), BF16),
            ((dec_count, feat), BF16),
        ],
        flops=16 * spots * feat * feat,
    )

    def backward(*refs):
        returned_refs, refs = refs[:arrived_count], refs[arrived_count:]
        (
            spot_ref,
            grid_part_ref,
            select_t_ref,
            cot_rows_ref,
            cot_turned_ref,
            mesh_cot_ref,
            mesh_cot_turned_ref,
            enc_pick_ref,
            enc_pool_ref,
            dec_pick_ref,
            dec_pool_ref,
            grid_first_ref,
            grid_wide_ref,
            grid_back_ref,
            mesh_first_ref,
            mesh_wide_ref,
            enc_first_ref,
            enc_second_ref,
            dec_first_ref,
            enc_normed_ref,
            enc_scale_ref,
            enc_pre_ref,
            dec_normed_ref,
            dec_gain_ref,
            dec_turned_ref,
            mesh_normed_ref,
            mesh_scale_ref,
            mesh_slope_ref,
            mesh_turned_ref,
        ) = refs[:29]
        refs = refs[29:]
        out_refs, refs = refs[:sent_count], refs[sent_count:]
        (
            grid_normed_ref,
            grid_gpre_ref,
            dec_gpre_ref,
            enc_gpre_ref,
            mesh_gin_ref,
            mesh_gpre_ref,
            agg_ref,
            grid_act_ref,
            grid_slope_ref,
            spot_grad_ref,
            mesh_in_ref,
            mesh_back_ref,
            enc_gain_ref,
            enc_turned_ref,
        ) = refs
        agg_ref[:grid_count, :] = (
            spot_ref[:grid_count, :] + mm(select_t_ref[:, :slots], by_row(returned_refs, low))
        ).astype(BF16)
        agg_ref[grid_count:, :] = (
            spot_ref[grid_count:, :] + by_slot(returned_refs, high).astype(F32)
        ).astype(BF16)
        pre = grid_part_ref[...] + mm(agg_ref[...], grid_first_ref[high, :])
        mesh_in_ref[low, :] = dec_first_ref[high, :]
        mesh_in_ref[high, :] = mm(mesh_wide_ref[:, low], dec_first_ref[high, :]).astype(BF16)
        for rows in row_chunks(spots):
            act, slope = silu_and_slope(pre[rows, :])
            grid_act_ref[rows, :] = act.astype(BF16)
            grid_slope_ref[rows, :] = slope
        both = mm(grid_act_ref[...], grid_wide_ref[...])
        mesh_back_ref[low, :] = centred(mesh_first_ref[high, :], 0).astype(BF16)
        mesh_back_ref[high, :] = mm(enc_second_ref[...], mesh_back_ref[low, :]).astype(BF16)
        for rows in row_chunks(spots):
            part = both[rows, low]
            scale_inv = scale_rows(part)
            normed = part * scale_inv
            grid_normed_ref[rows, :] = normed
            mean = jnp.mean(cot_rows_ref[rows, :].astype(F32) * normed, axis=-1, keepdims=True)
            raw = scale_inv * (cot_turned_ref[rows, :] - (mean * scale_inv) * both[rows, high])
            grid_gpre_ref[rows, :] = (raw * grid_slope_ref[rows, :]).astype(BF16)
        spot_grad_ref[:spots, :] = mm_t(grid_gpre_ref[...], grid_back_ref[...]).astype(BF16)
        spot_grad_ref[spots:, :] = jnp.zeros((total - spots, 2 * feat), BF16)
        write_slopes(
            enc_pre_ref,
            enc_normed_ref,
            enc_scale_ref,
            enc_second_ref,
            enc_gain_ref,
            enc_turned_ref,
        )
        edge_back(
            mm(dec_pick_ref[...], spot_grad_ref[...]),
            dec_normed_ref,
            dec_gain_ref,
            dec_turned_ref,
            dec_gpre_ref,
        )
        mesh_sum = mm(dec_pool_ref[mesh_rows, :], dec_gpre_ref[...]).astype(BF16)
        both = mm_t(mesh_sum, mesh_in_ref[...])
        mesh_gin = mesh_cot_ref[...].astype(F32) + both[:, low]
        mesh_gin_ref[...] = mesh_gin
        mean = jnp.mean(mesh_gin * mesh_normed_ref[...], axis=-1, keepdims=True)
        raw = mesh_cot_turned_ref[...] + both[:, high] - mean * mesh_turned_ref[...]
        mesh_gpre_ref[...] = (mesh_scale_ref[...] * raw * mesh_slope_ref[...]).astype(BF16)
        mesh_gagg = mm_t(mesh_gpre_ref[...], mesh_back_ref[...]).astype(BF16)
        pooled = mm(dec_pool_ref[grid_count:spots, :], dec_gpre_ref[...]).astype(BF16)
        slot_back = mm_t(pooled, dec_first_ref[low, :])
        edge_back(
            mm(enc_pick_ref[:, mesh_rows], mesh_gagg),
            enc_normed_ref,
            enc_gain_ref,
            enc_turned_ref,
            enc_gpre_ref,
        )
        pooled = mm(enc_pool_ref[grid_count:spots, :], enc_gpre_ref[...]).astype(BF16)
        slot_back = (slot_back + mm_t(pooled, enc_first_ref[low, :])).astype(BF16)
        send(out_refs, lambda j: slot_back[reverse[j] * width : (reverse[j] + 1) * width, :])

    results = call(
        backward,
        "edges_backward",
        [
            *returned,
            spot_msg,
            grid_part,
            select_t,
            cot_rows,
            cot_turned,
            mesh_cot,
            mesh_cot_turned,
            enc_pick,
            enc_pool,
            dec_pick,
            dec_pool,
            grid_first,
            grid_wide,
            grid_back,
            mesh_first,
            mesh_wide,
            enc_first,
            enc_second,
            dec_first,
            enc_normed,
            enc_scale,
            enc_pre,
            dec_normed,
            dec_gain,
            dec_turned,
            mesh_normed,
            mesh_scale,
            mesh_slope,
            mesh_turned,
        ],
        sent_shapes(feat)
        + [
            ((spots, feat), F32),
            ((spots, feat), BF16),
            ((dec_count, feat), BF16),
            ((enc_count, feat), BF16),
            ((mesh_count, feat), F32),
            ((mesh_count, feat), BF16),
        ],
        scratch=[
            ((spots, feat), BF16),
            ((spots, feat), BF16),
            ((spots, feat), F32),
            ((total, 2 * feat), BF16),
            ((2 * feat, feat), BF16),
            ((2 * feat, feat), BF16),
            ((enc_count, feat), BF16),
            ((enc_count, feat), BF16),
        ],
        flops=2 * feat * feat * (4 * spots + 3 * dec_count + 2 * enc_count),
    )
    outgoing, results = results[:sent_count], results[sent_count:]
    grid_normed, grid_gpre, dec_gpre, enc_gpre, mesh_gin, mesh_gpre = results
    final = exchange(outgoing)

    def tail(
        nodes_ref,
        grid_normed_ref,
        cot_ref,
        grid_gpre_ref,
        enc_pool_ref,
        enc_gpre_ref,
        dec_pool_ref,
        dec_gpre_ref,
        mesh_gin_ref,
        mesh_gpre_ref,
        grid_wn_ref,
        enc_wg_ref,
        dec_wg_ref,
        mesh_wn_ref,
        enc_wm_ref,
        base_ref,
        grad_mesh_ref,
        grid_out_ref,
    ):
        grid_out_ref[...] = (
            nodes_ref[...].astype(F32) + grid_normed_ref[:grid_count, :]
        ).astype(BF16)
        enc_sums = mm(enc_pool_ref[...], enc_gpre_ref[...]).astype(BF16)
        dec_sums = mm(dec_pool_ref[:grid_count, :], dec_gpre_ref[...]).astype(BF16)
        base_ref[...] = (
            cot_ref[...].astype(F32)
            + mm_t(grid_gpre_ref[:grid_count, :], grid_wn_ref[low, :])
            + mm_t(enc_sums[:grid_count, :], enc_wg_ref[low, :])
            + mm_t(dec_sums, dec_wg_ref[low, :])
        )
        grad_mesh_ref[...] = (
            mesh_gin_ref[...]
            + mm_t(mesh_gpre_ref[...], mesh_wn_ref[low, :])
            + mm_t(enc_sums[mesh_rows, :], enc_wm_ref[high, :])
        )

    base, grad_mesh, grid_out = call(
        tail,
        "local_gradients",
        [
            grid_nodes,
            grid_normed,
            grid_cot,
            grid_gpre,
            enc_pool,
            enc_gpre,
            dec_pool,
            dec_gpre,
            mesh_gin,
            mesh_gpre,
            grid_first,
            enc_first,
            dec_first,
            mesh_first,
            enc_first,
        ],
        [((grid_count, feat), F32), ((mesh_count, feat), F32), ((grid_count, feat), BF16)],
        flops=2 * feat * feat * 3 * grid_count,
    )

    def finish(*refs):
        back_refs = refs[:arrived_count]
        base_ref, select_t_ref, out_ref = refs[arrived_count:]
        out_ref[...] = base_ref[...] + mm(select_t_ref[:, :slots], by_row(back_refs))

    (grad_grid,) = call(
        finish,
        "add_returned",
        [*final, base, select_t],
        [((grid_count, feat), F32)],
        flops=2 * grid_count * slots * feat,
    )
    return (grid_out, mesh_out, grad_grid, grad_mesh)


def solution(mesh):
    rows = P(("groups", "tile"), None)
    flat = P(("groups", "tile"))
    in_specs = (rows,) * 6 + (P(),) * 8 + (rows,) + (flat,) * 5
    return jax.shard_map(
        per_device, mesh=mesh, in_specs=in_specs, out_specs=(rows,) * 4, check_vma=False
    )
```

```python
import jax
import jax.numpy as jnp
from jax import lax
from jax.experimental import pallas as pl
from jax.experimental.pallas import tpu as pltpu
from jax.sharding import PartitionSpec as P

TW = 4
CHUNK = 32
ROUND_FLOPS = 2 * 10**10
F32 = jnp.float32
BF16 = jnp.bfloat16
VMEM_LIMIT = 30 * 1024 * 1024


def mm(left, right):
    return jnp.dot(left, right, preferred_element_type=F32)


def mm_t(left, right):
    return lax.dot_general(left, right, (((1,), (1,)), ((), ())), preferred_element_type=F32)


def centred(values, axis):
    values = values.astype(F32)
    return values - jnp.mean(values, axis=axis, keepdims=True)


def silu_and_slope(pre):
    half = 0.5 * pre
    lifted = 1.0 + jnp.tanh(half)
    return half * lifted, lifted * (0.5 + 0.5 * half * (2.0 - lifted))


def silu(pre):
    half = 0.5 * pre
    return half * (1.0 + jnp.tanh(half))


def scale_rows(raw):
    return lax.rsqrt(jnp.mean(raw * raw, axis=-1, keepdims=True) + 1e-05)


def row_chunks(rows, size=CHUNK):
    return [slice(start, min(start + size, rows)) for start in range(0, rows, size)]


def row_halves(rows):
    size = -(-rows // 32) * 16
    return row_chunks(rows, size)


def in_step(chains):
    chains = list(chains)
    while chains:
        left = []
        for chain in chains:
            try:
                next(chain)
                left.append(chain)
            except StopIteration:
                pass
        chains = left


def parts_of(block):
    return [
        (part, slice(block.start + part.start, block.start + part.stop))
        for part in row_chunks(block.stop - block.start)
    ]


def write_silu(pre, act_ref, block):
    for part, rows in parts_of(block):
        act_ref[rows, :] = silu(pre[part, :]).astype(BF16)


def write_norm(raw, normed_ref, scale_ref, block):
    for part, rows in parts_of(block):
        values = raw[part, :]
        scale_inv = scale_rows(values)
        normed_ref[rows, :] = (values * scale_inv).astype(normed_ref.dtype)
        scale_ref[rows, :] = scale_inv


def forward_chain(make_pre, pre_ref, act_ref, second_ref, normed_ref, scale_ref, block):
    pre = make_pre(block)
    pre_ref[block, :] = pre
    yield
    write_silu(pre, act_ref, block)
    yield
    raw = mm(act_ref[block, :], second_ref[...])
    yield
    write_norm(raw, normed_ref, scale_ref, block)


def write_slopes(pre_ref, normed_ref, scale_ref, second_ref, gain_ref, turned_ref):
    raw = mm_t(normed_ref[...], second_ref[...])
    for rows in row_chunks(pre_ref.shape[0]):
        gain = silu_and_slope(pre_ref[rows, :])[1] * scale_ref[rows, :]
        gain_ref[rows, :] = gain.astype(BF16)
        turned_ref[rows, :] = (gain * raw[rows, :]).astype(BF16)


def edge_back(make_both, normed_ref, gain_ref, turned_ref, out_ref, block):
    features = normed_ref.shape[1]
    both = make_both(block)
    yield
    for part, rows in parts_of(block):
        mean = jnp.mean(
            both[part, :features] * normed_ref[rows, :].astype(F32), axis=-1, keepdims=True
        )
        out_ref[rows, :] = (
            gain_ref[rows, :] * both[part, features:].astype(BF16)
            - turned_ref[rows, :] * mean.astype(BF16)
        )


def neighbour_offsets(peer_count):
    forward_half = [1, TW, TW + 1, TW - 1]
    return forward_half + [-offset for offset in forward_half] + [peer_count // 2]


def onehot_pair(spot_ref, mesh_ref, spots, mesh_count, by_edge_ref, by_spot_ref):
    edges, total = by_edge_ref.shape
    spot_row = spot_ref[...].reshape(1, -1)
    mesh_row = mesh_ref[...].reshape(1, -1) + spots
    one, zero = jnp.ones((), BF16), jnp.zeros((), BF16)

    def ones(ids, index):
        shape = jnp.broadcast_shapes(ids.shape, index.shape)
        hit = jnp.broadcast_to(ids, shape) == jnp.broadcast_to(index, shape)
        return jnp.where(hit, jnp.broadcast_to(one, shape), jnp.broadcast_to(zero, shape))

    for row, first, count in ((spot_row, 0, spots), (mesh_row, spots, mesh_count)):
        ids = lax.broadcasted_iota(jnp.int32, (16, edges), 0).astype(jnp.int16)
        wide = jnp.broadcast_to(row, (16, edges)).astype(jnp.int16)
        for rows in row_chunks(count, 16):
            rows = slice(rows.start + first, rows.stop + first)
            by_spot_ref[rows, :] = ones(ids, wide - jnp.int16(rows.start))
    by_spot_ref[spots + mesh_count :, :] = jnp.zeros((total - spots - mesh_count, edges), BF16)
    lane = lax.broadcasted_iota(jnp.int32, (16, 128), 1).astype(jnp.int16)
    for rows in row_chunks(edges, 128):
        spot_col = jnp.broadcast_to(spot_row[:, rows], (128, 128)).T.astype(jnp.int16)
        mesh_col = jnp.broadcast_to(mesh_row[:, rows], (128, 128)).T.astype(jnp.int16)
        for columns in row_chunks(total, 128):
            for part in row_chunks(128, 16):
                place = slice(rows.start + part.start, rows.start + part.stop)
                ids = lane + jnp.int16(columns.start)
                hits = []
                if columns.start < spots:
                    hits.append(ones(ids, spot_col[part, :]))
                if columns.stop > spots:
                    hits.append(ones(ids, mesh_col[part, :]))
                by_edge_ref[place, columns] = sum(hits[1:], hits[0])


class Fetched:
    def __init__(self, source, target, semaphore):
        self.copy = pltpu.make_async_copy(source, target, semaphore)
        self.target = target
        self.landed = False
        self.copy.start()

    def land(self):
        if not self.landed:
            self.copy.wait()
            self.landed = True

    def __getitem__(self, key):
        self.land()
        return self.target[key]


def call(body, name, inputs, outputs, scratch=(), flops=0):
    arrays, specs, moved, fetches = [], [], 0, []
    for place, entry in enumerate(inputs):
        if isinstance(entry, tuple):
            array, first, rows = entry
            array = pltpu.with_memory_space_constraint(array, pltpu.HBM)
            specs.append(pl.BlockSpec(memory_space=pltpu.HBM))
            shape = (rows,) + array.shape[1:]
            fetches.append((place, first, rows, shape, array.dtype))
            moved += rows * (array.size // array.shape[0]) * array.dtype.itemsize
        else:
            array = entry
            specs.append(pl.BlockSpec(memory_space=pltpu.VMEM))
            moved += array.size * array.dtype.itemsize
        arrays.append(array)
    shapes = [jax.ShapeDtypeStruct(shape, dtype) for shape, dtype in outputs]
    for shape in shapes:
        moved += shape.size * shape.dtype.itemsize
    buffers = [pltpu.VMEM(shape, dtype) for _, _, _, shape, dtype in fetches]
    if fetches:
        buffers.append(pltpu.SemaphoreType.DMA((len(fetches),)))

    def kernel(*refs):
        refs = list(refs)
        waiting = []
        if fetches:
            targets, semaphores = refs[-len(buffers) : -1], refs[-1]
            refs = refs[: -len(buffers)]
        for slot, (place, first, rows, shape, _) in enumerate(fetches):
            source = refs[place]
            if source.shape != shape:
                source = source.at[pl.ds(first, rows)]
            refs[place] = Fetched(source, targets[slot], semaphores.at[slot])
            waiting.append(refs[place])
        body(*refs)
        for fetched in waiting:
            fetched.land()

    return pl.pallas_call(
        kernel,
        name=name,
        in_specs=specs,
        out_specs=[pl.BlockSpec(memory_space=pltpu.VMEM) for _ in shapes],
        out_shape=shapes,
        scratch_shapes=[pltpu.VMEM(shape, dtype) for shape, dtype in scratch]
        + buffers,
        compiler_params=pltpu.CompilerParams(vmem_limit_bytes=VMEM_LIMIT),
        cost_estimate=pl.CostEstimate(flops=flops, bytes_accessed=moved, transcendentals=0),
    )(*arrays)


def per_device(
    grid_nodes,
    mesh_nodes,
    enc_edges,
    dec_edges,
    grid_cot,
    mesh_cot,
    enc_first,
    enc_second,
    mesh_first,
    mesh_second,
    dec_first,
    dec_second,
    grid_first,
    grid_second,
    send_index,
    send_count,
    enc_grid,
    enc_mesh,
    dec_grid,
    dec_mesh,
):
    grid_count, feat = grid_nodes.shape
    mesh_count = mesh_nodes.shape[0]
    enc_count = enc_edges.shape[0]
    dec_count = dec_edges.shape[0]
    links, width = send_index.shape
    slots = links * width
    slots_pad = -(-slots // 128) * 128
    spots = grid_count + slots
    total = -(-(spots + mesh_count) // 128) * 128
    peer_count = lax.axis_size("tile")
    offsets = neighbour_offsets(peer_count)
    half = (links - 1) // 2
    reverse = [(j + half) % (links - 1) for j in range(links - 1)] + [links - 1]
    low, high = slice(0, feat), slice(feat, 2 * feat)
    mesh_rows = slice(spots, spots + mesh_count)

    one, four, five, three = range(half)
    minus = [j + half for j in range(half)]
    across = links - 1
    peers = range(peer_count)

    def permute(part, steps, odd_row_steps=None):
        rows = (steps, odd_row_steps or steps)
        pairs = [(s, (s + rows[s // TW % 2][s % 2]) % peer_count) for s in peers]
        return lax.ppermute(part, "tile", pairs)

    def exchange(parts):
        late_pair, early_pair, behind_one, ahead_three, five_off, opposite, own_chip = parts
        late_pair = permute(late_pair, (-4, -4), (4, 4))
        early_pair = permute(early_pair, (4, 4), (-4, -4))
        behind_one = permute(behind_one, (-1, 1))
        ahead_three = permute(ahead_three, (3, -3))
        five_off = permute(five_off, (-5, 5))
        opposite = permute(opposite, (peer_count // 2, peer_count // 2))
        late_pair, own_chip = lax.optimization_barrier((late_pair, own_chip))
        late_passed = permute(late_pair, (1, -1))
        own_chip = permute(own_chip, (1, -1))
        early_passed = permute(early_pair, (1, -1))
        return [
            late_pair,
            early_pair,
            behind_one,
            ahead_three,
            five_off,
            opposite,
            own_chip,
            late_passed,
            early_passed,
        ]

    arrived_count = 9

    def sent_shapes(columns):
        rows = (2, 2, 1, 1, 1, 1, 1)
        return [((count * width, columns), BF16) for count in rows]

    sent_count = len(sent_shapes(feat))

    def place_bits():
        own = lax.axis_index("tile")
        return lax.rem(own, 2) == 1, lax.rem(lax.div(own, TW), 2) == 1

    def send(refs, message, columns=slice(None)):
        odd, odd_row = place_bits()

        def by_parity(even, odd_one):
            return jnp.where(odd, message(odd_one), message(even))

        late_pair, early_pair, behind_one, ahead_three, five_off, opposite, own_chip = refs
        first, second = slice(0, width), slice(width, 2 * width)
        ahead = message(four), by_parity(five, three)
        behind = message(minus[four]), by_parity(minus[three], minus[five])
        for rows, go_ahead, go_behind in zip((first, second), ahead, behind):
            late_pair[rows, columns] = jnp.where(odd_row, go_ahead, go_behind)
            early_pair[rows, columns] = jnp.where(odd_row, go_behind, go_ahead)
        behind_one[:, columns] = by_parity(minus[one], one)
        ahead_three[:, columns] = by_parity(three, minus[three])
        five_off[:, columns] = by_parity(minus[five], five)
        opposite[:, columns] = message(across)
        own_chip[:, columns] = by_parity(one, minus[one])

    def receive(refs, columns=slice(None)):
        odd, odd_row = place_bits()
        late_pair, early_pair, behind_one, ahead_three, five_off, opposite, own_chip = refs[:7]
        late_passed, early_passed = refs[7:]
        first, second = slice(0, width), slice(width, 2 * width)
        near, near_three = behind_one[:, columns], ahead_three[:, columns]
        far, own = five_off[:, columns], own_chip[:, columns]
        late_rows, early_rows = late_passed[second, columns], early_passed[second, columns]
        from_behind = jnp.where(odd_row, early_rows, late_rows)
        from_ahead = jnp.where(odd_row, late_rows, early_rows)
        late_rows, early_rows = late_pair[first, columns], early_pair[first, columns]
        slot_rows = [None] * links
        slot_rows[one] = jnp.where(odd, own, near)
        slot_rows[minus[one]] = jnp.where(odd, near, own)
        slot_rows[three] = jnp.where(odd, near_three, from_behind)
        slot_rows[minus[three]] = jnp.where(odd, from_ahead, near_three)
        slot_rows[five] = jnp.where(odd, from_behind, far)
        slot_rows[minus[five]] = jnp.where(odd, far, from_ahead)
        slot_rows[four] = jnp.where(odd_row, early_rows, late_rows)
        slot_rows[minus[four]] = jnp.where(odd_row, late_rows, early_rows)
        slot_rows[across] = opposite[:, columns]
        return slot_rows

    def by_slot(refs, columns=slice(None)):
        return jnp.concatenate(receive(refs, columns), axis=0)

    def by_row(refs, columns=slice(None)):
        slot_rows = receive(refs, columns)
        return jnp.concatenate([slot_rows[reverse[j]] for j in range(links)], axis=0)

    def pack(index_ref, count_ref, nodes_ref, cot_ref, select_ref, *out_refs):
        def column(row):
            count = row.shape[1]
            eye = lax.broadcasted_iota(jnp.int32, (count, count), 0) == lax.broadcasted_iota(
                jnp.int32, (count, count), 1
            )
            return jnp.sum(
                jnp.where(eye, jnp.broadcast_to(row, (count, count)), 0.0), axis=1, keepdims=True
            )

        counts = column(count_ref[...].reshape(1, -1).astype(F32))
        place = lax.broadcasted_iota(jnp.int32, (links, width), 1).astype(F32)
        index = jnp.where(place < counts, index_ref[...].astype(F32), -1.0)
        lane = lax.broadcasted_iota(jnp.int32, (width, grid_count), 1).astype(F32)
        picks = [
            jnp.where(lane == column(index[j : j + 1, :]), 1.0, 0.0).astype(BF16)
            for j in range(links)
        ]
        select = jnp.concatenate(picks, axis=0)
        select_ref[:slots, :] = select
        select_ref[slots:, :] = jnp.zeros((slots_pad - slots, grid_count), BF16)
        sent_nodes = mm(select, nodes_ref[...]).astype(BF16)
        sent_cot = mm(select, cot_ref[...]).astype(BF16)
        send(out_refs, lambda j: sent_nodes[j * width : (j + 1) * width, :], low)
        send(out_refs, lambda j: sent_cot[j * width : (j + 1) * width, :], high)

    select, *outgoing = call(
        pack,
        "pack_rows",
        [
            (send_index, 0, links),
            (send_count, 0, links),
            (grid_nodes, 0, grid_count),
            (grid_cot, 0, grid_count),
        ],
        [((slots_pad, grid_count), BF16)] + sent_shapes(2 * feat),
        flops=4 * slots * grid_count * feat,
    )
    def turn(select_ref, select_t_ref):
        select_t_ref[...] = select_ref[...].astype(F32).T.astype(BF16)

    (select_t,) = call(
        turn, "turn_select", [select], [((grid_count, slots_pad), BF16)], flops=ROUND_FLOPS
    )
    *outgoing, select_t = lax.optimization_barrier((*outgoing, select_t))
    arrived = exchange(outgoing)

    def local(
        select_ref,
        nodes_ref,
        mesh_ref,
        enc_edges_ref,
        dec_edges_ref,
        enc_first_ref,
        dec_first_ref,
        mesh_first_ref,
        enc_grid_ref,
        enc_mesh_ref,
        dec_grid_ref,
        dec_mesh_ref,
        enc_second_ref,
        mesh_second_ref,
        dec_second_ref,
        enc_part_ref,
        dec_part_ref,
        mesh_part_ref,
        enc_pick_ref,
        enc_pool_ref,
        dec_pick_ref,
        dec_pool_ref,
        enc_centred_ref,
        dec_centred_ref,
        mesh_wide_ref,
        mesh_base_ref,
        shared_pool_ref,
        table_ref,
    ):
        onehot_pair(enc_grid_ref, enc_mesh_ref, spots, mesh_count, enc_pick_ref, enc_pool_ref)
        onehot_pair(dec_grid_ref, dec_mesh_ref, spots, mesh_count, dec_pick_ref, dec_pool_ref)
        enc_centred_ref[...] = centred(enc_second_ref[...], 1).astype(BF16)
        mesh_centred = centred(mesh_second_ref[...], 1).astype(BF16)
        mesh_wide_ref[:, low] = mesh_centred
        mesh_wide_ref[:, high] = mm(mesh_centred, dec_first_ref[high, :]).astype(BF16)
        mesh_base_ref[...] = mm(mesh_ref[...], dec_first_ref[high, :])
        shared_pool_ref[...] = mm(
            select_ref[:slots, :], dec_pool_ref[:grid_count, :]
        ).astype(BF16)
        dec_centred_ref[...] = centred(dec_second_ref[...], 1).astype(BF16)
        nodes = nodes_ref[...]
        mesh_part_ref[...] = mm(mesh_ref[...], mesh_first_ref[low, :])
        table_ref[:grid_count, :] = mm(nodes, enc_first_ref[low, :]).astype(BF16)
        table_ref[grid_count:, :] = jnp.zeros((total - grid_count, feat), BF16)
        table_ref[mesh_rows, :] = mm(mesh_ref[...], enc_first_ref[high, :]).astype(BF16)
        enc_part_ref[...] = mm(enc_edges_ref[...], enc_first_ref[2 * feat :, :])
        enc_part_ref[...] += mm(enc_pick_ref[...], table_ref[...])
        pd = mm(nodes, dec_first_ref[low, :]).astype(BF16)
        dec_part_ref[...] = mm(dec_edges_ref[...], dec_first_ref[2 * feat :, :])
        dec_part_ref[...] += mm(dec_pick_ref[:, :grid_count], pd)

    (
        enc_part,
        dec_part,
        mesh_part,
        enc_pick,
        enc_pool,
        dec_pick,
        dec_pool,
        enc_centred,
        dec_centred,
        mesh_wide,
        mesh_base,
        shared_pool,
    ) = call(
        local,
        "local_products",
        [
            select,
            grid_nodes,
            mesh_nodes,
            enc_edges,
            dec_edges,
            enc_first,
            dec_first,
            mesh_first,
            enc_grid,
            enc_mesh,
            dec_grid,
            dec_mesh,
            enc_second,
            mesh_second,
            dec_second,
        ],
        [
            ((enc_count, feat), F32),
            ((dec_count, feat), F32),
            ((mesh_count, feat), F32),
            ((enc_count, total), BF16),
            ((total, enc_count), BF16),
            ((dec_count, total), BF16),
            ((total, dec_count), BF16),
        ]
        + [
            ((feat, feat), BF16),
            ((feat, feat), BF16),
            ((feat, 2 * feat), BF16),
            ((mesh_count, feat), F32),
            ((slots, dec_count), BF16),
        ],
        scratch=[((total, feat), BF16)],
        flops=2 * feat * (feat * (2 * grid_count + enc_count + dec_count) + total * dec_count),
    )

    def forward(*refs):
        arrived_refs, refs = refs[:arrived_count], refs[arrived_count:]
        (
            shared_pool_ref,
            enc_part_ref,
            dec_part_ref,
            mesh_part_ref,
            enc_pick_ref,
            enc_pool_ref,
            dec_pick_ref,
            dec_pool_ref,
            enc_wg_ref,
            dec_wg_ref,
            enc_w2_ref,
            mesh_wa_ref,
            mesh_w2_ref,
            mesh_base_ref,
            dec_w2_ref,
        ) = refs[:15]
        refs = refs[15:]
        out_refs, refs = refs[:sent_count], refs[sent_count:]
        (
            spot_ref,
            enc_normed_ref,
            enc_scale_ref,
            enc_pre_ref,
            dec_normed_ref,
            dec_scale_ref,
            dec_pre_ref,
            mesh_normed_ref,
            mesh_scale_ref,
            mesh_pre_ref,
            enc_act_ref,
            dec_act_ref,
            mesh_act_ref,
            table_ref,
        ) = refs
        rows = by_slot(arrived_refs, low)
        pe = mm(rows, enc_wg_ref[low, :]).astype(BF16)

        def enc_pre(block):
            return enc_part_ref[block, :] + mm(enc_pick_ref[block, grid_count:spots], pe)

        in_step(
            forward_chain(
                enc_pre,
                enc_pre_ref,
                enc_act_ref,
                enc_w2_ref,
                enc_normed_ref,
                enc_scale_ref,
                block,
            )
            for block in row_halves(enc_count)
        )
        agg = mm(enc_pool_ref[mesh_rows, :], enc_normed_ref[...]).astype(BF16)
        mesh_pre_ref[...] = mesh_part_ref[...] + mm(agg, mesh_wa_ref[high, :])
        whole = slice(0, mesh_count)
        write_silu(mesh_pre_ref[...], mesh_act_ref, whole)
        both = mm(mesh_act_ref[...], mesh_w2_ref[...])
        write_norm(both[:, low], mesh_normed_ref, mesh_scale_ref, whole)
        mesh_sent = mesh_base_ref[...] + mesh_scale_ref[...] * both[:, high]
        table_ref[:slots, :] = mm(rows, dec_wg_ref[low, :]).astype(BF16)
        table_ref[slots : slots + mesh_count, :] = mesh_sent.astype(BF16)
        table_ref[slots + mesh_count :, :] = jnp.zeros(
            (total - spots - mesh_count, feat), BF16
        )

        def dec_pre(block):
            return dec_part_ref[block, :] + mm(dec_pick_ref[block, grid_count:], table_ref[...])

        in_step(
            forward_chain(
                dec_pre,
                dec_pre_ref,
                dec_act_ref,
                dec_w2_ref,
                dec_normed_ref,
                dec_scale_ref,
                block,
            )
            for block in row_halves(dec_count)
        )
        spot_ref[...] = mm(dec_pool_ref[:spots, :], dec_normed_ref[...])
        shared = mm(shared_pool_ref[...], dec_normed_ref[...]).astype(BF16)
        slot_msg = spot_ref[grid_count:, :].astype(BF16)
        send(
            out_refs, lambda j: slot_msg[reverse[j] * width : (reverse[j] + 1) * width, :], low
        )
        send(out_refs, lambda j: shared[j * width : (j + 1) * width, :], high)

    saved_shapes = [
        ((enc_count, feat), BF16),
        ((enc_count, 1), F32),
        ((enc_count, feat), F32),
        ((dec_count, feat), BF16),
        ((dec_count, 1), F32),
        ((dec_count, feat), F32),
        ((mesh_count, feat), F32),
        ((mesh_count, 1), F32),
        ((mesh_count, feat), F32),
    ]
    results = call(
        forward,
        "edges_forward",
        [
            *arrived,
            shared_pool,
            enc_part,
            dec_part,
            mesh_part,
            enc_pick,
            enc_pool,
            dec_pick,
            dec_pool,
            enc_first,
            dec_first,
            enc_centred,
            mesh_first,
            mesh_wide,
            mesh_base,
            dec_centred,
        ],
        sent_shapes(2 * feat)
        + [((spots, feat), F32)]
        + saved_shapes,
        scratch=[
            ((enc_count, feat), BF16),
            ((dec_count, feat), BF16),
            ((mesh_count, feat), BF16),
            ((total - grid_count, feat), BF16),
        ],
        flops=2 * feat * feat * 2 * (enc_count + dec_count),
    )
    outgoing, results = results[:sent_count], results[sent_count:]
    spot_msg, *saved = results
    enc_normed, enc_scale, enc_pre, dec_normed, dec_scale, dec_pre = saved[:6]
    mesh_normed, mesh_scale, mesh_pre = saved[6:]
    returned = exchange(outgoing)

    def between(*refs):
        arrived_refs, refs = refs[:arrived_count], refs[arrived_count:]
        (
            nodes_ref,
            grid_first_ref,
            grid_second_ref,
            cot_ref,
            mesh_second_ref,
            dec_second_ref,
            mesh_ref,
            mesh_cot_ref,
            dec_normed_ref,
            dec_scale_ref,
            dec_pre_ref,
            mesh_normed_ref,
            mesh_pre_ref,
            mesh_wide_ref,
            part_ref,
            cot_rows_ref,
            cot_turned_ref,
            grid_wide_ref,
            grid_back_ref,
            mesh_out_ref,
            mesh_cot_turned_ref,
            mesh_slope_ref,
            mesh_turned_ref,
            dec_gain_ref,
            dec_turned_ref,
        ) = refs
        part_ref[:grid_count, :] = mm(nodes_ref[...], grid_first_ref[low, :])
        part_ref[grid_count:, :] = mm(by_slot(arrived_refs, low), grid_first_ref[low, :])
        mesh_out_ref[...] = (mesh_ref[...].astype(F32) + mesh_normed_ref[...]).astype(BF16)
        cot_rows_ref[:grid_count, :] = cot_ref[...]
        cot_rows_ref[grid_count:, :] = by_slot(arrived_refs, high)
        second = centred(grid_second_ref[...], 1).astype(BF16)
        grid_wide_ref[:, low] = second
        grid_wide_ref[:, high] = mm_t(second, grid_second_ref[...]).astype(BF16)
        cot_turned_ref[...] = mm_t(cot_rows_ref[...], second)
        grid_back_ref[low, :] = centred(grid_first_ref[high, :], 0).astype(BF16)
        grid_back_ref[high, :] = mm(dec_second_ref[...], grid_back_ref[low, :]).astype(BF16)
        mesh_cot_turned_ref[...] = mm_t(mesh_cot_ref[...], mesh_wide_ref[:, low])
        mesh_turned_ref[...] = mm_t(mesh_normed_ref[...].astype(BF16), mesh_second_ref[...])
        mesh_slope_ref[...] = silu_and_slope(mesh_pre_ref[...])[1]
        write_slopes(
            dec_pre_ref,
            dec_normed_ref,
            dec_scale_ref,
            dec_second_ref,
            dec_gain_ref,
            dec_turned_ref,
        )

    (
        grid_part,
        cot_rows,
        cot_turned,
        grid_wide,
        grid_back,
        mesh_out,
        mesh_cot_turned,
        mesh_slope,
        mesh_turned,
        dec_gain,
        dec_turned,
    ) = call(
        between,
        "slopes_and_nodes",
        [
            *arrived,
            grid_nodes,
            grid_first,
            grid_second,
            grid_cot,
            mesh_second,
            dec_second,
            mesh_nodes,
            mesh_cot,
            dec_normed,
            dec_scale,
            dec_pre,
            mesh_normed,
            mesh_pre,
            mesh_wide,
        ],
        [
            ((spots, feat), F32),
            ((spots, feat), BF16),
            ((spots, feat), F32),
            ((feat, 2 * feat), BF16),
            ((2 * feat, feat), BF16),
            ((mesh_count, feat), BF16),
            ((mesh_count, feat), F32),
            ((mesh_count, feat), F32),
            ((mesh_count, feat), F32),
            ((dec_count, feat), BF16),
            ((dec_count, feat), BF16),
        ],
        flops=16 * spots * feat * feat,
    )

    def backward(*refs):
        returned_refs, refs = refs[:arrived_count], refs[arrived_count:]
        (
            spot_ref,
            grid_part_ref,
            select_t_ref,
            cot_rows_ref,
            cot_turned_ref,
            mesh_cot_ref,
            mesh_cot_turned_ref,
            enc_pick_ref,
            enc_pool_ref,
            dec_pick_ref,
            dec_pool_ref,
            grid_first_ref,
            grid_wide_ref,
            grid_back_ref,
            mesh_first_ref,
            mesh_wide_ref,
            enc_first_ref,
            enc_second_ref,
            dec_first_ref,
            enc_normed_ref,
            enc_scale_ref,
            enc_pre_ref,
            dec_normed_ref,
            dec_gain_ref,
            dec_turned_ref,
            mesh_normed_ref,
            mesh_scale_ref,
            mesh_slope_ref,
            mesh_turned_ref,
        ) = refs[:29]
        refs = refs[29:]
        out_refs, refs = refs[:sent_count], refs[sent_count:]
        (
            grid_normed_ref,
            grid_gpre_ref,
            dec_gpre_ref,
            enc_gpre_ref,
            mesh_gin_ref,
            mesh_gpre_ref,
            agg_ref,
            grid_act_ref,
            grid_slope_ref,
            spot_grad_ref,
            mesh_in_ref,
            mesh_back_ref,
            enc_gain_ref,
            enc_turned_ref,
        ) = refs
        agg_ref[:grid_count, :] = (
            spot_ref[:grid_count, :] + mm(select_t_ref[:, :slots], by_row(returned_refs, low))
        ).astype(BF16)
        agg_ref[grid_count:, :] = (
            spot_ref[grid_count:, :] + by_slot(returned_refs, high).astype(F32)
        ).astype(BF16)
        mesh_in_ref[low, :] = dec_first_ref[high, :]
        mesh_in_ref[high, :] = mm(mesh_wide_ref[:, low], dec_first_ref[high, :]).astype(BF16)

        def grid_chain(block):
            pre = grid_part_ref[block, :] + mm(agg_ref[block, :], grid_first_ref[high, :])
            yield
            for part, rows in parts_of(block):
                act, slope = silu_and_slope(pre[part, :])
                grid_act_ref[rows, :] = act.astype(BF16)
                grid_slope_ref[rows, :] = slope
            yield
            both = mm(grid_act_ref[block, :], grid_wide_ref[...])
            yield
            for part, rows in parts_of(block):
                raw = both[part, low]
                scale_inv = scale_rows(raw)
                normed = raw * scale_inv
                grid_normed_ref[rows, :] = normed
                mean = jnp.mean(cot_rows_ref[rows, :].astype(F32) * normed, axis=-1, keepdims=True)
                raw = scale_inv * (cot_turned_ref[rows, :] - (mean * scale_inv) * both[part, high])
                grid_gpre_ref[rows, :] = (raw * grid_slope_ref[rows, :]).astype(BF16)
            yield
            spot_grad_ref[block, :] = mm_t(grid_gpre_ref[block, :], grid_back_ref[...]).astype(BF16)

        in_step(grid_chain(block) for block in row_halves(spots))
        mesh_back_ref[low, :] = centred(mesh_first_ref[high, :], 0).astype(BF16)
        mesh_back_ref[high, :] = mm(enc_second_ref[...], mesh_back_ref[low, :]).astype(BF16)
        spot_grad_ref[spots:, :] = jnp.zeros((total - spots, 2 * feat), BF16)
        write_slopes(
            enc_pre_ref,
            enc_normed_ref,
            enc_scale_ref,
            enc_second_ref,
            enc_gain_ref,
            enc_turned_ref,
        )
        in_step(
            edge_back(
                lambda rows: mm(dec_pick_ref[rows, :], spot_grad_ref[...]),
                dec_normed_ref,
                dec_gain_ref,
                dec_turned_ref,
                dec_gpre_ref,
                block,
            )
            for block in row_halves(dec_count)
        )
        mesh_sum = mm(dec_pool_ref[mesh_rows, :], dec_gpre_ref[...]).astype(BF16)
        both = mm_t(mesh_sum, mesh_in_ref[...])
        mesh_gin = mesh_cot_ref[...].astype(F32) + both[:, low]
        mesh_gin_ref[...] = mesh_gin
        mean = jnp.mean(mesh_gin * mesh_normed_ref[...], axis=-1, keepdims=True)
        raw = mesh_cot_turned_ref[...] + both[:, high] - mean * mesh_turned_ref[...]
        mesh_gpre_ref[...] = (mesh_scale_ref[...] * raw * mesh_slope_ref[...]).astype(BF16)
        mesh_gagg = mm_t(mesh_gpre_ref[...], mesh_back_ref[...]).astype(BF16)
        pooled = mm(dec_pool_ref[grid_count:spots, :], dec_gpre_ref[...]).astype(BF16)
        slot_back = mm_t(pooled, dec_first_ref[low, :])
        in_step(
            edge_back(
                lambda rows: mm(enc_pick_ref[rows, mesh_rows], mesh_gagg),
                enc_normed_ref,
                enc_gain_ref,
                enc_turned_ref,
                enc_gpre_ref,
                block,
            )
            for block in row_halves(enc_count)
        )
        pooled = mm(enc_pool_ref[grid_count:spots, :], enc_gpre_ref[...]).astype(BF16)
        slot_back = (slot_back + mm_t(pooled, enc_first_ref[low, :])).astype(BF16)
        send(out_refs, lambda j: slot_back[reverse[j] * width : (reverse[j] + 1) * width, :])

    results = call(
        backward,
        "edges_backward",
        [
            *returned,
            spot_msg,
            grid_part,
            select_t,
            cot_rows,
            cot_turned,
            mesh_cot,
            mesh_cot_turned,
            enc_pick,
            enc_pool,
            dec_pick,
            dec_pool,
            grid_first,
            grid_wide,
            grid_back,
            mesh_first,
            mesh_wide,
            enc_first,
            enc_second,
            dec_first,
            enc_normed,
            enc_scale,
            enc_pre,
            dec_normed,
            dec_gain,
            dec_turned,
            mesh_normed,
            mesh_scale,
            mesh_slope,
            mesh_turned,
        ],
        sent_shapes(feat)
        + [
            ((spots, feat), F32),
            ((spots, feat), BF16),
            ((dec_count, feat), BF16),
            ((enc_count, feat), BF16),
            ((mesh_count, feat), F32),
            ((mesh_count, feat), BF16),
        ],
        scratch=[
            ((spots, feat), BF16),
            ((spots, feat), BF16),
            ((spots, feat), F32),
            ((total, 2 * feat), BF16),
            ((2 * feat, feat), BF16),
            ((2 * feat, feat), BF16),
            ((enc_count, feat), BF16),
            ((enc_count, feat), BF16),
        ],
        flops=2 * feat * feat * (4 * spots + 3 * dec_count + 2 * enc_count),
    )
    outgoing, results = results[:sent_count], results[sent_count:]
    grid_normed, grid_gpre, dec_gpre, enc_gpre, mesh_gin, mesh_gpre = results
    final = exchange(outgoing)

    def tail(
        nodes_ref,
        grid_normed_ref,
        cot_ref,
        grid_gpre_ref,
        enc_pool_ref,
        enc_gpre_ref,
        dec_pool_ref,
        dec_gpre_ref,
        mesh_gin_ref,
        mesh_gpre_ref,
        grid_wn_ref,
        enc_wg_ref,
        dec_wg_ref,
        mesh_wn_ref,
        enc_wm_ref,
        base_ref,
        grad_mesh_ref,
        grid_out_ref,
    ):
        grid_out_ref[...] = (
            nodes_ref[...].astype(F32) + grid_normed_ref[:grid_count, :]
        ).astype(BF16)
        enc_sums = mm(enc_pool_ref[...], enc_gpre_ref[...]).astype(BF16)
        dec_sums = mm(dec_pool_ref[:grid_count, :], dec_gpre_ref[...]).astype(BF16)
        base_ref[...] = (
            cot_ref[...].astype(F32)
            + mm_t(grid_gpre_ref[:grid_count, :], grid_wn_ref[low, :])
            + mm_t(enc_sums[:grid_count, :], enc_wg_ref[low, :])
            + mm_t(dec_sums, dec_wg_ref[low, :])
        )
        grad_mesh_ref[...] = (
            mesh_gin_ref[...]
            + mm_t(mesh_gpre_ref[...], mesh_wn_ref[low, :])
            + mm_t(enc_sums[mesh_rows, :], enc_wm_ref[high, :])
        )

    base, grad_mesh, grid_out = call(
        tail,
        "local_gradients",
        [
            grid_nodes,
            grid_normed,
            grid_cot,
            grid_gpre,
            enc_pool,
            enc_gpre,
            dec_pool,
            dec_gpre,
            mesh_gin,
            mesh_gpre,
            grid_first,
            enc_first,
            dec_first,
            mesh_first,
            enc_first,
        ],
        [((grid_count, feat), F32), ((mesh_count, feat), F32), ((grid_count, feat), BF16)],
        flops=2 * feat * feat * 3 * grid_count,
    )

    def finish(*refs):
        back_refs = refs[:arrived_count]
        base_ref, select_t_ref, out_ref = refs[arrived_count:]
        out_ref[...] = base_ref[...] + mm(select_t_ref[:, :slots], by_row(back_refs))

    (grad_grid,) = call(
        finish,
        "add_returned",
        [*final, base, select_t],
        [((grid_count, feat), F32)],
        flops=2 * grid_count * slots * feat,
    )
    return (grid_out, mesh_out, grad_grid, grad_mesh)


def solution(mesh):
    rows = P(("groups", "tile"), None)
    flat = P(("groups", "tile"))
    in_specs = (rows,) * 6 + (P(),) * 8 + (rows,) + (flat,) * 5
    return jax.shard_map(
        per_device, mesh=mesh, in_specs=in_specs, out_specs=(rows,) * 4, check_vma=False
    )
```

```python
import jax
import jax.numpy as jnp
from jax import lax
from jax.experimental import pallas as pl
from jax.experimental.pallas import tpu as pltpu
from jax.sharding import PartitionSpec as P

TW = 4
CHUNK = 32
ROUND_FLOPS = 2 * 10**10
F32 = jnp.float32
BF16 = jnp.bfloat16
VMEM_LIMIT = 30 * 1024 * 1024


def mm(left, right):
    return jnp.dot(left, right, preferred_element_type=F32)


def mm_t(left, right):
    return lax.dot_general(left, right, (((1,), (1,)), ((), ())), preferred_element_type=F32)


def centred(values, axis):
    values = values.astype(F32)
    return values - jnp.mean(values, axis=axis, keepdims=True)


def silu_and_slope(pre):
    half = 0.5 * pre
    lifted = 1.0 + jnp.tanh(half)
    return half * lifted, lifted * (0.5 + 0.5 * half * (2.0 - lifted))


def silu(pre):
    half = 0.5 * pre
    return half * (1.0 + jnp.tanh(half))


def scale_rows(raw):
    return lax.rsqrt(jnp.mean(raw * raw, axis=-1, keepdims=True) + 1e-05)


def row_chunks(rows, size=CHUNK):
    return [slice(start, min(start + size, rows)) for start in range(0, rows, size)]


def write_silu(pre, act_ref):
    for rows in row_chunks(pre.shape[0]):
        act_ref[rows, :] = silu(pre[rows, :]).astype(BF16)


def write_norm(raw, normed_ref, scale_ref):
    for rows in row_chunks(raw.shape[0]):
        part = raw[rows, :]
        scale_inv = scale_rows(part)
        normed_ref[rows, :] = (part * scale_inv).astype(normed_ref.dtype)
        scale_ref[rows, :] = scale_inv


def write_slopes(pre_ref, normed_ref, scale_ref, second_ref, gain_ref, turned_ref):
    raw = mm_t(normed_ref[...], second_ref[...])
    for rows in row_chunks(pre_ref.shape[0]):
        gain = silu_and_slope(pre_ref[rows, :])[1] * scale_ref[rows, :]
        gain_ref[rows, :] = gain.astype(BF16)
        turned_ref[rows, :] = (gain * raw[rows, :]).astype(BF16)


def edge_back(both, normed_ref, gain_ref, turned_ref, out_ref):
    edges, features = normed_ref.shape
    for rows in row_chunks(edges):
        mean = jnp.mean(
            both[rows, :features] * normed_ref[rows, :].astype(F32), axis=-1, keepdims=True
        )
        out_ref[rows, :] = (
            gain_ref[rows, :] * both[rows, features:].astype(BF16)
            - turned_ref[rows, :] * mean.astype(BF16)
        )


def neighbour_offsets(peer_count):
    forward_half = [1, TW, TW + 1, TW - 1]
    return forward_half + [-offset for offset in forward_half] + [peer_count // 2]


def onehot_pair(spot_ref, mesh_ref, spots, mesh_count, by_edge_ref, by_spot_ref):
    edges, total = by_edge_ref.shape
    spot_row = spot_ref[...].reshape(1, -1)
    mesh_row = mesh_ref[...].reshape(1, -1) + spots
    one, zero = jnp.ones((), BF16), jnp.zeros((), BF16)

    def ones(ids, index):
        shape = jnp.broadcast_shapes(ids.shape, index.shape)
        hit = jnp.broadcast_to(ids, shape) == jnp.broadcast_to(index, shape)
        return jnp.where(hit, jnp.broadcast_to(one, shape), jnp.broadcast_to(zero, shape))

    for row, first, count in ((spot_row, 0, spots), (mesh_row, spots, mesh_count)):
        ids = lax.broadcasted_iota(jnp.int32, (16, edges), 0).astype(jnp.int16)
        wide = jnp.broadcast_to(row, (16, edges)).astype(jnp.int16)
        for rows in row_chunks(count, 16):
            rows = slice(rows.start + first, rows.stop + first)
            by_spot_ref[rows, :] = ones(ids, wide - jnp.int16(rows.start))
    by_spot_ref[spots + mesh_count :, :] = jnp.zeros((total - spots - mesh_count, edges), BF16)
    lane = lax.broadcasted_iota(jnp.int32, (16, 128), 1).astype(jnp.int16)
    for rows in row_chunks(edges, 128):
        spot_col = jnp.broadcast_to(spot_row[:, rows], (128, 128)).T.astype(jnp.int16)
        mesh_col = jnp.broadcast_to(mesh_row[:, rows], (128, 128)).T.astype(jnp.int16)
        for columns in row_chunks(total, 128):
            for part in row_chunks(128, 16):
                place = slice(rows.start + part.start, rows.start + part.stop)
                ids = lane + jnp.int16(columns.start)
                hits = []
                if columns.start < spots:
                    hits.append(ones(ids, spot_col[part, :]))
                if columns.stop > spots:
                    hits.append(ones(ids, mesh_col[part, :]))
                by_edge_ref[place, columns] = sum(hits[1:], hits[0])


class Fetched:
    def __init__(self, source, target, semaphore):
        self.copy = pltpu.make_async_copy(source, target, semaphore)
        self.target = target
        self.landed = False
        self.copy.start()

    def land(self):
        if not self.landed:
            self.copy.wait()
            self.landed = True

    def __getitem__(self, key):
        self.land()
        return self.target[key]


def call(body, name, inputs, outputs, scratch=(), flops=0):
    arrays, specs, moved, fetches = [], [], 0, []
    for place, entry in enumerate(inputs):
        if isinstance(entry, tuple):
            array, first, rows = entry
            array = pltpu.with_memory_space_constraint(array, pltpu.HBM)
            specs.append(pl.BlockSpec(memory_space=pltpu.HBM))
            shape = (rows,) + array.shape[1:]
            fetches.append((place, first, rows, shape, array.dtype))
            moved += rows * (array.size // array.shape[0]) * array.dtype.itemsize
        else:
            array = entry
            specs.append(pl.BlockSpec(memory_space=pltpu.VMEM))
            moved += array.size * array.dtype.itemsize
        arrays.append(array)
    shapes = [jax.ShapeDtypeStruct(shape, dtype) for shape, dtype in outputs]
    for shape in shapes:
        moved += shape.size * shape.dtype.itemsize
    buffers = [pltpu.VMEM(shape, dtype) for _, _, _, shape, dtype in fetches]
    if fetches:
        buffers.append(pltpu.SemaphoreType.DMA((len(fetches),)))

    def kernel(*refs):
        refs = list(refs)
        waiting = []
        if fetches:
            targets, semaphores = refs[-len(buffers) : -1], refs[-1]
            refs = refs[: -len(buffers)]
        for slot, (place, first, rows, shape, _) in enumerate(fetches):
            source = refs[place]
            if source.shape != shape:
                source = source.at[pl.ds(first, rows)]
            refs[place] = Fetched(source, targets[slot], semaphores.at[slot])
            waiting.append(refs[place])
        body(*refs)
        for fetched in waiting:
            fetched.land()

    return pl.pallas_call(
        kernel,
        name=name,
        in_specs=specs,
        out_specs=[pl.BlockSpec(memory_space=pltpu.VMEM) for _ in shapes],
        out_shape=shapes,
        scratch_shapes=[pltpu.VMEM(shape, dtype) for shape, dtype in scratch]
        + buffers,
        compiler_params=pltpu.CompilerParams(vmem_limit_bytes=VMEM_LIMIT),
        cost_estimate=pl.CostEstimate(flops=flops, bytes_accessed=moved, transcendentals=0),
    )(*arrays)


def per_device(
    grid_nodes,
    mesh_nodes,
    enc_edges,
    dec_edges,
    grid_cot,
    mesh_cot,
    enc_first,
    enc_second,
    mesh_first,
    mesh_second,
    dec_first,
    dec_second,
    grid_first,
    grid_second,
    send_index,
    send_count,
    enc_grid,
    enc_mesh,
    dec_grid,
    dec_mesh,
):
    grid_count, feat = grid_nodes.shape
    mesh_count = mesh_nodes.shape[0]
    enc_count = enc_edges.shape[0]
    dec_count = dec_edges.shape[0]
    links, width = send_index.shape
    slots = links * width
    slots_pad = -(-slots // 128) * 128
    spots = grid_count + slots
    total = -(-(spots + mesh_count) // 128) * 128
    peer_count = lax.axis_size("tile")
    offsets = neighbour_offsets(peer_count)
    half = (links - 1) // 2
    reverse = [(j + half) % (links - 1) for j in range(links - 1)] + [links - 1]
    low, high = slice(0, feat), slice(feat, 2 * feat)
    mesh_rows = slice(spots, spots + mesh_count)

    one, four, five, three = range(half)
    minus = [j + half for j in range(half)]
    across = links - 1
    peers = range(peer_count)

    def permute(part, steps, odd_row_steps=None):
        rows = (steps, odd_row_steps or steps)
        pairs = [(s, (s + rows[s // TW % 2][s % 2]) % peer_count) for s in peers]
        return lax.ppermute(part, "tile", pairs)

    planes = peer_count // TW

    def plane(step):
        return lax.rem(lax.div(lax.axis_index("tile"), TW) + (planes + step), planes)

    def pass_rows(planes_ref, passed_ref):
        passed_ref[:width, :] = planes_ref[plane(-1), width:, :]
        passed_ref[width:, :] = planes_ref[plane(1), width:, :]

    def exchange(parts):
        to_planes, behind_one, ahead_three, five_off, own_chip = parts
        columns = to_planes.shape[2]
        to_planes = lax.all_to_all(
            to_planes,
            "tile",
            split_axis=0,
            concat_axis=0,
            tiled=True,
            axis_index_groups=[[z * TW + row for z in range(planes)] for row in range(TW)],
        )
        behind_one = permute(behind_one, (-1, 1))
        ahead_three = permute(ahead_three, (3, -3))
        five_off = permute(five_off, (-5, 5))
        own_chip = permute(own_chip, (1, -1))
        (passed,) = call(pass_rows, "pass_rows", [to_planes], [((2 * width, columns), BF16)])
        passed = permute(passed, (1, -1))
        return [to_planes, behind_one, ahead_three, five_off, own_chip, passed]

    arrived_count = 6

    def sent_shapes(columns):
        return [((planes, 2 * width, columns), BF16)] + [((width, columns), BF16)] * 4

    sent_count = len(sent_shapes(feat))

    def send(refs, message, columns=slice(None)):
        odd = lax.rem(lax.axis_index("tile"), 2) == 1

        def by_parity(even, odd_one):
            return jnp.where(odd, message(odd_one), message(even))

        to_planes, behind_one, ahead_three, five_off, own_chip = refs
        first, second = slice(0, width), slice(width, 2 * width)
        if columns.start in (None, 0):
            to_planes[...] = jnp.zeros(to_planes.shape, BF16)
        to_planes[plane(1), first, columns] = message(four)
        to_planes[plane(1), second, columns] = by_parity(five, three)
        to_planes[plane(-1), first, columns] = message(minus[four])
        to_planes[plane(-1), second, columns] = by_parity(minus[three], minus[five])
        to_planes[plane(planes // 2), first, columns] = message(across)
        behind_one[:, columns] = by_parity(minus[one], one)
        ahead_three[:, columns] = by_parity(three, minus[three])
        five_off[:, columns] = by_parity(minus[five], five)
        own_chip[:, columns] = by_parity(one, minus[one])

    def receive(refs, columns=slice(None)):
        odd = lax.rem(lax.axis_index("tile"), 2) == 1
        from_planes, behind_one, ahead_three, five_off, own_chip, passed = refs
        first, second = slice(0, width), slice(width, 2 * width)
        near, near_three = behind_one[:, columns], ahead_three[:, columns]
        far, own = five_off[:, columns], own_chip[:, columns]
        from_behind, from_ahead = passed[first, columns], passed[second, columns]
        slot_rows = [None] * links
        slot_rows[one] = jnp.where(odd, own, near)
        slot_rows[minus[one]] = jnp.where(odd, near, own)
        slot_rows[three] = jnp.where(odd, near_three, from_behind)
        slot_rows[minus[three]] = jnp.where(odd, from_ahead, near_three)
        slot_rows[five] = jnp.where(odd, from_behind, far)
        slot_rows[minus[five]] = jnp.where(odd, far, from_ahead)
        slot_rows[four] = from_planes[plane(-1), first, columns]
        slot_rows[minus[four]] = from_planes[plane(1), first, columns]
        slot_rows[across] = from_planes[plane(planes // 2), first, columns]
        return slot_rows

    def by_slot(refs, columns=slice(None)):
        return jnp.concatenate(receive(refs, columns), axis=0)

    def by_row(refs, columns=slice(None)):
        slot_rows = receive(refs, columns)
        return jnp.concatenate([slot_rows[reverse[j]] for j in range(links)], axis=0)

    def pack(index_ref, count_ref, nodes_ref, cot_ref, select_ref, *out_refs):
        def column(row):
            count = row.shape[1]
            eye = lax.broadcasted_iota(jnp.int32, (count, count), 0) == lax.broadcasted_iota(
                jnp.int32, (count, count), 1
            )
            return jnp.sum(
                jnp.where(eye, jnp.broadcast_to(row, (count, count)), 0.0), axis=1, keepdims=True
            )

        counts = column(count_ref[...].reshape(1, -1).astype(F32))
        place = lax.broadcasted_iota(jnp.int32, (links, width), 1).astype(F32)
        index = jnp.where(place < counts, index_ref[...].astype(F32), -1.0)
        lane = lax.broadcasted_iota(jnp.int32, (width, grid_count), 1).astype(F32)
        picks = [
            jnp.where(lane == column(index[j : j + 1, :]), 1.0, 0.0).astype(BF16)
            for j in range(links)
        ]
        select = jnp.concatenate(picks, axis=0)
        select_ref[:slots, :] = select
        select_ref[slots:, :] = jnp.zeros((slots_pad - slots, grid_count), BF16)
        sent_nodes = mm(select, nodes_ref[...]).astype(BF16)
        sent_cot = mm(select, cot_ref[...]).astype(BF16)
        send(out_refs, lambda j: sent_nodes[j * width : (j + 1) * width, :], low)
        send(out_refs, lambda j: sent_cot[j * width : (j + 1) * width, :], high)

    select, *outgoing = call(
        pack,
        "pack_rows",
        [
            (send_index, 0, links),
            (send_count, 0, links),
            (grid_nodes, 0, grid_count),
            (grid_cot, 0, grid_count),
        ],
        [((slots_pad, grid_count), BF16)] + sent_shapes(2 * feat),
        flops=4 * slots * grid_count * feat,
    )
    def turn(select_ref, select_t_ref):
        select_t_ref[...] = select_ref[...].astype(F32).T.astype(BF16)

    (select_t,) = call(
        turn, "turn_select", [select], [((grid_count, slots_pad), BF16)], flops=ROUND_FLOPS
    )
    *outgoing, select_t = lax.optimization_barrier((*outgoing, select_t))
    arrived = exchange(outgoing)

    def local(
        select_ref,
        nodes_ref,
        mesh_ref,
        enc_edges_ref,
        dec_edges_ref,
        enc_first_ref,
        dec_first_ref,
        mesh_first_ref,
        enc_grid_ref,
        enc_mesh_ref,
        dec_grid_ref,
        dec_mesh_ref,
        enc_second_ref,
        mesh_second_ref,
        dec_second_ref,
        enc_part_ref,
        dec_part_ref,
        mesh_part_ref,
        enc_pick_ref,
        enc_pool_ref,
        dec_pick_ref,
        dec_pool_ref,
        enc_centred_ref,
        dec_centred_ref,
        mesh_wide_ref,
        mesh_base_ref,
        shared_pool_ref,
        table_ref,
    ):
        onehot_pair(enc_grid_ref, enc_mesh_ref, spots, mesh_count, enc_pick_ref, enc_pool_ref)
        onehot_pair(dec_grid_ref, dec_mesh_ref, spots, mesh_count, dec_pick_ref, dec_pool_ref)
        enc_centred_ref[...] = centred(enc_second_ref[...], 1).astype(BF16)
        mesh_centred = centred(mesh_second_ref[...], 1).astype(BF16)
        mesh_wide_ref[:, low] = mesh_centred
        mesh_wide_ref[:, high] = mm(mesh_centred, dec_first_ref[high, :]).astype(BF16)
        mesh_base_ref[...] = mm(mesh_ref[...], dec_first_ref[high, :])
        shared_pool_ref[...] = mm(
            select_ref[:slots, :], dec_pool_ref[:grid_count, :]
        ).astype(BF16)
        dec_centred_ref[...] = centred(dec_second_ref[...], 1).astype(BF16)
        nodes = nodes_ref[...]
        mesh_part_ref[...] = mm(mesh_ref[...], mesh_first_ref[low, :])
        table_ref[:grid_count, :] = mm(nodes, enc_first_ref[low, :]).astype(BF16)
        table_ref[grid_count:, :] = jnp.zeros((total - grid_count, feat), BF16)
        table_ref[mesh_rows, :] = mm(mesh_ref[...], enc_first_ref[high, :]).astype(BF16)
        enc_part_ref[...] = mm(enc_edges_ref[...], enc_first_ref[2 * feat :, :])
        enc_part_ref[...] += mm(enc_pick_ref[...], table_ref[...])
        pd = mm(nodes, dec_first_ref[low, :]).astype(BF16)
        dec_part_ref[...] = mm(dec_edges_ref[...], dec_first_ref[2 * feat :, :])
        dec_part_ref[...] += mm(dec_pick_ref[:, :grid_count], pd)

    (
        enc_part,
        dec_part,
        mesh_part,
        enc_pick,
        enc_pool,
        dec_pick,
        dec_pool,
        enc_centred,
        dec_centred,
        mesh_wide,
        mesh_base,
        shared_pool,
    ) = call(
        local,
        "local_products",
        [
            select,
            grid_nodes,
            mesh_nodes,
            enc_edges,
            dec_edges,
            enc_first,
            dec_first,
            mesh_first,
            enc_grid,
            enc_mesh,
            dec_grid,
            dec_mesh,
            enc_second,
            mesh_second,
            dec_second,
        ],
        [
            ((enc_count, feat), F32),
            ((dec_count, feat), F32),
            ((mesh_count, feat), F32),
            ((enc_count, total), BF16),
            ((total, enc_count), BF16),
            ((dec_count, total), BF16),
            ((total, dec_count), BF16),
        ]
        + [
            ((feat, feat), BF16),
            ((feat, feat), BF16),
            ((feat, 2 * feat), BF16),
            ((mesh_count, feat), F32),
            ((slots, dec_count), BF16),
        ],
        scratch=[((total, feat), BF16)],
        flops=2 * feat * (feat * (2 * grid_count + enc_count + dec_count) + total * dec_count),
    )

    def forward(*refs):
        arrived_refs, refs = refs[:arrived_count], refs[arrived_count:]
        (
            shared_pool_ref,
            enc_part_ref,
            dec_part_ref,
            mesh_part_ref,
            enc_pick_ref,
            enc_pool_ref,
            dec_pick_ref,
            dec_pool_ref,
            enc_wg_ref,
            dec_wg_ref,
            enc_w2_ref,
            mesh_wa_ref,
            mesh_w2_ref,
            mesh_base_ref,
            dec_w2_ref,
        ) = refs[:15]
        refs = refs[15:]
        out_refs, refs = refs[:sent_count], refs[sent_count:]
        (
            spot_ref,
            enc_normed_ref,
            enc_scale_ref,
            enc_pre_ref,
            dec_normed_ref,
            dec_scale_ref,
            dec_pre_ref,
            mesh_normed_ref,
            mesh_scale_ref,
            mesh_pre_ref,
            enc_act_ref,
            dec_act_ref,
            mesh_act_ref,
            table_ref,
        ) = refs
        rows = by_slot(arrived_refs, low)
        pe = mm(rows, enc_wg_ref[low, :]).astype(BF16)
        enc_pre_ref[...] = enc_part_ref[...] + mm(enc_pick_ref[:, grid_count:spots], pe)
        write_silu(enc_pre_ref, enc_act_ref)
        write_norm(mm(enc_act_ref[...], enc_w2_ref[...]), enc_normed_ref, enc_scale_ref)
        agg = mm(enc_pool_ref[mesh_rows, :], enc_normed_ref[...]).astype(BF16)
        mesh_pre_ref[...] = mesh_part_ref[...] + mm(agg, mesh_wa_ref[high, :])
        write_silu(mesh_pre_ref, mesh_act_ref)
        both = mm(mesh_act_ref[...], mesh_w2_ref[...])
        write_norm(both[:, low], mesh_normed_ref, mesh_scale_ref)
        mesh_sent = mesh_base_ref[...] + mesh_scale_ref[...] * both[:, high]
        table_ref[:slots, :] = mm(rows, dec_wg_ref[low, :]).astype(BF16)
        table_ref[slots : slots + mesh_count, :] = mesh_sent.astype(BF16)
        table_ref[slots + mesh_count :, :] = jnp.zeros(
            (total - spots - mesh_count, feat), BF16
        )
        dec_pre_ref[...] = dec_part_ref[...] + mm(dec_pick_ref[:, grid_count:], table_ref[...])
        write_silu(dec_pre_ref, dec_act_ref)
        write_norm(mm(dec_act_ref[...], dec_w2_ref[...]), dec_normed_ref, dec_scale_ref)
        spot_ref[...] = mm(dec_pool_ref[:spots, :], dec_normed_ref[...])
        shared = mm(shared_pool_ref[...], dec_normed_ref[...]).astype(BF16)
        slot_msg = spot_ref[grid_count:, :].astype(BF16)
        send(
            out_refs, lambda j: slot_msg[reverse[j] * width : (reverse[j] + 1) * width, :], low
        )
        send(out_refs, lambda j: shared[j * width : (j + 1) * width, :], high)

    saved_shapes = [
        ((enc_count, feat), BF16),
        ((enc_count, 1), F32),
        ((enc_count, feat), F32),
        ((dec_count, feat), BF16),
        ((dec_count, 1), F32),
        ((dec_count, feat), F32),
        ((mesh_count, feat), F32),
        ((mesh_count, 1), F32),
        ((mesh_count, feat), F32),
    ]
    results = call(
        forward,
        "edges_forward",
        [
            *arrived,
            shared_pool,
            enc_part,
            dec_part,
            mesh_part,
            enc_pick,
            enc_pool,
            dec_pick,
            dec_pool,
            enc_first,
            dec_first,
            enc_centred,
            mesh_first,
            mesh_wide,
            mesh_base,
            dec_centred,
        ],
        sent_shapes(2 * feat)
        + [((spots, feat), F32)]
        + saved_shapes,
        scratch=[
            ((enc_count, feat), BF16),
            ((dec_count, feat), BF16),
            ((mesh_count, feat), BF16),
            ((total - grid_count, feat), BF16),
        ],
        flops=2 * feat * feat * 2 * (enc_count + dec_count),
    )
    outgoing, results = results[:sent_count], results[sent_count:]
    spot_msg, *saved = results
    enc_normed, enc_scale, enc_pre, dec_normed, dec_scale, dec_pre = saved[:6]
    mesh_normed, mesh_scale, mesh_pre = saved[6:]
    returned = exchange(outgoing)

    def between(*refs):
        arrived_refs, refs = refs[:arrived_count], refs[arrived_count:]
        (
            nodes_ref,
            grid_first_ref,
            grid_second_ref,
            cot_ref,
            mesh_second_ref,
            dec_second_ref,
            mesh_ref,
            mesh_cot_ref,
            dec_normed_ref,
            dec_scale_ref,
            dec_pre_ref,
            mesh_normed_ref,
            mesh_pre_ref,
            mesh_wide_ref,
            part_ref,
            cot_rows_ref,
            cot_turned_ref,
            grid_wide_ref,
            grid_back_ref,
            mesh_out_ref,
            mesh_cot_turned_ref,
            mesh_slope_ref,
            mesh_turned_ref,
            dec_gain_ref,
            dec_turned_ref,
        ) = refs
        part_ref[:grid_count, :] = mm(nodes_ref[...], grid_first_ref[low, :])
        part_ref[grid_count:, :] = mm(by_slot(arrived_refs, low), grid_first_ref[low, :])
        mesh_out_ref[...] = (mesh_ref[...].astype(F32) + mesh_normed_ref[...]).astype(BF16)
        cot_rows_ref[:grid_count, :] = cot_ref[...]
        cot_rows_ref[grid_count:, :] = by_slot(arrived_refs, high)
        second = centred(grid_second_ref[...], 1).astype(BF16)
        grid_wide_ref[:, low] = second
        grid_wide_ref[:, high] = mm_t(second, grid_second_ref[...]).astype(BF16)
        cot_turned_ref[...] = mm_t(cot_rows_ref[...], second)
        grid_back_ref[low, :] = centred(grid_first_ref[high, :], 0).astype(BF16)
        grid_back_ref[high, :] = mm(dec_second_ref[...], grid_back_ref[low, :]).astype(BF16)
        mesh_cot_turned_ref[...] = mm_t(mesh_cot_ref[...], mesh_wide_ref[:, low])
        mesh_turned_ref[...] = mm_t(mesh_normed_ref[...].astype(BF16), mesh_second_ref[...])
        mesh_slope_ref[...] = silu_and_slope(mesh_pre_ref[...])[1]
        write_slopes(
            dec_pre_ref,
            dec_normed_ref,
            dec_scale_ref,
            dec_second_ref,
            dec_gain_ref,
            dec_turned_ref,
        )

    (
        grid_part,
        cot_rows,
        cot_turned,
        grid_wide,
        grid_back,
        mesh_out,
        mesh_cot_turned,
        mesh_slope,
        mesh_turned,
        dec_gain,
        dec_turned,
    ) = call(
        between,
        "slopes_and_nodes",
        [
            *arrived,
            grid_nodes,
            grid_first,
            grid_second,
            grid_cot,
            mesh_second,
            dec_second,
            mesh_nodes,
            mesh_cot,
            dec_normed,
            dec_scale,
            dec_pre,
            mesh_normed,
            mesh_pre,
            mesh_wide,
        ],
        [
            ((spots, feat), F32),
            ((spots, feat), BF16),
            ((spots, feat), F32),
            ((feat, 2 * feat), BF16),
            ((2 * feat, feat), BF16),
            ((mesh_count, feat), BF16),
            ((mesh_count, feat), F32),
            ((mesh_count, feat), F32),
            ((mesh_count, feat), F32),
            ((dec_count, feat), BF16),
            ((dec_count, feat), BF16),
        ],
        flops=16 * spots * feat * feat,
    )

    def backward(*refs):
        returned_refs, refs = refs[:arrived_count], refs[arrived_count:]
        (
            spot_ref,
            grid_part_ref,
            select_t_ref,
            cot_rows_ref,
            cot_turned_ref,
            mesh_cot_ref,
            mesh_cot_turned_ref,
            enc_pick_ref,
            enc_pool_ref,
            dec_pick_ref,
            dec_pool_ref,
            grid_first_ref,
            grid_wide_ref,
            grid_back_ref,
            mesh_first_ref,
            mesh_wide_ref,
            enc_first_ref,
            enc_second_ref,
            dec_first_ref,
            enc_normed_ref,
            enc_scale_ref,
            enc_pre_ref,
            dec_normed_ref,
            dec_gain_ref,
            dec_turned_ref,
            mesh_normed_ref,
            mesh_scale_ref,
            mesh_slope_ref,
            mesh_turned_ref,
        ) = refs[:29]
        refs = refs[29:]
        out_refs, refs = refs[:sent_count], refs[sent_count:]
        (
            grid_normed_ref,
            grid_gpre_ref,
            dec_gpre_ref,
            enc_gpre_ref,
            mesh_gin_ref,
            mesh_gpre_ref,
            agg_ref,
            grid_act_ref,
            grid_slope_ref,
            spot_grad_ref,
            mesh_in_ref,
            mesh_back_ref,
            enc_gain_ref,
            enc_turned_ref,
        ) = refs
        agg_ref[:grid_count, :] = (
            spot_ref[:grid_count, :] + mm(select_t_ref[:, :slots], by_row(returned_refs, low))
        ).astype(BF16)
        agg_ref[grid_count:, :] = (
            spot_ref[grid_count:, :] + by_slot(returned_refs, high).astype(F32)
        ).astype(BF16)
        pre = grid_part_ref[...] + mm(agg_ref[...], grid_first_ref[high, :])
        mesh_in_ref[low, :] = dec_first_ref[high, :]
        mesh_in_ref[high, :] = mm(mesh_wide_ref[:, low], dec_first_ref[high, :]).astype(BF16)
        for rows in row_chunks(spots):
            act, slope = silu_and_slope(pre[rows, :])
            grid_act_ref[rows, :] = act.astype(BF16)
            grid_slope_ref[rows, :] = slope
        both = mm(grid_act_ref[...], grid_wide_ref[...])
        mesh_back_ref[low, :] = centred(mesh_first_ref[high, :], 0).astype(BF16)
        mesh_back_ref[high, :] = mm(enc_second_ref[...], mesh_back_ref[low, :]).astype(BF16)
        for rows in row_chunks(spots):
            part = both[rows, low]
            scale_inv = scale_rows(part)
            normed = part * scale_inv
            grid_normed_ref[rows, :] = normed
            mean = jnp.mean(cot_rows_ref[rows, :].astype(F32) * normed, axis=-1, keepdims=True)
            raw = scale_inv * (cot_turned_ref[rows, :] - (mean * scale_inv) * both[rows, high])
            grid_gpre_ref[rows, :] = (raw * grid_slope_ref[rows, :]).astype(BF16)
        spot_grad_ref[:spots, :] = mm_t(grid_gpre_ref[...], grid_back_ref[...]).astype(BF16)
        spot_grad_ref[spots:, :] = jnp.zeros((total - spots, 2 * feat), BF16)
        write_slopes(
            enc_pre_ref,
            enc_normed_ref,
            enc_scale_ref,
            enc_second_ref,
            enc_gain_ref,
            enc_turned_ref,
        )
        edge_back(
            mm(dec_pick_ref[...], spot_grad_ref[...]),
            dec_normed_ref,
            dec_gain_ref,
            dec_turned_ref,
            dec_gpre_ref,
        )
        mesh_sum = mm(dec_pool_ref[mesh_rows, :], dec_gpre_ref[...]).astype(BF16)
        both = mm_t(mesh_sum, mesh_in_ref[...])
        mesh_gin = mesh_cot_ref[...].astype(F32) + both[:, low]
        mesh_gin_ref[...] = mesh_gin
        mean = jnp.mean(mesh_gin * mesh_normed_ref[...], axis=-1, keepdims=True)
        raw = mesh_cot_turned_ref[...] + both[:, high] - mean * mesh_turned_ref[...]
        mesh_gpre_ref[...] = (mesh_scale_ref[...] * raw * mesh_slope_ref[...]).astype(BF16)
        mesh_gagg = mm_t(mesh_gpre_ref[...], mesh_back_ref[...]).astype(BF16)
        pooled = mm(dec_pool_ref[grid_count:spots, :], dec_gpre_ref[...]).astype(BF16)
        slot_back = mm_t(pooled, dec_first_ref[low, :])
        edge_back(
            mm(enc_pick_ref[:, mesh_rows], mesh_gagg),
            enc_normed_ref,
            enc_gain_ref,
            enc_turned_ref,
            enc_gpre_ref,
        )
        pooled = mm(enc_pool_ref[grid_count:spots, :], enc_gpre_ref[...]).astype(BF16)
        slot_back = (slot_back + mm_t(pooled, enc_first_ref[low, :])).astype(BF16)
        send(out_refs, lambda j: slot_back[reverse[j] * width : (reverse[j] + 1) * width, :])

    results = call(
        backward,
        "edges_backward",
        [
            *returned,
            spot_msg,
            grid_part,
            select_t,
            cot_rows,
            cot_turned,
            mesh_cot,
            mesh_cot_turned,
            enc_pick,
            enc_pool,
            dec_pick,
            dec_pool,
            grid_first,
            grid_wide,
            grid_back,
            mesh_first,
            mesh_wide,
            enc_first,
            enc_second,
            dec_first,
            enc_normed,
            enc_scale,
            enc_pre,
            dec_normed,
            dec_gain,
            dec_turned,
            mesh_normed,
            mesh_scale,
            mesh_slope,
            mesh_turned,
        ],
        sent_shapes(feat)
        + [
            ((spots, feat), F32),
            ((spots, feat), BF16),
            ((dec_count, feat), BF16),
            ((enc_count, feat), BF16),
            ((mesh_count, feat), F32),
            ((mesh_count, feat), BF16),
        ],
        scratch=[
            ((spots, feat), BF16),
            ((spots, feat), BF16),
            ((spots, feat), F32),
            ((total, 2 * feat), BF16),
            ((2 * feat, feat), BF16),
            ((2 * feat, feat), BF16),
            ((enc_count, feat), BF16),
            ((enc_count, feat), BF16),
        ],
        flops=2 * feat * feat * (4 * spots + 3 * dec_count + 2 * enc_count),
    )
    outgoing, results = results[:sent_count], results[sent_count:]
    grid_normed, grid_gpre, dec_gpre, enc_gpre, mesh_gin, mesh_gpre = results
    final = exchange(outgoing)

    def tail(
        nodes_ref,
        grid_normed_ref,
        cot_ref,
        grid_gpre_ref,
        enc_pool_ref,
        enc_gpre_ref,
        dec_pool_ref,
        dec_gpre_ref,
        mesh_gin_ref,
        mesh_gpre_ref,
        grid_wn_ref,
        enc_wg_ref,
        dec_wg_ref,
        mesh_wn_ref,
        enc_wm_ref,
        base_ref,
        grad_mesh_ref,
        grid_out_ref,
    ):
        grid_out_ref[...] = (
            nodes_ref[...].astype(F32) + grid_normed_ref[:grid_count, :]
        ).astype(BF16)
        enc_sums = mm(enc_pool_ref[...], enc_gpre_ref[...]).astype(BF16)
        dec_sums = mm(dec_pool_ref[:grid_count, :], dec_gpre_ref[...]).astype(BF16)
        base_ref[...] = (
            cot_ref[...].astype(F32)
            + mm_t(grid_gpre_ref[:grid_count, :], grid_wn_ref[low, :])
            + mm_t(enc_sums[:grid_count, :], enc_wg_ref[low, :])
            + mm_t(dec_sums, dec_wg_ref[low, :])
        )
        grad_mesh_ref[...] = (
            mesh_gin_ref[...]
            + mm_t(mesh_gpre_ref[...], mesh_wn_ref[low, :])
            + mm_t(enc_sums[mesh_rows, :], enc_wm_ref[high, :])
        )

    base, grad_mesh, grid_out = call(
        tail,
        "local_gradients",
        [
            grid_nodes,
            grid_normed,
            grid_cot,
            grid_gpre,
            enc_pool,
            enc_gpre,
            dec_pool,
            dec_gpre,
            mesh_gin,
            mesh_gpre,
            grid_first,
            enc_first,
            dec_first,
            mesh_first,
            enc_first,
        ],
        [((grid_count, feat), F32), ((mesh_count, feat), F32), ((grid_count, feat), BF16)],
        flops=2 * feat * feat * 3 * grid_count,
    )

    def finish(*refs):
        back_refs = refs[:arrived_count]
        base_ref, select_t_ref, out_ref = refs[arrived_count:]
        out_ref[...] = base_ref[...] + mm(select_t_ref[:, :slots], by_row(back_refs))

    (grad_grid,) = call(
        finish,
        "add_returned",
        [*final, base, select_t],
        [((grid_count, feat), F32)],
        flops=2 * grid_count * slots * feat,
    )
    return (grid_out, mesh_out, grad_grid, grad_mesh)


def solution(mesh):
    rows = P(("groups", "tile"), None)
    flat = P(("groups", "tile"))
    in_specs = (rows,) * 6 + (P(),) * 8 + (rows,) + (flat,) * 5
    return jax.shard_map(
        per_device, mesh=mesh, in_specs=in_specs, out_specs=(rows,) * 4, check_vma=False
    )
```

```python
import jax
import jax.numpy as jnp
from jax import lax
from jax.experimental import pallas as pl
from jax.experimental.pallas import tpu as pltpu
from jax.sharding import PartitionSpec as P

TW = 4
CHUNK = 32
ROUND_FLOPS = 2 * 10**10
F32 = jnp.float32
BF16 = jnp.bfloat16
VMEM_LIMIT = 30 * 1024 * 1024


def mm(left, right):
    return jnp.dot(left, right, preferred_element_type=F32)


def mm_t(left, right):
    return lax.dot_general(left, right, (((1,), (1,)), ((), ())), preferred_element_type=F32)


def centred(values, axis):
    values = values.astype(F32)
    return values - jnp.mean(values, axis=axis, keepdims=True)


def silu_and_slope(pre):
    half = 0.5 * pre
    lifted = 1.0 + jnp.tanh(half)
    return half * lifted, lifted * (0.5 + 0.5 * half * (2.0 - lifted))


def silu(pre):
    half = 0.5 * pre
    return half * (1.0 + jnp.tanh(half))


def scale_rows(raw):
    return lax.rsqrt(jnp.mean(raw * raw, axis=-1, keepdims=True) + 1e-05)


def row_chunks(rows, size=CHUNK):
    return [slice(start, min(start + size, rows)) for start in range(0, rows, size)]


def write_silu(pre, act_ref):
    for rows in row_chunks(pre.shape[0]):
        act_ref[rows, :] = silu(pre[rows, :]).astype(BF16)


def write_norm(raw, normed_ref, scale_ref):
    for rows in row_chunks(raw.shape[0]):
        part = raw[rows, :]
        scale_inv = scale_rows(part)
        normed_ref[rows, :] = (part * scale_inv).astype(normed_ref.dtype)
        scale_ref[rows, :] = scale_inv


def write_slopes(pre_ref, normed_ref, scale_ref, second_ref, gain_ref, turned_ref):
    raw = mm_t(normed_ref[...], second_ref[...])
    for rows in row_chunks(pre_ref.shape[0]):
        gain = silu_and_slope(pre_ref[rows, :])[1] * scale_ref[rows, :]
        gain_ref[rows, :] = gain.astype(BF16)
        turned_ref[rows, :] = (gain * raw[rows, :]).astype(BF16)


def edge_back(both, normed_ref, gain_ref, turned_ref, out_ref):
    edges, features = normed_ref.shape
    for rows in row_chunks(edges):
        mean = jnp.mean(
            both[rows, :features] * normed_ref[rows, :].astype(F32), axis=-1, keepdims=True
        )
        out_ref[rows, :] = (
            gain_ref[rows, :] * both[rows, features:].astype(BF16)
            - turned_ref[rows, :] * mean.astype(BF16)
        )


def neighbour_offsets(peer_count):
    forward_half = [1, TW, TW + 1, TW - 1]
    return forward_half + [-offset for offset in forward_half] + [peer_count // 2]


def onehot_pair(spot_ref, mesh_ref, spots, mesh_count, by_edge_ref, by_spot_ref):
    edges, total = by_edge_ref.shape
    spot_row = spot_ref[...].reshape(1, -1)
    mesh_row = mesh_ref[...].reshape(1, -1) + spots
    one, zero = jnp.ones((), BF16), jnp.zeros((), BF16)

    def ones(ids, index):
        shape = jnp.broadcast_shapes(ids.shape, index.shape)
        hit = jnp.broadcast_to(ids, shape) == jnp.broadcast_to(index, shape)
        return jnp.where(hit, jnp.broadcast_to(one, shape), jnp.broadcast_to(zero, shape))

    for row, first, count in ((spot_row, 0, spots), (mesh_row, spots, mesh_count)):
        ids = lax.broadcasted_iota(jnp.int32, (16, edges), 0).astype(jnp.int16)
        wide = jnp.broadcast_to(row, (16, edges)).astype(jnp.int16)
        for rows in row_chunks(count, 16):
            rows = slice(rows.start + first, rows.stop + first)
            by_spot_ref[rows, :] = ones(ids, wide - jnp.int16(rows.start))
    by_spot_ref[spots + mesh_count :, :] = jnp.zeros((total - spots - mesh_count, edges), BF16)
    lane = lax.broadcasted_iota(jnp.int32, (16, 128), 1).astype(jnp.int16)
    for rows in row_chunks(edges, 128):
        spot_col = jnp.broadcast_to(spot_row[:, rows], (128, 128)).T.astype(jnp.int16)
        mesh_col = jnp.broadcast_to(mesh_row[:, rows], (128, 128)).T.astype(jnp.int16)
        for columns in row_chunks(total, 128):
            for part in row_chunks(128, 16):
                place = slice(rows.start + part.start, rows.start + part.stop)
                ids = lane + jnp.int16(columns.start)
                hits = []
                if columns.start < spots:
                    hits.append(ones(ids, spot_col[part, :]))
                if columns.stop > spots:
                    hits.append(ones(ids, mesh_col[part, :]))
                by_edge_ref[place, columns] = sum(hits[1:], hits[0])


class Fetched:
    def __init__(self, source, target, semaphore):
        self.copy = pltpu.make_async_copy(source, target, semaphore)
        self.target = target
        self.landed = False
        self.copy.start()

    def land(self):
        if not self.landed:
            self.copy.wait()
            self.landed = True

    def __getitem__(self, key):
        self.land()
        return self.target[key]


def call(body, name, inputs, outputs, scratch=(), flops=0):
    arrays, specs, moved, fetches = [], [], 0, []
    for place, entry in enumerate(inputs):
        if isinstance(entry, tuple):
            array, first, rows = entry
            array = pltpu.with_memory_space_constraint(array, pltpu.HBM)
            specs.append(pl.BlockSpec(memory_space=pltpu.HBM))
            shape = (rows,) + array.shape[1:]
            fetches.append((place, first, rows, shape, array.dtype))
            moved += rows * (array.size // array.shape[0]) * array.dtype.itemsize
        else:
            array = entry
            specs.append(pl.BlockSpec(memory_space=pltpu.VMEM))
            moved += array.size * array.dtype.itemsize
        arrays.append(array)
    shapes = [jax.ShapeDtypeStruct(shape, dtype) for shape, dtype in outputs]
    for shape in shapes:
        moved += shape.size * shape.dtype.itemsize
    buffers = [pltpu.VMEM(shape, dtype) for _, _, _, shape, dtype in fetches]
    if fetches:
        buffers.append(pltpu.SemaphoreType.DMA((len(fetches),)))

    def kernel(*refs):
        refs = list(refs)
        waiting = []
        if fetches:
            targets, semaphores = refs[-len(buffers) : -1], refs[-1]
            refs = refs[: -len(buffers)]
        for slot, (place, first, rows, shape, _) in enumerate(fetches):
            source = refs[place]
            if source.shape != shape:
                source = source.at[pl.ds(first, rows)]
            refs[place] = Fetched(source, targets[slot], semaphores.at[slot])
            waiting.append(refs[place])
        body(*refs)
        for fetched in waiting:
            fetched.land()

    return pl.pallas_call(
        kernel,
        name=name,
        in_specs=specs,
        out_specs=[pl.BlockSpec(memory_space=pltpu.VMEM) for _ in shapes],
        out_shape=shapes,
        scratch_shapes=[pltpu.VMEM(shape, dtype) for shape, dtype in scratch]
        + buffers,
        compiler_params=pltpu.CompilerParams(vmem_limit_bytes=VMEM_LIMIT),
        cost_estimate=pl.CostEstimate(flops=flops, bytes_accessed=moved, transcendentals=0),
    )(*arrays)


def per_device(
    grid_nodes,
    mesh_nodes,
    enc_edges,
    dec_edges,
    grid_cot,
    mesh_cot,
    enc_first,
    enc_second,
    mesh_first,
    mesh_second,
    dec_first,
    dec_second,
    grid_first,
    grid_second,
    send_index,
    send_count,
    enc_grid,
    enc_mesh,
    dec_grid,
    dec_mesh,
):
    grid_count, feat = grid_nodes.shape
    mesh_count = mesh_nodes.shape[0]
    enc_count = enc_edges.shape[0]
    dec_count = dec_edges.shape[0]
    links, width = send_index.shape
    slots = links * width
    slots_pad = -(-slots // 128) * 128
    spots = grid_count + slots
    total = -(-(spots + mesh_count) // 128) * 128
    peer_count = lax.axis_size("tile")
    offsets = neighbour_offsets(peer_count)
    half = (links - 1) // 2
    reverse = [(j + half) % (links - 1) for j in range(links - 1)] + [links - 1]
    low, high = slice(0, feat), slice(feat, 2 * feat)
    mesh_rows = slice(spots, spots + mesh_count)

    one, four, five, three = range(half)
    minus = [j + half for j in range(half)]
    across = links - 1
    peers = range(peer_count)

    def permute(part, steps, odd_row_steps=None):
        rows = (steps, odd_row_steps or steps)
        pairs = [(s, (s + rows[s // TW % 2][s % 2]) % peer_count) for s in peers]
        return lax.ppermute(part, "tile", pairs)

    steady = ("late", "early", "behind", "ahead", "five", "opposite", "own")
    staggered = ("early", "late", "ahead", "five", "behind", "opposite", "own")
    arrived_count = 9

    def exchange(parts, order):
        moves = {
            "late": ((-4, -4), (4, 4)),
            "early": ((4, 4), (-4, -4)),
            "behind": ((-1, 1),),
            "ahead": ((3, -3),),
            "five": ((-5, 5),),
            "opposite": ((peer_count // 2, peer_count // 2),),
            "own": ((1, -1),),
        }
        parts = dict(zip(order, parts))
        own_chip = parts.pop("own")
        got = {name: permute(part, *moves[name]) for name, part in parts.items()}
        first = order[0]
        got[first], own_chip = lax.optimization_barrier((got[first], own_chip))
        late_passed = permute(got["late"], (1, -1))
        got["own"] = permute(own_chip, (1, -1))
        early_passed = permute(got["early"], (1, -1))
        return [got[name] for name in order] + [late_passed, early_passed]

    def sent_shapes(columns, order=steady):
        double = ("late", "early")
        return [((width * (1 + (name in double)), columns), BF16) for name in order]

    sent_count = len(steady)

    def place_bits():
        own = lax.axis_index("tile")
        return lax.rem(own, 2) == 1, lax.rem(lax.div(own, TW), 2) == 1

    def send(refs, message, columns=slice(None), order=steady):
        odd, odd_row = place_bits()
        refs = dict(zip(order, refs))

        def by_parity(even, odd_one):
            return jnp.where(odd, message(odd_one), message(even))

        late_pair, early_pair, behind_one, ahead_three, five_off, opposite, own_chip = [
            refs[name] for name in steady
        ]
        first, second = slice(0, width), slice(width, 2 * width)
        ahead = message(four), by_parity(five, three)
        behind = message(minus[four]), by_parity(minus[three], minus[five])
        for rows, go_ahead, go_behind in zip((first, second), ahead, behind):
            late_pair[rows, columns] = jnp.where(odd_row, go_ahead, go_behind)
            early_pair[rows, columns] = jnp.where(odd_row, go_behind, go_ahead)
        behind_one[:, columns] = by_parity(minus[one], one)
        ahead_three[:, columns] = by_parity(three, minus[three])
        five_off[:, columns] = by_parity(minus[five], five)
        opposite[:, columns] = message(across)
        own_chip[:, columns] = by_parity(one, minus[one])

    def receive(refs, columns=slice(None), order=steady):
        odd, odd_row = place_bits()
        late_passed, early_passed = refs[sent_count:]
        refs = dict(zip(order, refs))
        late_pair, early_pair, behind_one, ahead_three, five_off, opposite, own_chip = [
            refs[name] for name in steady
        ]
        first, second = slice(0, width), slice(width, 2 * width)
        near, near_three = behind_one[:, columns], ahead_three[:, columns]
        far, own = five_off[:, columns], own_chip[:, columns]
        late_rows, early_rows = late_passed[second, columns], early_passed[second, columns]
        from_behind = jnp.where(odd_row, early_rows, late_rows)
        from_ahead = jnp.where(odd_row, late_rows, early_rows)
        late_rows, early_rows = late_pair[first, columns], early_pair[first, columns]
        slot_rows = [None] * links
        slot_rows[one] = jnp.where(odd, own, near)
        slot_rows[minus[one]] = jnp.where(odd, near, own)
        slot_rows[three] = jnp.where(odd, near_three, from_behind)
        slot_rows[minus[three]] = jnp.where(odd, from_ahead, near_three)
        slot_rows[five] = jnp.where(odd, from_behind, far)
        slot_rows[minus[five]] = jnp.where(odd, far, from_ahead)
        slot_rows[four] = jnp.where(odd_row, early_rows, late_rows)
        slot_rows[minus[four]] = jnp.where(odd_row, late_rows, early_rows)
        slot_rows[across] = opposite[:, columns]
        return slot_rows

    def by_slot(refs, columns=slice(None), order=steady):
        return jnp.concatenate(receive(refs, columns, order), axis=0)

    def by_row(refs, columns=slice(None)):
        slot_rows = receive(refs, columns)
        return jnp.concatenate([slot_rows[reverse[j]] for j in range(links)], axis=0)

    def pack(index_ref, count_ref, nodes_ref, cot_ref, select_ref, *out_refs):
        def column(row):
            count = row.shape[1]
            eye = lax.broadcasted_iota(jnp.int32, (count, count), 0) == lax.broadcasted_iota(
                jnp.int32, (count, count), 1
            )
            return jnp.sum(
                jnp.where(eye, jnp.broadcast_to(row, (count, count)), 0.0), axis=1, keepdims=True
            )

        counts = column(count_ref[...].reshape(1, -1).astype(F32))
        place = lax.broadcasted_iota(jnp.int32, (links, width), 1).astype(F32)
        index = jnp.where(place < counts, index_ref[...].astype(F32), -1.0)
        lane = lax.broadcasted_iota(jnp.int32, (width, grid_count), 1).astype(F32)
        picks = [
            jnp.where(lane == column(index[j : j + 1, :]), 1.0, 0.0).astype(BF16)
            for j in range(links)
        ]
        select = jnp.concatenate(picks, axis=0)
        select_ref[:slots, :] = select
        select_ref[slots:, :] = jnp.zeros((slots_pad - slots, grid_count), BF16)
        sent_nodes = mm(select, nodes_ref[...]).astype(BF16)
        sent_cot = mm(select, cot_ref[...]).astype(BF16)
        send(
            out_refs, lambda j: sent_nodes[j * width : (j + 1) * width, :], low, staggered
        )
        send(out_refs, lambda j: sent_cot[j * width : (j + 1) * width, :], high, staggered)

    select, *outgoing = call(
        pack,
        "pack_rows",
        [
            (send_index, 0, links),
            (send_count, 0, links),
            (grid_nodes, 0, grid_count),
            (grid_cot, 0, grid_count),
        ],
        [((slots_pad, grid_count), BF16)] + sent_shapes(2 * feat, staggered),
        flops=4 * slots * grid_count * feat,
    )
    def turn(select_ref, select_t_ref):
        select_t_ref[...] = select_ref[...].astype(F32).T.astype(BF16)

    (select_t,) = call(
        turn, "turn_select", [select], [((grid_count, slots_pad), BF16)], flops=ROUND_FLOPS
    )
    *outgoing, select_t = lax.optimization_barrier((*outgoing, select_t))
    arrived = exchange(outgoing, staggered)

    def local(
        select_ref,
        nodes_ref,
        mesh_ref,
        enc_edges_ref,
        dec_edges_ref,
        enc_first_ref,
        dec_first_ref,
        mesh_first_ref,
        enc_grid_ref,
        enc_mesh_ref,
        dec_grid_ref,
        dec_mesh_ref,
        enc_second_ref,
        mesh_second_ref,
        dec_second_ref,
        enc_part_ref,
        dec_part_ref,
        mesh_part_ref,
        enc_pick_ref,
        enc_pool_ref,
        dec_pick_ref,
        dec_pool_ref,
        enc_centred_ref,
        dec_centred_ref,
        mesh_wide_ref,
        mesh_base_ref,
        shared_pool_ref,
        table_ref,
    ):
        onehot_pair(enc_grid_ref, enc_mesh_ref, spots, mesh_count, enc_pick_ref, enc_pool_ref)
        onehot_pair(dec_grid_ref, dec_mesh_ref, spots, mesh_count, dec_pick_ref, dec_pool_ref)
        enc_centred_ref[...] = centred(enc_second_ref[...], 1).astype(BF16)
        mesh_centred = centred(mesh_second_ref[...], 1).astype(BF16)
        mesh_wide_ref[:, low] = mesh_centred
        mesh_wide_ref[:, high] = mm(mesh_centred, dec_first_ref[high, :]).astype(BF16)
        mesh_base_ref[...] = mm(mesh_ref[...], dec_first_ref[high, :])
        shared_pool_ref[...] = mm(
            select_ref[:slots, :], dec_pool_ref[:grid_count, :]
        ).astype(BF16)
        dec_centred_ref[...] = centred(dec_second_ref[...], 1).astype(BF16)
        nodes = nodes_ref[...]
        mesh_part_ref[...] = mm(mesh_ref[...], mesh_first_ref[low, :])
        table_ref[:grid_count, :] = mm(nodes, enc_first_ref[low, :]).astype(BF16)
        table_ref[grid_count:, :] = jnp.zeros((total - grid_count, feat), BF16)
        table_ref[mesh_rows, :] = mm(mesh_ref[...], enc_first_ref[high, :]).astype(BF16)
        enc_part_ref[...] = mm(enc_edges_ref[...], enc_first_ref[2 * feat :, :])
        enc_part_ref[...] += mm(enc_pick_ref[...], table_ref[...])
        pd = mm(nodes, dec_first_ref[low, :]).astype(BF16)
        dec_part_ref[...] = mm(dec_edges_ref[...], dec_first_ref[2 * feat :, :])
        dec_part_ref[...] += mm(dec_pick_ref[:, :grid_count], pd)

    (
        enc_part,
        dec_part,
        mesh_part,
        enc_pick,
        enc_pool,
        dec_pick,
        dec_pool,
        enc_centred,
        dec_centred,
        mesh_wide,
        mesh_base,
        shared_pool,
    ) = call(
        local,
        "local_products",
        [
            select,
            grid_nodes,
            mesh_nodes,
            enc_edges,
            dec_edges,
            enc_first,
            dec_first,
            mesh_first,
            enc_grid,
            enc_mesh,
            dec_grid,
            dec_mesh,
            enc_second,
            mesh_second,
            dec_second,
        ],
        [
            ((enc_count, feat), F32),
            ((dec_count, feat), F32),
            ((mesh_count, feat), F32),
            ((enc_count, total), BF16),
            ((total, enc_count), BF16),
            ((dec_count, total), BF16),
            ((total, dec_count), BF16),
        ]
        + [
            ((feat, feat), BF16),
            ((feat, feat), BF16),
            ((feat, 2 * feat), BF16),
            ((mesh_count, feat), F32),
            ((slots, dec_count), BF16),
        ],
        scratch=[((total, feat), BF16)],
        flops=2 * feat * (feat * (2 * grid_count + enc_count + dec_count) + total * dec_count),
    )

    def forward(*refs):
        arrived_refs, refs = refs[:arrived_count], refs[arrived_count:]
        (
            shared_pool_ref,
            enc_part_ref,
            dec_part_ref,
            mesh_part_ref,
            enc_pick_ref,
            enc_pool_ref,
            dec_pick_ref,
            dec_pool_ref,
            enc_wg_ref,
            dec_wg_ref,
            enc_w2_ref,
            mesh_wa_ref,
            mesh_w2_ref,
            mesh_base_ref,
            dec_w2_ref,
        ) = refs[:15]
        refs = refs[15:]
        out_refs, refs = refs[:sent_count], refs[sent_count:]
        (
            spot_ref,
            enc_normed_ref,
            enc_scale_ref,
            enc_pre_ref,
            dec_normed_ref,
            dec_scale_ref,
            dec_pre_ref,
            mesh_normed_ref,
            mesh_scale_ref,
            mesh_pre_ref,
            enc_act_ref,
            dec_act_ref,
            mesh_act_ref,
            table_ref,
        ) = refs
        rows = by_slot(arrived_refs, low, staggered)
        pe = mm(rows, enc_wg_ref[low, :]).astype(BF16)
        enc_pre_ref[...] = enc_part_ref[...] + mm(enc_pick_ref[:, grid_count:spots], pe)
        write_silu(enc_pre_ref, enc_act_ref)
        write_norm(mm(enc_act_ref[...], enc_w2_ref[...]), enc_normed_ref, enc_scale_ref)
        agg = mm(enc_pool_ref[mesh_rows, :], enc_normed_ref[...]).astype(BF16)
        mesh_pre_ref[...] = mesh_part_ref[...] + mm(agg, mesh_wa_ref[high, :])
        write_silu(mesh_pre_ref, mesh_act_ref)
        both = mm(mesh_act_ref[...], mesh_w2_ref[...])
        write_norm(both[:, low], mesh_normed_ref, mesh_scale_ref)
        mesh_sent = mesh_base_ref[...] + mesh_scale_ref[...] * both[:, high]
        table_ref[:slots, :] = mm(rows, dec_wg_ref[low, :]).astype(BF16)
        table_ref[slots : slots + mesh_count, :] = mesh_sent.astype(BF16)
        table_ref[slots + mesh_count :, :] = jnp.zeros(
            (total - spots - mesh_count, feat), BF16
        )
        dec_pre_ref[...] = dec_part_ref[...] + mm(dec_pick_ref[:, grid_count:], table_ref[...])
        write_silu(dec_pre_ref, dec_act_ref)
        write_norm(mm(dec_act_ref[...], dec_w2_ref[...]), dec_normed_ref, dec_scale_ref)
        spot_ref[...] = mm(dec_pool_ref[:spots, :], dec_normed_ref[...])
        shared = mm(shared_pool_ref[...], dec_normed_ref[...]).astype(BF16)
        slot_msg = spot_ref[grid_count:, :].astype(BF16)
        send(
            out_refs, lambda j: slot_msg[reverse[j] * width : (reverse[j] + 1) * width, :], low
        )
        send(out_refs, lambda j: shared[j * width : (j + 1) * width, :], high)

    saved_shapes = [
        ((enc_count, feat), BF16),
        ((enc_count, 1), F32),
        ((enc_count, feat), F32),
        ((dec_count, feat), BF16),
        ((dec_count, 1), F32),
        ((dec_count, feat), F32),
        ((mesh_count, feat), F32),
        ((mesh_count, 1), F32),
        ((mesh_count, feat), F32),
    ]
    results = call(
        forward,
        "edges_forward",
        [
            *arrived,
            shared_pool,
            enc_part,
            dec_part,
            mesh_part,
            enc_pick,
            enc_pool,
            dec_pick,
            dec_pool,
            enc_first,
            dec_first,
            enc_centred,
            mesh_first,
            mesh_wide,
            mesh_base,
            dec_centred,
        ],
        sent_shapes(2 * feat)
        + [((spots, feat), F32)]
        + saved_shapes,
        scratch=[
            ((enc_count, feat), BF16),
            ((dec_count, feat), BF16),
            ((mesh_count, feat), BF16),
            ((total - grid_count, feat), BF16),
        ],
        flops=2 * feat * feat * 2 * (enc_count + dec_count),
    )
    outgoing, results = results[:sent_count], results[sent_count:]
    spot_msg, *saved = results
    enc_normed, enc_scale, enc_pre, dec_normed, dec_scale, dec_pre = saved[:6]
    mesh_normed, mesh_scale, mesh_pre = saved[6:]
    returned = exchange(outgoing, steady)

    def between(*refs):
        arrived_refs, refs = refs[:arrived_count], refs[arrived_count:]
        (
            nodes_ref,
            grid_first_ref,
            grid_second_ref,
            cot_ref,
            mesh_second_ref,
            dec_second_ref,
            mesh_ref,
            mesh_cot_ref,
            dec_normed_ref,
            dec_scale_ref,
            dec_pre_ref,
            mesh_normed_ref,
            mesh_pre_ref,
            mesh_wide_ref,
            part_ref,
            cot_rows_ref,
            cot_turned_ref,
            grid_wide_ref,
            grid_back_ref,
            mesh_out_ref,
            mesh_cot_turned_ref,
            mesh_slope_ref,
            mesh_turned_ref,
            dec_gain_ref,
            dec_turned_ref,
        ) = refs
        part_ref[:grid_count, :] = mm(nodes_ref[...], grid_first_ref[low, :])
        part_ref[grid_count:, :] = mm(by_slot(arrived_refs, low, staggered), grid_first_ref[low, :])
        mesh_out_ref[...] = (mesh_ref[...].astype(F32) + mesh_normed_ref[...]).astype(BF16)
        cot_rows_ref[:grid_count, :] = cot_ref[...]
        cot_rows_ref[grid_count:, :] = by_slot(arrived_refs, high, staggered)
        second = centred(grid_second_ref[...], 1).astype(BF16)
        grid_wide_ref[:, low] = second
        grid_wide_ref[:, high] = mm_t(second, grid_second_ref[...]).astype(BF16)
        cot_turned_ref[...] = mm_t(cot_rows_ref[...], second)
        grid_back_ref[low, :] = centred(grid_first_ref[high, :], 0).astype(BF16)
        grid_back_ref[high, :] = mm(dec_second_ref[...], grid_back_ref[low, :]).astype(BF16)
        mesh_cot_turned_ref[...] = mm_t(mesh_cot_ref[...], mesh_wide_ref[:, low])
        mesh_turned_ref[...] = mm_t(mesh_normed_ref[...].astype(BF16), mesh_second_ref[...])
        mesh_slope_ref[...] = silu_and_slope(mesh_pre_ref[...])[1]
        write_slopes(
            dec_pre_ref,
            dec_normed_ref,
            dec_scale_ref,
            dec_second_ref,
            dec_gain_ref,
            dec_turned_ref,
        )

    (
        grid_part,
        cot_rows,
        cot_turned,
        grid_wide,
        grid_back,
        mesh_out,
        mesh_cot_turned,
        mesh_slope,
        mesh_turned,
        dec_gain,
        dec_turned,
    ) = call(
        between,
        "slopes_and_nodes",
        [
            *arrived,
            grid_nodes,
            grid_first,
            grid_second,
            grid_cot,
            mesh_second,
            dec_second,
            mesh_nodes,
            mesh_cot,
            dec_normed,
            dec_scale,
            dec_pre,
            mesh_normed,
            mesh_pre,
            mesh_wide,
        ],
        [
            ((spots, feat), F32),
            ((spots, feat), BF16),
            ((spots, feat), F32),
            ((feat, 2 * feat), BF16),
            ((2 * feat, feat), BF16),
            ((mesh_count, feat), BF16),
            ((mesh_count, feat), F32),
            ((mesh_count, feat), F32),
            ((mesh_count, feat), F32),
            ((dec_count, feat), BF16),
            ((dec_count, feat), BF16),
        ],
        flops=16 * spots * feat * feat,
    )

    def backward(*refs):
        returned_refs, refs = refs[:arrived_count], refs[arrived_count:]
        (
            spot_ref,
            grid_part_ref,
            select_t_ref,
            cot_rows_ref,
            cot_turned_ref,
            mesh_cot_ref,
            mesh_cot_turned_ref,
            enc_pick_ref,
            enc_pool_ref,
            dec_pick_ref,
            dec_pool_ref,
            grid_first_ref,
            grid_wide_ref,
            grid_back_ref,
            mesh_first_ref,
            mesh_wide_ref,
            enc_first_ref,
            enc_second_ref,
            dec_first_ref,
            enc_normed_ref,
            enc_scale_ref,
            enc_pre_ref,
            dec_normed_ref,
            dec_gain_ref,
            dec_turned_ref,
            mesh_normed_ref,
            mesh_scale_ref,
            mesh_slope_ref,
            mesh_turned_ref,
        ) = refs[:29]
        refs = refs[29:]
        out_refs, refs = refs[:sent_count], refs[sent_count:]
        (
            grid_normed_ref,
            grid_gpre_ref,
            dec_gpre_ref,
            enc_gpre_ref,
            mesh_gin_ref,
            mesh_gpre_ref,
            agg_ref,
            grid_act_ref,
            grid_slope_ref,
            spot_grad_ref,
            mesh_in_ref,
            mesh_back_ref,
            enc_gain_ref,
            enc_turned_ref,
        ) = refs
        agg_ref[:grid_count, :] = (
            spot_ref[:grid_count, :] + mm(select_t_ref[:, :slots], by_row(returned_refs, low))
        ).astype(BF16)
        agg_ref[grid_count:, :] = (
            spot_ref[grid_count:, :] + by_slot(returned_refs, high).astype(F32)
        ).astype(BF16)
        pre = grid_part_ref[...] + mm(agg_ref[...], grid_first_ref[high, :])
        mesh_in_ref[low, :] = dec_first_ref[high, :]
        mesh_in_ref[high, :] = mm(mesh_wide_ref[:, low], dec_first_ref[high, :]).astype(BF16)
        for rows in row_chunks(spots):
            act, slope = silu_and_slope(pre[rows, :])
            grid_act_ref[rows, :] = act.astype(BF16)
            grid_slope_ref[rows, :] = slope
        both = mm(grid_act_ref[...], grid_wide_ref[...])
        mesh_back_ref[low, :] = centred(mesh_first_ref[high, :], 0).astype(BF16)
        mesh_back_ref[high, :] = mm(enc_second_ref[...], mesh_back_ref[low, :]).astype(BF16)
        for rows in row_chunks(spots):
            part = both[rows, low]
            scale_inv = scale_rows(part)
            normed = part * scale_inv
            grid_normed_ref[rows, :] = normed
            mean = jnp.mean(cot_rows_ref[rows, :].astype(F32) * normed, axis=-1, keepdims=True)
            raw = scale_inv * (cot_turned_ref[rows, :] - (mean * scale_inv) * both[rows, high])
            grid_gpre_ref[rows, :] = (raw * grid_slope_ref[rows, :]).astype(BF16)
        spot_grad_ref[:spots, :] = mm_t(grid_gpre_ref[...], grid_back_ref[...]).astype(BF16)
        spot_grad_ref[spots:, :] = jnp.zeros((total - spots, 2 * feat), BF16)
        write_slopes(
            enc_pre_ref,
            enc_normed_ref,
            enc_scale_ref,
            enc_second_ref,
            enc_gain_ref,
            enc_turned_ref,
        )
        edge_back(
            mm(dec_pick_ref[...], spot_grad_ref[...]),
            dec_normed_ref,
            dec_gain_ref,
            dec_turned_ref,
            dec_gpre_ref,
        )
        mesh_sum = mm(dec_pool_ref[mesh_rows, :], dec_gpre_ref[...]).astype(BF16)
        both = mm_t(mesh_sum, mesh_in_ref[...])
        mesh_gin = mesh_cot_ref[...].astype(F32) + both[:, low]
        mesh_gin_ref[...] = mesh_gin
        mean = jnp.mean(mesh_gin * mesh_normed_ref[...], axis=-1, keepdims=True)
        raw = mesh_cot_turned_ref[...] + both[:, high] - mean * mesh_turned_ref[...]
        mesh_gpre_ref[...] = (mesh_scale_ref[...] * raw * mesh_slope_ref[...]).astype(BF16)
        mesh_gagg = mm_t(mesh_gpre_ref[...], mesh_back_ref[...]).astype(BF16)
        pooled = mm(dec_pool_ref[grid_count:spots, :], dec_gpre_ref[...]).astype(BF16)
        slot_back = mm_t(pooled, dec_first_ref[low, :])
        edge_back(
            mm(enc_pick_ref[:, mesh_rows], mesh_gagg),
            enc_normed_ref,
            enc_gain_ref,
            enc_turned_ref,
            enc_gpre_ref,
        )
        pooled = mm(enc_pool_ref[grid_count:spots, :], enc_gpre_ref[...]).astype(BF16)
        slot_back = (slot_back + mm_t(pooled, enc_first_ref[low, :])).astype(BF16)
        send(out_refs, lambda j: slot_back[reverse[j] * width : (reverse[j] + 1) * width, :])

    results = call(
        backward,
        "edges_backward",
        [
            *returned,
            spot_msg,
            grid_part,
            select_t,
            cot_rows,
            cot_turned,
            mesh_cot,
            mesh_cot_turned,
            enc_pick,
            enc_pool,
            dec_pick,
            dec_pool,
            grid_first,
            grid_wide,
            grid_back,
            mesh_first,
            mesh_wide,
            enc_first,
            enc_second,
            dec_first,
            enc_normed,
            enc_scale,
            enc_pre,
            dec_normed,
            dec_gain,
            dec_turned,
            mesh_normed,
            mesh_scale,
            mesh_slope,
            mesh_turned,
        ],
        sent_shapes(feat)
        + [
            ((spots, feat), F32),
            ((spots, feat), BF16),
            ((dec_count, feat), BF16),
            ((enc_count, feat), BF16),
            ((mesh_count, feat), F32),
            ((mesh_count, feat), BF16),
        ],
        scratch=[
            ((spots, feat), BF16),
            ((spots, feat), BF16),
            ((spots, feat), F32),
            ((total, 2 * feat), BF16),
            ((2 * feat, feat), BF16),
            ((2 * feat, feat), BF16),
            ((enc_count, feat), BF16),
            ((enc_count, feat), BF16),
        ],
        flops=2 * feat * feat * (4 * spots + 3 * dec_count + 2 * enc_count),
    )
    outgoing, results = results[:sent_count], results[sent_count:]
    grid_normed, grid_gpre, dec_gpre, enc_gpre, mesh_gin, mesh_gpre = results
    final = exchange(outgoing, steady)

    def tail(
        nodes_ref,
        grid_normed_ref,
        cot_ref,
        grid_gpre_ref,
        enc_pool_ref,
        enc_gpre_ref,
        dec_pool_ref,
        dec_gpre_ref,
        mesh_gin_ref,
        mesh_gpre_ref,
        grid_wn_ref,
        enc_wg_ref,
        dec_wg_ref,
        mesh_wn_ref,
        enc_wm_ref,
        base_ref,
        grad_mesh_ref,
        grid_out_ref,
    ):
        grid_out_ref[...] = (
            nodes_ref[...].astype(F32) + grid_normed_ref[:grid_count, :]
        ).astype(BF16)
        enc_sums = mm(enc_pool_ref[...], enc_gpre_ref[...]).astype(BF16)
        dec_sums = mm(dec_pool_ref[:grid_count, :], dec_gpre_ref[...]).astype(BF16)
        base_ref[...] = (
            cot_ref[...].astype(F32)
            + mm_t(grid_gpre_ref[:grid_count, :], grid_wn_ref[low, :])
            + mm_t(enc_sums[:grid_count, :], enc_wg_ref[low, :])
            + mm_t(dec_sums, dec_wg_ref[low, :])
        )
        grad_mesh_ref[...] = (
            mesh_gin_ref[...]
            + mm_t(mesh_gpre_ref[...], mesh_wn_ref[low, :])
            + mm_t(enc_sums[mesh_rows, :], enc_wm_ref[high, :])
        )

    base, grad_mesh, grid_out = call(
        tail,
        "local_gradients",
        [
            grid_nodes,
            grid_normed,
            grid_cot,
            grid_gpre,
            enc_pool,
            enc_gpre,
            dec_pool,
            dec_gpre,
            mesh_gin,
            mesh_gpre,
            grid_first,
            enc_first,
            dec_first,
            mesh_first,
            enc_first,
        ],
        [((grid_count, feat), F32), ((mesh_count, feat), F32), ((grid_count, feat), BF16)],
        flops=2 * feat * feat * 3 * grid_count,
    )

    pieces = row_chunks(grid_count, 64)

    def finish(*refs):
        back_refs = refs[:arrived_count]
        base_ref, select_t_ref, out_ref, piece_ref, semaphores = refs[arrived_count:]
        back = by_row(back_refs)
        copies = []
        for place, rows in enumerate(pieces):
            piece_ref[rows, :] = base_ref[rows, :] + mm(select_t_ref[rows, :slots], back)
            copies.append(
                pltpu.make_async_copy(
                    piece_ref.at[rows, :], out_ref.at[rows, :], semaphores.at[place]
                )
            )
            copies[-1].start()
        for copy in copies:
            copy.wait()

    grad_grid = pl.pallas_call(
        finish,
        name="add_returned",
        in_specs=[pl.BlockSpec(memory_space=pltpu.VMEM)] * (arrived_count + 2),
        out_specs=pl.BlockSpec(memory_space=pltpu.HBM),
        out_shape=jax.ShapeDtypeStruct((grid_count, feat), F32),
        scratch_shapes=[
            pltpu.VMEM((grid_count, feat), F32),
            pltpu.SemaphoreType.DMA((len(pieces),)),
        ],
        compiler_params=pltpu.CompilerParams(vmem_limit_bytes=VMEM_LIMIT),
    )(*final, base, select_t)
    return (grid_out, mesh_out, grad_grid, grad_mesh)


def solution(mesh):
    rows = P(("groups", "tile"), None)
    flat = P(("groups", "tile"))
    in_specs = (rows,) * 6 + (P(),) * 8 + (rows,) + (flat,) * 5
    return jax.shard_map(
        per_device, mesh=mesh, in_specs=in_specs, out_specs=(rows,) * 4, check_vma=False
    )
```

```python
import jax
import jax.numpy as jnp
from jax import lax
from jax.experimental import pallas as pl
from jax.experimental.pallas import tpu as pltpu
from jax.sharding import PartitionSpec as P

TW = 4
CHUNK = 32
ROUND_FLOPS = 2 * 10**10
F32 = jnp.float32
BF16 = jnp.bfloat16
VMEM_LIMIT = 30 * 1024 * 1024


def mm(left, right):
    return jnp.dot(left, right, preferred_element_type=F32)


def mm_t(left, right):
    return lax.dot_general(left, right, (((1,), (1,)), ((), ())), preferred_element_type=F32)


def centred(values, axis):
    values = values.astype(F32)
    return values - jnp.mean(values, axis=axis, keepdims=True)


def silu_and_slope(pre):
    half = 0.5 * pre
    lifted = 1.0 + jnp.tanh(half)
    return half * lifted, lifted * (0.5 + 0.5 * half * (2.0 - lifted))


def silu(pre):
    half = 0.5 * pre
    return half * (1.0 + jnp.tanh(half))


def scale_rows(raw):
    return lax.rsqrt(jnp.mean(raw * raw, axis=-1, keepdims=True) + 1e-05)


def row_chunks(rows, size=CHUNK):
    return [slice(start, min(start + size, rows)) for start in range(0, rows, size)]


def write_silu(pre, act_ref):
    for rows in row_chunks(pre.shape[0]):
        act_ref[rows, :] = silu(pre[rows, :]).astype(BF16)


def write_norm(raw, normed_ref, scale_ref):
    for rows in row_chunks(raw.shape[0]):
        part = raw[rows, :]
        scale_inv = scale_rows(part)
        normed_ref[rows, :] = (part * scale_inv).astype(normed_ref.dtype)
        scale_ref[rows, :] = scale_inv


def write_slope(pre_ref, slope_ref):
    for rows in row_chunks(pre_ref.shape[0]):
        slope_ref[rows, :] = silu_and_slope(pre_ref[rows, :])[1].astype(BF16)


def edge_back(upstream, normed_ref, scale_ref, second_ref, slope_ref, out_ref):
    for rows in row_chunks(upstream.shape[0]):
        part, normed = upstream[rows, :], normed_ref[rows, :]
        mean = jnp.mean(part * normed.astype(F32), axis=-1, keepdims=True)
        out_ref[rows, :] = scale_ref[rows, :].astype(BF16) * (
            part.astype(BF16) - normed * mean.astype(BF16)
        )
    raw = mm_t(out_ref[...], second_ref[...])
    for rows in row_chunks(upstream.shape[0]):
        out_ref[rows, :] = raw[rows, :].astype(BF16) * slope_ref[rows, :]


def neighbour_offsets(peer_count):
    forward_half = [1, TW, TW + 1, TW - 1]
    return forward_half + [-offset for offset in forward_half] + [peer_count // 2]


def onehot_pair(spot_ref, mesh_ref, spots, mesh_count, by_edge_ref, by_spot_ref):
    edges, total = by_edge_ref.shape
    spot_row = spot_ref[...].reshape(1, -1)
    mesh_row = mesh_ref[...].reshape(1, -1) + spots
    one, zero = jnp.ones((), BF16), jnp.zeros((), BF16)

    def ones(ids, index):
        shape = jnp.broadcast_shapes(ids.shape, index.shape)
        hit = jnp.broadcast_to(ids, shape) == jnp.broadcast_to(index, shape)
        return jnp.where(hit, jnp.broadcast_to(one, shape), jnp.broadcast_to(zero, shape))

    for row, first, count in ((spot_row, 0, spots), (mesh_row, spots, mesh_count)):
        ids = lax.broadcasted_iota(jnp.int32, (16, edges), 0).astype(jnp.int16)
        wide = jnp.broadcast_to(row, (16, edges)).astype(jnp.int16)
        for rows in row_chunks(count, 16):
            rows = slice(rows.start + first, rows.stop + first)
            by_spot_ref[rows, :] = ones(ids, wide - jnp.int16(rows.start))
    by_spot_ref[spots + mesh_count :, :] = jnp.zeros((total - spots - mesh_count, edges), BF16)
    lane = lax.broadcasted_iota(jnp.int32, (16, 128), 1).astype(jnp.int16)
    for rows in row_chunks(edges, 128):
        spot_col = jnp.broadcast_to(spot_row[:, rows], (128, 128)).T.astype(jnp.int16)
        mesh_col = jnp.broadcast_to(mesh_row[:, rows], (128, 128)).T.astype(jnp.int16)
        for columns in row_chunks(total, 128):
            for part in row_chunks(128, 16):
                place = slice(rows.start + part.start, rows.start + part.stop)
                ids = lane + jnp.int16(columns.start)
                hits = []
                if columns.start < spots:
                    hits.append(ones(ids, spot_col[part, :]))
                if columns.stop > spots:
                    hits.append(ones(ids, mesh_col[part, :]))
                by_edge_ref[place, columns] = sum(hits[1:], hits[0])


class Fetched:
    def __init__(self, source, target, semaphore):
        self.copy = pltpu.make_async_copy(source, target, semaphore)
        self.target = target
        self.landed = False
        self.copy.start()

    def land(self):
        if not self.landed:
            self.copy.wait()
            self.landed = True

    def __getitem__(self, key):
        self.land()
        return self.target[key]


def call(body, name, inputs, outputs, scratch=(), flops=0):
    arrays, specs, moved, fetches = [], [], 0, []
    for place, entry in enumerate(inputs):
        if isinstance(entry, tuple):
            array, first, rows = entry
            array = pltpu.with_memory_space_constraint(array, pltpu.HBM)
            specs.append(pl.BlockSpec(memory_space=pltpu.HBM))
            shape = (rows,) + array.shape[1:]
            fetches.append((place, first, rows, shape, array.dtype))
            moved += rows * (array.size // array.shape[0]) * array.dtype.itemsize
        else:
            array = entry
            specs.append(pl.BlockSpec(memory_space=pltpu.VMEM))
            moved += array.size * array.dtype.itemsize
        arrays.append(array)
    shapes = [jax.ShapeDtypeStruct(shape, dtype) for shape, dtype in outputs]
    for shape in shapes:
        moved += shape.size * shape.dtype.itemsize
    buffers = [pltpu.VMEM(shape, dtype) for _, _, _, shape, dtype in fetches]
    if fetches:
        buffers.append(pltpu.SemaphoreType.DMA((len(fetches),)))

    def kernel(*refs):
        refs = list(refs)
        waiting = []
        if fetches:
            targets, semaphores = refs[-len(buffers) : -1], refs[-1]
            refs = refs[: -len(buffers)]
        for slot, (place, first, rows, shape, _) in enumerate(fetches):
            source = refs[place]
            if source.shape != shape:
                source = source.at[pl.ds(first, rows)]
            refs[place] = Fetched(source, targets[slot], semaphores.at[slot])
            waiting.append(refs[place])
        body(*refs)
        for fetched in waiting:
            fetched.land()

    return pl.pallas_call(
        kernel,
        name=name,
        in_specs=specs,
        out_specs=[pl.BlockSpec(memory_space=pltpu.VMEM) for _ in shapes],
        out_shape=shapes,
        scratch_shapes=[pltpu.VMEM(shape, dtype) for shape, dtype in scratch]
        + buffers,
        compiler_params=pltpu.CompilerParams(vmem_limit_bytes=VMEM_LIMIT),
        cost_estimate=pl.CostEstimate(flops=flops, bytes_accessed=moved, transcendentals=0),
    )(*arrays)


def per_device(
    grid_nodes,
    mesh_nodes,
    enc_edges,
    dec_edges,
    grid_cot,
    mesh_cot,
    enc_first,
    enc_second,
    mesh_first,
    mesh_second,
    dec_first,
    dec_second,
    grid_first,
    grid_second,
    send_index,
    send_count,
    enc_grid,
    enc_mesh,
    dec_grid,
    dec_mesh,
):
    grid_count, feat = grid_nodes.shape
    mesh_count = mesh_nodes.shape[0]
    enc_count = enc_edges.shape[0]
    dec_count = dec_edges.shape[0]
    links, width = send_index.shape
    slots = links * width
    slots_pad = -(-slots // 128) * 128
    spots = grid_count + slots
    total = -(-(spots + mesh_count) // 128) * 128
    peer_count = lax.axis_size("tile")
    offsets = neighbour_offsets(peer_count)
    half = (links - 1) // 2
    reverse = [(j + half) % (links - 1) for j in range(links - 1)] + [links - 1]
    low, high = slice(0, feat), slice(feat, 2 * feat)
    mesh_rows = slice(spots, spots + mesh_count)

    one, four, five, three = range(half)
    minus = [j + half for j in range(half)]
    across = links - 1
    peers = range(peer_count)

    def permute(part, steps, odd_row_steps=None):
        rows = (steps, odd_row_steps or steps)
        pairs = [(s, (s + rows[s // TW % 2][s % 2]) % peer_count) for s in peers]
        return lax.ppermute(part, "tile", pairs)

    steady = ("late", "early", "behind", "ahead", "five", "opposite", "own")
    staggered = ("early", "late", "ahead", "five", "behind", "opposite", "own")
    arrived_count = 9

    def exchange(parts, order):
        moves = {
            "late": ((-4, -4), (4, 4)),
            "early": ((4, 4), (-4, -4)),
            "behind": ((-1, 1),),
            "ahead": ((3, -3),),
            "five": ((-5, 5),),
            "opposite": ((peer_count // 2, peer_count // 2),),
            "own": ((1, -1),),
        }
        parts = dict(zip(order, parts))
        own_chip = parts.pop("own")
        got = {name: permute(part, *moves[name]) for name, part in parts.items()}
        first = order[0]
        got[first], own_chip = lax.optimization_barrier((got[first], own_chip))
        late_passed = permute(got["late"], (1, -1))
        got["own"] = permute(own_chip, (1, -1))
        early_passed = permute(got["early"], (1, -1))
        return [got[name] for name in order] + [late_passed, early_passed]

    def sent_shapes(columns, order=steady):
        double = ("late", "early")
        return [((width * (1 + (name in double)), columns), BF16) for name in order]

    sent_count = len(steady)

    def place_bits():
        own = lax.axis_index("tile")
        return lax.rem(own, 2) == 1, lax.rem(lax.div(own, TW), 2) == 1

    def send(refs, message, columns=slice(None), order=steady):
        odd, odd_row = place_bits()
        refs = dict(zip(order, refs))

        def by_parity(even, odd_one):
            return jnp.where(odd, message(odd_one), message(even))

        late_pair, early_pair, behind_one, ahead_three, five_off, opposite, own_chip = [
            refs[name] for name in steady
        ]
        first, second = slice(0, width), slice(width, 2 * width)
        ahead = message(four), by_parity(five, three)
        behind = message(minus[four]), by_parity(minus[three], minus[five])
        for rows, go_ahead, go_behind in zip((first, second), ahead, behind):
            late_pair[rows, columns] = jnp.where(odd_row, go_ahead, go_behind)
            early_pair[rows, columns] = jnp.where(odd_row, go_behind, go_ahead)
        behind_one[:, columns] = by_parity(minus[one], one)
        ahead_three[:, columns] = by_parity(three, minus[three])
        five_off[:, columns] = by_parity(minus[five], five)
        opposite[:, columns] = message(across)
        own_chip[:, columns] = by_parity(one, minus[one])

    def receive(refs, columns=slice(None), order=steady):
        odd, odd_row = place_bits()
        late_passed, early_passed = refs[sent_count:]
        refs = dict(zip(order, refs))
        late_pair, early_pair, behind_one, ahead_three, five_off, opposite, own_chip = [
            refs[name] for name in steady
        ]
        first, second = slice(0, width), slice(width, 2 * width)
        near, near_three = behind_one[:, columns], ahead_three[:, columns]
        far, own = five_off[:, columns], own_chip[:, columns]
        late_rows, early_rows = late_passed[second, columns], early_passed[second, columns]
        from_behind = jnp.where(odd_row, early_rows, late_rows)
        from_ahead = jnp.where(odd_row, late_rows, early_rows)
        late_rows, early_rows = late_pair[first, columns], early_pair[first, columns]
        slot_rows = [None] * links
        slot_rows[one] = jnp.where(odd, own, near)
        slot_rows[minus[one]] = jnp.where(odd, near, own)
        slot_rows[three] = jnp.where(odd, near_three, from_behind)
        slot_rows[minus[three]] = jnp.where(odd, from_ahead, near_three)
        slot_rows[five] = jnp.where(odd, from_behind, far)
        slot_rows[minus[five]] = jnp.where(odd, far, from_ahead)
        slot_rows[four] = jnp.where(odd_row, early_rows, late_rows)
        slot_rows[minus[four]] = jnp.where(odd_row, late_rows, early_rows)
        slot_rows[across] = opposite[:, columns]
        return slot_rows

    def by_slot(refs, columns=slice(None), order=steady):
        return jnp.concatenate(receive(refs, columns, order), axis=0)

    def by_row(refs, columns=slice(None)):
        slot_rows = receive(refs, columns)
        return jnp.concatenate([slot_rows[reverse[j]] for j in range(links)], axis=0)

    def pack(index_ref, count_ref, nodes_ref, cot_ref, select_ref, *out_refs):
        def column(row):
            count = row.shape[1]
            eye = lax.broadcasted_iota(jnp.int32, (count, count), 0) == lax.broadcasted_iota(
                jnp.int32, (count, count), 1
            )
            return jnp.sum(
                jnp.where(eye, jnp.broadcast_to(row, (count, count)), 0.0), axis=1, keepdims=True
            )

        counts = column(count_ref[...].reshape(1, -1).astype(F32))
        place = lax.broadcasted_iota(jnp.int32, (links, width), 1).astype(F32)
        index = jnp.where(place < counts, index_ref[...].astype(F32), -1.0)
        lane = lax.broadcasted_iota(jnp.int32, (width, grid_count), 1).astype(F32)
        picks = [
            jnp.where(lane == column(index[j : j + 1, :]), 1.0, 0.0).astype(BF16)
            for j in range(links)
        ]
        select = jnp.concatenate(picks, axis=0)
        select_ref[:slots, :] = select
        select_ref[slots:, :] = jnp.zeros((slots_pad - slots, grid_count), BF16)
        sent_nodes = mm(select, nodes_ref[...]).astype(BF16)
        sent_cot = mm(select, cot_ref[...]).astype(BF16)
        send(
            out_refs, lambda j: sent_nodes[j * width : (j + 1) * width, :], low, staggered
        )
        send(out_refs, lambda j: sent_cot[j * width : (j + 1) * width, :], high, staggered)

    select, *outgoing = call(
        pack,
        "pack_rows",
        [
            (send_index, 0, links),
            (send_count, 0, links),
            (grid_nodes, 0, grid_count),
            (grid_cot, 0, grid_count),
        ],
        [((slots_pad, grid_count), BF16)] + sent_shapes(2 * feat, staggered),
        flops=4 * slots * grid_count * feat,
    )
    def turn(select_ref, select_t_ref):
        select_t_ref[...] = select_ref[...].astype(F32).T.astype(BF16)

    (select_t,) = call(
        turn, "turn_select", [select], [((grid_count, slots_pad), BF16)], flops=ROUND_FLOPS
    )
    *outgoing, select_t = lax.optimization_barrier((*outgoing, select_t))
    arrived = exchange(outgoing, staggered)

    def local(
        select_ref,
        nodes_ref,
        mesh_ref,
        enc_edges_ref,
        dec_edges_ref,
        enc_first_ref,
        dec_first_ref,
        mesh_first_ref,
        enc_grid_ref,
        enc_mesh_ref,
        dec_grid_ref,
        dec_mesh_ref,
        enc_second_ref,
        mesh_second_ref,
        dec_second_ref,
        enc_part_ref,
        dec_part_ref,
        mesh_part_ref,
        enc_pick_ref,
        enc_pool_ref,
        dec_pick_ref,
        dec_pool_ref,
        enc_centred_ref,
        dec_centred_ref,
        mesh_wide_ref,
        mesh_base_ref,
        shared_pool_ref,
        table_ref,
    ):
        onehot_pair(enc_grid_ref, enc_mesh_ref, spots, mesh_count, enc_pick_ref, enc_pool_ref)
        onehot_pair(dec_grid_ref, dec_mesh_ref, spots, mesh_count, dec_pick_ref, dec_pool_ref)
        enc_centred_ref[...] = centred(enc_second_ref[...], 1).astype(BF16)
        mesh_centred = centred(mesh_second_ref[...], 1).astype(BF16)
        mesh_wide_ref[:, low] = mesh_centred
        mesh_wide_ref[:, high] = mm(mesh_centred, dec_first_ref[high, :]).astype(BF16)
        mesh_base_ref[...] = mm(mesh_ref[...], dec_first_ref[high, :])
        shared_pool_ref[...] = mm(
            select_ref[:slots, :], dec_pool_ref[:grid_count, :]
        ).astype(BF16)
        dec_centred_ref[...] = centred(dec_second_ref[...], 1).astype(BF16)
        nodes = nodes_ref[...]
        mesh_part_ref[...] = mm(mesh_ref[...], mesh_first_ref[low, :])
        table_ref[:grid_count, :] = mm(nodes, enc_first_ref[low, :]).astype(BF16)
        table_ref[grid_count:, :] = jnp.zeros((total - grid_count, feat), BF16)
        table_ref[mesh_rows, :] = mm(mesh_ref[...], enc_first_ref[high, :]).astype(BF16)
        enc_part_ref[...] = mm(enc_edges_ref[...], enc_first_ref[2 * feat :, :])
        enc_part_ref[...] += mm(enc_pick_ref[...], table_ref[...])
        pd = mm(nodes, dec_first_ref[low, :]).astype(BF16)
        dec_part_ref[...] = mm(dec_edges_ref[...], dec_first_ref[2 * feat :, :])
        dec_part_ref[...] += mm(dec_pick_ref[:, :grid_count], pd)

    (
        enc_part,
        dec_part,
        mesh_part,
        enc_pick,
        enc_pool,
        dec_pick,
        dec_pool,
        enc_centred,
        dec_centred,
        mesh_wide,
        mesh_base,
        shared_pool,
    ) = call(
        local,
        "local_products",
        [
            select,
            grid_nodes,
            mesh_nodes,
            enc_edges,
            dec_edges,
            enc_first,
            dec_first,
            mesh_first,
            enc_grid,
            enc_mesh,
            dec_grid,
            dec_mesh,
            enc_second,
            mesh_second,
            dec_second,
        ],
        [
            ((enc_count, feat), F32),
            ((dec_count, feat), F32),
            ((mesh_count, feat), F32),
            ((enc_count, total), BF16),
            ((total, enc_count), BF16),
            ((dec_count, total), BF16),
            ((total, dec_count), BF16),
        ]
        + [
            ((feat, feat), BF16),
            ((feat, feat), BF16),
            ((feat, 2 * feat), BF16),
            ((mesh_count, feat), F32),
            ((slots, dec_count), BF16),
        ],
        scratch=[((total, feat), BF16)],
        flops=2 * feat * (feat * (2 * grid_count + enc_count + dec_count) + total * dec_count),
    )

    def forward(*refs):
        arrived_refs, refs = refs[:arrived_count], refs[arrived_count:]
        (
            shared_pool_ref,
            enc_part_ref,
            dec_part_ref,
            mesh_part_ref,
            enc_pick_ref,
            enc_pool_ref,
            dec_pick_ref,
            dec_pool_ref,
            enc_wg_ref,
            dec_wg_ref,
            enc_w2_ref,
            mesh_wa_ref,
            mesh_w2_ref,
            mesh_base_ref,
            dec_w2_ref,
        ) = refs[:15]
        refs = refs[15:]
        out_refs, refs = refs[:sent_count], refs[sent_count:]
        (
            spot_ref,
            enc_normed_ref,
            enc_scale_ref,
            enc_pre_ref,
            dec_normed_ref,
            dec_scale_ref,
            dec_pre_ref,
            mesh_normed_ref,
            mesh_scale_ref,
            mesh_pre_ref,
            enc_act_ref,
            dec_act_ref,
            mesh_act_ref,
            table_ref,
        ) = refs
        rows = by_slot(arrived_refs, low, staggered)
        pe = mm(rows, enc_wg_ref[low, :]).astype(BF16)
        enc_pre_ref[...] = enc_part_ref[...] + mm(enc_pick_ref[:, grid_count:spots], pe)
        write_silu(enc_pre_ref, enc_act_ref)
        write_norm(mm(enc_act_ref[...], enc_w2_ref[...]), enc_normed_ref, enc_scale_ref)
        agg = mm(enc_pool_ref[mesh_rows, :], enc_normed_ref[...]).astype(BF16)
        mesh_pre_ref[...] = mesh_part_ref[...] + mm(agg, mesh_wa_ref[high, :])
        write_silu(mesh_pre_ref, mesh_act_ref)
        both = mm(mesh_act_ref[...], mesh_w2_ref[...])
        write_norm(both[:, low], mesh_normed_ref, mesh_scale_ref)
        mesh_sent = mesh_base_ref[...] + mesh_scale_ref[...] * both[:, high]
        table_ref[:slots, :] = mm(rows, dec_wg_ref[low, :]).astype(BF16)
        table_ref[slots : slots + mesh_count, :] = mesh_sent.astype(BF16)
        table_ref[slots + mesh_count :, :] = jnp.zeros(
            (total - spots - mesh_count, feat), BF16
        )
        dec_pre_ref[...] = dec_part_ref[...] + mm(dec_pick_ref[:, grid_count:], table_ref[...])
        write_silu(dec_pre_ref, dec_act_ref)
        write_norm(mm(dec_act_ref[...], dec_w2_ref[...]), dec_normed_ref, dec_scale_ref)
        spot_ref[...] = mm(dec_pool_ref[:spots, :], dec_normed_ref[...])
        shared = mm(shared_pool_ref[...], dec_normed_ref[...]).astype(BF16)
        slot_msg = spot_ref[grid_count:, :].astype(BF16)
        send(
            out_refs, lambda j: slot_msg[reverse[j] * width : (reverse[j] + 1) * width, :], low
        )
        send(out_refs, lambda j: shared[j * width : (j + 1) * width, :], high)

    saved_shapes = [
        ((enc_count, feat), BF16),
        ((enc_count, 1), F32),
        ((enc_count, feat), F32),
        ((dec_count, feat), BF16),
        ((dec_count, 1), F32),
        ((dec_count, feat), F32),
        ((mesh_count, feat), F32),
        ((mesh_count, 1), F32),
        ((mesh_count, feat), F32),
    ]
    results = call(
        forward,
        "edges_forward",
        [
            *arrived,
            shared_pool,
            enc_part,
            dec_part,
            mesh_part,
            enc_pick,
            enc_pool,
            dec_pick,
            dec_pool,
            enc_first,
            dec_first,
            enc_centred,
            mesh_first,
            mesh_wide,
            mesh_base,
            dec_centred,
        ],
        sent_shapes(2 * feat)
        + [((spots, feat), F32)]
        + saved_shapes,
        scratch=[
            ((enc_count, feat), BF16),
            ((dec_count, feat), BF16),
            ((mesh_count, feat), BF16),
            ((total - grid_count, feat), BF16),
        ],
        flops=2 * feat * feat * 2 * (enc_count + dec_count),
    )
    outgoing, results = results[:sent_count], results[sent_count:]
    spot_msg, *saved = results
    enc_normed, enc_scale, enc_pre, dec_normed, dec_scale, dec_pre = saved[:6]
    mesh_normed, mesh_scale, mesh_pre = saved[6:]
    returned = exchange(outgoing, steady)

    def between(*refs):
        arrived_refs, refs = refs[:arrived_count], refs[arrived_count:]
        (
            nodes_ref,
            grid_first_ref,
            grid_second_ref,
            cot_ref,
            mesh_first_ref,
            mesh_second_ref,
            dec_first_ref,
            mesh_ref,
            mesh_cot_ref,
            enc_pre_ref,
            dec_pre_ref,
            mesh_normed_ref,
            mesh_pre_ref,
            mesh_wide_ref,
            part_ref,
            cot_rows_ref,
            cot_turned_ref,
            grid_wide_ref,
            grid_back_ref,
            mesh_back_ref,
            mesh_in_ref,
            mesh_out_ref,
            mesh_cot_turned_ref,
            mesh_slope_ref,
            mesh_turned_ref,
            enc_slope_ref,
            dec_slope_ref,
        ) = refs
        part_ref[:grid_count, :] = mm(nodes_ref[...], grid_first_ref[low, :])
        part_ref[grid_count:, :] = mm(by_slot(arrived_refs, low, staggered), grid_first_ref[low, :])
        mesh_out_ref[...] = (mesh_ref[...].astype(F32) + mesh_normed_ref[...]).astype(BF16)
        cot_rows_ref[:grid_count, :] = cot_ref[...]
        cot_rows_ref[grid_count:, :] = by_slot(arrived_refs, high, staggered)
        second = centred(grid_second_ref[...], 1).astype(BF16)
        grid_wide_ref[:, low] = second
        grid_wide_ref[:, high] = mm_t(second, grid_second_ref[...]).astype(BF16)
        cot_turned_ref[...] = mm_t(cot_rows_ref[...], second)
        grid_back_ref[...] = centred(grid_first_ref[high, :], 0).astype(BF16)
        mesh_back_ref[...] = centred(mesh_first_ref[high, :], 0).astype(BF16)
        mesh_in_ref[low, :] = dec_first_ref[high, :]
        mesh_in_ref[high, :] = mm(mesh_wide_ref[:, low], dec_first_ref[high, :]).astype(BF16)
        mesh_cot_turned_ref[...] = mm_t(mesh_cot_ref[...], mesh_wide_ref[:, low])
        mesh_turned_ref[...] = mm_t(mesh_normed_ref[...].astype(BF16), mesh_second_ref[...])
        mesh_slope_ref[...] = silu_and_slope(mesh_pre_ref[...])[1]
        write_slope(enc_pre_ref, enc_slope_ref)
        write_slope(dec_pre_ref, dec_slope_ref)

    (
        grid_part,
        cot_rows,
        cot_turned,
        grid_wide,
        grid_back,
        mesh_back,
        mesh_in,
        mesh_out,
        mesh_cot_turned,
        mesh_slope,
        mesh_turned,
        enc_slope,
        dec_slope,
    ) = call(
        between,
        "slopes_and_nodes",
        [
            *arrived,
            grid_nodes,
            grid_first,
            grid_second,
            grid_cot,
            mesh_first,
            mesh_second,
            dec_first,
            mesh_nodes,
            mesh_cot,
            enc_pre,
            dec_pre,
            mesh_normed,
            mesh_pre,
            mesh_wide,
        ],
        [
            ((spots, feat), F32),
            ((spots, feat), BF16),
            ((spots, feat), F32),
            ((feat, 2 * feat), BF16),
            ((feat, feat), BF16),
            ((feat, feat), BF16),
            ((2 * feat, feat), BF16),
            ((mesh_count, feat), BF16),
            ((mesh_count, feat), F32),
            ((mesh_count, feat), F32),
            ((mesh_count, feat), F32),
            ((enc_count, feat), BF16),
            ((dec_count, feat), BF16),
        ],
        flops=16 * spots * feat * feat,
    )

    def backward(*refs):
        returned_refs, refs = refs[:arrived_count], refs[arrived_count:]
        (
            spot_ref,
            grid_part_ref,
            select_t_ref,
            cot_rows_ref,
            cot_turned_ref,
            mesh_cot_ref,
            mesh_cot_turned_ref,
            enc_pick_ref,
            enc_pool_ref,
            dec_pick_ref,
            dec_pool_ref,
            grid_first_ref,
            grid_wide_ref,
            grid_back_ref,
            mesh_back_ref,
            mesh_in_ref,
            enc_first_ref,
            enc_second_ref,
            dec_first_ref,
            dec_second_ref,
            enc_normed_ref,
            enc_scale_ref,
            enc_slope_ref,
            dec_normed_ref,
            dec_scale_ref,
            dec_slope_ref,
            mesh_normed_ref,
            mesh_scale_ref,
            mesh_slope_ref,
            mesh_turned_ref,
        ) = refs[:30]
        refs = refs[30:]
        out_refs, refs = refs[:sent_count], refs[sent_count:]
        (
            grid_normed_ref,
            grid_gpre_ref,
            dec_gpre_ref,
            enc_gpre_ref,
            mesh_gin_ref,
            mesh_gpre_ref,
            agg_ref,
            grid_act_ref,
            grid_slope_ref,
            spot_grad_ref,
        ) = refs
        agg_ref[:grid_count, :] = (
            spot_ref[:grid_count, :] + mm(select_t_ref[:, :slots], by_row(returned_refs, low))
        ).astype(BF16)
        agg_ref[grid_count:, :] = (
            spot_ref[grid_count:, :] + by_slot(returned_refs, high).astype(F32)
        ).astype(BF16)
        pre = grid_part_ref[...] + mm(agg_ref[...], grid_first_ref[high, :])
        for rows in row_chunks(spots):
            act, slope = silu_and_slope(pre[rows, :])
            grid_act_ref[rows, :] = act.astype(BF16)
            grid_slope_ref[rows, :] = slope
        both = mm(grid_act_ref[...], grid_wide_ref[...])
        for rows in row_chunks(spots):
            part = both[rows, low]
            scale_inv = scale_rows(part)
            normed = part * scale_inv
            grid_normed_ref[rows, :] = normed
            mean = jnp.mean(cot_rows_ref[rows, :].astype(F32) * normed, axis=-1, keepdims=True)
            raw = scale_inv * (cot_turned_ref[rows, :] - (mean * scale_inv) * both[rows, high])
            grid_gpre_ref[rows, :] = (raw * grid_slope_ref[rows, :]).astype(BF16)
        spot_grad_ref[:spots, :] = mm_t(grid_gpre_ref[...], grid_back_ref[...]).astype(BF16)
        spot_grad_ref[spots:, :] = jnp.zeros((total - spots, feat), BF16)
        edge_back(
            mm(dec_pick_ref[...], spot_grad_ref[...]),
            dec_normed_ref,
            dec_scale_ref,
            dec_second_ref,
            dec_slope_ref,
            dec_gpre_ref,
        )
        mesh_sum = mm(dec_pool_ref[mesh_rows, :], dec_gpre_ref[...]).astype(BF16)
        both = mm_t(mesh_sum, mesh_in_ref[...])
        mesh_gin = mesh_cot_ref[...].astype(F32) + both[:, low]
        mesh_gin_ref[...] = mesh_gin
        mean = jnp.mean(mesh_gin * mesh_normed_ref[...], axis=-1, keepdims=True)
        raw = mesh_cot_turned_ref[...] + both[:, high] - mean * mesh_turned_ref[...]
        mesh_gpre_ref[...] = (mesh_scale_ref[...] * raw * mesh_slope_ref[...]).astype(BF16)
        mesh_gagg = mm_t(mesh_gpre_ref[...], mesh_back_ref[...]).astype(BF16)
        pooled = mm(dec_pool_ref[grid_count:spots, :], dec_gpre_ref[...]).astype(BF16)
        slot_back = mm_t(pooled, dec_first_ref[low, :])
        edge_back(
            mm(enc_pick_ref[:, mesh_rows], mesh_gagg),
            enc_normed_ref,
            enc_scale_ref,
            enc_second_ref,
            enc_slope_ref,
            enc_gpre_ref,
        )
        pooled = mm(enc_pool_ref[grid_count:spots, :], enc_gpre_ref[...]).astype(BF16)
        slot_back = (slot_back + mm_t(pooled, enc_first_ref[low, :])).astype(BF16)
        send(out_refs, lambda j: slot_back[reverse[j] * width : (reverse[j] + 1) * width, :])

    results = call(
        backward,
        "edges_backward",
        [
            *returned,
            spot_msg,
            grid_part,
            select_t,
            cot_rows,
            cot_turned,
            mesh_cot,
            mesh_cot_turned,
            enc_pick,
            enc_pool,
            dec_pick,
            dec_pool,
            grid_first,
            grid_wide,
            grid_back,
            mesh_back,
            mesh_in,
            enc_first,
            enc_second,
            dec_first,
            dec_second,
            enc_normed,
            enc_scale,
            enc_slope,
            dec_normed,
            dec_scale,
            dec_slope,
            mesh_normed,
            mesh_scale,
            mesh_slope,
            mesh_turned,
        ],
        sent_shapes(feat)
        + [
            ((spots, feat), F32),
            ((spots, feat), BF16),
            ((dec_count, feat), BF16),
            ((enc_count, feat), BF16),
            ((mesh_count, feat), F32),
            ((mesh_count, feat), BF16),
        ],
        scratch=[
            ((spots, feat), BF16),
            ((spots, feat), BF16),
            ((spots, feat), F32),
            ((total, feat), BF16),
        ],
        flops=2 * feat * feat * (4 * spots + 3 * dec_count + 2 * enc_count),
    )
    outgoing, results = results[:sent_count], results[sent_count:]
    grid_normed, grid_gpre, dec_gpre, enc_gpre, mesh_gin, mesh_gpre = results
    final = exchange(outgoing, steady)

    def tail(
        nodes_ref,
        grid_normed_ref,
        cot_ref,
        grid_gpre_ref,
        enc_pool_ref,
        enc_gpre_ref,
        dec_pool_ref,
        dec_gpre_ref,
        mesh_gin_ref,
        mesh_gpre_ref,
        grid_wn_ref,
        enc_wg_ref,
        dec_wg_ref,
        mesh_wn_ref,
        enc_wm_ref,
        base_ref,
        grad_mesh_ref,
        grid_out_ref,
    ):
        grid_out_ref[...] = (
            nodes_ref[...].astype(F32) + grid_normed_ref[:grid_count, :]
        ).astype(BF16)
        enc_sums = mm(enc_pool_ref[...], enc_gpre_ref[...]).astype(BF16)
        dec_sums = mm(dec_pool_ref[:grid_count, :], dec_gpre_ref[...]).astype(BF16)
        base_ref[...] = (
            cot_ref[...].astype(F32)
            + mm_t(grid_gpre_ref[:grid_count, :], grid_wn_ref[low, :])
            + mm_t(enc_sums[:grid_count, :], enc_wg_ref[low, :])
            + mm_t(dec_sums, dec_wg_ref[low, :])
        )
        grad_mesh_ref[...] = (
            mesh_gin_ref[...]
            + mm_t(mesh_gpre_ref[...], mesh_wn_ref[low, :])
            + mm_t(enc_sums[mesh_rows, :], enc_wm_ref[high, :])
        )

    base, grad_mesh, grid_out = call(
        tail,
        "local_gradients",
        [
            grid_nodes,
            grid_normed,
            grid_cot,
            grid_gpre,
            enc_pool,
            enc_gpre,
            dec_pool,
            dec_gpre,
            mesh_gin,
            mesh_gpre,
            grid_first,
            enc_first,
            dec_first,
            mesh_first,
            enc_first,
        ],
        [((grid_count, feat), F32), ((mesh_count, feat), F32), ((grid_count, feat), BF16)],
        flops=2 * feat * feat * 3 * grid_count,
    )

    pieces = row_chunks(grid_count, 64)

    def finish(*refs):
        back_refs = refs[:arrived_count]
        base_ref, select_t_ref, out_ref, piece_ref, semaphores = refs[arrived_count:]
        back = by_row(back_refs)
        copies = []
        for place, rows in enumerate(pieces):
            piece_ref[rows, :] = base_ref[rows, :] + mm(select_t_ref[rows, :slots], back)
            copies.append(
                pltpu.make_async_copy(
                    piece_ref.at[rows, :], out_ref.at[rows, :], semaphores.at[place]
                )
            )
            copies[-1].start()
        for copy in copies:
            copy.wait()

    grad_grid = pl.pallas_call(
        finish,
        name="add_returned",
        in_specs=[pl.BlockSpec(memory_space=pltpu.VMEM)] * (arrived_count + 2),
        out_specs=pl.BlockSpec(memory_space=pltpu.HBM),
        out_shape=jax.ShapeDtypeStruct((grid_count, feat), F32),
        scratch_shapes=[
            pltpu.VMEM((grid_count, feat), F32),
            pltpu.SemaphoreType.DMA((len(pieces),)),
        ],
        compiler_params=pltpu.CompilerParams(vmem_limit_bytes=VMEM_LIMIT),
    )(*final, base, select_t)
    return (grid_out, mesh_out, grad_grid, grad_mesh)


def solution(mesh):
    rows = P(("groups", "tile"), None)
    flat = P(("groups", "tile"))
    in_specs = (rows,) * 6 + (P(),) * 8 + (rows,) + (flat,) * 5
    return jax.shard_map(
        per_device, mesh=mesh, in_specs=in_specs, out_specs=(rows,) * 4, check_vma=False
    )
```

```python
import jax
import jax.numpy as jnp
from jax import lax
from jax.experimental import pallas as pl
from jax.experimental.pallas import tpu as pltpu
from jax.sharding import PartitionSpec as P

TW = 4
CHUNK = 32
ROUND_FLOPS = 2 * 10**10
F32 = jnp.float32
BF16 = jnp.bfloat16
VMEM_LIMIT = 30 * 1024 * 1024


def mm(left, right):
    return jnp.dot(left, right, preferred_element_type=F32)


def mm_t(left, right):
    return lax.dot_general(left, right, (((1,), (1,)), ((), ())), preferred_element_type=F32)


def centred(values, axis):
    values = values.astype(F32)
    return values - jnp.mean(values, axis=axis, keepdims=True)


def silu_and_slope(pre):
    half = 0.5 * pre
    lifted = 1.0 + jnp.tanh(half)
    return half * lifted, lifted * (0.5 + 0.5 * half * (2.0 - lifted))


def silu(pre):
    half = 0.5 * pre
    return half * (1.0 + jnp.tanh(half))


def scale_rows(raw):
    return lax.rsqrt(jnp.mean(raw * raw, axis=-1, keepdims=True) + 1e-05)


def row_chunks(rows, size=CHUNK):
    return [slice(start, min(start + size, rows)) for start in range(0, rows, size)]


def write_silu(pre, act_ref):
    for rows in row_chunks(pre.shape[0]):
        act_ref[rows, :] = silu(pre[rows, :]).astype(BF16)


def write_norm(raw, normed_ref, scale_ref):
    for rows in row_chunks(raw.shape[0]):
        part = raw[rows, :]
        scale_inv = scale_rows(part)
        normed_ref[rows, :] = (part * scale_inv).astype(normed_ref.dtype)
        scale_ref[rows, :] = scale_inv


def write_slope(pre_ref, slope_ref):
    for rows in row_chunks(pre_ref.shape[0]):
        slope_ref[rows, :] = silu_and_slope(pre_ref[rows, :])[1].astype(BF16)


def edge_back(upstream, normed_ref, scale_ref, second_ref, slope_ref, out_ref):
    for rows in row_chunks(upstream.shape[0]):
        part, normed = upstream[rows, :], normed_ref[rows, :]
        mean = jnp.mean(part * normed.astype(F32), axis=-1, keepdims=True)
        out_ref[rows, :] = scale_ref[rows, :].astype(BF16) * (
            part.astype(BF16) - normed * mean.astype(BF16)
        )
    raw = mm_t(out_ref[...], second_ref[...])
    for rows in row_chunks(upstream.shape[0]):
        out_ref[rows, :] = raw[rows, :].astype(BF16) * slope_ref[rows, :]


def neighbour_offsets(peer_count):
    forward_half = [1, TW, TW + 1, TW - 1]
    return forward_half + [-offset for offset in forward_half] + [peer_count // 2]


def onehot_pair(spot_ref, mesh_ref, spots, mesh_count, by_edge_ref, by_spot_ref):
    edges, total = by_edge_ref.shape
    spot_row = spot_ref[...].reshape(1, -1)
    mesh_row = mesh_ref[...].reshape(1, -1) + spots
    one, zero = jnp.ones((), BF16), jnp.zeros((), BF16)

    def ones(ids, index):
        shape = jnp.broadcast_shapes(ids.shape, index.shape)
        hit = jnp.broadcast_to(ids, shape) == jnp.broadcast_to(index, shape)
        return jnp.where(hit, jnp.broadcast_to(one, shape), jnp.broadcast_to(zero, shape))

    for row, first, count in ((spot_row, 0, spots), (mesh_row, spots, mesh_count)):
        ids = lax.broadcasted_iota(jnp.int32, (16, edges), 0).astype(jnp.int16)
        wide = jnp.broadcast_to(row, (16, edges)).astype(jnp.int16)
        for rows in row_chunks(count, 16):
            rows = slice(rows.start + first, rows.stop + first)
            by_spot_ref[rows, :] = ones(ids, wide - jnp.int16(rows.start))
    by_spot_ref[spots + mesh_count :, :] = jnp.zeros((total - spots - mesh_count, edges), BF16)
    lane = lax.broadcasted_iota(jnp.int32, (16, 128), 1).astype(jnp.int16)
    for rows in row_chunks(edges, 128):
        spot_col = jnp.broadcast_to(spot_row[:, rows], (128, 128)).T.astype(jnp.int16)
        mesh_col = jnp.broadcast_to(mesh_row[:, rows], (128, 128)).T.astype(jnp.int16)
        for columns in row_chunks(total, 128):
            for part in row_chunks(128, 16):
                place = slice(rows.start + part.start, rows.start + part.stop)
                ids = lane + jnp.int16(columns.start)
                hits = []
                if columns.start < spots:
                    hits.append(ones(ids, spot_col[part, :]))
                if columns.stop > spots:
                    hits.append(ones(ids, mesh_col[part, :]))
                by_edge_ref[place, columns] = sum(hits[1:], hits[0])


class Fetched:
    def __init__(self, source, target, semaphore):
        self.copy = pltpu.make_async_copy(source, target, semaphore)
        self.target = target
        self.landed = False
        self.copy.start()

    def land(self):
        if not self.landed:
            self.copy.wait()
            self.landed = True

    def __getitem__(self, key):
        self.land()
        return self.target[key]


def call(body, name, inputs, outputs, scratch=(), flops=0):
    arrays, specs, moved, fetches = [], [], 0, []
    for place, entry in enumerate(inputs):
        if isinstance(entry, tuple):
            array, first, rows = entry
            array = pltpu.with_memory_space_constraint(array, pltpu.HBM)
            specs.append(pl.BlockSpec(memory_space=pltpu.HBM))
            shape = (rows,) + array.shape[1:]
            fetches.append((place, first, rows, shape, array.dtype))
            moved += rows * (array.size // array.shape[0]) * array.dtype.itemsize
        else:
            array = entry
            specs.append(pl.BlockSpec(memory_space=pltpu.VMEM))
            moved += array.size * array.dtype.itemsize
        arrays.append(array)
    shapes = [jax.ShapeDtypeStruct(shape, dtype) for shape, dtype in outputs]
    for shape in shapes:
        moved += shape.size * shape.dtype.itemsize
    buffers = [pltpu.VMEM(shape, dtype) for _, _, _, shape, dtype in fetches]
    if fetches:
        buffers.append(pltpu.SemaphoreType.DMA((len(fetches),)))

    def kernel(*refs):
        refs = list(refs)
        waiting = []
        if fetches:
            targets, semaphores = refs[-len(buffers) : -1], refs[-1]
            refs = refs[: -len(buffers)]
        for slot, (place, first, rows, shape, _) in enumerate(fetches):
            source = refs[place]
            if source.shape != shape:
                source = source.at[pl.ds(first, rows)]
            refs[place] = Fetched(source, targets[slot], semaphores.at[slot])
            waiting.append(refs[place])
        body(*refs)
        for fetched in waiting:
            fetched.land()

    return pl.pallas_call(
        kernel,
        name=name,
        in_specs=specs,
        out_specs=[pl.BlockSpec(memory_space=pltpu.VMEM) for _ in shapes],
        out_shape=shapes,
        scratch_shapes=[pltpu.VMEM(shape, dtype) for shape, dtype in scratch]
        + buffers,
        compiler_params=pltpu.CompilerParams(vmem_limit_bytes=VMEM_LIMIT),
        cost_estimate=pl.CostEstimate(flops=flops, bytes_accessed=moved, transcendentals=0),
    )(*arrays)


def per_device(
    grid_nodes,
    mesh_nodes,
    enc_edges,
    dec_edges,
    grid_cot,
    mesh_cot,
    enc_first,
    enc_second,
    mesh_first,
    mesh_second,
    dec_first,
    dec_second,
    grid_first,
    grid_second,
    send_index,
    send_count,
    enc_grid,
    enc_mesh,
    dec_grid,
    dec_mesh,
):
    grid_count, feat = grid_nodes.shape
    mesh_count = mesh_nodes.shape[0]
    enc_count = enc_edges.shape[0]
    dec_count = dec_edges.shape[0]
    links, width = send_index.shape
    slots = links * width
    slots_pad = -(-slots // 128) * 128
    spots = grid_count + slots
    total = -(-(spots + mesh_count) // 128) * 128
    peer_count = lax.axis_size("tile")
    offsets = neighbour_offsets(peer_count)
    half = (links - 1) // 2
    reverse = [(j + half) % (links - 1) for j in range(links - 1)] + [links - 1]
    low, high = slice(0, feat), slice(feat, 2 * feat)
    mesh_rows = slice(spots, spots + mesh_count)

    one, four, five, three = range(half)
    minus = [j + half for j in range(half)]
    across = links - 1
    peers = range(peer_count)

    def permute(part, steps, odd_row_steps=None):
        rows = (steps, odd_row_steps or steps)
        pairs = [(s, (s + rows[s // TW % 2][s % 2]) % peer_count) for s in peers]
        return lax.ppermute(part, "tile", pairs)

    steady = ("late", "early", "behind", "ahead", "five", "opposite", "own")
    staggered = ("early", "late", "ahead", "five", "behind", "opposite", "own")
    arrived_count = 9

    def exchange(parts, order):
        moves = {
            "late": ((-4, -4), (4, 4)),
            "early": ((4, 4), (-4, -4)),
            "behind": ((-1, 1),),
            "ahead": ((3, -3),),
            "five": ((-5, 5),),
            "opposite": ((peer_count // 2, peer_count // 2),),
            "own": ((1, -1),),
        }
        parts = dict(zip(order, parts))
        own_chip = parts.pop("own")
        got = {name: permute(part, *moves[name]) for name, part in parts.items()}
        first = order[0]
        got[first], own_chip = lax.optimization_barrier((got[first], own_chip))
        late_passed = permute(got["late"], (1, -1))
        got["own"] = permute(own_chip, (1, -1))
        early_passed = permute(got["early"], (1, -1))
        return [got[name] for name in order] + [late_passed, early_passed]

    def sent_shapes(columns, order=steady):
        double = ("late", "early")
        return [((width * (1 + (name in double)), columns), BF16) for name in order]

    sent_count = len(steady)

    def place_bits():
        own = lax.axis_index("tile")
        return lax.rem(own, 2) == 1, lax.rem(lax.div(own, TW), 2) == 1

    def send(refs, message, columns=slice(None), order=steady):
        odd, odd_row = place_bits()
        refs = dict(zip(order, refs))

        def by_parity(even, odd_one):
            return jnp.where(odd, message(odd_one), message(even))

        late_pair, early_pair, behind_one, ahead_three, five_off, opposite, own_chip = [
            refs[name] for name in steady
        ]
        first, second = slice(0, width), slice(width, 2 * width)
        ahead = message(four), by_parity(five, three)
        behind = message(minus[four]), by_parity(minus[three], minus[five])
        for rows, go_ahead, go_behind in zip((first, second), ahead, behind):
            late_pair[rows, columns] = jnp.where(odd_row, go_ahead, go_behind)
            early_pair[rows, columns] = jnp.where(odd_row, go_behind, go_ahead)
        behind_one[:, columns] = by_parity(minus[one], one)
        ahead_three[:, columns] = by_parity(three, minus[three])
        five_off[:, columns] = by_parity(minus[five], five)
        opposite[:, columns] = message(across)
        own_chip[:, columns] = by_parity(one, minus[one])

    def receive(refs, columns=slice(None), order=steady):
        odd, odd_row = place_bits()
        late_passed, early_passed = refs[sent_count:]
        refs = dict(zip(order, refs))
        late_pair, early_pair, behind_one, ahead_three, five_off, opposite, own_chip = [
            refs[name] for name in steady
        ]
        first, second = slice(0, width), slice(width, 2 * width)
        near, near_three = behind_one[:, columns], ahead_three[:, columns]
        far, own = five_off[:, columns], own_chip[:, columns]
        late_rows, early_rows = late_passed[second, columns], early_passed[second, columns]
        from_behind = jnp.where(odd_row, early_rows, late_rows)
        from_ahead = jnp.where(odd_row, late_rows, early_rows)
        late_rows, early_rows = late_pair[first, columns], early_pair[first, columns]
        slot_rows = [None] * links
        slot_rows[one] = jnp.where(odd, own, near)
        slot_rows[minus[one]] = jnp.where(odd, near, own)
        slot_rows[three] = jnp.where(odd, near_three, from_behind)
        slot_rows[minus[three]] = jnp.where(odd, from_ahead, near_three)
        slot_rows[five] = jnp.where(odd, from_behind, far)
        slot_rows[minus[five]] = jnp.where(odd, far, from_ahead)
        slot_rows[four] = jnp.where(odd_row, early_rows, late_rows)
        slot_rows[minus[four]] = jnp.where(odd_row, late_rows, early_rows)
        slot_rows[across] = opposite[:, columns]
        return slot_rows

    def by_slot(refs, columns=slice(None), order=steady):
        return jnp.concatenate(receive(refs, columns, order), axis=0)

    def by_row(refs, columns=slice(None)):
        slot_rows = receive(refs, columns)
        return jnp.concatenate([slot_rows[reverse[j]] for j in range(links)], axis=0)

    def pack(index_ref, count_ref, nodes_ref, cot_ref, select_ref, *out_refs):
        def column(row):
            count = row.shape[1]
            eye = lax.broadcasted_iota(jnp.int32, (count, count), 0) == lax.broadcasted_iota(
                jnp.int32, (count, count), 1
            )
            return jnp.sum(
                jnp.where(eye, jnp.broadcast_to(row, (count, count)), 0.0), axis=1, keepdims=True
            )

        counts = column(count_ref[...].reshape(1, -1).astype(F32))
        place = lax.broadcasted_iota(jnp.int32, (links, width), 1).astype(F32)
        index = jnp.where(place < counts, index_ref[...].astype(F32), -1.0)
        lane = lax.broadcasted_iota(jnp.int32, (width, grid_count), 1).astype(F32)
        picks = [
            jnp.where(lane == column(index[j : j + 1, :]), 1.0, 0.0).astype(BF16)
            for j in range(links)
        ]
        select = jnp.concatenate(picks, axis=0)
        select_ref[:slots, :] = select
        select_ref[slots:, :] = jnp.zeros((slots_pad - slots, grid_count), BF16)
        sent_nodes = mm(select, nodes_ref[...]).astype(BF16)
        sent_cot = mm(select, cot_ref[...]).astype(BF16)
        send(
            out_refs, lambda j: sent_nodes[j * width : (j + 1) * width, :], low, staggered
        )
        send(out_refs, lambda j: sent_cot[j * width : (j + 1) * width, :], high, staggered)

    select, *outgoing = call(
        pack,
        "pack_rows",
        [
            (send_index, 0, links),
            (send_count, 0, links),
            (grid_nodes, 0, grid_count),
            (grid_cot, 0, grid_count),
        ],
        [((slots_pad, grid_count), BF16)] + sent_shapes(2 * feat, staggered),
        flops=4 * slots * grid_count * feat,
    )
    def turn(select_ref, select_t_ref):
        select_t_ref[...] = select_ref[...].astype(F32).T.astype(BF16)

    (select_t,) = call(
        turn, "turn_select", [select], [((grid_count, slots_pad), BF16)], flops=ROUND_FLOPS
    )
    *outgoing, select_t = lax.optimization_barrier((*outgoing, select_t))
    arrived = exchange(outgoing, staggered)

    def local(
        select_ref,
        nodes_ref,
        mesh_ref,
        enc_edges_ref,
        dec_edges_ref,
        enc_first_ref,
        dec_first_ref,
        mesh_first_ref,
        enc_grid_ref,
        enc_mesh_ref,
        dec_grid_ref,
        dec_mesh_ref,
        enc_second_ref,
        mesh_second_ref,
        dec_second_ref,
        enc_part_ref,
        dec_part_ref,
        mesh_part_ref,
        enc_pick_ref,
        enc_pool_ref,
        dec_pick_ref,
        dec_pool_ref,
        enc_centred_ref,
        dec_centred_ref,
        mesh_centred_ref,
        shared_pool_ref,
        table_ref,
    ):
        onehot_pair(enc_grid_ref, enc_mesh_ref, spots, mesh_count, enc_pick_ref, enc_pool_ref)
        onehot_pair(dec_grid_ref, dec_mesh_ref, spots, mesh_count, dec_pick_ref, dec_pool_ref)
        enc_centred_ref[...] = centred(enc_second_ref[...], 1).astype(BF16)
        mesh_centred_ref[...] = centred(mesh_second_ref[...], 1).astype(BF16)
        shared_pool_ref[...] = mm(
            select_ref[:slots, :], dec_pool_ref[:grid_count, :]
        ).astype(BF16)
        dec_centred_ref[...] = centred(dec_second_ref[...], 1).astype(BF16)
        nodes = nodes_ref[...]
        mesh_part_ref[...] = mm(mesh_ref[...], mesh_first_ref[low, :])
        table_ref[:grid_count, :] = mm(nodes, enc_first_ref[low, :]).astype(BF16)
        table_ref[grid_count:, :] = jnp.zeros((total - grid_count, feat), BF16)
        table_ref[mesh_rows, :] = mm(mesh_ref[...], enc_first_ref[high, :]).astype(BF16)
        enc_part_ref[...] = mm(enc_edges_ref[...], enc_first_ref[2 * feat :, :])
        enc_part_ref[...] += mm(enc_pick_ref[...], table_ref[...])
        pd = mm(nodes, dec_first_ref[low, :]).astype(BF16)
        dec_part_ref[...] = mm(dec_edges_ref[...], dec_first_ref[2 * feat :, :])
        dec_part_ref[...] += mm(dec_pick_ref[:, :grid_count], pd)

    (
        enc_part,
        dec_part,
        mesh_part,
        enc_pick,
        enc_pool,
        dec_pick,
        dec_pool,
        enc_centred,
        dec_centred,
        mesh_centred,
        shared_pool,
    ) = call(
        local,
        "local_products",
        [
            select,
            grid_nodes,
            mesh_nodes,
            enc_edges,
            dec_edges,
            enc_first,
            dec_first,
            mesh_first,
            enc_grid,
            enc_mesh,
            dec_grid,
            dec_mesh,
            enc_second,
            mesh_second,
            dec_second,
        ],
        [
            ((enc_count, feat), F32),
            ((dec_count, feat), F32),
            ((mesh_count, feat), F32),
            ((enc_count, total), BF16),
            ((total, enc_count), BF16),
            ((dec_count, total), BF16),
            ((total, dec_count), BF16),
        ]
        + [
            ((feat, feat), BF16),
            ((feat, feat), BF16),
            ((feat, feat), BF16),
            ((slots, dec_count), BF16),
        ],
        scratch=[((total, feat), BF16)],
        flops=2 * feat * (feat * (2 * grid_count + enc_count + dec_count) + total * dec_count),
    )

    def forward(*refs):
        arrived_refs, refs = refs[:arrived_count], refs[arrived_count:]
        (
            shared_pool_ref,
            enc_part_ref,
            dec_part_ref,
            mesh_part_ref,
            enc_pick_ref,
            enc_pool_ref,
            dec_pick_ref,
            dec_pool_ref,
            enc_wg_ref,
            dec_wg_ref,
            enc_w2_ref,
            mesh_wa_ref,
            mesh_w2_ref,
            mesh_ref,
            dec_wm_ref,
            dec_w2_ref,
        ) = refs[:16]
        refs = refs[16:]
        out_refs, refs = refs[:sent_count], refs[sent_count:]
        (
            slot_ref,
            enc_normed_ref,
            enc_scale_ref,
            enc_pre_ref,
            dec_normed_ref,
            dec_scale_ref,
            dec_pre_ref,
            mesh_normed_ref,
            mesh_scale_ref,
            mesh_pre_ref,
            enc_act_ref,
            dec_act_ref,
            mesh_act_ref,
            table_ref,
        ) = refs
        rows = by_slot(arrived_refs, low, staggered)
        pe = mm(rows, enc_wg_ref[low, :]).astype(BF16)
        enc_pre_ref[...] = enc_part_ref[...] + mm(enc_pick_ref[:, grid_count:spots], pe)
        write_silu(enc_pre_ref, enc_act_ref)
        write_norm(mm(enc_act_ref[...], enc_w2_ref[...]), enc_normed_ref, enc_scale_ref)
        agg = mm(enc_pool_ref[mesh_rows, :], enc_normed_ref[...]).astype(BF16)
        mesh_pre_ref[...] = mesh_part_ref[...] + mm(agg, mesh_wa_ref[high, :])
        write_silu(mesh_pre_ref, mesh_act_ref)
        write_norm(mm(mesh_act_ref[...], mesh_w2_ref[...]), mesh_normed_ref, mesh_scale_ref)
        mesh_out = (mesh_ref[...].astype(F32) + mesh_normed_ref[...]).astype(BF16)
        table_ref[:slots, :] = mm(rows, dec_wg_ref[low, :]).astype(BF16)
        table_ref[slots : slots + mesh_count, :] = mm(mesh_out, dec_wm_ref[high, :]).astype(BF16)
        table_ref[slots + mesh_count :, :] = jnp.zeros(
            (total - spots - mesh_count, feat), BF16
        )
        dec_pre_ref[...] = dec_part_ref[...] + mm(dec_pick_ref[:, grid_count:], table_ref[...])
        write_silu(dec_pre_ref, dec_act_ref)
        write_norm(mm(dec_act_ref[...], dec_w2_ref[...]), dec_normed_ref, dec_scale_ref)
        slot_sums = mm(dec_pool_ref[grid_count:spots, :], dec_normed_ref[...])
        slot_ref[...] = slot_sums
        shared = mm(shared_pool_ref[...], dec_normed_ref[...]).astype(BF16)
        slot_msg = slot_sums.astype(BF16)
        send(
            out_refs, lambda j: slot_msg[reverse[j] * width : (reverse[j] + 1) * width, :], low
        )
        send(out_refs, lambda j: shared[j * width : (j + 1) * width, :], high)

    saved_shapes = [
        ((enc_count, feat), BF16),
        ((enc_count, 1), F32),
        ((enc_count, feat), F32),
        ((dec_count, feat), BF16),
        ((dec_count, 1), F32),
        ((dec_count, feat), F32),
        ((mesh_count, feat), F32),
        ((mesh_count, 1), F32),
        ((mesh_count, feat), F32),
    ]
    results = call(
        forward,
        "edges_forward",
        [
            *arrived,
            shared_pool,
            enc_part,
            dec_part,
            mesh_part,
            enc_pick,
            enc_pool,
            dec_pick,
            dec_pool,
            enc_first,
            dec_first,
            enc_centred,
            mesh_first,
            mesh_centred,
            mesh_nodes,
            dec_first,
            dec_centred,
        ],
        sent_shapes(2 * feat)
        + [((slots, feat), F32)]
        + saved_shapes,
        scratch=[
            ((enc_count, feat), BF16),
            ((dec_count, feat), BF16),
            ((mesh_count, feat), BF16),
            ((total - grid_count, feat), BF16),
        ],
        flops=2 * feat * feat * 2 * (enc_count + dec_count),
    )
    outgoing, results = results[:sent_count], results[sent_count:]
    slot_sums, *saved = results
    enc_normed, enc_scale, enc_pre, dec_normed, dec_scale, dec_pre = saved[:6]
    mesh_normed, mesh_scale, mesh_pre = saved[6:]
    returned = exchange(outgoing, steady)

    def between(*refs):
        arrived_refs, refs = refs[:arrived_count], refs[arrived_count:]
        (
            nodes_ref,
            grid_first_ref,
            grid_second_ref,
            cot_ref,
            mesh_first_ref,
            dec_pool_ref,
            dec_normed_ref,
            mesh_ref,
            enc_pre_ref,
            dec_pre_ref,
            mesh_normed_ref,
            mesh_pre_ref,
            local_sums_ref,
            part_ref,
            cot_rows_ref,
            cot_turned_ref,
            grid_wide_ref,
            grid_back_ref,
            mesh_back_ref,
            mesh_out_ref,
            mesh_slope_ref,
            enc_slope_ref,
            dec_slope_ref,
        ) = refs
        part_ref[:grid_count, :] = mm(nodes_ref[...], grid_first_ref[low, :])
        part_ref[grid_count:, :] = mm(by_slot(arrived_refs, low, staggered), grid_first_ref[low, :])
        mesh_out_ref[...] = (mesh_ref[...].astype(F32) + mesh_normed_ref[...]).astype(BF16)
        cot_rows_ref[:grid_count, :] = cot_ref[...]
        cot_rows_ref[grid_count:, :] = by_slot(arrived_refs, high, staggered)
        second = centred(grid_second_ref[...], 1).astype(BF16)
        grid_wide_ref[:, low] = second
        grid_wide_ref[:, high] = mm_t(second, grid_second_ref[...]).astype(BF16)
        cot_turned_ref[...] = mm_t(cot_rows_ref[...], second)
        grid_back_ref[...] = centred(grid_first_ref[high, :], 0).astype(BF16)
        mesh_back_ref[...] = centred(mesh_first_ref[high, :], 0).astype(BF16)
        local_sums_ref[...] = mm(dec_pool_ref[:grid_count, :], dec_normed_ref[...])
        mesh_slope_ref[...] = silu_and_slope(mesh_pre_ref[...])[1]
        write_slope(enc_pre_ref, enc_slope_ref)
        write_slope(dec_pre_ref, dec_slope_ref)

    (
        local_sums,
        grid_part,
        cot_rows,
        cot_turned,
        grid_wide,
        grid_back,
        mesh_back,
        mesh_out,
        mesh_slope,
        enc_slope,
        dec_slope,
    ) = call(
        between,
        "slopes_and_nodes",
        [
            *arrived,
            grid_nodes,
            grid_first,
            grid_second,
            grid_cot,
            mesh_first,
            dec_pool,
            dec_normed,
            mesh_nodes,
            enc_pre,
            dec_pre,
            mesh_normed,
            mesh_pre,
        ],
        [
            ((grid_count, feat), F32),
            ((spots, feat), F32),
            ((spots, feat), BF16),
            ((spots, feat), F32),
            ((feat, 2 * feat), BF16),
            ((feat, feat), BF16),
            ((feat, feat), BF16),
            ((mesh_count, feat), BF16),
            ((mesh_count, feat), F32),
            ((enc_count, feat), BF16),
            ((dec_count, feat), BF16),
        ],
        flops=16 * spots * feat * feat,
    )

    def backward(*refs):
        returned_refs, refs = refs[:arrived_count], refs[arrived_count:]
        (
            local_sums_ref,
            slot_sums_ref,
            grid_part_ref,
            select_t_ref,
            cot_rows_ref,
            cot_turned_ref,
            mesh_cot_ref,
            enc_pick_ref,
            enc_pool_ref,
            dec_pick_ref,
            dec_pool_ref,
            grid_first_ref,
            grid_wide_ref,
            grid_back_ref,
            mesh_back_ref,
            mesh_second_ref,
            enc_first_ref,
            enc_second_ref,
            dec_first_ref,
            dec_second_ref,
            enc_normed_ref,
            enc_scale_ref,
            enc_slope_ref,
            dec_normed_ref,
            dec_scale_ref,
            dec_slope_ref,
            mesh_normed_ref,
            mesh_scale_ref,
            mesh_slope_ref,
        ) = refs[:29]
        refs = refs[29:]
        out_refs, refs = refs[:sent_count], refs[sent_count:]
        (
            grid_normed_ref,
            grid_gpre_ref,
            dec_gpre_ref,
            enc_gpre_ref,
            mesh_gin_ref,
            mesh_gpre_ref,
            agg_ref,
            grid_act_ref,
            grid_slope_ref,
            spot_grad_ref,
        ) = refs
        agg_ref[:grid_count, :] = (
            local_sums_ref[...] + mm(select_t_ref[:, :slots], by_row(returned_refs, low))
        ).astype(BF16)
        agg_ref[grid_count:, :] = (
            slot_sums_ref[...] + by_slot(returned_refs, high).astype(F32)
        ).astype(BF16)
        pre = grid_part_ref[...] + mm(agg_ref[...], grid_first_ref[high, :])
        for rows in row_chunks(spots):
            act, slope = silu_and_slope(pre[rows, :])
            grid_act_ref[rows, :] = act.astype(BF16)
            grid_slope_ref[rows, :] = slope
        both = mm(grid_act_ref[...], grid_wide_ref[...])
        for rows in row_chunks(spots):
            part = both[rows, low]
            scale_inv = scale_rows(part)
            normed = part * scale_inv
            grid_normed_ref[rows, :] = normed
            mean = jnp.mean(cot_rows_ref[rows, :].astype(F32) * normed, axis=-1, keepdims=True)
            raw = scale_inv * (cot_turned_ref[rows, :] - (mean * scale_inv) * both[rows, high])
            grid_gpre_ref[rows, :] = (raw * grid_slope_ref[rows, :]).astype(BF16)
        spot_grad_ref[:spots, :] = mm_t(grid_gpre_ref[...], grid_back_ref[...]).astype(BF16)
        spot_grad_ref[spots:, :] = jnp.zeros((total - spots, feat), BF16)
        edge_back(
            mm(dec_pick_ref[...], spot_grad_ref[...]),
            dec_normed_ref,
            dec_scale_ref,
            dec_second_ref,
            dec_slope_ref,
            dec_gpre_ref,
        )
        mesh_sum = mm(dec_pool_ref[mesh_rows, :], dec_gpre_ref[...]).astype(BF16)
        mesh_gin = mesh_cot_ref[...].astype(F32) + mm_t(mesh_sum, dec_first_ref[high, :])
        mesh_gin_ref[...] = mesh_gin
        normed = mesh_normed_ref[...]
        upstream = centred(mesh_gin, 1)
        mean = jnp.mean(upstream * normed, axis=-1, keepdims=True)
        mesh_gout = (mesh_scale_ref[...] * (upstream - normed * mean)).astype(BF16)
        raw = mm_t(mesh_gout, mesh_second_ref[...])
        mesh_gpre_ref[...] = (raw * mesh_slope_ref[...]).astype(BF16)
        mesh_gagg = mm_t(mesh_gpre_ref[...], mesh_back_ref[...]).astype(BF16)
        pooled = mm(dec_pool_ref[grid_count:spots, :], dec_gpre_ref[...]).astype(BF16)
        slot_back = mm_t(pooled, dec_first_ref[low, :])
        edge_back(
            mm(enc_pick_ref[:, mesh_rows], mesh_gagg),
            enc_normed_ref,
            enc_scale_ref,
            enc_second_ref,
            enc_slope_ref,
            enc_gpre_ref,
        )
        pooled = mm(enc_pool_ref[grid_count:spots, :], enc_gpre_ref[...]).astype(BF16)
        slot_back = (slot_back + mm_t(pooled, enc_first_ref[low, :])).astype(BF16)
        send(out_refs, lambda j: slot_back[reverse[j] * width : (reverse[j] + 1) * width, :])

    results = call(
        backward,
        "edges_backward",
        [
            *returned,
            local_sums,
            slot_sums,
            grid_part,
            select_t,
            cot_rows,
            cot_turned,
            mesh_cot,
            enc_pick,
            enc_pool,
            dec_pick,
            dec_pool,
            grid_first,
            grid_wide,
            grid_back,
            mesh_back,
            mesh_second,
            enc_first,
            enc_second,
            dec_first,
            dec_second,
            enc_normed,
            enc_scale,
            enc_slope,
            dec_normed,
            dec_scale,
            dec_slope,
            mesh_normed,
            mesh_scale,
            mesh_slope,
        ],
        sent_shapes(feat)
        + [
            ((spots, feat), F32),
            ((spots, feat), BF16),
            ((dec_count, feat), BF16),
            ((enc_count, feat), BF16),
            ((mesh_count, feat), F32),
            ((mesh_count, feat), BF16),
        ],
        scratch=[
            ((spots, feat), BF16),
            ((spots, feat), BF16),
            ((spots, feat), F32),
            ((total, feat), BF16),
        ],
        flops=2 * feat * feat * (4 * spots + 3 * dec_count + 2 * enc_count),
    )
    outgoing, results = results[:sent_count], results[sent_count:]
    grid_normed, grid_gpre, dec_gpre, enc_gpre, mesh_gin, mesh_gpre = results
    final = exchange(outgoing, steady)

    def tail(
        nodes_ref,
        grid_normed_ref,
        cot_ref,
        grid_gpre_ref,
        enc_pool_ref,
        enc_gpre_ref,
        dec_pool_ref,
        dec_gpre_ref,
        mesh_gin_ref,
        mesh_gpre_ref,
        grid_wn_ref,
        enc_wg_ref,
        dec_wg_ref,
        mesh_wn_ref,
        enc_wm_ref,
        base_ref,
        grad_mesh_ref,
        grid_out_ref,
    ):
        grid_out_ref[...] = (
            nodes_ref[...].astype(F32) + grid_normed_ref[:grid_count, :]
        ).astype(BF16)
        enc_sums = mm(enc_pool_ref[:grid_count, :], enc_gpre_ref[...]).astype(BF16)
        mesh_sums = mm(enc_pool_ref[mesh_rows, :], enc_gpre_ref[...]).astype(BF16)
        dec_sums = mm(dec_pool_ref[:grid_count, :], dec_gpre_ref[...]).astype(BF16)
        base_ref[...] = (
            cot_ref[...].astype(F32)
            + mm_t(grid_gpre_ref[:grid_count, :], grid_wn_ref[low, :])
            + mm_t(enc_sums, enc_wg_ref[low, :])
            + mm_t(dec_sums, dec_wg_ref[low, :])
        )
        grad_mesh_ref[...] = (
            mesh_gin_ref[...]
            + mm_t(mesh_gpre_ref[...], mesh_wn_ref[low, :])
            + mm_t(mesh_sums, enc_wm_ref[high, :])
        )

    base, grad_mesh, grid_out = call(
        tail,
        "local_gradients",
        [
            grid_nodes,
            grid_normed,
            grid_cot,
            grid_gpre,
            enc_pool,
            enc_gpre,
            dec_pool,
            dec_gpre,
            mesh_gin,
            mesh_gpre,
            grid_first,
            enc_first,
            dec_first,
            mesh_first,
            enc_first,
        ],
        [((grid_count, feat), F32), ((mesh_count, feat), F32), ((grid_count, feat), BF16)],
        flops=2 * feat * feat * 3 * grid_count,
    )

    pieces = row_chunks(grid_count, 64)

    def finish(*refs):
        back_refs = refs[:arrived_count]
        base_ref, select_t_ref, out_ref, piece_ref, semaphores = refs[arrived_count:]
        back = by_row(back_refs)
        copies = []
        for place, rows in enumerate(pieces):
            piece_ref[rows, :] = base_ref[rows, :] + mm(select_t_ref[rows, :slots], back)
            copies.append(
                pltpu.make_async_copy(
                    piece_ref.at[rows, :], out_ref.at[rows, :], semaphores.at[place]
                )
            )
            copies[-1].start()
        for copy in copies:
            copy.wait()

    grad_grid = pl.pallas_call(
        finish,
        name="add_returned",
        in_specs=[pl.BlockSpec(memory_space=pltpu.VMEM)] * (arrived_count + 2),
        out_specs=pl.BlockSpec(memory_space=pltpu.HBM),
        out_shape=jax.ShapeDtypeStruct((grid_count, feat), F32),
        scratch_shapes=[
            pltpu.VMEM((grid_count, feat), F32),
            pltpu.SemaphoreType.DMA((len(pieces),)),
        ],
        compiler_params=pltpu.CompilerParams(vmem_limit_bytes=VMEM_LIMIT),
    )(*final, base, select_t)
    return (grid_out, mesh_out, grad_grid, grad_mesh)


def solution(mesh):
    rows = P(("groups", "tile"), None)
    flat = P(("groups", "tile"))
    in_specs = (rows,) * 6 + (P(),) * 8 + (rows,) + (flat,) * 5
    return jax.shard_map(
        per_device, mesh=mesh, in_specs=in_specs, out_specs=(rows,) * 4, check_vma=False
    )
```

```python
import jax
import jax.numpy as jnp
from jax import lax
from jax.experimental import pallas as pl
from jax.experimental.pallas import tpu as pltpu
from jax.sharding import PartitionSpec as P

TW = 4
CHUNK = 32
ROUND_FLOPS = 2 * 10**10
F32 = jnp.float32
BF16 = jnp.bfloat16
VMEM_LIMIT = 30 * 1024 * 1024


def mm(left, right):
    return jnp.dot(left, right, preferred_element_type=F32)


def mm_t(left, right):
    return lax.dot_general(left, right, (((1,), (1,)), ((), ())), preferred_element_type=F32)


def centred(values, axis):
    values = values.astype(F32)
    return values - jnp.mean(values, axis=axis, keepdims=True)


def silu_and_slope(pre):
    half = 0.5 * pre
    lifted = 1.0 + jnp.tanh(half)
    return half * lifted, lifted * (0.5 + 0.5 * half * (2.0 - lifted))


def silu(pre):
    half = 0.5 * pre
    return half * (1.0 + jnp.tanh(half))


def scale_rows(raw):
    return lax.rsqrt(jnp.mean(raw * raw, axis=-1, keepdims=True) + 1e-05)


def row_chunks(rows, size=CHUNK):
    return [slice(start, min(start + size, rows)) for start in range(0, rows, size)]


def write_silu(pre, act_ref):
    for rows in row_chunks(pre.shape[0]):
        act_ref[rows, :] = silu(pre[rows, :]).astype(BF16)


def write_norm(raw, normed_ref, scale_ref):
    for rows in row_chunks(raw.shape[0]):
        part = raw[rows, :]
        scale_inv = scale_rows(part)
        normed_ref[rows, :] = (part * scale_inv).astype(normed_ref.dtype)
        scale_ref[rows, :] = scale_inv


def write_slope(pre_ref, slope_ref):
    for rows in row_chunks(pre_ref.shape[0]):
        slope_ref[rows, :] = silu_and_slope(pre_ref[rows, :])[1].astype(BF16)


def edge_back(upstream, normed_ref, scale_ref, second_ref, slope_ref, out_ref):
    for rows in row_chunks(upstream.shape[0]):
        part, normed = upstream[rows, :], normed_ref[rows, :]
        mean = jnp.mean(part * normed.astype(F32), axis=-1, keepdims=True)
        out_ref[rows, :] = scale_ref[rows, :].astype(BF16) * (
            part.astype(BF16) - normed * mean.astype(BF16)
        )
    raw = mm_t(out_ref[...], second_ref[...])
    for rows in row_chunks(upstream.shape[0]):
        out_ref[rows, :] = raw[rows, :].astype(BF16) * slope_ref[rows, :]


def neighbour_offsets(peer_count):
    forward_half = [1, TW, TW + 1, TW - 1]
    return forward_half + [-offset for offset in forward_half] + [peer_count // 2]


def onehot_pair(spot_ref, mesh_ref, spots, mesh_count, by_edge_ref, by_spot_ref):
    edges, total = by_edge_ref.shape
    spot_row = spot_ref[...].reshape(1, -1)
    mesh_row = mesh_ref[...].reshape(1, -1) + spots
    one, zero = jnp.ones((), BF16), jnp.zeros((), BF16)

    def ones(ids, index):
        shape = jnp.broadcast_shapes(ids.shape, index.shape)
        hit = jnp.broadcast_to(ids, shape) == jnp.broadcast_to(index, shape)
        return jnp.where(hit, jnp.broadcast_to(one, shape), jnp.broadcast_to(zero, shape))

    for row, first, count in ((spot_row, 0, spots), (mesh_row, spots, mesh_count)):
        ids = lax.broadcasted_iota(jnp.int32, (16, edges), 0).astype(jnp.int16)
        wide = jnp.broadcast_to(row, (16, edges)).astype(jnp.int16)
        for rows in row_chunks(count, 16):
            rows = slice(rows.start + first, rows.stop + first)
            by_spot_ref[rows, :] = ones(ids, wide - jnp.int16(rows.start))
    by_spot_ref[spots + mesh_count :, :] = jnp.zeros((total - spots - mesh_count, edges), BF16)
    lane = lax.broadcasted_iota(jnp.int32, (16, 128), 1).astype(jnp.int16)
    for rows in row_chunks(edges, 128):
        spot_col = jnp.broadcast_to(spot_row[:, rows], (128, 128)).T.astype(jnp.int16)
        mesh_col = jnp.broadcast_to(mesh_row[:, rows], (128, 128)).T.astype(jnp.int16)
        for columns in row_chunks(total, 128):
            for part in row_chunks(128, 16):
                place = slice(rows.start + part.start, rows.start + part.stop)
                ids = lane + jnp.int16(columns.start)
                hits = []
                if columns.start < spots:
                    hits.append(ones(ids, spot_col[part, :]))
                if columns.stop > spots:
                    hits.append(ones(ids, mesh_col[part, :]))
                by_edge_ref[place, columns] = sum(hits[1:], hits[0])


class Fetched:
    def __init__(self, source, target, semaphore):
        self.copy = pltpu.make_async_copy(source, target, semaphore)
        self.target = target
        self.landed = False
        self.copy.start()

    def land(self):
        if not self.landed:
            self.copy.wait()
            self.landed = True

    def __getitem__(self, key):
        self.land()
        return self.target[key]


def call(body, name, inputs, outputs, scratch=(), flops=0):
    arrays, specs, moved, fetches = [], [], 0, []
    for place, entry in enumerate(inputs):
        if isinstance(entry, tuple):
            array, first, rows = entry
            array = pltpu.with_memory_space_constraint(array, pltpu.HBM)
            specs.append(pl.BlockSpec(memory_space=pltpu.HBM))
            shape = (rows,) + array.shape[1:]
            fetches.append((place, first, rows, shape, array.dtype))
            moved += rows * (array.size // array.shape[0]) * array.dtype.itemsize
        else:
            array = entry
            specs.append(pl.BlockSpec(memory_space=pltpu.VMEM))
            moved += array.size * array.dtype.itemsize
        arrays.append(array)
    shapes = [jax.ShapeDtypeStruct(shape, dtype) for shape, dtype in outputs]
    for shape in shapes:
        moved += shape.size * shape.dtype.itemsize
    buffers = [pltpu.VMEM(shape, dtype) for _, _, _, shape, dtype in fetches]
    if fetches:
        buffers.append(pltpu.SemaphoreType.DMA((len(fetches),)))

    def kernel(*refs):
        refs = list(refs)
        waiting = []
        if fetches:
            targets, semaphores = refs[-len(buffers) : -1], refs[-1]
            refs = refs[: -len(buffers)]
        for slot, (place, first, rows, shape, _) in enumerate(fetches):
            source = refs[place]
            if source.shape != shape:
                source = source.at[pl.ds(first, rows)]
            refs[place] = Fetched(source, targets[slot], semaphores.at[slot])
            waiting.append(refs[place])
        body(*refs)
        for fetched in waiting:
            fetched.land()

    return pl.pallas_call(
        kernel,
        name=name,
        in_specs=specs,
        out_specs=[pl.BlockSpec(memory_space=pltpu.VMEM) for _ in shapes],
        out_shape=shapes,
        scratch_shapes=[pltpu.VMEM(shape, dtype) for shape, dtype in scratch]
        + buffers,
        compiler_params=pltpu.CompilerParams(vmem_limit_bytes=VMEM_LIMIT),
        cost_estimate=pl.CostEstimate(flops=flops, bytes_accessed=moved, transcendentals=0),
    )(*arrays)


def per_device(
    grid_nodes,
    mesh_nodes,
    enc_edges,
    dec_edges,
    grid_cot,
    mesh_cot,
    enc_first,
    enc_second,
    mesh_first,
    mesh_second,
    dec_first,
    dec_second,
    grid_first,
    grid_second,
    send_index,
    send_count,
    enc_grid,
    enc_mesh,
    dec_grid,
    dec_mesh,
):
    grid_count, feat = grid_nodes.shape
    mesh_count = mesh_nodes.shape[0]
    enc_count = enc_edges.shape[0]
    dec_count = dec_edges.shape[0]
    links, width = send_index.shape
    slots = links * width
    slots_pad = -(-slots // 128) * 128
    spots = grid_count + slots
    total = -(-(spots + mesh_count) // 128) * 128
    peer_count = lax.axis_size("tile")
    offsets = neighbour_offsets(peer_count)
    half = (links - 1) // 2
    reverse = [(j + half) % (links - 1) for j in range(links - 1)] + [links - 1]
    low, high = slice(0, feat), slice(feat, 2 * feat)
    mesh_rows = slice(spots, spots + mesh_count)

    one, four, five, three = range(half)
    minus = [j + half for j in range(half)]
    across = links - 1
    peers = range(peer_count)

    def permute(part, steps, odd_row_steps=None):
        rows = (steps, odd_row_steps or steps)
        pairs = [(s, (s + rows[s // TW % 2][s % 2]) % peer_count) for s in peers]
        return lax.ppermute(part, "tile", pairs)

    steady = ("late", "early", "behind", "ahead", "five", "opposite", "own")
    staggered = ("early", "late", "ahead", "five", "behind", "opposite", "own")
    arrived_count = 9

    def exchange(parts, order):
        moves = {
            "late": ((-4, -4), (4, 4)),
            "early": ((4, 4), (-4, -4)),
            "behind": ((-1, 1),),
            "ahead": ((3, -3),),
            "five": ((-5, 5),),
            "opposite": ((peer_count // 2, peer_count // 2),),
            "own": ((1, -1),),
        }
        parts = dict(zip(order, parts))
        own_chip = parts.pop("own")
        got = {name: permute(part, *moves[name]) for name, part in parts.items()}
        first = order[0]
        got[first], own_chip = lax.optimization_barrier((got[first], own_chip))
        late_passed = permute(got["late"], (1, -1))
        got["own"] = permute(own_chip, (1, -1))
        early_passed = permute(got["early"], (1, -1))
        return [got[name] for name in order] + [late_passed, early_passed]

    def sent_shapes(columns, order=steady):
        double = ("late", "early")
        return [((width * (1 + (name in double)), columns), BF16) for name in order]

    sent_count = len(steady)

    def place_bits():
        own = lax.axis_index("tile")
        return lax.rem(own, 2) == 1, lax.rem(lax.div(own, TW), 2) == 1

    def send(refs, message, columns=slice(None), order=steady):
        odd, odd_row = place_bits()
        refs = dict(zip(order, refs))

        def by_parity(even, odd_one):
            return jnp.where(odd, message(odd_one), message(even))

        late_pair, early_pair, behind_one, ahead_three, five_off, opposite, own_chip = [
            refs[name] for name in steady
        ]
        first, second = slice(0, width), slice(width, 2 * width)
        ahead = message(four), by_parity(five, three)
        behind = message(minus[four]), by_parity(minus[three], minus[five])
        for rows, go_ahead, go_behind in zip((first, second), ahead, behind):
            late_pair[rows, columns] = jnp.where(odd_row, go_ahead, go_behind)
            early_pair[rows, columns] = jnp.where(odd_row, go_behind, go_ahead)
        behind_one[:, columns] = by_parity(minus[one], one)
        ahead_three[:, columns] = by_parity(three, minus[three])
        five_off[:, columns] = by_parity(minus[five], five)
        opposite[:, columns] = message(across)
        own_chip[:, columns] = by_parity(one, minus[one])

    def receive(refs, columns=slice(None), order=steady):
        odd, odd_row = place_bits()
        late_passed, early_passed = refs[sent_count:]
        refs = dict(zip(order, refs))
        late_pair, early_pair, behind_one, ahead_three, five_off, opposite, own_chip = [
            refs[name] for name in steady
        ]
        first, second = slice(0, width), slice(width, 2 * width)
        near, near_three = behind_one[:, columns], ahead_three[:, columns]
        far, own = five_off[:, columns], own_chip[:, columns]
        late_rows, early_rows = late_passed[second, columns], early_passed[second, columns]
        from_behind = jnp.where(odd_row, early_rows, late_rows)
        from_ahead = jnp.where(odd_row, late_rows, early_rows)
        late_rows, early_rows = late_pair[first, columns], early_pair[first, columns]
        slot_rows = [None] * links
        slot_rows[one] = jnp.where(odd, own, near)
        slot_rows[minus[one]] = jnp.where(odd, near, own)
        slot_rows[three] = jnp.where(odd, near_three, from_behind)
        slot_rows[minus[three]] = jnp.where(odd, from_ahead, near_three)
        slot_rows[five] = jnp.where(odd, from_behind, far)
        slot_rows[minus[five]] = jnp.where(odd, far, from_ahead)
        slot_rows[four] = jnp.where(odd_row, early_rows, late_rows)
        slot_rows[minus[four]] = jnp.where(odd_row, late_rows, early_rows)
        slot_rows[across] = opposite[:, columns]
        return slot_rows

    def by_slot(refs, columns=slice(None), order=steady):
        return jnp.concatenate(receive(refs, columns, order), axis=0)

    def by_row(refs, columns=slice(None)):
        slot_rows = receive(refs, columns)
        return jnp.concatenate([slot_rows[reverse[j]] for j in range(links)], axis=0)

    def pack(index_ref, count_ref, nodes_ref, cot_ref, select_ref, *out_refs):
        def column(row):
            count = row.shape[1]
            eye = lax.broadcasted_iota(jnp.int32, (count, count), 0) == lax.broadcasted_iota(
                jnp.int32, (count, count), 1
            )
            return jnp.sum(
                jnp.where(eye, jnp.broadcast_to(row, (count, count)), 0.0), axis=1, keepdims=True
            )

        counts = column(count_ref[...].reshape(1, -1).astype(F32))
        place = lax.broadcasted_iota(jnp.int32, (links, width), 1).astype(F32)
        index = jnp.where(place < counts, index_ref[...].astype(F32), -1.0)
        lane = lax.broadcasted_iota(jnp.int32, (width, grid_count), 1).astype(F32)
        picks = [
            jnp.where(lane == column(index[j : j + 1, :]), 1.0, 0.0).astype(BF16)
            for j in range(links)
        ]
        select = jnp.concatenate(picks, axis=0)
        select_ref[:slots, :] = select
        select_ref[slots:, :] = jnp.zeros((slots_pad - slots, grid_count), BF16)
        sent_nodes = mm(select, nodes_ref[...]).astype(BF16)
        sent_cot = mm(select, cot_ref[...]).astype(BF16)
        send(
            out_refs, lambda j: sent_nodes[j * width : (j + 1) * width, :], low, staggered
        )
        send(out_refs, lambda j: sent_cot[j * width : (j + 1) * width, :], high, staggered)

    select, *outgoing = call(
        pack,
        "pack_rows",
        [
            (send_index, 0, links),
            (send_count, 0, links),
            (grid_nodes, 0, grid_count),
            (grid_cot, 0, grid_count),
        ],
        [((slots_pad, grid_count), BF16)] + sent_shapes(2 * feat, staggered),
        flops=4 * slots * grid_count * feat,
    )
    def turn(select_ref, select_t_ref):
        select_t_ref[...] = select_ref[...].astype(F32).T.astype(BF16)

    (select_t,) = call(
        turn, "turn_select", [select], [((grid_count, slots_pad), BF16)], flops=ROUND_FLOPS
    )
    *outgoing, select_t = lax.optimization_barrier((*outgoing, select_t))
    arrived = exchange(outgoing, staggered)

    def local(
        select_ref,
        nodes_ref,
        mesh_ref,
        enc_edges_ref,
        dec_edges_ref,
        enc_first_ref,
        dec_first_ref,
        mesh_first_ref,
        enc_grid_ref,
        enc_mesh_ref,
        dec_grid_ref,
        dec_mesh_ref,
        enc_second_ref,
        mesh_second_ref,
        dec_second_ref,
        enc_part_ref,
        dec_part_ref,
        mesh_part_ref,
        enc_pick_ref,
        enc_pool_ref,
        dec_pick_ref,
        dec_pool_ref,
        enc_centred_ref,
        dec_centred_ref,
        mesh_centred_ref,
        shared_pool_ref,
        table_ref,
    ):
        onehot_pair(enc_grid_ref, enc_mesh_ref, spots, mesh_count, enc_pick_ref, enc_pool_ref)
        onehot_pair(dec_grid_ref, dec_mesh_ref, spots, mesh_count, dec_pick_ref, dec_pool_ref)
        enc_centred_ref[...] = centred(enc_second_ref[...], 1).astype(BF16)
        mesh_centred_ref[...] = centred(mesh_second_ref[...], 1).astype(BF16)
        shared_pool_ref[...] = mm(
            select_ref[:slots, :], dec_pool_ref[:grid_count, :]
        ).astype(BF16)
        dec_centred_ref[...] = centred(dec_second_ref[...], 1).astype(BF16)
        nodes = nodes_ref[...]
        mesh_part_ref[...] = mm(mesh_ref[...], mesh_first_ref[low, :])
        table_ref[:grid_count, :] = mm(nodes, enc_first_ref[low, :]).astype(BF16)
        table_ref[grid_count:, :] = jnp.zeros((total - grid_count, feat), BF16)
        table_ref[mesh_rows, :] = mm(mesh_ref[...], enc_first_ref[high, :]).astype(BF16)
        enc_part_ref[...] = mm(enc_edges_ref[...], enc_first_ref[2 * feat :, :])
        enc_part_ref[...] += mm(enc_pick_ref[...], table_ref[...])
        pd = mm(nodes, dec_first_ref[low, :]).astype(BF16)
        dec_part_ref[...] = mm(dec_edges_ref[...], dec_first_ref[2 * feat :, :])
        dec_part_ref[...] += mm(dec_pick_ref[:, :grid_count], pd)

    (
        enc_part,
        dec_part,
        mesh_part,
        enc_pick,
        enc_pool,
        dec_pick,
        dec_pool,
        enc_centred,
        dec_centred,
        mesh_centred,
        shared_pool,
    ) = call(
        local,
        "local_products",
        [
            select,
            grid_nodes,
            mesh_nodes,
            enc_edges,
            dec_edges,
            enc_first,
            dec_first,
            mesh_first,
            enc_grid,
            enc_mesh,
            dec_grid,
            dec_mesh,
            enc_second,
            mesh_second,
            dec_second,
        ],
        [
            ((enc_count, feat), F32),
            ((dec_count, feat), F32),
            ((mesh_count, feat), F32),
            ((enc_count, total), BF16),
            ((total, enc_count), BF16),
            ((dec_count, total), BF16),
            ((total, dec_count), BF16),
        ]
        + [
            ((feat, feat), BF16),
            ((feat, feat), BF16),
            ((feat, feat), BF16),
            ((slots, dec_count), BF16),
        ],
        scratch=[((total, feat), BF16)],
        flops=2 * feat * (feat * (2 * grid_count + enc_count + dec_count) + total * dec_count),
    )

    def forward(*refs):
        arrived_refs, refs = refs[:arrived_count], refs[arrived_count:]
        (
            shared_pool_ref,
            enc_part_ref,
            dec_part_ref,
            mesh_part_ref,
            enc_pick_ref,
            enc_pool_ref,
            dec_pick_ref,
            dec_pool_ref,
            enc_wg_ref,
            dec_wg_ref,
            enc_w2_ref,
            mesh_wa_ref,
            mesh_w2_ref,
            mesh_ref,
            dec_wm_ref,
            dec_w2_ref,
        ) = refs[:16]
        refs = refs[16:]
        out_refs, refs = refs[:sent_count], refs[sent_count:]
        (
            slot_ref,
            enc_normed_ref,
            enc_scale_ref,
            enc_pre_ref,
            dec_normed_ref,
            dec_scale_ref,
            dec_pre_ref,
            mesh_normed_ref,
            mesh_scale_ref,
            mesh_pre_ref,
            enc_act_ref,
            dec_act_ref,
            mesh_act_ref,
            table_ref,
        ) = refs
        rows = by_slot(arrived_refs, low, staggered)
        pe = mm(rows, enc_wg_ref[low, :]).astype(BF16)
        enc_pre_ref[...] = enc_part_ref[...] + mm(enc_pick_ref[:, grid_count:spots], pe)
        write_silu(enc_pre_ref, enc_act_ref)
        write_norm(mm(enc_act_ref[...], enc_w2_ref[...]), enc_normed_ref, enc_scale_ref)
        agg = mm(enc_pool_ref[mesh_rows, :], enc_normed_ref[...]).astype(BF16)
        mesh_pre_ref[...] = mesh_part_ref[...] + mm(agg, mesh_wa_ref[high, :])
        write_silu(mesh_pre_ref, mesh_act_ref)
        write_norm(mm(mesh_act_ref[...], mesh_w2_ref[...]), mesh_normed_ref, mesh_scale_ref)
        mesh_out = (mesh_ref[...].astype(F32) + mesh_normed_ref[...]).astype(BF16)
        table_ref[:slots, :] = mm(rows, dec_wg_ref[low, :]).astype(BF16)
        table_ref[slots : slots + mesh_count, :] = mm(mesh_out, dec_wm_ref[high, :]).astype(BF16)
        table_ref[slots + mesh_count :, :] = jnp.zeros(
            (total - spots - mesh_count, feat), BF16
        )
        dec_pre_ref[...] = dec_part_ref[...] + mm(dec_pick_ref[:, grid_count:], table_ref[...])
        write_silu(dec_pre_ref, dec_act_ref)
        write_norm(mm(dec_act_ref[...], dec_w2_ref[...]), dec_normed_ref, dec_scale_ref)
        slot_sums = mm(dec_pool_ref[grid_count:spots, :], dec_normed_ref[...])
        slot_ref[...] = slot_sums
        shared = mm(shared_pool_ref[...], dec_normed_ref[...]).astype(BF16)
        slot_msg = slot_sums.astype(BF16)
        send(
            out_refs, lambda j: slot_msg[reverse[j] * width : (reverse[j] + 1) * width, :], low
        )
        send(out_refs, lambda j: shared[j * width : (j + 1) * width, :], high)

    saved_shapes = [
        ((enc_count, feat), BF16),
        ((enc_count, 1), F32),
        ((enc_count, feat), F32),
        ((dec_count, feat), BF16),
        ((dec_count, 1), F32),
        ((dec_count, feat), F32),
        ((mesh_count, feat), F32),
        ((mesh_count, 1), F32),
        ((mesh_count, feat), F32),
    ]
    results = call(
        forward,
        "edges_forward",
        [
            *arrived,
            shared_pool,
            enc_part,
            dec_part,
            mesh_part,
            enc_pick,
            enc_pool,
            dec_pick,
            dec_pool,
            enc_first,
            dec_first,
            enc_centred,
            mesh_first,
            mesh_centred,
            mesh_nodes,
            dec_first,
            dec_centred,
        ],
        sent_shapes(2 * feat)
        + [((slots, feat), F32)]
        + saved_shapes,
        scratch=[
            ((enc_count, feat), BF16),
            ((dec_count, feat), BF16),
            ((mesh_count, feat), BF16),
            ((total - grid_count, feat), BF16),
        ],
        flops=2 * feat * feat * 2 * (enc_count + dec_count),
    )
    outgoing, results = results[:sent_count], results[sent_count:]
    slot_sums, *saved = results
    enc_normed, enc_scale, enc_pre, dec_normed, dec_scale, dec_pre = saved[:6]
    mesh_normed, mesh_scale, mesh_pre = saved[6:]
    returned = exchange(outgoing, steady)

    def between(*refs):
        arrived_refs, refs = refs[:arrived_count], refs[arrived_count:]
        (
            nodes_ref,
            grid_first_ref,
            grid_second_ref,
            cot_ref,
            mesh_first_ref,
            dec_pool_ref,
            dec_normed_ref,
            mesh_second_ref,
            mesh_centred_ref,
            dec_first_ref,
            mesh_cot_ref,
            mesh_ref,
            enc_pre_ref,
            dec_pre_ref,
            mesh_normed_ref,
            mesh_pre_ref,
            local_sums_ref,
            part_ref,
            cot_rows_ref,
            cot_turned_ref,
            grid_wide_ref,
            grid_back_ref,
            mesh_back_ref,
            mesh_in_ref,
            mesh_cot_turned_ref,
            mesh_turned_ref,
            mesh_out_ref,
            mesh_slope_ref,
            enc_slope_ref,
            dec_slope_ref,
        ) = refs
        part_ref[:grid_count, :] = mm(nodes_ref[...], grid_first_ref[low, :])
        part_ref[grid_count:, :] = mm(by_slot(arrived_refs, low, staggered), grid_first_ref[low, :])
        mesh_out_ref[...] = (mesh_ref[...].astype(F32) + mesh_normed_ref[...]).astype(BF16)
        cot_rows_ref[:grid_count, :] = cot_ref[...]
        cot_rows_ref[grid_count:, :] = by_slot(arrived_refs, high, staggered)
        second = centred(grid_second_ref[...], 1).astype(BF16)
        grid_wide_ref[:, low] = second
        grid_wide_ref[:, high] = mm_t(second, grid_second_ref[...]).astype(BF16)
        cot_turned_ref[...] = mm_t(cot_rows_ref[...], second)
        grid_back_ref[...] = centred(grid_first_ref[high, :], 0).astype(BF16)
        mesh_back_ref[...] = centred(mesh_first_ref[high, :], 0).astype(BF16)
        mesh_in_ref[low, :] = dec_first_ref[high, :]
        mesh_in_ref[high, :] = mm(mesh_centred_ref[...], dec_first_ref[high, :]).astype(BF16)
        mesh_cot_turned_ref[...] = mm_t(mesh_cot_ref[...], mesh_centred_ref[...])
        mesh_turned_ref[...] = mm_t(mesh_normed_ref[...].astype(BF16), mesh_second_ref[...])
        local_sums_ref[...] = mm(dec_pool_ref[:grid_count, :], dec_normed_ref[...])
        mesh_slope_ref[...] = silu_and_slope(mesh_pre_ref[...])[1]
        write_slope(enc_pre_ref, enc_slope_ref)
        write_slope(dec_pre_ref, dec_slope_ref)

    (
        local_sums,
        grid_part,
        cot_rows,
        cot_turned,
        grid_wide,
        grid_back,
        mesh_back,
        mesh_in,
        mesh_cot_turned,
        mesh_turned,
        mesh_out,
        mesh_slope,
        enc_slope,
        dec_slope,
    ) = call(
        between,
        "slopes_and_nodes",
        [
            *arrived,
            grid_nodes,
            grid_first,
            grid_second,
            grid_cot,
            mesh_first,
            dec_pool,
            dec_normed,
            mesh_second,
            mesh_centred,
            dec_first,
            mesh_cot,
            mesh_nodes,
            enc_pre,
            dec_pre,
            mesh_normed,
            mesh_pre,
        ],
        [
            ((grid_count, feat), F32),
            ((spots, feat), F32),
            ((spots, feat), BF16),
            ((spots, feat), F32),
            ((feat, 2 * feat), BF16),
            ((feat, feat), BF16),
            ((feat, feat), BF16),
            ((2 * feat, feat), BF16),
            ((mesh_count, feat), F32),
            ((mesh_count, feat), F32),
            ((mesh_count, feat), BF16),
            ((mesh_count, feat), F32),
            ((enc_count, feat), BF16),
            ((dec_count, feat), BF16),
        ],
        flops=16 * spots * feat * feat,
    )

    def backward(*refs):
        returned_refs, refs = refs[:arrived_count], refs[arrived_count:]
        (
            local_sums_ref,
            slot_sums_ref,
            grid_part_ref,
            select_t_ref,
            cot_rows_ref,
            cot_turned_ref,
            mesh_cot_ref,
            mesh_cot_turned_ref,
            enc_pick_ref,
            enc_pool_ref,
            dec_pick_ref,
            dec_pool_ref,
            grid_first_ref,
            grid_wide_ref,
            grid_back_ref,
            mesh_back_ref,
            mesh_in_ref,
            enc_first_ref,
            enc_second_ref,
            dec_first_ref,
            dec_second_ref,
            enc_normed_ref,
            enc_scale_ref,
            enc_slope_ref,
            dec_normed_ref,
            dec_scale_ref,
            dec_slope_ref,
            mesh_normed_ref,
            mesh_scale_ref,
            mesh_slope_ref,
            mesh_turned_ref,
        ) = refs[:31]
        refs = refs[31:]
        out_refs, refs = refs[:sent_count], refs[sent_count:]
        (
            grid_normed_ref,
            grid_gpre_ref,
            dec_gpre_ref,
            enc_gpre_ref,
            mesh_gin_ref,
            mesh_gpre_ref,
            agg_ref,
            grid_act_ref,
            grid_slope_ref,
            spot_grad_ref,
        ) = refs
        agg_ref[:grid_count, :] = (
            local_sums_ref[...] + mm(select_t_ref[:, :slots], by_row(returned_refs, low))
        ).astype(BF16)
        agg_ref[grid_count:, :] = (
            slot_sums_ref[...] + by_slot(returned_refs, high).astype(F32)
        ).astype(BF16)
        pre = grid_part_ref[...] + mm(agg_ref[...], grid_first_ref[high, :])
        for rows in row_chunks(spots):
            act, slope = silu_and_slope(pre[rows, :])
            grid_act_ref[rows, :] = act.astype(BF16)
            grid_slope_ref[rows, :] = slope
        both = mm(grid_act_ref[...], grid_wide_ref[...])
        for rows in row_chunks(spots):
            part = both[rows, low]
            scale_inv = scale_rows(part)
            normed = part * scale_inv
            grid_normed_ref[rows, :] = normed
            mean = jnp.mean(cot_rows_ref[rows, :].astype(F32) * normed, axis=-1, keepdims=True)
            raw = scale_inv * (cot_turned_ref[rows, :] - (mean * scale_inv) * both[rows, high])
            grid_gpre_ref[rows, :] = (raw * grid_slope_ref[rows, :]).astype(BF16)
        spot_grad_ref[:spots, :] = mm_t(grid_gpre_ref[...], grid_back_ref[...]).astype(BF16)
        spot_grad_ref[spots:, :] = jnp.zeros((total - spots, feat), BF16)
        edge_back(
            mm(dec_pick_ref[...], spot_grad_ref[...]),
            dec_normed_ref,
            dec_scale_ref,
            dec_second_ref,
            dec_slope_ref,
            dec_gpre_ref,
        )
        mesh_sum = mm(dec_pool_ref[mesh_rows, :], dec_gpre_ref[...]).astype(BF16)
        both = mm_t(mesh_sum, mesh_in_ref[...])
        mesh_gin = mesh_cot_ref[...].astype(F32) + both[:, low]
        mesh_gin_ref[...] = mesh_gin
        mean = jnp.mean(mesh_gin * mesh_normed_ref[...], axis=-1, keepdims=True)
        raw = mesh_cot_turned_ref[...] + both[:, high] - mean * mesh_turned_ref[...]
        mesh_gpre_ref[...] = (mesh_scale_ref[...] * raw * mesh_slope_ref[...]).astype(BF16)
        mesh_gagg = mm_t(mesh_gpre_ref[...], mesh_back_ref[...]).astype(BF16)
        pooled = mm(dec_pool_ref[grid_count:spots, :], dec_gpre_ref[...]).astype(BF16)
        slot_back = mm_t(pooled, dec_first_ref[low, :])
        edge_back(
            mm(enc_pick_ref[:, mesh_rows], mesh_gagg),
            enc_normed_ref,
            enc_scale_ref,
            enc_second_ref,
            enc_slope_ref,
            enc_gpre_ref,
        )
        pooled = mm(enc_pool_ref[grid_count:spots, :], enc_gpre_ref[...]).astype(BF16)
        slot_back = (slot_back + mm_t(pooled, enc_first_ref[low, :])).astype(BF16)
        send(out_refs, lambda j: slot_back[reverse[j] * width : (reverse[j] + 1) * width, :])

    results = call(
        backward,
        "edges_backward",
        [
            *returned,
            local_sums,
            slot_sums,
            grid_part,
            select_t,
            cot_rows,
            cot_turned,
            mesh_cot,
            mesh_cot_turned,
            enc_pick,
            enc_pool,
            dec_pick,
            dec_pool,
            grid_first,
            grid_wide,
            grid_back,
            mesh_back,
            mesh_in,
            enc_first,
            enc_second,
            dec_first,
            dec_second,
            enc_normed,
            enc_scale,
            enc_slope,
            dec_normed,
            dec_scale,
            dec_slope,
            mesh_normed,
            mesh_scale,
            mesh_slope,
            mesh_turned,
        ],
        sent_shapes(feat)
        + [
            ((spots, feat), F32),
            ((spots, feat), BF16),
            ((dec_count, feat), BF16),
            ((enc_count, feat), BF16),
            ((mesh_count, feat), F32),
            ((mesh_count, feat), BF16),
        ],
        scratch=[
            ((spots, feat), BF16),
            ((spots, feat), BF16),
            ((spots, feat), F32),
            ((total, feat), BF16),
        ],
        flops=2 * feat * feat * (4 * spots + 3 * dec_count + 2 * enc_count),
    )
    outgoing, results = results[:sent_count], results[sent_count:]
    grid_normed, grid_gpre, dec_gpre, enc_gpre, mesh_gin, mesh_gpre = results
    final = exchange(outgoing, steady)

    def tail(
        nodes_ref,
        grid_normed_ref,
        cot_ref,
        grid_gpre_ref,
        enc_pool_ref,
        enc_gpre_ref,
        dec_pool_ref,
        dec_gpre_ref,
        mesh_gin_ref,
        mesh_gpre_ref,
        grid_wn_ref,
        enc_wg_ref,
        dec_wg_ref,
        mesh_wn_ref,
        enc_wm_ref,
        base_ref,
        grad_mesh_ref,
        grid_out_ref,
    ):
        grid_out_ref[...] = (
            nodes_ref[...].astype(F32) + grid_normed_ref[:grid_count, :]
        ).astype(BF16)
        enc_sums = mm(enc_pool_ref[:grid_count, :], enc_gpre_ref[...]).astype(BF16)
        mesh_sums = mm(enc_pool_ref[mesh_rows, :], enc_gpre_ref[...]).astype(BF16)
        dec_sums = mm(dec_pool_ref[:grid_count, :], dec_gpre_ref[...]).astype(BF16)
        base_ref[...] = (
            cot_ref[...].astype(F32)
            + mm_t(grid_gpre_ref[:grid_count, :], grid_wn_ref[low, :])
            + mm_t(enc_sums, enc_wg_ref[low, :])
            + mm_t(dec_sums, dec_wg_ref[low, :])
        )
        grad_mesh_ref[...] = (
            mesh_gin_ref[...]
            + mm_t(mesh_gpre_ref[...], mesh_wn_ref[low, :])
            + mm_t(mesh_sums, enc_wm_ref[high, :])
        )

    base, grad_mesh, grid_out = call(
        tail,
        "local_gradients",
        [
            grid_nodes,
            grid_normed,
            grid_cot,
            grid_gpre,
            enc_pool,
            enc_gpre,
            dec_pool,
            dec_gpre,
            mesh_gin,
            mesh_gpre,
            grid_first,
            enc_first,
            dec_first,
            mesh_first,
            enc_first,
        ],
        [((grid_count, feat), F32), ((mesh_count, feat), F32), ((grid_count, feat), BF16)],
        flops=2 * feat * feat * 3 * grid_count,
    )

    pieces = row_chunks(grid_count, 64)

    def finish(*refs):
        back_refs = refs[:arrived_count]
        base_ref, select_t_ref, out_ref, piece_ref, semaphores = refs[arrived_count:]
        back = by_row(back_refs)
        copies = []
        for place, rows in enumerate(pieces):
            piece_ref[rows, :] = base_ref[rows, :] + mm(select_t_ref[rows, :slots], back)
            copies.append(
                pltpu.make_async_copy(
                    piece_ref.at[rows, :], out_ref.at[rows, :], semaphores.at[place]
                )
            )
            copies[-1].start()
        for copy in copies:
            copy.wait()

    grad_grid = pl.pallas_call(
        finish,
        name="add_returned",
        in_specs=[pl.BlockSpec(memory_space=pltpu.VMEM)] * (arrived_count + 2),
        out_specs=pl.BlockSpec(memory_space=pltpu.HBM),
        out_shape=jax.ShapeDtypeStruct((grid_count, feat), F32),
        scratch_shapes=[
            pltpu.VMEM((grid_count, feat), F32),
            pltpu.SemaphoreType.DMA((len(pieces),)),
        ],
        compiler_params=pltpu.CompilerParams(vmem_limit_bytes=VMEM_LIMIT),
    )(*final, base, select_t)
    return (grid_out, mesh_out, grad_grid, grad_mesh)


def solution(mesh):
    rows = P(("groups", "tile"), None)
    flat = P(("groups", "tile"))
    in_specs = (rows,) * 6 + (P(),) * 8 + (rows,) + (flat,) * 5
    return jax.shard_map(
        per_device, mesh=mesh, in_specs=in_specs, out_specs=(rows,) * 4, check_vma=False
    )
```

```python
import jax
import jax.numpy as jnp
from jax import lax
from jax.experimental import pallas as pl
from jax.experimental.pallas import tpu as pltpu
from jax.sharding import PartitionSpec as P

TW = 4
CHUNK = 128
ROUND_FLOPS = 2 * 10**10
F32 = jnp.float32
BF16 = jnp.bfloat16
VMEM_LIMIT = 30 * 1024 * 1024


def mm(left, right):
    return jnp.dot(left, right, preferred_element_type=F32)


def mm_t(left, right):
    return lax.dot_general(left, right, (((1,), (1,)), ((), ())), preferred_element_type=F32)


def centred(values, axis):
    values = values.astype(F32)
    return values - jnp.mean(values, axis=axis, keepdims=True)


def silu_and_slope(pre):
    half = 0.5 * pre
    lifted = 1.0 + jnp.tanh(half)
    return half * lifted, lifted * (0.5 + 0.5 * half * (2.0 - lifted))


def silu(pre):
    half = 0.5 * pre
    return half * (1.0 + jnp.tanh(half))


def scale_rows(raw):
    return lax.rsqrt(jnp.mean(raw * raw, axis=-1, keepdims=True) + 1e-05)


def row_chunks(rows, size=CHUNK):
    return [slice(start, min(start + size, rows)) for start in range(0, rows, size)]


def write_silu(pre, act_ref):
    for rows in row_chunks(pre.shape[0]):
        act_ref[rows, :] = silu(pre[rows, :]).astype(BF16)


def write_norm(raw, normed_ref, scale_ref):
    for rows in row_chunks(raw.shape[0]):
        part = raw[rows, :]
        scale_inv = scale_rows(part)
        normed_ref[rows, :] = (part * scale_inv).astype(normed_ref.dtype)
        scale_ref[rows, :] = scale_inv


def write_slope(pre_ref, slope_ref):
    for rows in row_chunks(pre_ref.shape[0]):
        slope_ref[rows, :] = silu_and_slope(pre_ref[rows, :])[1].astype(BF16)


def edge_back(upstream, normed_ref, scale_ref, second_ref, slope_ref, out_ref):
    for rows in row_chunks(upstream.shape[0]):
        part, normed = upstream[rows, :], normed_ref[rows, :]
        mean = jnp.mean(part * normed.astype(F32), axis=-1, keepdims=True)
        out_ref[rows, :] = scale_ref[rows, :].astype(BF16) * (
            part.astype(BF16) - normed * mean.astype(BF16)
        )
    raw = mm_t(out_ref[...], second_ref[...])
    for rows in row_chunks(upstream.shape[0]):
        out_ref[rows, :] = raw[rows, :].astype(BF16) * slope_ref[rows, :]


def neighbour_offsets(peer_count):
    forward_half = [1, TW, TW + 1, TW - 1]
    return forward_half + [-offset for offset in forward_half] + [peer_count // 2]


def onehot_pair(spot_ref, mesh_ref, spots, mesh_count, by_edge_ref, by_spot_ref):
    edges, total = by_edge_ref.shape
    spot_row = spot_ref[...].reshape(1, -1)
    mesh_row = mesh_ref[...].reshape(1, -1) + spots
    one, zero = jnp.ones((), BF16), jnp.zeros((), BF16)

    def ones(ids, index):
        shape = jnp.broadcast_shapes(ids.shape, index.shape)
        hit = jnp.broadcast_to(ids, shape) == jnp.broadcast_to(index, shape)
        return jnp.where(hit, jnp.broadcast_to(one, shape), jnp.broadcast_to(zero, shape))

    for row, first, count in ((spot_row, 0, spots), (mesh_row, spots, mesh_count)):
        ids = lax.broadcasted_iota(jnp.int32, (16, edges), 0).astype(jnp.int16)
        wide = jnp.broadcast_to(row, (16, edges)).astype(jnp.int16)
        for rows in row_chunks(count, 16):
            rows = slice(rows.start + first, rows.stop + first)
            by_spot_ref[rows, :] = ones(ids, wide - jnp.int16(rows.start))
    by_spot_ref[spots + mesh_count :, :] = jnp.zeros((total - spots - mesh_count, edges), BF16)
    lane = lax.broadcasted_iota(jnp.int32, (16, 128), 1).astype(jnp.int16)
    for rows in row_chunks(edges, 128):
        spot_col = jnp.broadcast_to(spot_row[:, rows], (128, 128)).T.astype(jnp.int16)
        mesh_col = jnp.broadcast_to(mesh_row[:, rows], (128, 128)).T.astype(jnp.int16)
        for columns in row_chunks(total, 128):
            for part in row_chunks(128, 16):
                place = slice(rows.start + part.start, rows.start + part.stop)
                ids = lane + jnp.int16(columns.start)
                hits = []
                if columns.start < spots:
                    hits.append(ones(ids, spot_col[part, :]))
                if columns.stop > spots:
                    hits.append(ones(ids, mesh_col[part, :]))
                by_edge_ref[place, columns] = sum(hits[1:], hits[0])


class Fetched:
    def __init__(self, source, target, semaphore):
        self.copy = pltpu.make_async_copy(source, target, semaphore)
        self.target = target
        self.landed = False
        self.copy.start()

    def land(self):
        if not self.landed:
            self.copy.wait()
            self.landed = True

    def __getitem__(self, key):
        self.land()
        return self.target[key]


def call(body, name, inputs, outputs, scratch=(), flops=0):
    arrays, specs, moved, fetches = [], [], 0, []
    for place, entry in enumerate(inputs):
        if isinstance(entry, tuple):
            array, first, rows = entry
            array = pltpu.with_memory_space_constraint(array, pltpu.HBM)
            specs.append(pl.BlockSpec(memory_space=pltpu.HBM))
            shape = (rows,) + array.shape[1:]
            fetches.append((place, first, rows, shape, array.dtype))
            moved += rows * (array.size // array.shape[0]) * array.dtype.itemsize
        else:
            array = entry
            specs.append(pl.BlockSpec(memory_space=pltpu.VMEM))
            moved += array.size * array.dtype.itemsize
        arrays.append(array)
    shapes = [jax.ShapeDtypeStruct(shape, dtype) for shape, dtype in outputs]
    for shape in shapes:
        moved += shape.size * shape.dtype.itemsize
    buffers = [pltpu.VMEM(shape, dtype) for _, _, _, shape, dtype in fetches]
    if fetches:
        buffers.append(pltpu.SemaphoreType.DMA((len(fetches),)))

    def kernel(*refs):
        refs = list(refs)
        waiting = []
        if fetches:
            targets, semaphores = refs[-len(buffers) : -1], refs[-1]
            refs = refs[: -len(buffers)]
        for slot, (place, first, rows, shape, _) in enumerate(fetches):
            source = refs[place]
            if source.shape != shape:
                source = source.at[pl.ds(first, rows)]
            refs[place] = Fetched(source, targets[slot], semaphores.at[slot])
            waiting.append(refs[place])
        body(*refs)
        for fetched in waiting:
            fetched.land()

    return pl.pallas_call(
        kernel,
        name=name,
        in_specs=specs,
        out_specs=[pl.BlockSpec(memory_space=pltpu.VMEM) for _ in shapes],
        out_shape=shapes,
        scratch_shapes=[pltpu.VMEM(shape, dtype) for shape, dtype in scratch]
        + buffers,
        compiler_params=pltpu.CompilerParams(vmem_limit_bytes=VMEM_LIMIT),
        cost_estimate=pl.CostEstimate(flops=flops, bytes_accessed=moved, transcendentals=0),
    )(*arrays)


def per_device(
    grid_nodes,
    mesh_nodes,
    enc_edges,
    dec_edges,
    grid_cot,
    mesh_cot,
    enc_first,
    enc_second,
    mesh_first,
    mesh_second,
    dec_first,
    dec_second,
    grid_first,
    grid_second,
    send_index,
    send_count,
    enc_grid,
    enc_mesh,
    dec_grid,
    dec_mesh,
):
    grid_count, feat = grid_nodes.shape
    mesh_count = mesh_nodes.shape[0]
    enc_count = enc_edges.shape[0]
    dec_count = dec_edges.shape[0]
    links, width = send_index.shape
    slots = links * width
    slots_pad = -(-slots // 128) * 128
    spots = grid_count + slots
    total = -(-(spots + mesh_count) // 128) * 128
    peer_count = lax.axis_size("tile")
    offsets = neighbour_offsets(peer_count)
    half = (links - 1) // 2
    reverse = [(j + half) % (links - 1) for j in range(links - 1)] + [links - 1]
    low, high = slice(0, feat), slice(feat, 2 * feat)
    mesh_rows = slice(spots, spots + mesh_count)

    one, four, five, three = range(half)
    minus = [j + half for j in range(half)]
    across = links - 1
    peers = range(peer_count)

    def permute(part, steps, odd_row_steps=None):
        rows = (steps, odd_row_steps or steps)
        pairs = [(s, (s + rows[s // TW % 2][s % 2]) % peer_count) for s in peers]
        return lax.ppermute(part, "tile", pairs)

    steady = ("late", "early", "behind", "ahead", "five", "opposite", "own")
    staggered = ("early", "late", "ahead", "five", "behind", "opposite", "own")
    arrived_count = 9

    def exchange(parts, order):
        moves = {
            "late": ((-4, -4), (4, 4)),
            "early": ((4, 4), (-4, -4)),
            "behind": ((-1, 1),),
            "ahead": ((3, -3),),
            "five": ((-5, 5),),
            "opposite": ((peer_count // 2, peer_count // 2),),
            "own": ((1, -1),),
        }
        parts = dict(zip(order, parts))
        own_chip = parts.pop("own")
        got = {name: permute(part, *moves[name]) for name, part in parts.items()}
        first = order[0]
        got[first], own_chip = lax.optimization_barrier((got[first], own_chip))
        late_passed = permute(got["late"], (1, -1))
        got["own"] = permute(own_chip, (1, -1))
        early_passed = permute(got["early"], (1, -1))
        return [got[name] for name in order] + [late_passed, early_passed]

    def sent_shapes(columns, order=steady):
        double = ("late", "early")
        return [((width * (1 + (name in double)), columns), BF16) for name in order]

    sent_count = len(steady)

    def place_bits():
        own = lax.axis_index("tile")
        return lax.rem(own, 2) == 1, lax.rem(lax.div(own, TW), 2) == 1

    def send(refs, message, columns=slice(None), order=steady):
        odd, odd_row = place_bits()
        refs = dict(zip(order, refs))

        def by_parity(even, odd_one):
            return jnp.where(odd, message(odd_one), message(even))

        late_pair, early_pair, behind_one, ahead_three, five_off, opposite, own_chip = [
            refs[name] for name in steady
        ]
        first, second = slice(0, width), slice(width, 2 * width)
        ahead = message(four), by_parity(five, three)
        behind = message(minus[four]), by_parity(minus[three], minus[five])
        for rows, go_ahead, go_behind in zip((first, second), ahead, behind):
            late_pair[rows, columns] = jnp.where(odd_row, go_ahead, go_behind)
            early_pair[rows, columns] = jnp.where(odd_row, go_behind, go_ahead)
        behind_one[:, columns] = by_parity(minus[one], one)
        ahead_three[:, columns] = by_parity(three, minus[three])
        five_off[:, columns] = by_parity(minus[five], five)
        opposite[:, columns] = message(across)
        own_chip[:, columns] = by_parity(one, minus[one])

    def receive(refs, columns=slice(None), order=steady):
        odd, odd_row = place_bits()
        late_passed, early_passed = refs[sent_count:]
        refs = dict(zip(order, refs))
        late_pair, early_pair, behind_one, ahead_three, five_off, opposite, own_chip = [
            refs[name] for name in steady
        ]
        first, second = slice(0, width), slice(width, 2 * width)
        near, near_three = behind_one[:, columns], ahead_three[:, columns]
        far, own = five_off[:, columns], own_chip[:, columns]
        late_rows, early_rows = late_passed[second, columns], early_passed[second, columns]
        from_behind = jnp.where(odd_row, early_rows, late_rows)
        from_ahead = jnp.where(odd_row, late_rows, early_rows)
        late_rows, early_rows = late_pair[first, columns], early_pair[first, columns]
        slot_rows = [None] * links
        slot_rows[one] = jnp.where(odd, own, near)
        slot_rows[minus[one]] = jnp.where(odd, near, own)
        slot_rows[three] = jnp.where(odd, near_three, from_behind)
        slot_rows[minus[three]] = jnp.where(odd, from_ahead, near_three)
        slot_rows[five] = jnp.where(odd, from_behind, far)
        slot_rows[minus[five]] = jnp.where(odd, far, from_ahead)
        slot_rows[four] = jnp.where(odd_row, early_rows, late_rows)
        slot_rows[minus[four]] = jnp.where(odd_row, late_rows, early_rows)
        slot_rows[across] = opposite[:, columns]
        return slot_rows

    def by_slot(refs, columns=slice(None), order=steady):
        return jnp.concatenate(receive(refs, columns, order), axis=0)

    def by_row(refs, columns=slice(None)):
        slot_rows = receive(refs, columns)
        return jnp.concatenate([slot_rows[reverse[j]] for j in range(links)], axis=0)

    def pack(index_ref, count_ref, nodes_ref, cot_ref, select_ref, *out_refs):
        def column(row):
            count = row.shape[1]
            eye = lax.broadcasted_iota(jnp.int32, (count, count), 0) == lax.broadcasted_iota(
                jnp.int32, (count, count), 1
            )
            return jnp.sum(
                jnp.where(eye, jnp.broadcast_to(row, (count, count)), 0.0), axis=1, keepdims=True
            )

        counts = column(count_ref[...].reshape(1, -1).astype(F32))
        place = lax.broadcasted_iota(jnp.int32, (links, width), 1).astype(F32)
        index = jnp.where(place < counts, index_ref[...].astype(F32), -1.0)
        lane = lax.broadcasted_iota(jnp.int32, (width, grid_count), 1).astype(F32)
        picks = [
            jnp.where(lane == column(index[j : j + 1, :]), 1.0, 0.0).astype(BF16)
            for j in range(links)
        ]
        select = jnp.concatenate(picks, axis=0)
        select_ref[:slots, :] = select
        select_ref[slots:, :] = jnp.zeros((slots_pad - slots, grid_count), BF16)
        sent_nodes = mm(select, nodes_ref[...]).astype(BF16)
        sent_cot = mm(select, cot_ref[...]).astype(BF16)
        send(
            out_refs, lambda j: sent_nodes[j * width : (j + 1) * width, :], low, staggered
        )
        send(out_refs, lambda j: sent_cot[j * width : (j + 1) * width, :], high, staggered)

    select, *outgoing = call(
        pack,
        "pack_rows",
        [
            (send_index, 0, links),
            (send_count, 0, links),
            (grid_nodes, 0, grid_count),
            (grid_cot, 0, grid_count),
        ],
        [((slots_pad, grid_count), BF16)] + sent_shapes(2 * feat, staggered),
        flops=4 * slots * grid_count * feat,
    )
    def turn(select_ref, select_t_ref):
        select_t_ref[...] = select_ref[...].astype(F32).T.astype(BF16)

    (select_t,) = call(
        turn, "turn_select", [select], [((grid_count, slots_pad), BF16)], flops=ROUND_FLOPS
    )
    *outgoing, select_t = lax.optimization_barrier((*outgoing, select_t))
    arrived = exchange(outgoing, staggered)

    def local(
        select_ref,
        nodes_ref,
        mesh_ref,
        enc_edges_ref,
        dec_edges_ref,
        enc_first_ref,
        dec_first_ref,
        mesh_first_ref,
        enc_grid_ref,
        enc_mesh_ref,
        dec_grid_ref,
        dec_mesh_ref,
        enc_second_ref,
        mesh_second_ref,
        dec_second_ref,
        enc_part_ref,
        dec_part_ref,
        mesh_part_ref,
        enc_pick_ref,
        enc_pool_ref,
        dec_pick_ref,
        dec_pool_ref,
        enc_centred_ref,
        dec_centred_ref,
        mesh_centred_ref,
        shared_pool_ref,
        table_ref,
    ):
        onehot_pair(enc_grid_ref, enc_mesh_ref, spots, mesh_count, enc_pick_ref, enc_pool_ref)
        onehot_pair(dec_grid_ref, dec_mesh_ref, spots, mesh_count, dec_pick_ref, dec_pool_ref)
        enc_centred_ref[...] = centred(enc_second_ref[...], 1).astype(BF16)
        mesh_centred_ref[...] = centred(mesh_second_ref[...], 1).astype(BF16)
        shared_pool_ref[...] = mm(
            select_ref[:slots, :], dec_pool_ref[:grid_count, :]
        ).astype(BF16)
        dec_centred_ref[...] = centred(dec_second_ref[...], 1).astype(BF16)
        nodes = nodes_ref[...]
        mesh_part_ref[...] = mm(mesh_ref[...], mesh_first_ref[low, :])
        table_ref[:grid_count, :] = mm(nodes, enc_first_ref[low, :]).astype(BF16)
        table_ref[grid_count:, :] = jnp.zeros((total - grid_count, feat), BF16)
        table_ref[mesh_rows, :] = mm(mesh_ref[...], enc_first_ref[high, :]).astype(BF16)
        enc_part_ref[...] = mm(enc_edges_ref[...], enc_first_ref[2 * feat :, :])
        enc_part_ref[...] += mm(enc_pick_ref[...], table_ref[...])
        pd = mm(nodes, dec_first_ref[low, :]).astype(BF16)
        dec_part_ref[...] = mm(dec_edges_ref[...], dec_first_ref[2 * feat :, :])
        dec_part_ref[...] += mm(dec_pick_ref[:, :grid_count], pd)

    (
        enc_part,
        dec_part,
        mesh_part,
        enc_pick,
        enc_pool,
        dec_pick,
        dec_pool,
        enc_centred,
        dec_centred,
        mesh_centred,
        shared_pool,
    ) = call(
        local,
        "local_products",
        [
            select,
            grid_nodes,
            mesh_nodes,
            enc_edges,
            dec_edges,
            enc_first,
            dec_first,
            mesh_first,
            enc_grid,
            enc_mesh,
            dec_grid,
            dec_mesh,
            enc_second,
            mesh_second,
            dec_second,
        ],
        [
            ((enc_count, feat), F32),
            ((dec_count, feat), F32),
            ((mesh_count, feat), F32),
            ((enc_count, total), BF16),
            ((total, enc_count), BF16),
            ((dec_count, total), BF16),
            ((total, dec_count), BF16),
        ]
        + [
            ((feat, feat), BF16),
            ((feat, feat), BF16),
            ((feat, feat), BF16),
            ((slots, dec_count), BF16),
        ],
        scratch=[((total, feat), BF16)],
        flops=2 * feat * (feat * (2 * grid_count + enc_count + dec_count) + total * dec_count),
    )

    def forward(*refs):
        arrived_refs, refs = refs[:arrived_count], refs[arrived_count:]
        (
            shared_pool_ref,
            enc_part_ref,
            dec_part_ref,
            mesh_part_ref,
            enc_pick_ref,
            enc_pool_ref,
            dec_pick_ref,
            dec_pool_ref,
            enc_wg_ref,
            dec_wg_ref,
            enc_w2_ref,
            mesh_wa_ref,
            mesh_w2_ref,
            mesh_ref,
            dec_wm_ref,
            dec_w2_ref,
        ) = refs[:16]
        refs = refs[16:]
        out_refs, refs = refs[:sent_count], refs[sent_count:]
        (
            slot_ref,
            enc_normed_ref,
            enc_scale_ref,
            enc_pre_ref,
            dec_normed_ref,
            dec_scale_ref,
            dec_pre_ref,
            mesh_normed_ref,
            mesh_scale_ref,
            mesh_pre_ref,
            enc_act_ref,
            dec_act_ref,
            mesh_act_ref,
            table_ref,
        ) = refs
        rows = by_slot(arrived_refs, low, staggered)
        pe = mm(rows, enc_wg_ref[low, :]).astype(BF16)
        enc_pre_ref[...] = enc_part_ref[...] + mm(enc_pick_ref[:, grid_count:spots], pe)
        write_silu(enc_pre_ref, enc_act_ref)
        write_norm(mm(enc_act_ref[...], enc_w2_ref[...]), enc_normed_ref, enc_scale_ref)
        agg = mm(enc_pool_ref[mesh_rows, :], enc_normed_ref[...]).astype(BF16)
        mesh_pre_ref[...] = mesh_part_ref[...] + mm(agg, mesh_wa_ref[high, :])
        write_silu(mesh_pre_ref, mesh_act_ref)
        write_norm(mm(mesh_act_ref[...], mesh_w2_ref[...]), mesh_normed_ref, mesh_scale_ref)
        mesh_out = (mesh_ref[...].astype(F32) + mesh_normed_ref[...]).astype(BF16)
        table_ref[:slots, :] = mm(rows, dec_wg_ref[low, :]).astype(BF16)
        table_ref[slots : slots + mesh_count, :] = mm(mesh_out, dec_wm_ref[high, :]).astype(BF16)
        table_ref[slots + mesh_count :, :] = jnp.zeros(
            (total - spots - mesh_count, feat), BF16
        )
        dec_pre_ref[...] = dec_part_ref[...] + mm(dec_pick_ref[:, grid_count:], table_ref[...])
        write_silu(dec_pre_ref, dec_act_ref)
        write_norm(mm(dec_act_ref[...], dec_w2_ref[...]), dec_normed_ref, dec_scale_ref)
        slot_sums = mm(dec_pool_ref[grid_count:spots, :], dec_normed_ref[...])
        slot_ref[...] = slot_sums
        shared = mm(shared_pool_ref[...], dec_normed_ref[...]).astype(BF16)
        slot_msg = slot_sums.astype(BF16)
        send(
            out_refs, lambda j: slot_msg[reverse[j] * width : (reverse[j] + 1) * width, :], low
        )
        send(out_refs, lambda j: shared[j * width : (j + 1) * width, :], high)

    saved_shapes = [
        ((enc_count, feat), BF16),
        ((enc_count, 1), F32),
        ((enc_count, feat), F32),
        ((dec_count, feat), BF16),
        ((dec_count, 1), F32),
        ((dec_count, feat), F32),
        ((mesh_count, feat), F32),
        ((mesh_count, 1), F32),
        ((mesh_count, feat), F32),
    ]
    results = call(
        forward,
        "edges_forward",
        [
            *arrived,
            shared_pool,
            enc_part,
            dec_part,
            mesh_part,
            enc_pick,
            enc_pool,
            dec_pick,
            dec_pool,
            enc_first,
            dec_first,
            enc_centred,
            mesh_first,
            mesh_centred,
            mesh_nodes,
            dec_first,
            dec_centred,
        ],
        sent_shapes(2 * feat)
        + [((slots, feat), F32)]
        + saved_shapes,
        scratch=[
            ((enc_count, feat), BF16),
            ((dec_count, feat), BF16),
            ((mesh_count, feat), BF16),
            ((total - grid_count, feat), BF16),
        ],
        flops=2 * feat * feat * 2 * (enc_count + dec_count),
    )
    outgoing, results = results[:sent_count], results[sent_count:]
    slot_sums, *saved = results
    enc_normed, enc_scale, enc_pre, dec_normed, dec_scale, dec_pre = saved[:6]
    mesh_normed, mesh_scale, mesh_pre = saved[6:]
    returned = exchange(outgoing, steady)

    def between(*refs):
        arrived_refs, refs = refs[:arrived_count], refs[arrived_count:]
        (
            nodes_ref,
            grid_first_ref,
            grid_second_ref,
            cot_ref,
            mesh_first_ref,
            dec_pool_ref,
            dec_normed_ref,
            mesh_second_ref,
            mesh_centred_ref,
            dec_first_ref,
            mesh_cot_ref,
            mesh_ref,
            enc_pre_ref,
            dec_pre_ref,
            mesh_normed_ref,
            mesh_pre_ref,
            local_sums_ref,
            part_ref,
            cot_rows_ref,
            cot_turned_ref,
            grid_wide_ref,
            grid_back_ref,
            mesh_back_ref,
            mesh_in_ref,
            mesh_cot_turned_ref,
            mesh_turned_ref,
            mesh_out_ref,
            mesh_slope_ref,
            enc_slope_ref,
            dec_slope_ref,
        ) = refs
        part_ref[:grid_count, :] = mm(nodes_ref[...], grid_first_ref[low, :])
        part_ref[grid_count:, :] = mm(by_slot(arrived_refs, low, staggered), grid_first_ref[low, :])
        mesh_out_ref[...] = (mesh_ref[...].astype(F32) + mesh_normed_ref[...]).astype(BF16)
        cot_rows_ref[:grid_count, :] = cot_ref[...]
        cot_rows_ref[grid_count:, :] = by_slot(arrived_refs, high, staggered)
        second = centred(grid_second_ref[...], 1).astype(BF16)
        grid_wide_ref[:, low] = second
        grid_wide_ref[:, high] = mm_t(second, grid_second_ref[...]).astype(BF16)
        cot_turned_ref[...] = mm_t(cot_rows_ref[...], second)
        grid_back_ref[...] = centred(grid_first_ref[high, :], 0).astype(BF16)
        mesh_back_ref[...] = centred(mesh_first_ref[high, :], 0).astype(BF16)
        mesh_in_ref[low, :] = dec_first_ref[high, :]
        mesh_in_ref[high, :] = mm(mesh_centred_ref[...], dec_first_ref[high, :]).astype(BF16)
        mesh_cot_turned_ref[...] = mm_t(mesh_cot_ref[...], mesh_centred_ref[...])
        mesh_turned_ref[...] = mm_t(mesh_normed_ref[...].astype(BF16), mesh_second_ref[...])
        local_sums_ref[...] = mm(dec_pool_ref[:grid_count, :], dec_normed_ref[...])
        mesh_slope_ref[...] = silu_and_slope(mesh_pre_ref[...])[1]
        write_slope(enc_pre_ref, enc_slope_ref)
        write_slope(dec_pre_ref, dec_slope_ref)

    (
        local_sums,
        grid_part,
        cot_rows,
        cot_turned,
        grid_wide,
        grid_back,
        mesh_back,
        mesh_in,
        mesh_cot_turned,
        mesh_turned,
        mesh_out,
        mesh_slope,
        enc_slope,
        dec_slope,
    ) = call(
        between,
        "slopes_and_nodes",
        [
            *arrived,
            grid_nodes,
            grid_first,
            grid_second,
            grid_cot,
            mesh_first,
            dec_pool,
            dec_normed,
            mesh_second,
            mesh_centred,
            dec_first,
            mesh_cot,
            mesh_nodes,
            enc_pre,
            dec_pre,
            mesh_normed,
            mesh_pre,
        ],
        [
            ((grid_count, feat), F32),
            ((spots, feat), F32),
            ((spots, feat), BF16),
            ((spots, feat), F32),
            ((feat, 2 * feat), BF16),
            ((feat, feat), BF16),
            ((feat, feat), BF16),
            ((2 * feat, feat), BF16),
            ((mesh_count, feat), F32),
            ((mesh_count, feat), F32),
            ((mesh_count, feat), BF16),
            ((mesh_count, feat), F32),
            ((enc_count, feat), BF16),
            ((dec_count, feat), BF16),
        ],
        flops=16 * spots * feat * feat,
    )

    def backward(*refs):
        returned_refs, refs = refs[:arrived_count], refs[arrived_count:]
        (
            local_sums_ref,
            slot_sums_ref,
            grid_part_ref,
            select_t_ref,
            cot_rows_ref,
            cot_turned_ref,
            mesh_cot_ref,
            mesh_cot_turned_ref,
            enc_pick_ref,
            enc_pool_ref,
            dec_pick_ref,
            dec_pool_ref,
            grid_first_ref,
            grid_wide_ref,
            grid_back_ref,
            mesh_back_ref,
            mesh_in_ref,
            enc_first_ref,
            enc_second_ref,
            dec_first_ref,
            dec_second_ref,
            enc_normed_ref,
            enc_scale_ref,
            enc_slope_ref,
            dec_normed_ref,
            dec_scale_ref,
            dec_slope_ref,
            mesh_normed_ref,
            mesh_scale_ref,
            mesh_slope_ref,
            mesh_turned_ref,
        ) = refs[:31]
        refs = refs[31:]
        out_refs, refs = refs[:sent_count], refs[sent_count:]
        (
            grid_normed_ref,
            grid_gpre_ref,
            dec_gpre_ref,
            enc_gpre_ref,
            mesh_gin_ref,
            mesh_gpre_ref,
            agg_ref,
            grid_act_ref,
            grid_slope_ref,
            spot_grad_ref,
        ) = refs
        agg_ref[:grid_count, :] = (
            local_sums_ref[...] + mm(select_t_ref[:, :slots], by_row(returned_refs, low))
        ).astype(BF16)
        agg_ref[grid_count:, :] = (
            slot_sums_ref[...] + by_slot(returned_refs, high).astype(F32)
        ).astype(BF16)
        pre = grid_part_ref[...] + mm(agg_ref[...], grid_first_ref[high, :])
        for rows in row_chunks(spots):
            act, slope = silu_and_slope(pre[rows, :])
            grid_act_ref[rows, :] = act.astype(BF16)
            grid_slope_ref[rows, :] = slope
        both = mm(grid_act_ref[...], grid_wide_ref[...])
        for rows in row_chunks(spots):
            part = both[rows, low]
            scale_inv = scale_rows(part)
            normed = part * scale_inv
            grid_normed_ref[rows, :] = normed
            mean = jnp.mean(cot_rows_ref[rows, :].astype(F32) * normed, axis=-1, keepdims=True)
            raw = scale_inv * (cot_turned_ref[rows, :] - (mean * scale_inv) * both[rows, high])
            grid_gpre_ref[rows, :] = (raw * grid_slope_ref[rows, :]).astype(BF16)
        spot_grad_ref[:spots, :] = mm_t(grid_gpre_ref[...], grid_back_ref[...]).astype(BF16)
        spot_grad_ref[spots:, :] = jnp.zeros((total - spots, feat), BF16)
        edge_back(
            mm(dec_pick_ref[...], spot_grad_ref[...]),
            dec_normed_ref,
            dec_scale_ref,
            dec_second_ref,
            dec_slope_ref,
            dec_gpre_ref,
        )
        mesh_sum = mm(dec_pool_ref[mesh_rows, :], dec_gpre_ref[...]).astype(BF16)
        both = mm_t(mesh_sum, mesh_in_ref[...])
        mesh_gin = mesh_cot_ref[...].astype(F32) + both[:, low]
        mesh_gin_ref[...] = mesh_gin
        mean = jnp.mean(mesh_gin * mesh_normed_ref[...], axis=-1, keepdims=True)
        raw = mesh_cot_turned_ref[...] + both[:, high] - mean * mesh_turned_ref[...]
        mesh_gpre_ref[...] = (mesh_scale_ref[...] * raw * mesh_slope_ref[...]).astype(BF16)
        mesh_gagg = mm_t(mesh_gpre_ref[...], mesh_back_ref[...]).astype(BF16)
        pooled = mm(dec_pool_ref[grid_count:spots, :], dec_gpre_ref[...]).astype(BF16)
        slot_back = mm_t(pooled, dec_first_ref[low, :])
        edge_back(
            mm(enc_pick_ref[:, mesh_rows], mesh_gagg),
            enc_normed_ref,
            enc_scale_ref,
            enc_second_ref,
            enc_slope_ref,
            enc_gpre_ref,
        )
        pooled = mm(enc_pool_ref[grid_count:spots, :], enc_gpre_ref[...]).astype(BF16)
        slot_back = (slot_back + mm_t(pooled, enc_first_ref[low, :])).astype(BF16)
        send(out_refs, lambda j: slot_back[reverse[j] * width : (reverse[j] + 1) * width, :])

    results = call(
        backward,
        "edges_backward",
        [
            *returned,
            local_sums,
            slot_sums,
            grid_part,
            select_t,
            cot_rows,
            cot_turned,
            mesh_cot,
            mesh_cot_turned,
            enc_pick,
            enc_pool,
            dec_pick,
            dec_pool,
            grid_first,
            grid_wide,
            grid_back,
            mesh_back,
            mesh_in,
            enc_first,
            enc_second,
            dec_first,
            dec_second,
            enc_normed,
            enc_scale,
            enc_slope,
            dec_normed,
            dec_scale,
            dec_slope,
            mesh_normed,
            mesh_scale,
            mesh_slope,
            mesh_turned,
        ],
        sent_shapes(feat)
        + [
            ((spots, feat), F32),
            ((spots, feat), BF16),
            ((dec_count, feat), BF16),
            ((enc_count, feat), BF16),
            ((mesh_count, feat), F32),
            ((mesh_count, feat), BF16),
        ],
        scratch=[
            ((spots, feat), BF16),
            ((spots, feat), BF16),
            ((spots, feat), F32),
            ((total, feat), BF16),
        ],
        flops=2 * feat * feat * (4 * spots + 3 * dec_count + 2 * enc_count),
    )
    outgoing, results = results[:sent_count], results[sent_count:]
    grid_normed, grid_gpre, dec_gpre, enc_gpre, mesh_gin, mesh_gpre = results
    final = exchange(outgoing, steady)

    def tail(
        nodes_ref,
        grid_normed_ref,
        cot_ref,
        grid_gpre_ref,
        enc_pool_ref,
        enc_gpre_ref,
        dec_pool_ref,
        dec_gpre_ref,
        mesh_gin_ref,
        mesh_gpre_ref,
        grid_wn_ref,
        enc_wg_ref,
        dec_wg_ref,
        mesh_wn_ref,
        enc_wm_ref,
        base_ref,
        grad_mesh_ref,
        grid_out_ref,
    ):
        grid_out_ref[...] = (
            nodes_ref[...].astype(F32) + grid_normed_ref[:grid_count, :]
        ).astype(BF16)
        enc_sums = mm(enc_pool_ref[:grid_count, :], enc_gpre_ref[...]).astype(BF16)
        mesh_sums = mm(enc_pool_ref[mesh_rows, :], enc_gpre_ref[...]).astype(BF16)
        dec_sums = mm(dec_pool_ref[:grid_count, :], dec_gpre_ref[...]).astype(BF16)
        base_ref[...] = (
            cot_ref[...].astype(F32)
            + mm_t(grid_gpre_ref[:grid_count, :], grid_wn_ref[low, :])
            + mm_t(enc_sums, enc_wg_ref[low, :])
            + mm_t(dec_sums, dec_wg_ref[low, :])
        )
        grad_mesh_ref[...] = (
            mesh_gin_ref[...]
            + mm_t(mesh_gpre_ref[...], mesh_wn_ref[low, :])
            + mm_t(mesh_sums, enc_wm_ref[high, :])
        )

    base, grad_mesh, grid_out = call(
        tail,
        "local_gradients",
        [
            grid_nodes,
            grid_normed,
            grid_cot,
            grid_gpre,
            enc_pool,
            enc_gpre,
            dec_pool,
            dec_gpre,
            mesh_gin,
            mesh_gpre,
            grid_first,
            enc_first,
            dec_first,
            mesh_first,
            enc_first,
        ],
        [((grid_count, feat), F32), ((mesh_count, feat), F32), ((grid_count, feat), BF16)],
        flops=2 * feat * feat * 3 * grid_count,
    )

    pieces = row_chunks(grid_count, 64)

    def finish(*refs):
        back_refs = refs[:arrived_count]
        base_ref, select_t_ref, out_ref, piece_ref, semaphores = refs[arrived_count:]
        back = by_row(back_refs)
        copies = []
        for place, rows in enumerate(pieces):
            piece_ref[rows, :] = base_ref[rows, :] + mm(select_t_ref[rows, :slots], back)
            copies.append(
                pltpu.make_async_copy(
                    piece_ref.at[rows, :], out_ref.at[rows, :], semaphores.at[place]
                )
            )
            copies[-1].start()
        for copy in copies:
            copy.wait()

    grad_grid = pl.pallas_call(
        finish,
        name="add_returned",
        in_specs=[pl.BlockSpec(memory_space=pltpu.VMEM)] * (arrived_count + 2),
        out_specs=pl.BlockSpec(memory_space=pltpu.HBM),
        out_shape=jax.ShapeDtypeStruct((grid_count, feat), F32),
        scratch_shapes=[
            pltpu.VMEM((grid_count, feat), F32),
            pltpu.SemaphoreType.DMA((len(pieces),)),
        ],
        compiler_params=pltpu.CompilerParams(vmem_limit_bytes=VMEM_LIMIT),
    )(*final, base, select_t)
    return (grid_out, mesh_out, grad_grid, grad_mesh)


def solution(mesh):
    rows = P(("groups", "tile"), None)
    flat = P(("groups", "tile"))
    in_specs = (rows,) * 6 + (P(),) * 8 + (rows,) + (flat,) * 5
    return jax.shard_map(
        per_device, mesh=mesh, in_specs=in_specs, out_specs=(rows,) * 4, check_vma=False
    )
```

```python
import jax
import jax.numpy as jnp
from jax import lax
from jax.experimental import pallas as pl
from jax.experimental.pallas import tpu as pltpu
from jax.sharding import PartitionSpec as P

TW = 4
CHUNK = 32
ROUND_FLOPS = 2 * 10**10
F32 = jnp.float32
BF16 = jnp.bfloat16
VMEM_LIMIT = 30 * 1024 * 1024


def mm(left, right):
    return jnp.dot(left, right, preferred_element_type=F32)


def mm_t(left, right):
    return lax.dot_general(left, right, (((1,), (1,)), ((), ())), preferred_element_type=F32)


def centred(values, axis):
    values = values.astype(F32)
    return values - jnp.mean(values, axis=axis, keepdims=True)


def silu_and_slope(pre):
    half = 0.5 * pre
    lifted = 1.0 + jnp.tanh(half)
    return half * lifted, lifted * (0.5 + 0.5 * half * (2.0 - lifted))


def silu(pre):
    half = 0.5 * pre
    return half * (1.0 + jnp.tanh(half))


def scale_rows(raw):
    return lax.rsqrt(jnp.mean(raw * raw, axis=-1, keepdims=True) + 1e-05)


def row_chunks(rows, size=CHUNK):
    return [slice(start, min(start + size, rows)) for start in range(0, rows, size)]


def write_silu(pre, act_ref):
    for rows in row_chunks(pre.shape[0]):
        act_ref[rows, :] = silu(pre[rows, :]).astype(BF16)


def write_norm(raw, normed_ref, scale_ref):
    for rows in row_chunks(raw.shape[0]):
        part = raw[rows, :]
        scale_inv = scale_rows(part)
        normed_ref[rows, :] = (part * scale_inv).astype(normed_ref.dtype)
        scale_ref[rows, :] = scale_inv


def write_slope(pre_ref, slope_ref):
    for rows in row_chunks(pre_ref.shape[0]):
        slope_ref[rows, :] = silu_and_slope(pre_ref[rows, :])[1].astype(BF16)


def edge_back(upstream, normed_ref, scale_ref, second_ref, slope_ref, out_ref):
    for rows in row_chunks(upstream.shape[0]):
        part, normed = upstream[rows, :], normed_ref[rows, :]
        mean = jnp.mean(part * normed.astype(F32), axis=-1, keepdims=True)
        out_ref[rows, :] = scale_ref[rows, :].astype(BF16) * (
            part.astype(BF16) - normed * mean.astype(BF16)
        )
    raw = mm_t(out_ref[...], second_ref[...])
    for rows in row_chunks(upstream.shape[0]):
        out_ref[rows, :] = raw[rows, :].astype(BF16) * slope_ref[rows, :]


def neighbour_offsets(peer_count):
    forward_half = [1, TW, TW + 1, TW - 1]
    return forward_half + [-offset for offset in forward_half] + [peer_count // 2]


def onehot_pair(spot_ref, mesh_ref, spots, mesh_count, by_edge_ref, by_spot_ref):
    edges, total = by_edge_ref.shape
    spot_row = spot_ref[...].reshape(1, -1)
    mesh_row = mesh_ref[...].reshape(1, -1) + spots
    one, zero = jnp.ones((), BF16), jnp.zeros((), BF16)

    def ones(ids, index):
        shape = jnp.broadcast_shapes(ids.shape, index.shape)
        hit = jnp.broadcast_to(ids, shape) == jnp.broadcast_to(index, shape)
        return jnp.where(hit, jnp.broadcast_to(one, shape), jnp.broadcast_to(zero, shape))

    for row, first, count in ((spot_row, 0, spots), (mesh_row, spots, mesh_count)):
        ids = lax.broadcasted_iota(jnp.int32, (16, edges), 0).astype(jnp.int16)
        wide = jnp.broadcast_to(row, (16, edges)).astype(jnp.int16)
        for rows in row_chunks(count, 16):
            rows = slice(rows.start + first, rows.stop + first)
            by_spot_ref[rows, :] = ones(ids, wide - jnp.int16(rows.start))
    by_spot_ref[spots + mesh_count :, :] = jnp.zeros((total - spots - mesh_count, edges), BF16)
    lane = lax.broadcasted_iota(jnp.int32, (16, 128), 1).astype(jnp.int16)
    for rows in row_chunks(edges, 128):
        spot_col = jnp.broadcast_to(spot_row[:, rows], (128, 128)).T.astype(jnp.int16)
        mesh_col = jnp.broadcast_to(mesh_row[:, rows], (128, 128)).T.astype(jnp.int16)
        for columns in row_chunks(total, 128):
            for part in row_chunks(128, 16):
                place = slice(rows.start + part.start, rows.start + part.stop)
                ids = lane + jnp.int16(columns.start)
                hits = []
                if columns.start < spots:
                    hits.append(ones(ids, spot_col[part, :]))
                if columns.stop > spots:
                    hits.append(ones(ids, mesh_col[part, :]))
                by_edge_ref[place, columns] = sum(hits[1:], hits[0])


class Fetched:
    def __init__(self, source, target, semaphore):
        self.copy = pltpu.make_async_copy(source, target, semaphore)
        self.target = target
        self.landed = False
        self.copy.start()

    def land(self):
        if not self.landed:
            self.copy.wait()
            self.landed = True

    def __getitem__(self, key):
        self.land()
        return self.target[key]


def call(body, name, inputs, outputs, scratch=(), flops=0):
    arrays, specs, moved, fetches = [], [], 0, []
    for place, entry in enumerate(inputs):
        if isinstance(entry, tuple):
            array, first, rows = entry
            array = pltpu.with_memory_space_constraint(array, pltpu.HBM)
            specs.append(pl.BlockSpec(memory_space=pltpu.HBM))
            shape = (rows,) + array.shape[1:]
            fetches.append((place, first, rows, shape, array.dtype))
            moved += rows * (array.size // array.shape[0]) * array.dtype.itemsize
        else:
            array = entry
            specs.append(pl.BlockSpec(memory_space=pltpu.VMEM))
            moved += array.size * array.dtype.itemsize
        arrays.append(array)
    shapes = [jax.ShapeDtypeStruct(shape, dtype) for shape, dtype in outputs]
    for shape in shapes:
        moved += shape.size * shape.dtype.itemsize
    buffers = [pltpu.VMEM(shape, dtype) for _, _, _, shape, dtype in fetches]
    if fetches:
        buffers.append(pltpu.SemaphoreType.DMA((len(fetches),)))

    def kernel(*refs):
        refs = list(refs)
        waiting = []
        if fetches:
            targets, semaphores = refs[-len(buffers) : -1], refs[-1]
            refs = refs[: -len(buffers)]
        for slot, (place, first, rows, shape, _) in enumerate(fetches):
            source = refs[place]
            if source.shape != shape:
                source = source.at[pl.ds(first, rows)]
            refs[place] = Fetched(source, targets[slot], semaphores.at[slot])
            waiting.append(refs[place])
        body(*refs)
        for fetched in waiting:
            fetched.land()

    return pl.pallas_call(
        kernel,
        name=name,
        in_specs=specs,
        out_specs=[pl.BlockSpec(memory_space=pltpu.VMEM) for _ in shapes],
        out_shape=shapes,
        scratch_shapes=[pltpu.VMEM(shape, dtype) for shape, dtype in scratch]
        + buffers,
        compiler_params=pltpu.CompilerParams(vmem_limit_bytes=VMEM_LIMIT),
        cost_estimate=pl.CostEstimate(flops=flops, bytes_accessed=moved, transcendentals=0),
    )(*arrays)


def per_device(
    grid_nodes,
    mesh_nodes,
    enc_edges,
    dec_edges,
    grid_cot,
    mesh_cot,
    enc_first,
    enc_second,
    mesh_first,
    mesh_second,
    dec_first,
    dec_second,
    grid_first,
    grid_second,
    send_index,
    send_count,
    enc_grid,
    enc_mesh,
    dec_grid,
    dec_mesh,
):
    grid_count, feat = grid_nodes.shape
    mesh_count = mesh_nodes.shape[0]
    enc_count = enc_edges.shape[0]
    dec_count = dec_edges.shape[0]
    links, width = send_index.shape
    slots = links * width
    slots_pad = -(-slots // 128) * 128
    spots = grid_count + slots
    total = -(-(spots + mesh_count) // 128) * 128
    peer_count = lax.axis_size("tile")
    offsets = neighbour_offsets(peer_count)
    half = (links - 1) // 2
    reverse = [(j + half) % (links - 1) for j in range(links - 1)] + [links - 1]
    low, high = slice(0, feat), slice(feat, 2 * feat)
    mesh_rows = slice(spots, spots + mesh_count)

    one, four, five, three = range(half)
    minus = [j + half for j in range(half)]
    across = links - 1
    peers = range(peer_count)

    def permute(part, steps, odd_row_steps=None):
        rows = (steps, odd_row_steps or steps)
        pairs = [(s, (s + rows[s // TW % 2][s % 2]) % peer_count) for s in peers]
        return lax.ppermute(part, "tile", pairs)

    steady = ("late", "early", "behind", "ahead", "five", "opposite", "own")
    staggered = ("early", "late", "ahead", "five", "behind", "opposite", "own")
    arrived_count = 9

    def exchange(parts, order):
        moves = {
            "late": ((-4, -4), (4, 4)),
            "early": ((4, 4), (-4, -4)),
            "behind": ((-1, 1),),
            "ahead": ((3, -3),),
            "five": ((-5, 5),),
            "opposite": ((peer_count // 2, peer_count // 2),),
            "own": ((1, -1),),
        }
        parts = dict(zip(order, parts))
        own_chip = parts.pop("own")
        got = {name: permute(part, *moves[name]) for name, part in parts.items()}
        first = order[0]
        got[first], own_chip = lax.optimization_barrier((got[first], own_chip))
        late_passed = permute(got["late"], (1, -1))
        got["own"] = permute(own_chip, (1, -1))
        early_passed = permute(got["early"], (1, -1))
        return [got[name] for name in order] + [late_passed, early_passed]

    def sent_shapes(columns, order=steady):
        double = ("late", "early")
        return [((width * (1 + (name in double)), columns), BF16) for name in order]

    sent_count = len(steady)

    def place_bits():
        own = lax.axis_index("tile")
        return lax.rem(own, 2) == 1, lax.rem(lax.div(own, TW), 2) == 1

    def send(refs, message, columns=slice(None), order=steady):
        odd, odd_row = place_bits()
        refs = dict(zip(order, refs))

        def by_parity(even, odd_one):
            return jnp.where(odd, message(odd_one), message(even))

        late_pair, early_pair, behind_one, ahead_three, five_off, opposite, own_chip = [
            refs[name] for name in steady
        ]
        first, second = slice(0, width), slice(width, 2 * width)
        ahead = message(four), by_parity(five, three)
        behind = message(minus[four]), by_parity(minus[three], minus[five])
        for rows, go_ahead, go_behind in zip((first, second), ahead, behind):
            late_pair[rows, columns] = jnp.where(odd_row, go_ahead, go_behind)
            early_pair[rows, columns] = jnp.where(odd_row, go_behind, go_ahead)
        behind_one[:, columns] = by_parity(minus[one], one)
        ahead_three[:, columns] = by_parity(three, minus[three])
        five_off[:, columns] = by_parity(minus[five], five)
        opposite[:, columns] = message(across)
        own_chip[:, columns] = by_parity(one, minus[one])

    def receive(refs, columns=slice(None), order=steady):
        odd, odd_row = place_bits()
        late_passed, early_passed = refs[sent_count:]
        refs = dict(zip(order, refs))
        late_pair, early_pair, behind_one, ahead_three, five_off, opposite, own_chip = [
            refs[name] for name in steady
        ]
        first, second = slice(0, width), slice(width, 2 * width)
        near, near_three = behind_one[:, columns], ahead_three[:, columns]
        far, own = five_off[:, columns], own_chip[:, columns]
        late_rows, early_rows = late_passed[second, columns], early_passed[second, columns]
        from_behind = jnp.where(odd_row, early_rows, late_rows)
        from_ahead = jnp.where(odd_row, late_rows, early_rows)
        late_rows, early_rows = late_pair[first, columns], early_pair[first, columns]
        slot_rows = [None] * links
        slot_rows[one] = jnp.where(odd, own, near)
        slot_rows[minus[one]] = jnp.where(odd, near, own)
        slot_rows[three] = jnp.where(odd, near_three, from_behind)
        slot_rows[minus[three]] = jnp.where(odd, from_ahead, near_three)
        slot_rows[five] = jnp.where(odd, from_behind, far)
        slot_rows[minus[five]] = jnp.where(odd, far, from_ahead)
        slot_rows[four] = jnp.where(odd_row, early_rows, late_rows)
        slot_rows[minus[four]] = jnp.where(odd_row, late_rows, early_rows)
        slot_rows[across] = opposite[:, columns]
        return slot_rows

    def by_slot(refs, columns=slice(None), order=steady):
        return jnp.concatenate(receive(refs, columns, order), axis=0)

    def by_row(refs, columns=slice(None)):
        slot_rows = receive(refs, columns)
        return jnp.concatenate([slot_rows[reverse[j]] for j in range(links)], axis=0)

    def pack(index_ref, count_ref, nodes_ref, cot_ref, select_ref, *out_refs):
        def column(row):
            count = row.shape[1]
            eye = lax.broadcasted_iota(jnp.int32, (count, count), 0) == lax.broadcasted_iota(
                jnp.int32, (count, count), 1
            )
            return jnp.sum(
                jnp.where(eye, jnp.broadcast_to(row, (count, count)), 0.0), axis=1, keepdims=True
            )

        counts = column(count_ref[...].reshape(1, -1).astype(F32))
        place = lax.broadcasted_iota(jnp.int32, (links, width), 1).astype(F32)
        index = jnp.where(place < counts, index_ref[...].astype(F32), -1.0)
        lane = lax.broadcasted_iota(jnp.int32, (width, grid_count), 1).astype(F32)
        picks = [
            jnp.where(lane == column(index[j : j + 1, :]), 1.0, 0.0).astype(BF16)
            for j in range(links)
        ]
        select = jnp.concatenate(picks, axis=0)
        select_ref[:slots, :] = select
        select_ref[slots:, :] = jnp.zeros((slots_pad - slots, grid_count), BF16)
        sent_nodes = mm(select, nodes_ref[...]).astype(BF16)
        sent_cot = mm(select, cot_ref[...]).astype(BF16)
        send(
            out_refs, lambda j: sent_nodes[j * width : (j + 1) * width, :], low, staggered
        )
        send(out_refs, lambda j: sent_cot[j * width : (j + 1) * width, :], high, staggered)

    select, *outgoing = call(
        pack,
        "pack_rows",
        [
            (send_index, 0, links),
            (send_count, 0, links),
            (grid_nodes, 0, grid_count),
            (grid_cot, 0, grid_count),
        ],
        [((slots_pad, grid_count), BF16)] + sent_shapes(2 * feat, staggered),
        flops=4 * slots * grid_count * feat,
    )
    def turn(select_ref, select_t_ref):
        select_t_ref[...] = select_ref[...].astype(F32).T.astype(BF16)

    (select_t,) = call(
        turn, "turn_select", [select], [((grid_count, slots_pad), BF16)], flops=ROUND_FLOPS
    )
    *outgoing, select_t = lax.optimization_barrier((*outgoing, select_t))
    arrived = exchange(outgoing, staggered)

    def local(
        select_ref,
        nodes_ref,
        mesh_ref,
        enc_edges_ref,
        dec_edges_ref,
        enc_first_ref,
        dec_first_ref,
        mesh_first_ref,
        enc_grid_ref,
        enc_mesh_ref,
        dec_grid_ref,
        dec_mesh_ref,
        enc_second_ref,
        mesh_second_ref,
        dec_second_ref,
        enc_part_ref,
        dec_part_ref,
        mesh_part_ref,
        enc_pick_ref,
        enc_pool_ref,
        dec_pick_ref,
        dec_pool_ref,
        enc_centred_ref,
        dec_centred_ref,
        mesh_centred_ref,
        sent_pool_ref,
        table_ref,
    ):
        onehot_pair(enc_grid_ref, enc_mesh_ref, spots, mesh_count, enc_pick_ref, enc_pool_ref)
        onehot_pair(dec_grid_ref, dec_mesh_ref, spots, mesh_count, dec_pick_ref, dec_pool_ref)
        enc_centred_ref[...] = centred(enc_second_ref[...], 1).astype(BF16)
        mesh_centred_ref[...] = centred(mesh_second_ref[...], 1).astype(BF16)
        sent_pool_ref[:slots, :] = dec_pool_ref[grid_count:spots, :]
        sent_pool_ref[slots:, :] = mm(
            select_ref[:slots, :], dec_pool_ref[:grid_count, :]
        ).astype(BF16)
        dec_centred_ref[...] = centred(dec_second_ref[...], 1).astype(BF16)
        nodes = nodes_ref[...]
        mesh_part_ref[...] = mm(mesh_ref[...], mesh_first_ref[low, :])
        table_ref[:grid_count, :] = mm(nodes, enc_first_ref[low, :]).astype(BF16)
        table_ref[grid_count:, :] = jnp.zeros((total - grid_count, feat), BF16)
        table_ref[mesh_rows, :] = mm(mesh_ref[...], enc_first_ref[high, :]).astype(BF16)
        enc_part_ref[...] = mm(enc_edges_ref[...], enc_first_ref[2 * feat :, :])
        enc_part_ref[...] += mm(enc_pick_ref[...], table_ref[...])
        pd = mm(nodes, dec_first_ref[low, :]).astype(BF16)
        dec_part_ref[...] = mm(dec_edges_ref[...], dec_first_ref[2 * feat :, :])
        dec_part_ref[...] += mm(dec_pick_ref[:, :grid_count], pd)

    (
        enc_part,
        dec_part,
        mesh_part,
        enc_pick,
        enc_pool,
        dec_pick,
        dec_pool,
        enc_centred,
        dec_centred,
        mesh_centred,
        sent_pool,
    ) = call(
        local,
        "local_products",
        [
            select,
            grid_nodes,
            mesh_nodes,
            enc_edges,
            dec_edges,
            enc_first,
            dec_first,
            mesh_first,
            enc_grid,
            enc_mesh,
            dec_grid,
            dec_mesh,
            enc_second,
            mesh_second,
            dec_second,
        ],
        [
            ((enc_count, feat), F32),
            ((dec_count, feat), F32),
            ((mesh_count, feat), F32),
            ((enc_count, total), BF16),
            ((total, enc_count), BF16),
            ((dec_count, total), BF16),
            ((total, dec_count), BF16),
        ]
        + [
            ((feat, feat), BF16),
            ((feat, feat), BF16),
            ((feat, feat), BF16),
            ((2 * slots, dec_count), BF16),
        ],
        scratch=[((total, feat), BF16)],
        flops=2 * feat * (feat * (2 * grid_count + enc_count + dec_count) + total * dec_count),
    )

    def forward(*refs):
        arrived_refs, refs = refs[:arrived_count], refs[arrived_count:]
        (
            sent_pool_ref,
            enc_part_ref,
            dec_part_ref,
            mesh_part_ref,
            enc_pick_ref,
            enc_pool_ref,
            dec_pick_ref,
            enc_wg_ref,
            dec_wg_ref,
            enc_w2_ref,
            mesh_wa_ref,
            mesh_w2_ref,
            mesh_ref,
            dec_wm_ref,
            dec_w2_ref,
        ) = refs[:15]
        refs = refs[15:]
        out_refs, refs = refs[:sent_count], refs[sent_count:]
        (
            slot_ref,
            enc_normed_ref,
            enc_scale_ref,
            enc_pre_ref,
            dec_normed_ref,
            dec_scale_ref,
            dec_pre_ref,
            mesh_normed_ref,
            mesh_scale_ref,
            mesh_pre_ref,
            enc_act_ref,
            dec_act_ref,
            mesh_act_ref,
            table_ref,
        ) = refs
        rows = by_slot(arrived_refs, low, staggered)
        pe = mm(rows, enc_wg_ref[low, :]).astype(BF16)
        enc_pre_ref[...] = enc_part_ref[...] + mm(enc_pick_ref[:, grid_count:spots], pe)
        write_silu(enc_pre_ref, enc_act_ref)
        write_norm(mm(enc_act_ref[...], enc_w2_ref[...]), enc_normed_ref, enc_scale_ref)
        agg = mm(enc_pool_ref[mesh_rows, :], enc_normed_ref[...]).astype(BF16)
        mesh_pre_ref[...] = mesh_part_ref[...] + mm(agg, mesh_wa_ref[high, :])
        write_silu(mesh_pre_ref, mesh_act_ref)
        write_norm(mm(mesh_act_ref[...], mesh_w2_ref[...]), mesh_normed_ref, mesh_scale_ref)
        mesh_out = (mesh_ref[...].astype(F32) + mesh_normed_ref[...]).astype(BF16)
        table_ref[:slots, :] = mm(rows, dec_wg_ref[low, :]).astype(BF16)
        table_ref[slots : slots + mesh_count, :] = mm(mesh_out, dec_wm_ref[high, :]).astype(BF16)
        table_ref[slots + mesh_count :, :] = jnp.zeros(
            (total - spots - mesh_count, feat), BF16
        )
        dec_pre_ref[...] = dec_part_ref[...] + mm(dec_pick_ref[:, grid_count:], table_ref[...])
        write_silu(dec_pre_ref, dec_act_ref)
        write_norm(mm(dec_act_ref[...], dec_w2_ref[...]), dec_normed_ref, dec_scale_ref)
        sums = mm(sent_pool_ref[...], dec_normed_ref[...])
        slot_ref[...] = sums[:slots, :]
        shared = sums[slots:, :].astype(BF16)
        slot_msg = sums[:slots, :].astype(BF16)
        send(
            out_refs, lambda j: slot_msg[reverse[j] * width : (reverse[j] + 1) * width, :], low
        )
        send(out_refs, lambda j: shared[j * width : (j + 1) * width, :], high)

    saved_shapes = [
        ((enc_count, feat), BF16),
        ((enc_count, 1), F32),
        ((enc_count, feat), F32),
        ((dec_count, feat), BF16),
        ((dec_count, 1), F32),
        ((dec_count, feat), F32),
        ((mesh_count, feat), F32),
        ((mesh_count, 1), F32),
        ((mesh_count, feat), F32),
    ]
    results = call(
        forward,
        "edges_forward",
        [
            *arrived,
            sent_pool,
            enc_part,
            dec_part,
            mesh_part,
            enc_pick,
            enc_pool,
            dec_pick,
            enc_first,
            dec_first,
            enc_centred,
            mesh_first,
            mesh_centred,
            mesh_nodes,
            dec_first,
            dec_centred,
        ],
        sent_shapes(2 * feat)
        + [((slots, feat), F32)]
        + saved_shapes,
        scratch=[
            ((enc_count, feat), BF16),
            ((dec_count, feat), BF16),
            ((mesh_count, feat), BF16),
            ((total - grid_count, feat), BF16),
        ],
        flops=2 * feat * feat * 2 * (enc_count + dec_count),
    )
    outgoing, results = results[:sent_count], results[sent_count:]
    slot_sums, *saved = results
    enc_normed, enc_scale, enc_pre, dec_normed, dec_scale, dec_pre = saved[:6]
    mesh_normed, mesh_scale, mesh_pre = saved[6:]
    returned = exchange(outgoing, steady)

    def between(*refs):
        arrived_refs, refs = refs[:arrived_count], refs[arrived_count:]
        (
            nodes_ref,
            grid_first_ref,
            grid_second_ref,
            cot_ref,
            mesh_first_ref,
            dec_pool_ref,
            dec_normed_ref,
            mesh_second_ref,
            mesh_centred_ref,
            dec_first_ref,
            mesh_cot_ref,
            mesh_ref,
            enc_pre_ref,
            dec_pre_ref,
            mesh_normed_ref,
            mesh_pre_ref,
            local_sums_ref,
            part_ref,
            cot_rows_ref,
            cot_turned_ref,
            grid_wide_ref,
            grid_back_ref,
            mesh_back_ref,
            mesh_in_ref,
            mesh_cot_turned_ref,
            mesh_turned_ref,
            mesh_out_ref,
            mesh_slope_ref,
            enc_slope_ref,
            dec_slope_ref,
        ) = refs
        part_ref[:grid_count, :] = mm(nodes_ref[...], grid_first_ref[low, :])
        part_ref[grid_count:, :] = mm(by_slot(arrived_refs, low, staggered), grid_first_ref[low, :])
        mesh_out_ref[...] = (mesh_ref[...].astype(F32) + mesh_normed_ref[...]).astype(BF16)
        cot_rows_ref[:grid_count, :] = cot_ref[...]
        cot_rows_ref[grid_count:, :] = by_slot(arrived_refs, high, staggered)
        second = centred(grid_second_ref[...], 1).astype(BF16)
        grid_wide_ref[:, low] = second
        grid_wide_ref[:, high] = mm_t(second, grid_second_ref[...]).astype(BF16)
        cot_turned_ref[...] = mm_t(cot_rows_ref[...], second)
        grid_back_ref[...] = centred(grid_first_ref[high, :], 0).astype(BF16)
        mesh_back_ref[...] = centred(mesh_first_ref[high, :], 0).astype(BF16)
        mesh_in_ref[low, :] = dec_first_ref[high, :]
        mesh_in_ref[high, :] = mm(mesh_centred_ref[...], dec_first_ref[high, :]).astype(BF16)
        mesh_cot_turned_ref[...] = mm_t(mesh_cot_ref[...], mesh_centred_ref[...])
        mesh_turned_ref[...] = mm_t(mesh_normed_ref[...].astype(BF16), mesh_second_ref[...])
        local_sums_ref[...] = mm(dec_pool_ref[:grid_count, :], dec_normed_ref[...])
        mesh_slope_ref[...] = silu_and_slope(mesh_pre_ref[...])[1]
        write_slope(enc_pre_ref, enc_slope_ref)
        write_slope(dec_pre_ref, dec_slope_ref)

    (
        local_sums,
        grid_part,
        cot_rows,
        cot_turned,
        grid_wide,
        grid_back,
        mesh_back,
        mesh_in,
        mesh_cot_turned,
        mesh_turned,
        mesh_out,
        mesh_slope,
        enc_slope,
        dec_slope,
    ) = call(
        between,
        "slopes_and_nodes",
        [
            *arrived,
            grid_nodes,
            grid_first,
            grid_second,
            grid_cot,
            mesh_first,
            dec_pool,
            dec_normed,
            mesh_second,
            mesh_centred,
            dec_first,
            mesh_cot,
            mesh_nodes,
            enc_pre,
            dec_pre,
            mesh_normed,
            mesh_pre,
        ],
        [
            ((grid_count, feat), F32),
            ((spots, feat), F32),
            ((spots, feat), BF16),
            ((spots, feat), F32),
            ((feat, 2 * feat), BF16),
            ((feat, feat), BF16),
            ((feat, feat), BF16),
            ((2 * feat, feat), BF16),
            ((mesh_count, feat), F32),
            ((mesh_count, feat), F32),
            ((mesh_count, feat), BF16),
            ((mesh_count, feat), F32),
            ((enc_count, feat), BF16),
            ((dec_count, feat), BF16),
        ],
        flops=16 * spots * feat * feat,
    )

    def backward(*refs):
        returned_refs, refs = refs[:arrived_count], refs[arrived_count:]
        (
            local_sums_ref,
            slot_sums_ref,
            grid_part_ref,
            select_t_ref,
            cot_rows_ref,
            cot_turned_ref,
            mesh_cot_ref,
            mesh_cot_turned_ref,
            enc_pick_ref,
            enc_pool_ref,
            dec_pick_ref,
            dec_pool_ref,
            grid_first_ref,
            grid_wide_ref,
            grid_back_ref,
            mesh_back_ref,
            mesh_in_ref,
            enc_first_ref,
            enc_second_ref,
            dec_first_ref,
            dec_second_ref,
            enc_normed_ref,
            enc_scale_ref,
            enc_slope_ref,
            dec_normed_ref,
            dec_scale_ref,
            dec_slope_ref,
            mesh_normed_ref,
            mesh_scale_ref,
            mesh_slope_ref,
            mesh_turned_ref,
        ) = refs[:31]
        refs = refs[31:]
        out_refs, refs = refs[:sent_count], refs[sent_count:]
        (
            grid_normed_ref,
            grid_gpre_ref,
            dec_gpre_ref,
            enc_gpre_ref,
            mesh_gin_ref,
            mesh_gpre_ref,
            agg_ref,
            grid_act_ref,
            grid_slope_ref,
            spot_grad_ref,
        ) = refs
        agg_ref[:grid_count, :] = (
            local_sums_ref[...] + mm(select_t_ref[:, :slots], by_row(returned_refs, low))
        ).astype(BF16)
        agg_ref[grid_count:, :] = (
            slot_sums_ref[...] + by_slot(returned_refs, high).astype(F32)
        ).astype(BF16)
        pre = grid_part_ref[...] + mm(agg_ref[...], grid_first_ref[high, :])
        for rows in row_chunks(spots):
            act, slope = silu_and_slope(pre[rows, :])
            grid_act_ref[rows, :] = act.astype(BF16)
            grid_slope_ref[rows, :] = slope
        both = mm(grid_act_ref[...], grid_wide_ref[...])
        for rows in row_chunks(spots):
            part = both[rows, low]
            scale_inv = scale_rows(part)
            normed = part * scale_inv
            grid_normed_ref[rows, :] = normed
            mean = jnp.mean(cot_rows_ref[rows, :].astype(F32) * normed, axis=-1, keepdims=True)
            raw = scale_inv * (cot_turned_ref[rows, :] - (mean * scale_inv) * both[rows, high])
            grid_gpre_ref[rows, :] = (raw * grid_slope_ref[rows, :]).astype(BF16)
        spot_grad_ref[:spots, :] = mm_t(grid_gpre_ref[...], grid_back_ref[...]).astype(BF16)
        spot_grad_ref[spots:, :] = jnp.zeros((total - spots, feat), BF16)
        edge_back(
            mm(dec_pick_ref[...], spot_grad_ref[...]),
            dec_normed_ref,
            dec_scale_ref,
            dec_second_ref,
            dec_slope_ref,
            dec_gpre_ref,
        )
        sums = mm(
            dec_pool_ref[grid_count : spots + mesh_count, :], dec_gpre_ref[...]
        ).astype(BF16)
        both = mm_t(sums[slots:, :], mesh_in_ref[...])
        mesh_gin = mesh_cot_ref[...].astype(F32) + both[:, low]
        mesh_gin_ref[...] = mesh_gin
        mean = jnp.mean(mesh_gin * mesh_normed_ref[...], axis=-1, keepdims=True)
        raw = mesh_cot_turned_ref[...] + both[:, high] - mean * mesh_turned_ref[...]
        mesh_gpre_ref[...] = (mesh_scale_ref[...] * raw * mesh_slope_ref[...]).astype(BF16)
        mesh_gagg = mm_t(mesh_gpre_ref[...], mesh_back_ref[...]).astype(BF16)
        slot_back = mm_t(sums[:slots, :], dec_first_ref[low, :])
        edge_back(
            mm(enc_pick_ref[:, mesh_rows], mesh_gagg),
            enc_normed_ref,
            enc_scale_ref,
            enc_second_ref,
            enc_slope_ref,
            enc_gpre_ref,
        )
        pooled = mm(enc_pool_ref[grid_count:spots, :], enc_gpre_ref[...]).astype(BF16)
        slot_back = (slot_back + mm_t(pooled, enc_first_ref[low, :])).astype(BF16)
        send(out_refs, lambda j: slot_back[reverse[j] * width : (reverse[j] + 1) * width, :])

    results = call(
        backward,
        "edges_backward",
        [
            *returned,
            local_sums,
            slot_sums,
            grid_part,
            select_t,
            cot_rows,
            cot_turned,
            mesh_cot,
            mesh_cot_turned,
            enc_pick,
            enc_pool,
            dec_pick,
            dec_pool,
            grid_first,
            grid_wide,
            grid_back,
            mesh_back,
            mesh_in,
            enc_first,
            enc_second,
            dec_first,
            dec_second,
            enc_normed,
            enc_scale,
            enc_slope,
            dec_normed,
            dec_scale,
            dec_slope,
            mesh_normed,
            mesh_scale,
            mesh_slope,
            mesh_turned,
        ],
        sent_shapes(feat)
        + [
            ((spots, feat), F32),
            ((spots, feat), BF16),
            ((dec_count, feat), BF16),
            ((enc_count, feat), BF16),
            ((mesh_count, feat), F32),
            ((mesh_count, feat), BF16),
        ],
        scratch=[
            ((spots, feat), BF16),
            ((spots, feat), BF16),
            ((spots, feat), F32),
            ((total, feat), BF16),
        ],
        flops=2 * feat * feat * (4 * spots + 3 * dec_count + 2 * enc_count),
    )
    outgoing, results = results[:sent_count], results[sent_count:]
    grid_normed, grid_gpre, dec_gpre, enc_gpre, mesh_gin, mesh_gpre = results
    final = exchange(outgoing, steady)

    def tail(
        nodes_ref,
        grid_normed_ref,
        cot_ref,
        grid_gpre_ref,
        enc_pool_ref,
        enc_gpre_ref,
        dec_pool_ref,
        dec_gpre_ref,
        mesh_gin_ref,
        mesh_gpre_ref,
        grid_wn_ref,
        enc_wg_ref,
        dec_wg_ref,
        mesh_wn_ref,
        enc_wm_ref,
        base_ref,
        grad_mesh_ref,
        grid_out_ref,
    ):
        grid_out_ref[...] = (
            nodes_ref[...].astype(F32) + grid_normed_ref[:grid_count, :]
        ).astype(BF16)
        enc_sums = mm(enc_pool_ref[:grid_count, :], enc_gpre_ref[...]).astype(BF16)
        mesh_sums = mm(enc_pool_ref[mesh_rows, :], enc_gpre_ref[...]).astype(BF16)
        dec_sums = mm(dec_pool_ref[:grid_count, :], dec_gpre_ref[...]).astype(BF16)
        base_ref[...] = (
            cot_ref[...].astype(F32)
            + mm_t(grid_gpre_ref[:grid_count, :], grid_wn_ref[low, :])
            + mm_t(enc_sums, enc_wg_ref[low, :])
            + mm_t(dec_sums, dec_wg_ref[low, :])
        )
        grad_mesh_ref[...] = (
            mesh_gin_ref[...]
            + mm_t(mesh_gpre_ref[...], mesh_wn_ref[low, :])
            + mm_t(mesh_sums, enc_wm_ref[high, :])
        )

    base, grad_mesh, grid_out = call(
        tail,
        "local_gradients",
        [
            grid_nodes,
            grid_normed,
            grid_cot,
            grid_gpre,
            enc_pool,
            enc_gpre,
            dec_pool,
            dec_gpre,
            mesh_gin,
            mesh_gpre,
            grid_first,
            enc_first,
            dec_first,
            mesh_first,
            enc_first,
        ],
        [((grid_count, feat), F32), ((mesh_count, feat), F32), ((grid_count, feat), BF16)],
        flops=2 * feat * feat * 3 * grid_count,
    )

    pieces = row_chunks(grid_count, 64)

    def finish(*refs):
        back_refs = refs[:arrived_count]
        base_ref, select_t_ref, out_ref, piece_ref, semaphores = refs[arrived_count:]
        back = by_row(back_refs)
        copies = []
        for place, rows in enumerate(pieces):
            piece_ref[rows, :] = base_ref[rows, :] + mm(select_t_ref[rows, :slots], back)
            copies.append(
                pltpu.make_async_copy(
                    piece_ref.at[rows, :], out_ref.at[rows, :], semaphores.at[place]
                )
            )
            copies[-1].start()
        for copy in copies:
            copy.wait()

    grad_grid = pl.pallas_call(
        finish,
        name="add_returned",
        in_specs=[pl.BlockSpec(memory_space=pltpu.VMEM)] * (arrived_count + 2),
        out_specs=pl.BlockSpec(memory_space=pltpu.HBM),
        out_shape=jax.ShapeDtypeStruct((grid_count, feat), F32),
        scratch_shapes=[
            pltpu.VMEM((grid_count, feat), F32),
            pltpu.SemaphoreType.DMA((len(pieces),)),
        ],
        compiler_params=pltpu.CompilerParams(vmem_limit_bytes=VMEM_LIMIT),
    )(*final, base, select_t)
    return (grid_out, mesh_out, grad_grid, grad_mesh)


def solution(mesh):
    rows = P(("groups", "tile"), None)
    flat = P(("groups", "tile"))
    in_specs = (rows,) * 6 + (P(),) * 8 + (rows,) + (flat,) * 5
    return jax.shard_map(
        per_device, mesh=mesh, in_specs=in_specs, out_specs=(rows,) * 4, check_vma=False
    )
```

```python
import jax
import jax.numpy as jnp
from jax import lax
from jax.experimental import pallas as pl
from jax.experimental.pallas import tpu as pltpu
from jax.sharding import PartitionSpec as P

TW = 4
CHUNK = 32
ROUND_FLOPS = 2 * 10**10
F32 = jnp.float32
BF16 = jnp.bfloat16
VMEM_LIMIT = 30 * 1024 * 1024


def mm(left, right):
    return jnp.dot(left, right, preferred_element_type=F32)


def mm_t(left, right):
    return lax.dot_general(left, right, (((1,), (1,)), ((), ())), preferred_element_type=F32)


def centred(values, axis):
    values = values.astype(F32)
    return values - jnp.mean(values, axis=axis, keepdims=True)


def silu_and_slope(pre):
    half = 0.5 * pre
    lifted = 1.0 + jnp.tanh(half)
    return half * lifted, lifted * (0.5 + 0.5 * half * (2.0 - lifted))


def silu(pre):
    half = 0.5 * pre
    return half * (1.0 + jnp.tanh(half))


def scale_rows(raw):
    return lax.rsqrt(jnp.mean(raw * raw, axis=-1, keepdims=True) + 1e-05)


def row_chunks(rows, size=CHUNK):
    return [slice(start, min(start + size, rows)) for start in range(0, rows, size)]


def write_silu(pre, act_ref):
    for rows in row_chunks(pre.shape[0]):
        act_ref[rows, :] = silu(pre[rows, :]).astype(BF16)


def write_norm(raw, normed_ref, scale_ref):
    for rows in row_chunks(raw.shape[0]):
        part = raw[rows, :]
        scale_inv = scale_rows(part)
        normed_ref[rows, :] = (part * scale_inv).astype(normed_ref.dtype)
        scale_ref[rows, :] = scale_inv


def write_slope(pre_ref, slope_ref):
    for rows in row_chunks(pre_ref.shape[0]):
        slope_ref[rows, :] = silu_and_slope(pre_ref[rows, :])[1].astype(BF16)


def edge_back(upstream, normed_ref, scale_ref, second_ref, slope_ref, out_ref):
    for rows in row_chunks(upstream.shape[0]):
        part, normed = upstream[rows, :], normed_ref[rows, :]
        mean = jnp.mean(part * normed.astype(F32), axis=-1, keepdims=True)
        out_ref[rows, :] = scale_ref[rows, :].astype(BF16) * (
            part.astype(BF16) - normed * mean.astype(BF16)
        )
    raw = mm_t(out_ref[...], second_ref[...])
    for rows in row_chunks(upstream.shape[0]):
        out_ref[rows, :] = raw[rows, :].astype(BF16) * slope_ref[rows, :]


def neighbour_offsets(peer_count):
    forward_half = [1, TW, TW + 1, TW - 1]
    return forward_half + [-offset for offset in forward_half] + [peer_count // 2]


def onehot_pair(spot_ref, mesh_ref, spots, mesh_count, by_edge_ref, by_spot_ref):
    edges, total = by_edge_ref.shape
    spot_row = spot_ref[...].reshape(1, -1)
    mesh_row = mesh_ref[...].reshape(1, -1) + spots
    one, zero = jnp.ones((), BF16), jnp.zeros((), BF16)

    def ones(ids, index):
        shape = jnp.broadcast_shapes(ids.shape, index.shape)
        hit = jnp.broadcast_to(ids, shape) == jnp.broadcast_to(index, shape)
        return jnp.where(hit, jnp.broadcast_to(one, shape), jnp.broadcast_to(zero, shape))

    for row, first, count in ((spot_row, 0, spots), (mesh_row, spots, mesh_count)):
        ids = lax.broadcasted_iota(jnp.int32, (16, edges), 0).astype(jnp.int16)
        wide = jnp.broadcast_to(row, (16, edges)).astype(jnp.int16)
        for rows in row_chunks(count, 16):
            rows = slice(rows.start + first, rows.stop + first)
            by_spot_ref[rows, :] = ones(ids, wide - jnp.int16(rows.start))
    by_spot_ref[spots + mesh_count :, :] = jnp.zeros((total - spots - mesh_count, edges), BF16)
    lane = lax.broadcasted_iota(jnp.int32, (16, 128), 1).astype(jnp.int16)
    for rows in row_chunks(edges, 128):
        spot_col = jnp.broadcast_to(spot_row[:, rows], (128, 128)).T.astype(jnp.int16)
        mesh_col = jnp.broadcast_to(mesh_row[:, rows], (128, 128)).T.astype(jnp.int16)
        for columns in row_chunks(total, 128):
            for part in row_chunks(128, 16):
                place = slice(rows.start + part.start, rows.start + part.stop)
                ids = lane + jnp.int16(columns.start)
                hits = []
                if columns.start < spots:
                    hits.append(ones(ids, spot_col[part, :]))
                if columns.stop > spots:
                    hits.append(ones(ids, mesh_col[part, :]))
                by_edge_ref[place, columns] = sum(hits[1:], hits[0])


class Fetched:
    def __init__(self, source, target, semaphore):
        self.copy = pltpu.make_async_copy(source, target, semaphore)
        self.target = target
        self.landed = False
        self.copy.start()

    def land(self):
        if not self.landed:
            self.copy.wait()
            self.landed = True

    def __getitem__(self, key):
        self.land()
        return self.target[key]


def call(body, name, inputs, outputs, scratch=(), flops=0):
    arrays, specs, moved, fetches = [], [], 0, []
    for place, entry in enumerate(inputs):
        if isinstance(entry, tuple):
            array, first, rows = entry
            array = pltpu.with_memory_space_constraint(array, pltpu.HBM)
            specs.append(pl.BlockSpec(memory_space=pltpu.HBM))
            shape = (rows,) + array.shape[1:]
            fetches.append((place, first, rows, shape, array.dtype))
            moved += rows * (array.size // array.shape[0]) * array.dtype.itemsize
        else:
            array = entry
            specs.append(pl.BlockSpec(memory_space=pltpu.VMEM))
            moved += array.size * array.dtype.itemsize
        arrays.append(array)
    shapes = [jax.ShapeDtypeStruct(shape, dtype) for shape, dtype in outputs]
    for shape in shapes:
        moved += shape.size * shape.dtype.itemsize
    buffers = [pltpu.VMEM(shape, dtype) for _, _, _, shape, dtype in fetches]
    if fetches:
        buffers.append(pltpu.SemaphoreType.DMA((len(fetches),)))

    def kernel(*refs):
        refs = list(refs)
        waiting = []
        if fetches:
            targets, semaphores = refs[-len(buffers) : -1], refs[-1]
            refs = refs[: -len(buffers)]
        for slot, (place, first, rows, shape, _) in enumerate(fetches):
            source = refs[place]
            if source.shape != shape:
                source = source.at[pl.ds(first, rows)]
            refs[place] = Fetched(source, targets[slot], semaphores.at[slot])
            waiting.append(refs[place])
        body(*refs)
        for fetched in waiting:
            fetched.land()

    return pl.pallas_call(
        kernel,
        name=name,
        in_specs=specs,
        out_specs=[pl.BlockSpec(memory_space=pltpu.VMEM) for _ in shapes],
        out_shape=shapes,
        scratch_shapes=[pltpu.VMEM(shape, dtype) for shape, dtype in scratch]
        + buffers,
        compiler_params=pltpu.CompilerParams(vmem_limit_bytes=VMEM_LIMIT),
        cost_estimate=pl.CostEstimate(flops=flops, bytes_accessed=moved, transcendentals=0),
    )(*arrays)


def per_device(
    grid_nodes,
    mesh_nodes,
    enc_edges,
    dec_edges,
    grid_cot,
    mesh_cot,
    enc_first,
    enc_second,
    mesh_first,
    mesh_second,
    dec_first,
    dec_second,
    grid_first,
    grid_second,
    send_index,
    send_count,
    enc_grid,
    enc_mesh,
    dec_grid,
    dec_mesh,
):
    grid_count, feat = grid_nodes.shape
    mesh_count = mesh_nodes.shape[0]
    enc_count = enc_edges.shape[0]
    dec_count = dec_edges.shape[0]
    links, width = send_index.shape
    slots = links * width
    slots_pad = -(-slots // 128) * 128
    spots = grid_count + slots
    total = -(-(spots + mesh_count) // 128) * 128
    peer_count = lax.axis_size("tile")
    offsets = neighbour_offsets(peer_count)
    half = (links - 1) // 2
    reverse = [(j + half) % (links - 1) for j in range(links - 1)] + [links - 1]
    low, high = slice(0, feat), slice(feat, 2 * feat)
    mesh_rows = slice(spots, spots + mesh_count)

    one, four, five, three = range(half)
    minus = [j + half for j in range(half)]
    across = links - 1
    peers = range(peer_count)

    def permute(part, steps, odd_row_steps=None):
        rows = (steps, odd_row_steps or steps)
        pairs = [(s, (s + rows[s // TW % 2][s % 2]) % peer_count) for s in peers]
        return lax.ppermute(part, "tile", pairs)

    steady = ("late", "early", "opposite", "ahead", "five", "behind", "own")
    closing = ("late", "early", "behind", "ahead", "five", "opposite", "own")
    staggered = ("early", "late", "ahead", "five", "behind", "opposite", "own")
    arrived_count = 7

    def exchange(parts, order):
        moves = {
            "late": ((-4, -4), (4, 4)),
            "early": ((4, 4), (-4, -4)),
            "behind": ((-1, 1),),
            "ahead": ((3, -3),),
            "five": ((-5, 5),),
            "opposite": ((peer_count // 2, peer_count // 2),),
        }
        parts = dict(zip(order, parts))
        own_chip = parts.pop("own")
        got = {name: permute(part, *moves[name]) for name, part in parts.items()}

        def lay_together(own_ref, late_ref, early_ref, passed_ref):
            passed_ref[:width, :] = own_ref[...]
            passed_ref[width : 2 * width, :] = late_ref[width:, :]
            passed_ref[2 * width :, :] = early_ref[width:, :]

        (passed,) = call(
            lay_together,
            "lay_together",
            [own_chip, got["late"], got["early"]],
            [((3 * width, own_chip.shape[1]), BF16)],
        )
        return [got[name] for name in order if name in got] + [permute(passed, (1, -1))]

    def sent_shapes(columns, order=steady):
        double = ("late", "early")
        return [((width * (1 + (name in double)), columns), BF16) for name in order]

    sent_count = len(steady)

    def place_bits():
        own = lax.axis_index("tile")
        return lax.rem(own, 2) == 1, lax.rem(lax.div(own, TW), 2) == 1

    def send(refs, message, columns=slice(None), order=steady):
        odd, odd_row = place_bits()
        refs = dict(zip(order, refs))

        def by_parity(even, odd_one):
            return jnp.where(odd, message(odd_one), message(even))

        late_pair, early_pair, opposite, ahead_three, five_off, behind_one, own_chip = [
            refs[name] for name in steady
        ]
        first, second = slice(0, width), slice(width, 2 * width)
        ahead = message(four), by_parity(five, three)
        behind = message(minus[four]), by_parity(minus[three], minus[five])
        for rows, go_ahead, go_behind in zip((first, second), ahead, behind):
            late_pair[rows, columns] = jnp.where(odd_row, go_ahead, go_behind)
            early_pair[rows, columns] = jnp.where(odd_row, go_behind, go_ahead)
        behind_one[:, columns] = by_parity(minus[one], one)
        ahead_three[:, columns] = by_parity(three, minus[three])
        five_off[:, columns] = by_parity(minus[five], five)
        opposite[:, columns] = message(across)
        own_chip[:, columns] = by_parity(one, minus[one])

    def receive(refs, columns=slice(None), order=steady):
        odd, odd_row = place_bits()
        passed = refs[-1]
        refs = dict(zip([name for name in order if name != "own"], refs))
        late_pair, early_pair, opposite, ahead_three, five_off, behind_one = [
            refs[name] for name in steady if name != "own"
        ]
        first, second = slice(0, width), slice(width, 2 * width)
        near, near_three = behind_one[:, columns], ahead_three[:, columns]
        far, own = five_off[:, columns], passed[first, columns]
        late_rows = passed[second, columns]
        early_rows = passed[2 * width :, columns]
        from_behind = jnp.where(odd_row, early_rows, late_rows)
        from_ahead = jnp.where(odd_row, late_rows, early_rows)
        late_rows, early_rows = late_pair[first, columns], early_pair[first, columns]
        slot_rows = [None] * links
        slot_rows[one] = jnp.where(odd, own, near)
        slot_rows[minus[one]] = jnp.where(odd, near, own)
        slot_rows[three] = jnp.where(odd, near_three, from_behind)
        slot_rows[minus[three]] = jnp.where(odd, from_ahead, near_three)
        slot_rows[five] = jnp.where(odd, from_behind, far)
        slot_rows[minus[five]] = jnp.where(odd, far, from_ahead)
        slot_rows[four] = jnp.where(odd_row, early_rows, late_rows)
        slot_rows[minus[four]] = jnp.where(odd_row, late_rows, early_rows)
        slot_rows[across] = opposite[:, columns]
        return slot_rows

    def by_slot(refs, columns=slice(None), order=steady):
        return jnp.concatenate(receive(refs, columns, order), axis=0)

    def by_row(refs, columns=slice(None), order=steady):
        slot_rows = receive(refs, columns, order)
        return jnp.concatenate([slot_rows[reverse[j]] for j in range(links)], axis=0)

    def pack(index_ref, count_ref, nodes_ref, cot_ref, select_ref, *out_refs):
        def column(row):
            count = row.shape[1]
            eye = lax.broadcasted_iota(jnp.int32, (count, count), 0) == lax.broadcasted_iota(
                jnp.int32, (count, count), 1
            )
            return jnp.sum(
                jnp.where(eye, jnp.broadcast_to(row, (count, count)), 0.0), axis=1, keepdims=True
            )

        counts = column(count_ref[...].reshape(1, -1).astype(F32))
        place = lax.broadcasted_iota(jnp.int32, (links, width), 1).astype(F32)
        index = jnp.where(place < counts, index_ref[...].astype(F32), -1.0)
        lane = lax.broadcasted_iota(jnp.int32, (width, grid_count), 1).astype(F32)
        picks = [
            jnp.where(lane == column(index[j : j + 1, :]), 1.0, 0.0).astype(BF16)
            for j in range(links)
        ]
        select = jnp.concatenate(picks, axis=0)
        select_ref[:slots, :] = select
        select_ref[slots:, :] = jnp.zeros((slots_pad - slots, grid_count), BF16)
        sent_nodes = mm(select, nodes_ref[...]).astype(BF16)
        sent_cot = mm(select, cot_ref[...]).astype(BF16)
        send(
            out_refs, lambda j: sent_nodes[j * width : (j + 1) * width, :], low, staggered
        )
        send(out_refs, lambda j: sent_cot[j * width : (j + 1) * width, :], high, staggered)

    select, *outgoing = call(
        pack,
        "pack_rows",
        [
            (send_index, 0, links),
            (send_count, 0, links),
            (grid_nodes, 0, grid_count),
            (grid_cot, 0, grid_count),
        ],
        [((slots_pad, grid_count), BF16)] + sent_shapes(2 * feat, staggered),
        flops=4 * slots * grid_count * feat,
    )
    def turn(select_ref, select_t_ref):
        select_t_ref[...] = select_ref[...].astype(F32).T.astype(BF16)

    (select_t,) = call(
        turn, "turn_select", [select], [((grid_count, slots_pad), BF16)], flops=ROUND_FLOPS
    )
    *outgoing, select_t = lax.optimization_barrier((*outgoing, select_t))
    arrived = exchange(outgoing, staggered)

    def local(
        select_ref,
        nodes_ref,
        mesh_ref,
        enc_edges_ref,
        dec_edges_ref,
        enc_first_ref,
        dec_first_ref,
        mesh_first_ref,
        enc_grid_ref,
        enc_mesh_ref,
        dec_grid_ref,
        dec_mesh_ref,
        enc_second_ref,
        mesh_second_ref,
        dec_second_ref,
        enc_part_ref,
        dec_part_ref,
        mesh_part_ref,
        enc_pick_ref,
        enc_pool_ref,
        dec_pick_ref,
        dec_pool_ref,
        enc_centred_ref,
        dec_centred_ref,
        mesh_centred_ref,
        sent_pool_ref,
        table_ref,
    ):
        onehot_pair(enc_grid_ref, enc_mesh_ref, spots, mesh_count, enc_pick_ref, enc_pool_ref)
        onehot_pair(dec_grid_ref, dec_mesh_ref, spots, mesh_count, dec_pick_ref, dec_pool_ref)
        enc_centred_ref[...] = centred(enc_second_ref[...], 1).astype(BF16)
        mesh_centred_ref[...] = centred(mesh_second_ref[...], 1).astype(BF16)
        sent_pool_ref[:slots, :] = dec_pool_ref[grid_count:spots, :]
        sent_pool_ref[slots:, :] = mm(
            select_ref[:slots, :], dec_pool_ref[:grid_count, :]
        ).astype(BF16)
        dec_centred_ref[...] = centred(dec_second_ref[...], 1).astype(BF16)
        nodes = nodes_ref[...]
        mesh_part_ref[...] = mm(mesh_ref[...], mesh_first_ref[low, :])
        table_ref[:grid_count, :] = mm(nodes, enc_first_ref[low, :]).astype(BF16)
        table_ref[grid_count:, :] = jnp.zeros((total - grid_count, feat), BF16)
        table_ref[mesh_rows, :] = mm(mesh_ref[...], enc_first_ref[high, :]).astype(BF16)
        enc_part_ref[...] = mm(enc_edges_ref[...], enc_first_ref[2 * feat :, :])
        enc_part_ref[...] += mm(enc_pick_ref[...], table_ref[...])
        pd = mm(nodes, dec_first_ref[low, :]).astype(BF16)
        dec_part_ref[...] = mm(dec_edges_ref[...], dec_first_ref[2 * feat :, :])
        dec_part_ref[...] += mm(dec_pick_ref[:, :grid_count], pd)

    (
        enc_part,
        dec_part,
        mesh_part,
        enc_pick,
        enc_pool,
        dec_pick,
        dec_pool,
        enc_centred,
        dec_centred,
        mesh_centred,
        sent_pool,
    ) = call(
        local,
        "local_products",
        [
            select,
            grid_nodes,
            mesh_nodes,
            enc_edges,
            dec_edges,
            enc_first,
            dec_first,
            mesh_first,
            enc_grid,
            enc_mesh,
            dec_grid,
            dec_mesh,
            enc_second,
            mesh_second,
            dec_second,
        ],
        [
            ((enc_count, feat), F32),
            ((dec_count, feat), F32),
            ((mesh_count, feat), F32),
            ((enc_count, total), BF16),
            ((total, enc_count), BF16),
            ((dec_count, total), BF16),
            ((total, dec_count), BF16),
        ]
        + [
            ((feat, feat), BF16),
            ((feat, feat), BF16),
            ((feat, feat), BF16),
            ((2 * slots, dec_count), BF16),
        ],
        scratch=[((total, feat), BF16)],
        flops=2 * feat * (feat * (2 * grid_count + enc_count + dec_count) + total * dec_count),
    )

    def forward(*refs):
        arrived_refs, refs = refs[:arrived_count], refs[arrived_count:]
        (
            sent_pool_ref,
            enc_part_ref,
            dec_part_ref,
            mesh_part_ref,
            enc_pick_ref,
            enc_pool_ref,
            dec_pick_ref,
            enc_wg_ref,
            dec_wg_ref,
            enc_w2_ref,
            mesh_wa_ref,
            mesh_w2_ref,
            mesh_ref,
            dec_wm_ref,
            dec_w2_ref,
        ) = refs[:15]
        refs = refs[15:]
        out_refs, refs = refs[:sent_count], refs[sent_count:]
        (
            slot_ref,
            enc_normed_ref,
            enc_scale_ref,
            enc_pre_ref,
            dec_normed_ref,
            dec_scale_ref,
            dec_pre_ref,
            mesh_normed_ref,
            mesh_scale_ref,
            mesh_pre_ref,
            enc_act_ref,
            dec_act_ref,
            mesh_act_ref,
            table_ref,
        ) = refs
        rows = by_slot(arrived_refs, low, staggered)
        pe = mm(rows, enc_wg_ref[low, :]).astype(BF16)
        enc_pre_ref[...] = enc_part_ref[...] + mm(enc_pick_ref[:, grid_count:spots], pe)
        write_silu(enc_pre_ref, enc_act_ref)
        write_norm(mm(enc_act_ref[...], enc_w2_ref[...]), enc_normed_ref, enc_scale_ref)
        agg = mm(enc_pool_ref[mesh_rows, :], enc_normed_ref[...]).astype(BF16)
        mesh_pre_ref[...] = mesh_part_ref[...] + mm(agg, mesh_wa_ref[high, :])
        write_silu(mesh_pre_ref, mesh_act_ref)
        write_norm(mm(mesh_act_ref[...], mesh_w2_ref[...]), mesh_normed_ref, mesh_scale_ref)
        mesh_out = (mesh_ref[...].astype(F32) + mesh_normed_ref[...]).astype(BF16)
        table_ref[:slots, :] = mm(rows, dec_wg_ref[low, :]).astype(BF16)
        table_ref[slots : slots + mesh_count, :] = mm(mesh_out, dec_wm_ref[high, :]).astype(BF16)
        table_ref[slots + mesh_count :, :] = jnp.zeros(
            (total - spots - mesh_count, feat), BF16
        )
        dec_pre_ref[...] = dec_part_ref[...] + mm(dec_pick_ref[:, grid_count:], table_ref[...])
        write_silu(dec_pre_ref, dec_act_ref)
        write_norm(mm(dec_act_ref[...], dec_w2_ref[...]), dec_normed_ref, dec_scale_ref)
        sums = mm(sent_pool_ref[...], dec_normed_ref[...])
        slot_ref[...] = sums[:slots, :]
        shared = sums[slots:, :].astype(BF16)
        slot_msg = sums[:slots, :].astype(BF16)
        send(
            out_refs, lambda j: slot_msg[reverse[j] * width : (reverse[j] + 1) * width, :], low
        )
        send(out_refs, lambda j: shared[j * width : (j + 1) * width, :], high)

    saved_shapes = [
        ((enc_count, feat), BF16),
        ((enc_count, 1), F32),
        ((enc_count, feat), F32),
        ((dec_count, feat), BF16),
        ((dec_count, 1), F32),
        ((dec_count, feat), F32),
        ((mesh_count, feat), F32),
        ((mesh_count, 1), F32),
        ((mesh_count, feat), F32),
    ]
    results = call(
        forward,
        "edges_forward",
        [
            *arrived,
            sent_pool,
            enc_part,
            dec_part,
            mesh_part,
            enc_pick,
            enc_pool,
            dec_pick,
            enc_first,
            dec_first,
            enc_centred,
            mesh_first,
            mesh_centred,
            mesh_nodes,
            dec_first,
            dec_centred,
        ],
        sent_shapes(2 * feat)
        + [((slots, feat), F32)]
        + saved_shapes,
        scratch=[
            ((enc_count, feat), BF16),
            ((dec_count, feat), BF16),
            ((mesh_count, feat), BF16),
            ((total - grid_count, feat), BF16),
        ],
        flops=2 * feat * feat * 2 * (enc_count + dec_count),
    )
    outgoing, results = results[:sent_count], results[sent_count:]
    slot_sums, *saved = results
    enc_normed, enc_scale, enc_pre, dec_normed, dec_scale, dec_pre = saved[:6]
    mesh_normed, mesh_scale, mesh_pre = saved[6:]
    returned = exchange(outgoing, steady)

    def between(*refs):
        arrived_refs, refs = refs[:arrived_count], refs[arrived_count:]
        (
            nodes_ref,
            grid_first_ref,
            grid_second_ref,
            cot_ref,
            mesh_first_ref,
            dec_pool_ref,
            dec_normed_ref,
            mesh_second_ref,
            mesh_centred_ref,
            dec_first_ref,
            mesh_cot_ref,
            mesh_ref,
            enc_pre_ref,
            dec_pre_ref,
            mesh_normed_ref,
            mesh_pre_ref,
            local_sums_ref,
            part_ref,
            cot_rows_ref,
            cot_turned_ref,
            grid_wide_ref,
            grid_back_ref,
            mesh_back_ref,
            mesh_in_ref,
            mesh_cot_turned_ref,
            mesh_turned_ref,
            mesh_out_ref,
            mesh_slope_ref,
            enc_slope_ref,
            dec_slope_ref,
        ) = refs
        part_ref[:grid_count, :] = mm(nodes_ref[...], grid_first_ref[low, :])
        part_ref[grid_count:, :] = mm(by_slot(arrived_refs, low, staggered), grid_first_ref[low, :])
        mesh_out_ref[...] = (mesh_ref[...].astype(F32) + mesh_normed_ref[...]).astype(BF16)
        cot_rows_ref[:grid_count, :] = cot_ref[...]
        cot_rows_ref[grid_count:, :] = by_slot(arrived_refs, high, staggered)
        second = centred(grid_second_ref[...], 1).astype(BF16)
        grid_wide_ref[:, low] = second
        grid_wide_ref[:, high] = mm_t(second, grid_second_ref[...]).astype(BF16)
        cot_turned_ref[...] = mm_t(cot_rows_ref[...], second)
        grid_back_ref[...] = centred(grid_first_ref[high, :], 0).astype(BF16)
        mesh_back_ref[...] = centred(mesh_first_ref[high, :], 0).astype(BF16)
        mesh_in_ref[low, :] = dec_first_ref[high, :]
        mesh_in_ref[high, :] = mm(mesh_centred_ref[...], dec_first_ref[high, :]).astype(BF16)
        mesh_cot_turned_ref[...] = mm_t(mesh_cot_ref[...], mesh_centred_ref[...])
        mesh_turned_ref[...] = mm_t(mesh_normed_ref[...].astype(BF16), mesh_second_ref[...])
        local_sums_ref[...] = mm(dec_pool_ref[:grid_count, :], dec_normed_ref[...])
        mesh_slope_ref[...] = silu_and_slope(mesh_pre_ref[...])[1]
        write_slope(enc_pre_ref, enc_slope_ref)
        write_slope(dec_pre_ref, dec_slope_ref)

    (
        local_sums,
        grid_part,
        cot_rows,
        cot_turned,
        grid_wide,
        grid_back,
        mesh_back,
        mesh_in,
        mesh_cot_turned,
        mesh_turned,
        mesh_out,
        mesh_slope,
        enc_slope,
        dec_slope,
    ) = call(
        between,
        "slopes_and_nodes",
        [
            *arrived,
            grid_nodes,
            grid_first,
            grid_second,
            grid_cot,
            mesh_first,
            dec_pool,
            dec_normed,
            mesh_second,
            mesh_centred,
            dec_first,
            mesh_cot,
            mesh_nodes,
            enc_pre,
            dec_pre,
            mesh_normed,
            mesh_pre,
        ],
        [
            ((grid_count, feat), F32),
            ((spots, feat), F32),
            ((spots, feat), BF16),
            ((spots, feat), F32),
            ((feat, 2 * feat), BF16),
            ((feat, feat), BF16),
            ((feat, feat), BF16),
            ((2 * feat, feat), BF16),
            ((mesh_count, feat), F32),
            ((mesh_count, feat), F32),
            ((mesh_count, feat), BF16),
            ((mesh_count, feat), F32),
            ((enc_count, feat), BF16),
            ((dec_count, feat), BF16),
        ],
        flops=16 * spots * feat * feat,
    )

    def backward(*refs):
        returned_refs, refs = refs[:arrived_count], refs[arrived_count:]
        (
            local_sums_ref,
            slot_sums_ref,
            grid_part_ref,
            select_t_ref,
            cot_rows_ref,
            cot_turned_ref,
            mesh_cot_ref,
            mesh_cot_turned_ref,
            enc_pick_ref,
            enc_pool_ref,
            dec_pick_ref,
            dec_pool_ref,
            grid_first_ref,
            grid_wide_ref,
            grid_back_ref,
            mesh_back_ref,
            mesh_in_ref,
            enc_first_ref,
            enc_second_ref,
            dec_first_ref,
            dec_second_ref,
            enc_normed_ref,
            enc_scale_ref,
            enc_slope_ref,
            dec_normed_ref,
            dec_scale_ref,
            dec_slope_ref,
            mesh_normed_ref,
            mesh_scale_ref,
            mesh_slope_ref,
            mesh_turned_ref,
        ) = refs[:31]
        refs = refs[31:]
        out_refs, refs = refs[:sent_count], refs[sent_count:]
        (
            grid_normed_ref,
            grid_gpre_ref,
            dec_gpre_ref,
            enc_gpre_ref,
            mesh_gin_ref,
            mesh_gpre_ref,
            agg_ref,
            grid_act_ref,
            grid_slope_ref,
            spot_grad_ref,
        ) = refs
        agg_ref[:grid_count, :] = (
            local_sums_ref[...] + mm(select_t_ref[:, :slots], by_row(returned_refs, low))
        ).astype(BF16)
        agg_ref[grid_count:, :] = (
            slot_sums_ref[...] + by_slot(returned_refs, high).astype(F32)
        ).astype(BF16)
        pre = grid_part_ref[...] + mm(agg_ref[...], grid_first_ref[high, :])
        for rows in row_chunks(spots):
            act, slope = silu_and_slope(pre[rows, :])
            grid_act_ref[rows, :] = act.astype(BF16)
            grid_slope_ref[rows, :] = slope
        both = mm(grid_act_ref[...], grid_wide_ref[...])
        for rows in row_chunks(spots):
            part = both[rows, low]
            scale_inv = scale_rows(part)
            normed = part * scale_inv
            grid_normed_ref[rows, :] = normed
            mean = jnp.mean(cot_rows_ref[rows, :].astype(F32) * normed, axis=-1, keepdims=True)
            raw = scale_inv * (cot_turned_ref[rows, :] - (mean * scale_inv) * both[rows, high])
            grid_gpre_ref[rows, :] = (raw * grid_slope_ref[rows, :]).astype(BF16)
        spot_grad_ref[:spots, :] = mm_t(grid_gpre_ref[...], grid_back_ref[...]).astype(BF16)
        spot_grad_ref[spots:, :] = jnp.zeros((total - spots, feat), BF16)
        edge_back(
            mm(dec_pick_ref[...], spot_grad_ref[...]),
            dec_normed_ref,
            dec_scale_ref,
            dec_second_ref,
            dec_slope_ref,
            dec_gpre_ref,
        )
        sums = mm(
            dec_pool_ref[grid_count : spots + mesh_count, :], dec_gpre_ref[...]
        ).astype(BF16)
        both = mm_t(sums[slots:, :], mesh_in_ref[...])
        mesh_gin = mesh_cot_ref[...].astype(F32) + both[:, low]
        mesh_gin_ref[...] = mesh_gin
        mean = jnp.mean(mesh_gin * mesh_normed_ref[...], axis=-1, keepdims=True)
        raw = mesh_cot_turned_ref[...] + both[:, high] - mean * mesh_turned_ref[...]
        mesh_gpre_ref[...] = (mesh_scale_ref[...] * raw * mesh_slope_ref[...]).astype(BF16)
        mesh_gagg = mm_t(mesh_gpre_ref[...], mesh_back_ref[...]).astype(BF16)
        slot_back = mm_t(sums[:slots, :], dec_first_ref[low, :])
        edge_back(
            mm(enc_pick_ref[:, mesh_rows], mesh_gagg),
            enc_normed_ref,
            enc_scale_ref,
            enc_second_ref,
            enc_slope_ref,
            enc_gpre_ref,
        )
        pooled = mm(enc_pool_ref[grid_count:spots, :], enc_gpre_ref[...]).astype(BF16)
        slot_back = (slot_back + mm_t(pooled, enc_first_ref[low, :])).astype(BF16)
        send(
            out_refs,
            lambda j: slot_back[reverse[j] * width : (reverse[j] + 1) * width, :],
            order=closing,
        )

    results = call(
        backward,
        "edges_backward",
        [
            *returned,
            local_sums,
            slot_sums,
            grid_part,
            select_t,
            cot_rows,
            cot_turned,
            mesh_cot,
            mesh_cot_turned,
            enc_pick,
            enc_pool,
            dec_pick,
            dec_pool,
            grid_first,
            grid_wide,
            grid_back,
            mesh_back,
            mesh_in,
            enc_first,
            enc_second,
            dec_first,
            dec_second,
            enc_normed,
            enc_scale,
            enc_slope,
            dec_normed,
            dec_scale,
            dec_slope,
            mesh_normed,
            mesh_scale,
            mesh_slope,
            mesh_turned,
        ],
        sent_shapes(feat, closing)
        + [
            ((spots, feat), F32),
            ((spots, feat), BF16),
            ((dec_count, feat), BF16),
            ((enc_count, feat), BF16),
            ((mesh_count, feat), F32),
            ((mesh_count, feat), BF16),
        ],
        scratch=[
            ((spots, feat), BF16),
            ((spots, feat), BF16),
            ((spots, feat), F32),
            ((total, feat), BF16),
        ],
        flops=2 * feat * feat * (4 * spots + 3 * dec_count + 2 * enc_count),
    )
    outgoing, results = results[:sent_count], results[sent_count:]
    grid_normed, grid_gpre, dec_gpre, enc_gpre, mesh_gin, mesh_gpre = results
    final = exchange(outgoing, closing)

    def tail(
        nodes_ref,
        grid_normed_ref,
        cot_ref,
        grid_gpre_ref,
        enc_pool_ref,
        enc_gpre_ref,
        dec_pool_ref,
        dec_gpre_ref,
        mesh_gin_ref,
        mesh_gpre_ref,
        grid_wn_ref,
        enc_wg_ref,
        dec_wg_ref,
        mesh_wn_ref,
        enc_wm_ref,
        base_ref,
        grad_mesh_ref,
        grid_out_ref,
    ):
        grid_out_ref[...] = (
            nodes_ref[...].astype(F32) + grid_normed_ref[:grid_count, :]
        ).astype(BF16)
        enc_sums = mm(enc_pool_ref[:grid_count, :], enc_gpre_ref[...]).astype(BF16)
        mesh_sums = mm(enc_pool_ref[mesh_rows, :], enc_gpre_ref[...]).astype(BF16)
        dec_sums = mm(dec_pool_ref[:grid_count, :], dec_gpre_ref[...]).astype(BF16)
        base_ref[...] = (
            cot_ref[...].astype(F32)
            + mm_t(grid_gpre_ref[:grid_count, :], grid_wn_ref[low, :])
            + mm_t(enc_sums, enc_wg_ref[low, :])
            + mm_t(dec_sums, dec_wg_ref[low, :])
        )
        grad_mesh_ref[...] = (
            mesh_gin_ref[...]
            + mm_t(mesh_gpre_ref[...], mesh_wn_ref[low, :])
            + mm_t(mesh_sums, enc_wm_ref[high, :])
        )

    base, grad_mesh, grid_out = call(
        tail,
        "local_gradients",
        [
            grid_nodes,
            grid_normed,
            grid_cot,
            grid_gpre,
            enc_pool,
            enc_gpre,
            dec_pool,
            dec_gpre,
            mesh_gin,
            mesh_gpre,
            grid_first,
            enc_first,
            dec_first,
            mesh_first,
            enc_first,
        ],
        [((grid_count, feat), F32), ((mesh_count, feat), F32), ((grid_count, feat), BF16)],
        flops=16 * spots * feat * feat,
    )

    pieces = row_chunks(grid_count, 64)

    def finish(*refs):
        back_refs = refs[:arrived_count]
        base_ref, select_t_ref, out_ref, piece_ref, semaphores = refs[arrived_count:]
        back = by_row(back_refs, order=closing)
        copies = []
        for place, rows in enumerate(pieces):
            piece_ref[rows, :] = base_ref[rows, :] + mm(select_t_ref[rows, :slots], back)
            copies.append(
                pltpu.make_async_copy(
                    piece_ref.at[rows, :], out_ref.at[rows, :], semaphores.at[place]
                )
            )
            copies[-1].start()
        for copy in copies:
            copy.wait()

    grad_grid = pl.pallas_call(
        finish,
        name="add_returned",
        in_specs=[pl.BlockSpec(memory_space=pltpu.VMEM)] * (arrived_count + 2),
        out_specs=pl.BlockSpec(memory_space=pltpu.HBM),
        out_shape=jax.ShapeDtypeStruct((grid_count, feat), F32),
        scratch_shapes=[
            pltpu.VMEM((grid_count, feat), F32),
            pltpu.SemaphoreType.DMA((len(pieces),)),
        ],
        compiler_params=pltpu.CompilerParams(vmem_limit_bytes=VMEM_LIMIT),
    )(*final, base, select_t)
    return (grid_out, mesh_out, grad_grid, grad_mesh)


def solution(mesh):
    rows = P(("groups", "tile"), None)
    flat = P(("groups", "tile"))
    in_specs = (rows,) * 6 + (P(),) * 8 + (rows,) + (flat,) * 5
    return jax.shard_map(
        per_device, mesh=mesh, in_specs=in_specs, out_specs=(rows,) * 4, check_vma=False
    )
```

```python
import jax
import jax.numpy as jnp
from jax import lax
from jax.experimental import pallas as pl
from jax.experimental.pallas import tpu as pltpu
from jax.sharding import PartitionSpec as P

TW = 4
CHUNK = 32
ROUND_FLOPS = 2 * 10**10
F32 = jnp.float32
BF16 = jnp.bfloat16
VMEM_LIMIT = 30 * 1024 * 1024


def mm(left, right):
    return jnp.dot(left, right, preferred_element_type=F32)


def mm_t(left, right):
    return lax.dot_general(left, right, (((1,), (1,)), ((), ())), preferred_element_type=F32)


def centred(values, axis):
    values = values.astype(F32)
    return values - jnp.mean(values, axis=axis, keepdims=True)


def silu_and_slope(pre):
    half = 0.5 * pre
    lifted = 1.0 + jnp.tanh(half)
    return half * lifted, lifted * (0.5 + 0.5 * half * (2.0 - lifted))


def silu(pre):
    half = 0.5 * pre
    return half * (1.0 + jnp.tanh(half))


def scale_rows(raw):
    return lax.rsqrt(jnp.mean(raw * raw, axis=-1, keepdims=True) + 1e-05)


def row_chunks(rows, size=CHUNK):
    return [slice(start, min(start + size, rows)) for start in range(0, rows, size)]


def write_silu(pre, act_ref):
    for rows in row_chunks(pre.shape[0]):
        act_ref[rows, :] = silu(pre[rows, :]).astype(BF16)


def write_norm(raw, normed_ref, scale_ref):
    for rows in row_chunks(raw.shape[0]):
        part = raw[rows, :]
        scale_inv = scale_rows(part)
        normed_ref[rows, :] = (part * scale_inv).astype(normed_ref.dtype)
        scale_ref[rows, :] = scale_inv


def write_slope(pre_ref, slope_ref):
    for rows in row_chunks(pre_ref.shape[0]):
        slope_ref[rows, :] = silu_and_slope(pre_ref[rows, :])[1].astype(BF16)


def edge_back(upstream, normed_ref, scale_ref, second_ref, slope_ref, out_ref):
    for rows in row_chunks(upstream.shape[0]):
        part, normed = upstream[rows, :], normed_ref[rows, :]
        mean = jnp.mean(part * normed.astype(F32), axis=-1, keepdims=True)
        out_ref[rows, :] = scale_ref[rows, :].astype(BF16) * (
            part.astype(BF16) - normed * mean.astype(BF16)
        )
    raw = mm_t(out_ref[...], second_ref[...])
    for rows in row_chunks(upstream.shape[0]):
        out_ref[rows, :] = raw[rows, :].astype(BF16) * slope_ref[rows, :]


def neighbour_offsets(peer_count):
    forward_half = [1, TW, TW + 1, TW - 1]
    return forward_half + [-offset for offset in forward_half] + [peer_count // 2]


def onehot_pair(spot_ref, mesh_ref, spots, mesh_count, by_edge_ref, by_spot_ref):
    edges, total = by_edge_ref.shape
    spot_row = spot_ref[...].reshape(1, -1)
    mesh_row = mesh_ref[...].reshape(1, -1) + spots
    one, zero = jnp.ones((), BF16), jnp.zeros((), BF16)

    def ones(ids, index):
        shape = jnp.broadcast_shapes(ids.shape, index.shape)
        hit = jnp.broadcast_to(ids, shape) == jnp.broadcast_to(index, shape)
        return jnp.where(hit, jnp.broadcast_to(one, shape), jnp.broadcast_to(zero, shape))

    for row, first, count in ((spot_row, 0, spots), (mesh_row, spots, mesh_count)):
        ids = lax.broadcasted_iota(jnp.int32, (16, edges), 0).astype(jnp.int16)
        wide = jnp.broadcast_to(row, (16, edges)).astype(jnp.int16)
        for rows in row_chunks(count, 16):
            rows = slice(rows.start + first, rows.stop + first)
            by_spot_ref[rows, :] = ones(ids, wide - jnp.int16(rows.start))
    by_spot_ref[spots + mesh_count :, :] = jnp.zeros((total - spots - mesh_count, edges), BF16)
    lane = lax.broadcasted_iota(jnp.int32, (16, 128), 1).astype(jnp.int16)
    for rows in row_chunks(edges, 128):
        spot_col = jnp.broadcast_to(spot_row[:, rows], (128, 128)).T.astype(jnp.int16)
        mesh_col = jnp.broadcast_to(mesh_row[:, rows], (128, 128)).T.astype(jnp.int16)
        for columns in row_chunks(total, 128):
            for part in row_chunks(128, 16):
                place = slice(rows.start + part.start, rows.start + part.stop)
                ids = lane + jnp.int16(columns.start)
                hits = []
                if columns.start < spots:
                    hits.append(ones(ids, spot_col[part, :]))
                if columns.stop > spots:
                    hits.append(ones(ids, mesh_col[part, :]))
                by_edge_ref[place, columns] = sum(hits[1:], hits[0])


class Fetched:
    def __init__(self, source, target, semaphore):
        self.copy = pltpu.make_async_copy(source, target, semaphore)
        self.target = target
        self.landed = False
        self.copy.start()

    def land(self):
        if not self.landed:
            self.copy.wait()
            self.landed = True

    def __getitem__(self, key):
        self.land()
        return self.target[key]


def call(body, name, inputs, outputs, scratch=(), flops=0):
    arrays, specs, moved, fetches = [], [], 0, []
    for place, entry in enumerate(inputs):
        if isinstance(entry, tuple):
            array, first, rows = entry
            array = pltpu.with_memory_space_constraint(array, pltpu.HBM)
            specs.append(pl.BlockSpec(memory_space=pltpu.HBM))
            shape = (rows,) + array.shape[1:]
            fetches.append((place, first, rows, shape, array.dtype))
            moved += rows * (array.size // array.shape[0]) * array.dtype.itemsize
        else:
            array = entry
            specs.append(pl.BlockSpec(memory_space=pltpu.VMEM))
            moved += array.size * array.dtype.itemsize
        arrays.append(array)
    shapes = [jax.ShapeDtypeStruct(shape, dtype) for shape, dtype in outputs]
    for shape in shapes:
        moved += shape.size * shape.dtype.itemsize
    buffers = [pltpu.VMEM(shape, dtype) for _, _, _, shape, dtype in fetches]
    if fetches:
        buffers.append(pltpu.SemaphoreType.DMA((len(fetches),)))

    def kernel(*refs):
        refs = list(refs)
        waiting = []
        if fetches:
            targets, semaphores = refs[-len(buffers) : -1], refs[-1]
            refs = refs[: -len(buffers)]
        for slot, (place, first, rows, shape, _) in enumerate(fetches):
            source = refs[place]
            if source.shape != shape:
                source = source.at[pl.ds(first, rows)]
            refs[place] = Fetched(source, targets[slot], semaphores.at[slot])
            waiting.append(refs[place])
        body(*refs)
        for fetched in waiting:
            fetched.land()

    return pl.pallas_call(
        kernel,
        name=name,
        in_specs=specs,
        out_specs=[pl.BlockSpec(memory_space=pltpu.VMEM) for _ in shapes],
        out_shape=shapes,
        scratch_shapes=[pltpu.VMEM(shape, dtype) for shape, dtype in scratch]
        + buffers,
        compiler_params=pltpu.CompilerParams(vmem_limit_bytes=VMEM_LIMIT),
        cost_estimate=pl.CostEstimate(flops=flops, bytes_accessed=moved, transcendentals=0),
    )(*arrays)


def per_device(
    grid_nodes,
    mesh_nodes,
    enc_edges,
    dec_edges,
    grid_cot,
    mesh_cot,
    enc_first,
    enc_second,
    mesh_first,
    mesh_second,
    dec_first,
    dec_second,
    grid_first,
    grid_second,
    send_index,
    send_count,
    enc_grid,
    enc_mesh,
    dec_grid,
    dec_mesh,
):
    grid_count, feat = grid_nodes.shape
    mesh_count = mesh_nodes.shape[0]
    enc_count = enc_edges.shape[0]
    dec_count = dec_edges.shape[0]
    links, width = send_index.shape
    slots = links * width
    slots_pad = -(-slots // 128) * 128
    spots = grid_count + slots
    total = -(-(spots + mesh_count) // 128) * 128
    peer_count = lax.axis_size("tile")
    offsets = neighbour_offsets(peer_count)
    half = (links - 1) // 2
    reverse = [(j + half) % (links - 1) for j in range(links - 1)] + [links - 1]
    low, high = slice(0, feat), slice(feat, 2 * feat)
    mesh_rows = slice(spots, spots + mesh_count)

    one, four, five, three = range(half)
    minus = [j + half for j in range(half)]
    across = links - 1
    peers = range(peer_count)

    def permute(part, steps, odd_row_steps=None):
        rows = (steps, odd_row_steps or steps)
        pairs = [(s, (s + rows[s // TW % 2][s % 2]) % peer_count) for s in peers]
        return lax.ppermute(part, "tile", pairs)

    steady = ("late", "early", "opposite", "behind", "ahead", "five", "own")
    closing = ("late", "early", "behind", "ahead", "five", "opposite", "own")
    staggered = ("early", "late", "ahead", "five", "behind", "opposite", "own")
    arrived_count = 7

    def exchange(parts, order):
        moves = {
            "late": ((-4, -4), (4, 4)),
            "early": ((4, 4), (-4, -4)),
            "behind": ((-1, 1),),
            "ahead": ((3, -3),),
            "five": ((-5, 5),),
            "opposite": ((peer_count // 2, peer_count // 2),),
        }
        parts = dict(zip(order, parts))
        own_chip = parts.pop("own")
        got = {name: permute(part, *moves[name]) for name, part in parts.items()}

        def lay_together(own_ref, late_ref, early_ref, passed_ref):
            passed_ref[:width, :] = own_ref[...]
            passed_ref[width : 2 * width, :] = late_ref[width:, :]
            passed_ref[2 * width :, :] = early_ref[width:, :]

        (passed,) = call(
            lay_together,
            "lay_together",
            [own_chip, got["late"], got["early"]],
            [((3 * width, own_chip.shape[1]), BF16)],
        )
        return [got[name] for name in order if name in got] + [permute(passed, (1, -1))]

    def sent_shapes(columns, order=steady):
        double = ("late", "early")
        return [((width * (1 + (name in double)), columns), BF16) for name in order]

    sent_count = len(steady)

    def place_bits():
        own = lax.axis_index("tile")
        return lax.rem(own, 2) == 1, lax.rem(lax.div(own, TW), 2) == 1

    def send(refs, message, columns=slice(None), order=steady):
        odd, odd_row = place_bits()
        refs = dict(zip(order, refs))

        def by_parity(even, odd_one):
            return jnp.where(odd, message(odd_one), message(even))

        late_pair, early_pair, opposite, behind_one, ahead_three, five_off, own_chip = [
            refs[name] for name in steady
        ]
        first, second = slice(0, width), slice(width, 2 * width)
        ahead = message(four), by_parity(five, three)
        behind = message(minus[four]), by_parity(minus[three], minus[five])
        for rows, go_ahead, go_behind in zip((first, second), ahead, behind):
            late_pair[rows, columns] = jnp.where(odd_row, go_ahead, go_behind)
            early_pair[rows, columns] = jnp.where(odd_row, go_behind, go_ahead)
        behind_one[:, columns] = by_parity(minus[one], one)
        ahead_three[:, columns] = by_parity(three, minus[three])
        five_off[:, columns] = by_parity(minus[five], five)
        opposite[:, columns] = message(across)
        own_chip[:, columns] = by_parity(one, minus[one])

    def receive(refs, columns=slice(None), order=steady):
        odd, odd_row = place_bits()
        passed = refs[-1]
        refs = dict(zip([name for name in order if name != "own"], refs))
        late_pair, early_pair, opposite, behind_one, ahead_three, five_off = [
            refs[name] for name in steady if name != "own"
        ]
        first, second = slice(0, width), slice(width, 2 * width)
        near, near_three = behind_one[:, columns], ahead_three[:, columns]
        far, own = five_off[:, columns], passed[first, columns]
        late_rows = passed[second, columns]
        early_rows = passed[2 * width :, columns]
        from_behind = jnp.where(odd_row, early_rows, late_rows)
        from_ahead = jnp.where(odd_row, late_rows, early_rows)
        late_rows, early_rows = late_pair[first, columns], early_pair[first, columns]
        slot_rows = [None] * links
        slot_rows[one] = jnp.where(odd, own, near)
        slot_rows[minus[one]] = jnp.where(odd, near, own)
        slot_rows[three] = jnp.where(odd, near_three, from_behind)
        slot_rows[minus[three]] = jnp.where(odd, from_ahead, near_three)
        slot_rows[five] = jnp.where(odd, from_behind, far)
        slot_rows[minus[five]] = jnp.where(odd, far, from_ahead)
        slot_rows[four] = jnp.where(odd_row, early_rows, late_rows)
        slot_rows[minus[four]] = jnp.where(odd_row, late_rows, early_rows)
        slot_rows[across] = opposite[:, columns]
        return slot_rows

    def by_slot(refs, columns=slice(None), order=steady):
        return jnp.concatenate(receive(refs, columns, order), axis=0)

    def by_row(refs, columns=slice(None), order=steady):
        slot_rows = receive(refs, columns, order)
        return jnp.concatenate([slot_rows[reverse[j]] for j in range(links)], axis=0)

    def pack(index_ref, count_ref, nodes_ref, cot_ref, select_ref, *out_refs):
        def column(row):
            count = row.shape[1]
            eye = lax.broadcasted_iota(jnp.int32, (count, count), 0) == lax.broadcasted_iota(
                jnp.int32, (count, count), 1
            )
            return jnp.sum(
                jnp.where(eye, jnp.broadcast_to(row, (count, count)), 0.0), axis=1, keepdims=True
            )

        counts = column(count_ref[...].reshape(1, -1).astype(F32))
        place = lax.broadcasted_iota(jnp.int32, (links, width), 1).astype(F32)
        index = jnp.where(place < counts, index_ref[...].astype(F32), -1.0)
        lane = lax.broadcasted_iota(jnp.int32, (width, grid_count), 1).astype(F32)
        picks = [
            jnp.where(lane == column(index[j : j + 1, :]), 1.0, 0.0).astype(BF16)
            for j in range(links)
        ]
        select = jnp.concatenate(picks, axis=0)
        select_ref[:slots, :] = select
        select_ref[slots:, :] = jnp.zeros((slots_pad - slots, grid_count), BF16)
        sent_nodes = mm(select, nodes_ref[...]).astype(BF16)
        sent_cot = mm(select, cot_ref[...]).astype(BF16)
        send(
            out_refs, lambda j: sent_nodes[j * width : (j + 1) * width, :], low, staggered
        )
        send(out_refs, lambda j: sent_cot[j * width : (j + 1) * width, :], high, staggered)

    select, *outgoing = call(
        pack,
        "pack_rows",
        [
            (send_index, 0, links),
            (send_count, 0, links),
            (grid_nodes, 0, grid_count),
            (grid_cot, 0, grid_count),
        ],
        [((slots_pad, grid_count), BF16)] + sent_shapes(2 * feat, staggered),
        flops=4 * slots * grid_count * feat,
    )
    def turn(select_ref, select_t_ref):
        select_t_ref[...] = select_ref[...].astype(F32).T.astype(BF16)

    (select_t,) = call(
        turn, "turn_select", [select], [((grid_count, slots_pad), BF16)], flops=ROUND_FLOPS
    )
    *outgoing, select_t = lax.optimization_barrier((*outgoing, select_t))
    arrived = exchange(outgoing, staggered)

    def local(
        select_ref,
        nodes_ref,
        mesh_ref,
        enc_edges_ref,
        dec_edges_ref,
        enc_first_ref,
        dec_first_ref,
        mesh_first_ref,
        enc_grid_ref,
        enc_mesh_ref,
        dec_grid_ref,
        dec_mesh_ref,
        enc_second_ref,
        mesh_second_ref,
        dec_second_ref,
        enc_part_ref,
        dec_part_ref,
        mesh_part_ref,
        enc_pick_ref,
        enc_pool_ref,
        dec_pick_ref,
        dec_pool_ref,
        enc_centred_ref,
        dec_centred_ref,
        mesh_centred_ref,
        sent_pool_ref,
        table_ref,
    ):
        onehot_pair(enc_grid_ref, enc_mesh_ref, spots, mesh_count, enc_pick_ref, enc_pool_ref)
        onehot_pair(dec_grid_ref, dec_mesh_ref, spots, mesh_count, dec_pick_ref, dec_pool_ref)
        enc_centred_ref[...] = centred(enc_second_ref[...], 1).astype(BF16)
        mesh_centred_ref[...] = centred(mesh_second_ref[...], 1).astype(BF16)
        sent_pool_ref[:slots, :] = dec_pool_ref[grid_count:spots, :]
        sent_pool_ref[slots:, :] = mm(
            select_ref[:slots, :], dec_pool_ref[:grid_count, :]
        ).astype(BF16)
        dec_centred_ref[...] = centred(dec_second_ref[...], 1).astype(BF16)
        nodes = nodes_ref[...]
        mesh_part_ref[...] = mm(mesh_ref[...], mesh_first_ref[low, :])
        table_ref[:grid_count, :] = mm(nodes, enc_first_ref[low, :]).astype(BF16)
        table_ref[grid_count:, :] = jnp.zeros((total - grid_count, feat), BF16)
        table_ref[mesh_rows, :] = mm(mesh_ref[...], enc_first_ref[high, :]).astype(BF16)
        enc_part_ref[...] = mm(enc_edges_ref[...], enc_first_ref[2 * feat :, :])
        enc_part_ref[...] += mm(enc_pick_ref[...], table_ref[...])
        pd = mm(nodes, dec_first_ref[low, :]).astype(BF16)
        dec_part_ref[...] = mm(dec_edges_ref[...], dec_first_ref[2 * feat :, :])
        dec_part_ref[...] += mm(dec_pick_ref[:, :grid_count], pd)

    (
        enc_part,
        dec_part,
        mesh_part,
        enc_pick,
        enc_pool,
        dec_pick,
        dec_pool,
        enc_centred,
        dec_centred,
        mesh_centred,
        sent_pool,
    ) = call(
        local,
        "local_products",
        [
            select,
            grid_nodes,
            mesh_nodes,
            enc_edges,
            dec_edges,
            enc_first,
            dec_first,
            mesh_first,
            enc_grid,
            enc_mesh,
            dec_grid,
            dec_mesh,
            enc_second,
            mesh_second,
            dec_second,
        ],
        [
            ((enc_count, feat), F32),
            ((dec_count, feat), F32),
            ((mesh_count, feat), F32),
            ((enc_count, total), BF16),
            ((total, enc_count), BF16),
            ((dec_count, total), BF16),
            ((total, dec_count), BF16),
        ]
        + [
            ((feat, feat), BF16),
            ((feat, feat), BF16),
            ((feat, feat), BF16),
            ((2 * slots, dec_count), BF16),
        ],
        scratch=[((total, feat), BF16)],
        flops=2 * feat * (feat * (2 * grid_count + enc_count + dec_count) + total * dec_count),
    )

    def forward(*refs):
        arrived_refs, refs = refs[:arrived_count], refs[arrived_count:]
        (
            sent_pool_ref,
            enc_part_ref,
            dec_part_ref,
            mesh_part_ref,
            enc_pick_ref,
            enc_pool_ref,
            dec_pick_ref,
            enc_wg_ref,
            dec_wg_ref,
            enc_w2_ref,
            mesh_wa_ref,
            mesh_w2_ref,
            mesh_ref,
            dec_wm_ref,
            dec_w2_ref,
        ) = refs[:15]
        refs = refs[15:]
        out_refs, refs = refs[:sent_count], refs[sent_count:]
        (
            slot_ref,
            enc_normed_ref,
            enc_scale_ref,
            enc_pre_ref,
            dec_normed_ref,
            dec_scale_ref,
            dec_pre_ref,
            mesh_normed_ref,
            mesh_scale_ref,
            mesh_pre_ref,
            enc_act_ref,
            dec_act_ref,
            mesh_act_ref,
            table_ref,
        ) = refs
        rows = by_slot(arrived_refs, low, staggered)
        pe = mm(rows, enc_wg_ref[low, :]).astype(BF16)
        enc_pre_ref[...] = enc_part_ref[...] + mm(enc_pick_ref[:, grid_count:spots], pe)
        write_silu(enc_pre_ref, enc_act_ref)
        write_norm(mm(enc_act_ref[...], enc_w2_ref[...]), enc_normed_ref, enc_scale_ref)
        agg = mm(enc_pool_ref[mesh_rows, :], enc_normed_ref[...]).astype(BF16)
        mesh_pre_ref[...] = mesh_part_ref[...] + mm(agg, mesh_wa_ref[high, :])
        write_silu(mesh_pre_ref, mesh_act_ref)
        write_norm(mm(mesh_act_ref[...], mesh_w2_ref[...]), mesh_normed_ref, mesh_scale_ref)
        mesh_out = (mesh_ref[...].astype(F32) + mesh_normed_ref[...]).astype(BF16)
        table_ref[:slots, :] = mm(rows, dec_wg_ref[low, :]).astype(BF16)
        table_ref[slots : slots + mesh_count, :] = mm(mesh_out, dec_wm_ref[high, :]).astype(BF16)
        table_ref[slots + mesh_count :, :] = jnp.zeros(
            (total - spots - mesh_count, feat), BF16
        )
        dec_pre_ref[...] = dec_part_ref[...] + mm(dec_pick_ref[:, grid_count:], table_ref[...])
        write_silu(dec_pre_ref, dec_act_ref)
        write_norm(mm(dec_act_ref[...], dec_w2_ref[...]), dec_normed_ref, dec_scale_ref)
        sums = mm(sent_pool_ref[...], dec_normed_ref[...])
        slot_ref[...] = sums[:slots, :]
        shared = sums[slots:, :].astype(BF16)
        slot_msg = sums[:slots, :].astype(BF16)
        send(
            out_refs, lambda j: slot_msg[reverse[j] * width : (reverse[j] + 1) * width, :], low
        )
        send(out_refs, lambda j: shared[j * width : (j + 1) * width, :], high)

    saved_shapes = [
        ((enc_count, feat), BF16),
        ((enc_count, 1), F32),
        ((enc_count, feat), F32),
        ((dec_count, feat), BF16),
        ((dec_count, 1), F32),
        ((dec_count, feat), F32),
        ((mesh_count, feat), F32),
        ((mesh_count, 1), F32),
        ((mesh_count, feat), F32),
    ]
    results = call(
        forward,
        "edges_forward",
        [
            *arrived,
            sent_pool,
            enc_part,
            dec_part,
            mesh_part,
            enc_pick,
            enc_pool,
            dec_pick,
            enc_first,
            dec_first,
            enc_centred,
            mesh_first,
            mesh_centred,
            mesh_nodes,
            dec_first,
            dec_centred,
        ],
        sent_shapes(2 * feat)
        + [((slots, feat), F32)]
        + saved_shapes,
        scratch=[
            ((enc_count, feat), BF16),
            ((dec_count, feat), BF16),
            ((mesh_count, feat), BF16),
            ((total - grid_count, feat), BF16),
        ],
        flops=2 * feat * feat * 2 * (enc_count + dec_count),
    )
    outgoing, results = results[:sent_count], results[sent_count:]
    slot_sums, *saved = results
    enc_normed, enc_scale, enc_pre, dec_normed, dec_scale, dec_pre = saved[:6]
    mesh_normed, mesh_scale, mesh_pre = saved[6:]
    returned = exchange(outgoing, steady)

    def between(*refs):
        arrived_refs, refs = refs[:arrived_count], refs[arrived_count:]
        (
            nodes_ref,
            grid_first_ref,
            grid_second_ref,
            cot_ref,
            mesh_first_ref,
            dec_pool_ref,
            dec_normed_ref,
            mesh_second_ref,
            mesh_centred_ref,
            dec_first_ref,
            mesh_cot_ref,
            mesh_ref,
            enc_pre_ref,
            dec_pre_ref,
            mesh_normed_ref,
            mesh_pre_ref,
            local_sums_ref,
            part_ref,
            cot_rows_ref,
            cot_turned_ref,
            grid_wide_ref,
            grid_back_ref,
            mesh_back_ref,
            mesh_in_ref,
            mesh_cot_turned_ref,
            mesh_turned_ref,
            mesh_out_ref,
            mesh_slope_ref,
            enc_slope_ref,
            dec_slope_ref,
        ) = refs
        part_ref[:grid_count, :] = mm(nodes_ref[...], grid_first_ref[low, :])
        part_ref[grid_count:, :] = mm(by_slot(arrived_refs, low, staggered), grid_first_ref[low, :])
        mesh_out_ref[...] = (mesh_ref[...].astype(F32) + mesh_normed_ref[...]).astype(BF16)
        cot_rows_ref[:grid_count, :] = cot_ref[...]
        cot_rows_ref[grid_count:, :] = by_slot(arrived_refs, high, staggered)
        second = centred(grid_second_ref[...], 1).astype(BF16)
        grid_wide_ref[:, low] = second
        grid_wide_ref[:, high] = mm_t(second, grid_second_ref[...]).astype(BF16)
        cot_turned_ref[...] = mm_t(cot_rows_ref[...], second)
        grid_back_ref[...] = centred(grid_first_ref[high, :], 0).astype(BF16)
        mesh_back_ref[...] = centred(mesh_first_ref[high, :], 0).astype(BF16)
        mesh_in_ref[low, :] = dec_first_ref[high, :]
        mesh_in_ref[high, :] = mm(mesh_centred_ref[...], dec_first_ref[high, :]).astype(BF16)
        mesh_cot_turned_ref[...] = mm_t(mesh_cot_ref[...], mesh_centred_ref[...])
        mesh_turned_ref[...] = mm_t(mesh_normed_ref[...].astype(BF16), mesh_second_ref[...])
        local_sums_ref[...] = mm(dec_pool_ref[:grid_count, :], dec_normed_ref[...])
        mesh_slope_ref[...] = silu_and_slope(mesh_pre_ref[...])[1]
        write_slope(enc_pre_ref, enc_slope_ref)
        write_slope(dec_pre_ref, dec_slope_ref)

    (
        local_sums,
        grid_part,
        cot_rows,
        cot_turned,
        grid_wide,
        grid_back,
        mesh_back,
        mesh_in,
        mesh_cot_turned,
        mesh_turned,
        mesh_out,
        mesh_slope,
        enc_slope,
        dec_slope,
    ) = call(
        between,
        "slopes_and_nodes",
        [
            *arrived,
            grid_nodes,
            grid_first,
            grid_second,
            grid_cot,
            mesh_first,
            dec_pool,
            dec_normed,
            mesh_second,
            mesh_centred,
            dec_first,
            mesh_cot,
            mesh_nodes,
            enc_pre,
            dec_pre,
            mesh_normed,
            mesh_pre,
        ],
        [
            ((grid_count, feat), F32),
            ((spots, feat), F32),
            ((spots, feat), BF16),
            ((spots, feat), F32),
            ((feat, 2 * feat), BF16),
            ((feat, feat), BF16),
            ((feat, feat), BF16),
            ((2 * feat, feat), BF16),
            ((mesh_count, feat), F32),
            ((mesh_count, feat), F32),
            ((mesh_count, feat), BF16),
            ((mesh_count, feat), F32),
            ((enc_count, feat), BF16),
            ((dec_count, feat), BF16),
        ],
        flops=16 * spots * feat * feat,
    )

    def backward(*refs):
        returned_refs, refs = refs[:arrived_count], refs[arrived_count:]
        (
            local_sums_ref,
            slot_sums_ref,
            grid_part_ref,
            select_t_ref,
            cot_rows_ref,
            cot_turned_ref,
            mesh_cot_ref,
            mesh_cot_turned_ref,
            enc_pick_ref,
            enc_pool_ref,
            dec_pick_ref,
            dec_pool_ref,
            grid_first_ref,
            grid_wide_ref,
            grid_back_ref,
            mesh_back_ref,
            mesh_in_ref,
            enc_first_ref,
            enc_second_ref,
            dec_first_ref,
            dec_second_ref,
            enc_normed_ref,
            enc_scale_ref,
            enc_slope_ref,
            dec_normed_ref,
            dec_scale_ref,
            dec_slope_ref,
            mesh_normed_ref,
            mesh_scale_ref,
            mesh_slope_ref,
            mesh_turned_ref,
        ) = refs[:31]
        refs = refs[31:]
        out_refs, refs = refs[:sent_count], refs[sent_count:]
        (
            grid_normed_ref,
            grid_gpre_ref,
            dec_gpre_ref,
            enc_gpre_ref,
            mesh_gin_ref,
            mesh_gpre_ref,
            agg_ref,
            grid_act_ref,
            grid_slope_ref,
            spot_grad_ref,
        ) = refs
        agg_ref[:grid_count, :] = (
            local_sums_ref[...] + mm(select_t_ref[:, :slots], by_row(returned_refs, low))
        ).astype(BF16)
        agg_ref[grid_count:, :] = (
            slot_sums_ref[...] + by_slot(returned_refs, high).astype(F32)
        ).astype(BF16)
        pre = grid_part_ref[...] + mm(agg_ref[...], grid_first_ref[high, :])
        for rows in row_chunks(spots):
            act, slope = silu_and_slope(pre[rows, :])
            grid_act_ref[rows, :] = act.astype(BF16)
            grid_slope_ref[rows, :] = slope
        both = mm(grid_act_ref[...], grid_wide_ref[...])
        for rows in row_chunks(spots):
            part = both[rows, low]
            scale_inv = scale_rows(part)
            normed = part * scale_inv
            grid_normed_ref[rows, :] = normed
            mean = jnp.mean(cot_rows_ref[rows, :].astype(F32) * normed, axis=-1, keepdims=True)
            raw = scale_inv * (cot_turned_ref[rows, :] - (mean * scale_inv) * both[rows, high])
            grid_gpre_ref[rows, :] = (raw * grid_slope_ref[rows, :]).astype(BF16)
        spot_grad_ref[:spots, :] = mm_t(grid_gpre_ref[...], grid_back_ref[...]).astype(BF16)
        spot_grad_ref[spots:, :] = jnp.zeros((total - spots, feat), BF16)
        edge_back(
            mm(dec_pick_ref[...], spot_grad_ref[...]),
            dec_normed_ref,
            dec_scale_ref,
            dec_second_ref,
            dec_slope_ref,
            dec_gpre_ref,
        )
        sums = mm(
            dec_pool_ref[grid_count : spots + mesh_count, :], dec_gpre_ref[...]
        ).astype(BF16)
        both = mm_t(sums[slots:, :], mesh_in_ref[...])
        mesh_gin = mesh_cot_ref[...].astype(F32) + both[:, low]
        mesh_gin_ref[...] = mesh_gin
        mean = jnp.mean(mesh_gin * mesh_normed_ref[...], axis=-1, keepdims=True)
        raw = mesh_cot_turned_ref[...] + both[:, high] - mean * mesh_turned_ref[...]
        mesh_gpre_ref[...] = (mesh_scale_ref[...] * raw * mesh_slope_ref[...]).astype(BF16)
        mesh_gagg = mm_t(mesh_gpre_ref[...], mesh_back_ref[...]).astype(BF16)
        slot_back = mm_t(sums[:slots, :], dec_first_ref[low, :])
        edge_back(
            mm(enc_pick_ref[:, mesh_rows], mesh_gagg),
            enc_normed_ref,
            enc_scale_ref,
            enc_second_ref,
            enc_slope_ref,
            enc_gpre_ref,
        )
        pooled = mm(enc_pool_ref[grid_count:spots, :], enc_gpre_ref[...]).astype(BF16)
        slot_back = (slot_back + mm_t(pooled, enc_first_ref[low, :])).astype(BF16)
        send(
            out_refs,
            lambda j: slot_back[reverse[j] * width : (reverse[j] + 1) * width, :],
            order=closing,
        )

    results = call(
        backward,
        "edges_backward",
        [
            *returned,
            local_sums,
            slot_sums,
            grid_part,
            select_t,
            cot_rows,
            cot_turned,
            mesh_cot,
            mesh_cot_turned,
            enc_pick,
            enc_pool,
            dec_pick,
            dec_pool,
            grid_first,
            grid_wide,
            grid_back,
            mesh_back,
            mesh_in,
            enc_first,
            enc_second,
            dec_first,
            dec_second,
            enc_normed,
            enc_scale,
            enc_slope,
            dec_normed,
            dec_scale,
            dec_slope,
            mesh_normed,
            mesh_scale,
            mesh_slope,
            mesh_turned,
        ],
        sent_shapes(feat, closing)
        + [
            ((spots, feat), F32),
            ((spots, feat), BF16),
            ((dec_count, feat), BF16),
            ((enc_count, feat), BF16),
            ((mesh_count, feat), F32),
            ((mesh_count, feat), BF16),
        ],
        scratch=[
            ((spots, feat), BF16),
            ((spots, feat), BF16),
            ((spots, feat), F32),
            ((total, feat), BF16),
        ],
        flops=2 * feat * feat * (4 * spots + 3 * dec_count + 2 * enc_count),
    )
    outgoing, results = results[:sent_count], results[sent_count:]
    grid_normed, grid_gpre, dec_gpre, enc_gpre, mesh_gin, mesh_gpre = results
    final = exchange(outgoing, closing)

    def tail(
        nodes_ref,
        grid_normed_ref,
        cot_ref,
        grid_gpre_ref,
        enc_pool_ref,
        enc_gpre_ref,
        dec_pool_ref,
        dec_gpre_ref,
        mesh_gin_ref,
        mesh_gpre_ref,
        grid_wn_ref,
        enc_wg_ref,
        dec_wg_ref,
        mesh_wn_ref,
        enc_wm_ref,
        base_ref,
        grad_mesh_ref,
        grid_out_ref,
    ):
        grid_out_ref[...] = (
            nodes_ref[...].astype(F32) + grid_normed_ref[:grid_count, :]
        ).astype(BF16)
        enc_sums = mm(enc_pool_ref[:grid_count, :], enc_gpre_ref[...]).astype(BF16)
        mesh_sums = mm(enc_pool_ref[mesh_rows, :], enc_gpre_ref[...]).astype(BF16)
        dec_sums = mm(dec_pool_ref[:grid_count, :], dec_gpre_ref[...]).astype(BF16)
        base_ref[...] = (
            cot_ref[...].astype(F32)
            + mm_t(grid_gpre_ref[:grid_count, :], grid_wn_ref[low, :])
            + mm_t(enc_sums, enc_wg_ref[low, :])
            + mm_t(dec_sums, dec_wg_ref[low, :])
        )
        grad_mesh_ref[...] = (
            mesh_gin_ref[...]
            + mm_t(mesh_gpre_ref[...], mesh_wn_ref[low, :])
            + mm_t(mesh_sums, enc_wm_ref[high, :])
        )

    base, grad_mesh, grid_out = call(
        tail,
        "local_gradients",
        [
            grid_nodes,
            grid_normed,
            grid_cot,
            grid_gpre,
            enc_pool,
            enc_gpre,
            dec_pool,
            dec_gpre,
            mesh_gin,
            mesh_gpre,
            grid_first,
            enc_first,
            dec_first,
            mesh_first,
            enc_first,
        ],
        [((grid_count, feat), F32), ((mesh_count, feat), F32), ((grid_count, feat), BF16)],
        flops=16 * spots * feat * feat,
    )

    pieces = row_chunks(grid_count, 64)

    def finish(*refs):
        back_refs = refs[:arrived_count]
        base_ref, select_t_ref, out_ref, piece_ref, semaphores = refs[arrived_count:]
        back = by_row(back_refs, order=closing)
        copies = []
        for place, rows in enumerate(pieces):
            piece_ref[rows, :] = base_ref[rows, :] + mm(select_t_ref[rows, :slots], back)
            copies.append(
                pltpu.make_async_copy(
                    piece_ref.at[rows, :], out_ref.at[rows, :], semaphores.at[place]
                )
            )
            copies[-1].start()
        for copy in copies:
            copy.wait()

    grad_grid = pl.pallas_call(
        finish,
        name="add_returned",
        in_specs=[pl.BlockSpec(memory_space=pltpu.VMEM)] * (arrived_count + 2),
        out_specs=pl.BlockSpec(memory_space=pltpu.HBM),
        out_shape=jax.ShapeDtypeStruct((grid_count, feat), F32),
        scratch_shapes=[
            pltpu.VMEM((grid_count, feat), F32),
            pltpu.SemaphoreType.DMA((len(pieces),)),
        ],
        compiler_params=pltpu.CompilerParams(vmem_limit_bytes=VMEM_LIMIT),
    )(*final, base, select_t)
    return (grid_out, mesh_out, grad_grid, grad_mesh)


def solution(mesh):
    rows = P(("groups", "tile"), None)
    flat = P(("groups", "tile"))
    in_specs = (rows,) * 6 + (P(),) * 8 + (rows,) + (flat,) * 5
    return jax.shard_map(
        per_device, mesh=mesh, in_specs=in_specs, out_specs=(rows,) * 4, check_vma=False
    )
```
